32 devices in a mesh: wide: 8 (over z, y), narrow: 4 (over x, core).
Axes of the slice: x: 2, y: 2, z: 4, core: 2. Of those that a mesh axis runs over, the one named last changes fastest.
Arguments:
- tokens: bfloat16 [64, 512, 768], P(('wide', 'narrow')), may hold values from -18 to 18
- mask_place: int32 [64, 76], P(('wide', 'narrow')), may hold values from 0 to 511, as said below
- mask_count: int32 [64], P(('wide', 'narrow')), may hold values from 38 to 76, as said below
- masked_output_gradient: bfloat16 [64, 76, 768], P(('wide', 'narrow')), may hold values from -6 to 6
- query_key_value_weight: float32 [3, 768, 768], P(None, 'wide'), may hold values from -0.15625 to 0.15625
- qkv_first: float32 [3, 768, 768], P(None, 'wide'), may hold values from -0.00061035156 to 0.00061035156
- qkv_second: float32 [3, 768, 768], P(None, 'wide'), may hold values from 1.4110135e-10 to 5.644054e-10
- out_weight: float32 [768, 768], P(None, 'wide'), may hold values from -1.25 to 1.25
- out_first: float32 [768, 768], P(None, 'wide'), may hold values from -0.00061035156 to 0.00061035156
- out_second: float32 [768, 768], P(None, 'wide'), may hold values from 1.4110135e-10 to 5.644054e-10
- up_weight: float32 [768, 3072], P('wide'), may hold values from -0.21875 to 0.21875
- up_first: float32 [768, 3072], P('wide'), may hold values from -0.00061035156 to 0.00061035156
- up_second: float32 [768, 3072], P('wide'), may hold values from 1.4110135e-10 to 5.644054e-10
- down_weight: float32 [3072, 768], P(None, 'wide'), may hold values from -0.109375 to 0.109375
- down_first: float32 [3072, 768], P(None, 'wide'), may hold values from -0.00061035156 to 0.00061035156
- down_second_moment: float32 [3072, 768], P(None, 'wide'), may hold values from 1.4110135e-10 to 5.644054e-10
- vectors: float32 [8, 768], P(None, 'wide'), may hold values from -1 to 3
- vectors_first: float32 [8, 768], P(None, 'wide'), may hold values from -0.00061035156 to 0.00061035156
- vectors_second: float32 [8, 768], P(None, 'wide'), may hold values from 1.4110135e-10 to 5.644054e-10
- up_bias: float32 [3072], P('wide'), may hold values from -3 to 3
- up_bias_first: float32 [3072], P('wide'), may hold values from -0.00061035156 to 0.00061035156
- up_bias_second: float32 [3072], P('wide'), may hold values from 1.4110135e-10 to 5.644054e-10
Outputs:
- layer_out: bfloat16 [64, 512, 768], P(('wide', 'narrow'))
- tokens_grad: float32 [64, 512, 768], P(('wide', 'narrow'))
- grad_norm: float32 [], replicated
- qkv_new: float32 [3, 768, 768], P(None, 'wide')
- qkv_first_new: float32 [3, 768, 768], P(None, 'wide')
- qkv_second_new: float32 [3, 768, 768], P(None, 'wide')
- out_new: float32 [768, 768], P(None, 'wide')
- out_first_new: float32 [768, 768], P(None, 'wide')
- out_second_new: float32 [768, 768], P(None, 'wide')
- up_new: float32 [768, 3072], P('wide')
- up_first_new: float32 [768, 3072], P('wide')
- up_second_new: float32 [768, 3072], P('wide')
- down_new: float32 [3072, 768], P(None, 'wide')
- down_first_new: float32 [3072, 768], P(None, 'wide')
- down_second_new: float32 [3072, 768], P(None, 'wide')
- updated_gain_vectors: float32 [8, 768], P(None, 'wide')
- vectors_first_new: float32 [8, 768], P(None, 'wide')
- vectors_second_new: float32 [8, 768], P(None, 'wide')
- up_bias_new: float32 [3072], P('wide')
- up_bias_first_new: float32 [3072], P('wide')
- up_bias_second_new: float32 [3072], P('wide')
The draws below stay inside these ranges and needn't reach their ends.
Inputs may be any that keep to these rules, and one draw needn't show every extreme that they name: `mask_place`: the positions of one row are distinct; slots at and past the row's count are padding and carry no gradient. `mask_count`: some sequence uses all 76 slots.
All inputs are finite; a program needn't handle non-finite values.
Results may differ from the reference program's by a relative error of at most 0.02.
Values may be sent and summed in bfloat16 or wider, within the bound.
A program may use at most 256 MiB of HBM per device.

```python
import math
import jax
import jax.numpy as jnp
from jax import lax

D = 768
HEADS = 12
HEAD_DIM = 64
FF = 3072
LEN = 512
STEP = 10
SEQS = 64
MASK_MOST = 76
NPARAM = 7087104


def draw_tokens(key, part):
    key = jax.random.fold_in(key, 11)
    ramp = jnp.arange(D, dtype=jnp.float32) / (D - 1)
    base = jnp.clip(jax.random.normal(key, (SEQS, LEN, D), jnp.float32), -6.0, 6.0)
    scales = 3.0 ** ramp
    return (base * scales[None, None, :]).astype(jnp.bfloat16)


def draw_vectors(key, part):
    key = jax.random.fold_in(key, 12)
    ramp = jnp.arange(D, dtype=jnp.float32) / (D - 1)
    first_key, second_key = jax.random.split(key)
    spread = 0.3 * jnp.clip(jax.random.normal(first_key, (8, D), jnp.float32), -3.0, 3.0)
    rising = 0.6 * 3.0 ** ramp
    jitter = jax.random.uniform(second_key, (8, D), jnp.float32, 0.85, 1.15)
    rows = jnp.arange(8)
    is_gain = (rows == 3) | (rows == 6)
    return jnp.where(is_gain[:, None], rising[None, :] * jitter, spread)


def pick_places(row_key):
    return jax.random.permutation(row_key, LEN)[:MASK_MOST]


def draw_mask_place(key, part):
    key = jax.random.fold_in(key, 13)
    row_keys = jax.random.split(key, SEQS)
    return jax.vmap(pick_places)(row_keys).astype(jnp.int32)


def draw_mask_count(key, part):
    key = jax.random.fold_in(key, 14)
    first_key, second_key = jax.random.split(key)
    counts = jax.random.randint(first_key, (SEQS,), (MASK_MOST + 1) // 2, MASK_MOST + 1)
    fullest = jax.random.randint(second_key, (), 0, SEQS)
    return counts.at[fullest].set(MASK_MOST).astype(jnp.int32)


def shard_levels(key, dims, shards, smallest, largest):
    def one(dim, shards_of):
        steps = jax.random.uniform(jax.random.fold_in(jax.random.fold_in(key, 6), dim), (shards_of,), jnp.float32, smallest / len(shards), largest / len(shards))
        return jnp.repeat(jnp.exp(steps), dims[dim] // shards_of).reshape((-1,) + (1,) * (len(dims) - dim - 1))

    level = one(*shards[0])
    for cut in shards[1:]:
        level = level * one(*cut)
    return level


def normal_values(rng, dims, deviation, reach, pieces=(), held_as=jnp.bfloat16):
    result = jax.random.normal(rng, dims, jnp.float32) * deviation
    if len(pieces) > 0:
        result = shard_levels(rng, dims, pieces, -0.22, 0.18) * result
    return jnp.clip(result, min=-reach, max=reach).astype(held_as)


def setup_inputs(seed: int = 0) -> dict:
    streams_of = jax.random.split(jax.random.key(seed), 23)
    return {
        "tokens": draw_tokens(jax.random.fold_in(streams_of[22], 71), 0),
        "mask_place": draw_mask_place(jax.random.fold_in(streams_of[22], 71), 0),
        "mask_count": draw_mask_count(jax.random.fold_in(streams_of[22], 71), 0),
        "masked_output_gradient": normal_values(streams_of[3], (SEQS, MASK_MOST, D), 1.0, 6.0, ((0, 32),)),
        "query_key_value_weight": normal_values(streams_of[4], (3, D, D), (2 * D) ** -0.5, 0.15625, ((1, 8),), jnp.float32),
        "qkv_first": normal_values(streams_of[5], (3, D, D), (0.11 / NPARAM ** 0.5), 0.00061035156, ((1, 8),), jnp.float32),
        "qkv_second": jnp.clip(jnp.exp(math.log(5.644054112963204e-10) - 1.3862944 * jax.random.uniform(streams_of[6], (3, D, D), jnp.float32) ** shard_levels(streams_of[6], (3, D, D), ((1, 8),), -0.2, 0.2)), 1.411013528240801e-10, 5.644054112963204e-10),
        "out_weight": normal_values(streams_of[7], (D, D), (max(1, D * 16 // LEN)) ** -0.5, 1.25, ((1, 8),), jnp.float32),
        "out_first": normal_values(streams_of[8], (D, D), (0.11 / NPARAM ** 0.5), 0.00061035156, ((1, 8),), jnp.float32),
        "out_second": jnp.clip(jnp.exp(math.log(5.644054112963204e-10) - 1.3862944 * jax.random.uniform(streams_of[9], (D, D), jnp.float32) ** shard_levels(streams_of[9], (D, D), ((1, 8),), -0.2, 0.2)), 1.411013528240801e-10, 5.644054112963204e-10),
        "up_weight": normal_values(streams_of[10], (D, FF), D ** -0.5, 0.21875, ((0, 8),), jnp.float32),
        "up_first": normal_values(streams_of[11], (D, FF), (0.11 / NPARAM ** 0.5), 0.00061035156, ((0, 8),), jnp.float32),
        "up_second": jnp.clip(jnp.exp(math.log(5.644054112963204e-10) - 1.3862944 * jax.random.uniform(streams_of[12], (D, FF), jnp.float32) ** shard_levels(streams_of[12], (D, FF), ((0, 8),), -0.2, 0.2)), 1.411013528240801e-10, 5.644054112963204e-10),
        "down_weight": normal_values(streams_of[13], (FF, D), FF ** -0.5, 0.109375, ((1, 8),), jnp.float32),
        "down_first": normal_values(streams_of[14], (FF, D), (0.11 / NPARAM ** 0.5), 0.00061035156, ((1, 8),), jnp.float32),
        "down_second_moment": jnp.clip(jnp.exp(math.log(5.644054112963204e-10) - 1.3862944 * jax.random.uniform(streams_of[15], (FF, D), jnp.float32) ** shard_levels(streams_of[15], (FF, D), ((1, 8),), -0.2, 0.2)), 1.411013528240801e-10, 5.644054112963204e-10),
        "vectors": draw_vectors(jax.random.fold_in(streams_of[22], 71), 0),
        "vectors_first": normal_values(streams_of[17], (8, D), (0.11 / NPARAM ** 0.5), 0.00061035156, ((1, 8),), jnp.float32),
        "vectors_second": jnp.clip(jnp.exp(math.log(5.644054112963204e-10) - 1.3862944 * jax.random.uniform(streams_of[18], (8, D), jnp.float32) ** shard_levels(streams_of[18], (8, D), ((1, 8),), -0.2, 0.2)), 1.411013528240801e-10, 5.644054112963204e-10),
        "up_bias": normal_values(streams_of[19], (FF,), 0.3, 3.0, ((0, 8),), jnp.float32),
        "up_bias_first": normal_values(streams_of[20], (FF,), (0.11 / NPARAM ** 0.5), 0.00061035156, ((0, 8),), jnp.float32),
        "up_bias_second": jnp.clip(jnp.exp(math.log(5.644054112963204e-10) - 1.3862944 * jax.random.uniform(streams_of[21], (FF,), jnp.float32) ** shard_levels(streams_of[21], (FF,), ((0, 8),), -0.2, 0.2)), 1.411013528240801e-10, 5.644054112963204e-10),
    }


@jax.custom_vjp
def low(v):
    return lax.optimization_barrier(v.astype(jnp.bfloat16)).astype(jnp.float32)

@jax.custom_vjp
def low_back(v):
    return v

def low_keep(v):
    return (low(v), None)

def low_pass(kept, grad):
    return (grad,)

def back_keep(v):
    return (v, None)

def back_low(kept, grad):
    return (low(grad),)
low.defvjp(low_keep, low_pass)
low_back.defvjp(back_keep, back_low)
HIGHEST = lax.Precision.HIGHEST
LN_EPS = 1e-06
SQRT_HALF = 0.7071067811865476
CLIP_LIMIT = 1.0
BETA_ONE = 0.9
BETA_TWO = 0.999
LEARN_RATE = 0.05
OUTPUT_RATE = 0.2
VECTOR_RATE = 0.5
BIAS_RATE = 0.3
DECAY_RATE = 0.01
ADAM_EPS = 1e-08

def layer_norm(values, gain, shift):
    center = values - lax.optimization_barrier(jnp.mean(values, axis=-1, keepdims=True))
    inverse = lax.rsqrt(lax.optimization_barrier(jnp.mean(center * center, axis=-1, keepdims=True)) + LN_EPS)
    return center * inverse * gain + shift

def forward(inputs, qkv_w, out_w, up_w, down_w, vec_w, bias_weight_slot):
    qkv_low = low(qkv_w)
    out_low = low(out_w)
    up_low = low(up_w)
    down_low = low(down_w)
    vec_low = low(vec_w)
    bias_low = low(bias_weight_slot)
    group = math.gcd(SEQS, max(1, 4096 // LEN))
    scale = HEAD_DIM ** (-0.5)

    def block(rows):
        proj = jnp.einsum('gtd,kde->kgte', rows, qkv_low, precision=HIGHEST)
        query = low(low_back(proj[0]) + vec_low[0]).reshape(group, LEN, HEADS, HEAD_DIM)
        key = low(low_back(proj[1])).reshape(group, LEN, HEADS, HEAD_DIM)
        value = low(low_back(proj[2]) + vec_low[1]).reshape(group, LEN, HEADS, HEAD_DIM)
        raw = low_back(jnp.einsum('gqhe,gkhe->ghqk', query, key, precision=HIGHEST))
        probs = low(jax.nn.softmax(raw * scale, axis=-1))
        mixed = jnp.einsum('ghqk,gkhe->gqhe', probs, value, precision=HIGHEST).reshape(group, LEN, D)
        mixed = low_back(low(mixed))
        pre_one = rows + (low_back(jnp.einsum('gte,ed->gtd', mixed, out_low, precision=HIGHEST)) + vec_low[2])
        hidden = layer_norm(pre_one, vec_low[3], vec_low[4])
        upper = low_back(jnp.einsum('gtd,df->gtf', low(hidden), up_low, precision=HIGHEST)) + bias_low
        active = low(upper * (0.5 * (1.0 + lax.erf(upper * SQRT_HALF))))
        pre_two = hidden + (low_back(jnp.einsum('gtf,fd->gtd', active, down_low, precision=HIGHEST)) + vec_low[5])
        return layer_norm(pre_two, vec_low[6], vec_low[7])
    stacked = inputs.reshape(SEQS // group, group, LEN, D)
    return lax.map(jax.checkpoint(block), stacked).reshape(SEQS, LEN, D)

def adam_step(weight, first, second, grad, factor, decay, rate):
    grad = grad * factor
    first_new = BETA_ONE * first + (1.0 - BETA_ONE) * grad
    second_new = BETA_TWO * second + (1.0 - BETA_TWO) * grad * grad
    mean_hat = first_new / (1.0 - BETA_ONE ** STEP)
    square_hat = second_new / (1.0 - BETA_TWO ** STEP)
    weight_new = weight - rate * (mean_hat / (jnp.sqrt(square_hat) + ADAM_EPS) + decay * weight)
    return (weight_new, first_new, second_new)

def place_rows(masked_positions, values):
    return jnp.zeros((LEN, D), jnp.float32).at[masked_positions].add(values)

def reference(tokens, mask_place, mask_count, masked_output_gradient, query_key_value_weight, qkv_first, qkv_second, out_weight, out_first, out_second, up_weight, up_first, up_second, down_weight, down_first, down_second_moment, vectors, vectors_first, vectors_second, up_bias, up_bias_first, up_bias_second):
    inputs = tokens.astype(jnp.float32)
    layer_result, pullback = jax.vjp(forward, inputs, query_key_value_weight, out_weight, up_weight, down_weight, vectors, up_bias)
    valid = (jnp.arange(MASK_MOST)[None, :] < mask_count[:, None]).astype(jnp.float32)
    values = masked_output_gradient.astype(jnp.float32) * valid[:, :, None]
    cotangent = jax.vmap(place_rows)(mask_place, values)
    dinputs, dqkv, dout, dup, ddown, dvectors, dbias = pullback(cotangent)
    squares = jnp.sum(dqkv * dqkv) + jnp.sum(dout * dout) + jnp.sum(dup * dup) + jnp.sum(ddown * ddown) + jnp.sum(dvectors * dvectors) + jnp.sum(dbias * dbias)
    grad_norm = jnp.sqrt(squares)
    factor = CLIP_LIMIT / jnp.maximum(grad_norm, CLIP_LIMIT)
    qkv_n, qkv_m, qkv_v = adam_step(query_key_value_weight, qkv_first, qkv_second, dqkv, factor, DECAY_RATE, LEARN_RATE)
    out_n, out_m, out_v = adam_step(out_weight, out_first, out_second, dout, factor, DECAY_RATE, OUTPUT_RATE)
    up_n, up_m, up_v = adam_step(up_weight, up_first, up_second, dup, factor, DECAY_RATE, LEARN_RATE)
    down_n, down_m, down_v = adam_step(down_weight, down_first, down_second_moment, ddown, factor, DECAY_RATE, LEARN_RATE)
    vec_n, vec_m, vec_v = adam_step(vectors, vectors_first, vectors_second, dvectors, factor, 0.0, VECTOR_RATE)
    bias_n, bias_m, bias_v = adam_step(up_bias, up_bias_first, up_bias_second, dbias, factor, 0.0, BIAS_RATE)
    return (layer_result.astype(jnp.bfloat16), dinputs, grad_norm, qkv_n, qkv_m, qkv_v, out_n, out_m, out_v, up_n, up_m, up_v, down_n, down_m, down_v, vec_n, vec_m, vec_v, bias_n, bias_m, bias_v)
```

```python
import functools

import jax
import jax.numpy as jnp
from jax import lax
from jax.experimental import pallas as pl
from jax.experimental.pallas import tpu as pltpu
from jax.sharding import PartitionSpec as P

HEADS = 12
HEAD_DIM = 64
STEP = 10

LN_EPS = 1e-06
SQRT_HALF = 0.7071067811865476
INV_ROOT_TWO_PI = 0.3989422804014327
CLIP_LIMIT = 1.0
BETA_ONE = 0.9
BETA_TWO = 0.999
LEARN_RATE = 0.05
OUTPUT_RATE = 0.2
VECTOR_RATE = 0.5
BIAS_RATE = 0.3
DECAY_RATE = 0.01
ADAM_EPS = 1e-08

MESH = pl.DeviceIdType.MESH


def when(cond, body):
    if cond is None:
        body()
    else:
        pl.when(cond)(body)


class Sends:
    def __init__(self):
        self.started = []

    def start(self, cond, make):
        when(cond, lambda: make().start())
        self.started.append((cond, make))

    def finish(self):
        for cond, make in self.started:
            when(cond, lambda make=make: make().wait_send())


def both(a, b):
    return b if a is None else (a if b is None else jnp.logical_and(a, b))


def place():
    w, n = lax.axis_index("wide"), lax.axis_index("narrow")
    return w // 2, lax.rem(w, 2), n // 2, lax.rem(n, 2)


def flip(v):
    return 1 - v


def dev(z, y, x, c):
    return (z * 2 + y, x * 2 + c)


def meet(z, y, x, c, diagonal):
    bar = pltpu.get_barrier_semaphore()
    peers = [(None, dev(z, flip(y), x, c)), (None, dev(z, y, flip(x), c)), (None, dev(z, y, x, flip(c)))]
    if diagonal:
        peers.append((None, dev(z, y, flip(x), flip(c))))
    peers += [(z > 0, dev(z - 1, y, x, c)), (z < 3, dev(z + 1, y, x, c))]
    for cond, peer in peers:
        when(cond, lambda peer=peer: pl.semaphore_signal(bar, inc=1, device_id=peer, device_id_type=MESH))
    inner = jnp.logical_and(z > 0, z < 3)
    count = 4 if diagonal else 3
    pl.semaphore_wait(bar, count + 1 + jnp.where(inner, 1, 0))


def gather_kernel(rows, cols, attn, up, down, small, attn_full, up_full, down_full, small_full, send_sem, recv_sem, small_send, small_recv, own_sem):
    z, y, x, c = place()
    edge = x == c
    third = cols // 3
    mine, across = x + c, 2 * flip(x)
    fulls = (attn_full, up_full, down_full)
    shards = (attn, up, down)
    sends = Sends()
    zl, zh = z > 0, z < 3

    def spot(p, zz, yy, t):
        return fulls[p].at[pl.ds(pl.multiple_of((zz * 2 + yy) * rows, rows), rows), pl.ds(pl.multiple_of(t * third, third), third)]

    def push(cond, p, zz, yy, t, kind, to, src=None):
        def make():
            w = zz * 2 + yy
            where = spot(p, zz, yy, t)
            return pltpu.make_async_remote_copy(
                src_ref=where if src is None else src,
                dst_ref=where,
                send_sem=send_sem.at[kind, p, w],
                recv_sem=recv_sem.at[p, w, t],
                device_id=to,
                device_id_type=MESH,
            )

        sends.start(cond, make)

    def small_push(cond, zz, yy, kind, to, src=None):
        def make():
            w = zz * 2 + yy
            where = small_full.at[w]
            return pltpu.make_async_remote_copy(
                src_ref=where if src is None else src,
                dst_ref=where,
                send_sem=small_send.at[kind, w],
                recv_sem=small_recv.at[w],
                device_id=to,
                device_id_type=MESH,
            )

        sends.start(cond, make)

    def arrive(cond, p, zz, yy, t):
        def body():
            where = spot(p, zz, yy, t)
            w = zz * 2 + yy
            pltpu.make_async_remote_copy(where, where, send_sem.at[0, p, w], recv_sem.at[p, w, t], dev(z, y, x, c), device_id_type=MESH).wait_recv()

        when(cond, body)

    def small_arrive(cond, zz, yy):
        def body():
            w = zz * 2 + yy
            pltpu.make_async_remote_copy(small_full.at[w], small_full.at[w], small_send.at[0, w], small_recv.at[w], dev(z, y, x, c), device_id_type=MESH).wait_recv()

        when(cond, body)

    UP, DOWN, SIDE, OVER, NEAR, PASS = range(6)
    above, below, beside = dev(z + 1, y, x, c), dev(z - 1, y, x, c), dev(z, flip(y), x, c)
    over, near = dev(z, y, flip(x), c), dev(z, y, x, flip(c))

    def own(p):
        src = shards[p].at[:, pl.ds(pl.multiple_of(mine * third, third), third)]
        push(zh, p, z, y, mine, UP, above, src)
        push(zl, p, z, y, mine, DOWN, below, src)
        push(None, p, z, y, mine, SIDE, beside, src)

    def z_step(p, d):
        for cond, zz, onward, kind, to in ((z - d >= 0, z - d, zh, UP, above), (z + d <= 3, z + d, zl, DOWN, below)):
            arrive(cond, p, zz, y, mine)
            push(both(cond, onward), p, zz, y, mine, kind, to)
            push(cond, p, zz, y, mine, SIDE, beside)
            push(both(cond, edge), p, zz, y, mine, OVER, over)
            push(cond, p, zz, y, mine, NEAR, near)

    def y_step(p, d):
        steps = ((None, z),) if d == 0 else ((z - d >= 0, z - d), (z + d <= 3, z + d))
        for cond, zz in steps:
            arrive(cond, p, zz, flip(y), mine)
            push(both(cond, edge), p, zz, flip(y), mine, OVER, over)
            push(cond, p, zz, flip(y), mine, NEAR, near)

    def x_step(p, d):
        mid = jnp.logical_not(edge)
        for yy in (y, flip(y)):
            if d == 0:
                steps = () if yy is y else ((None, z),)
            else:
                steps = ((z - d >= 0, z - d), (z + d <= 3, z + d))
            for cond, zz in steps:
                cond = both(cond, mid)
                arrive(cond, p, zz, yy, across)
                push(cond, p, zz, yy, across, PASS, near)

    def last(p, d):
        for yy in (y, flip(y)):
            if d == 0:
                steps = () if yy is y else ((None, z),)
            else:
                steps = ((z - d >= 0, z - d), (z + d <= 3, z + d))
            for cond, zz in steps:
                arrive(cond, p, zz, yy, x + flip(c))
                arrive(both(cond, edge), p, zz, yy, across)

    def small_z(d):
        for cond, zz, onward, kind, to in ((z - d >= 0, z - d, zh, UP, above), (z + d <= 3, z + d, zl, DOWN, below)):
            small_arrive(cond, zz, y)
            small_push(both(cond, onward), zz, y, kind, to)
            small_push(cond, zz, y, SIDE, beside)

    meet(z, y, x, c, False)
    small_push(zh, z, y, UP, above, small)
    small_push(zl, z, y, DOWN, below, small)
    small_push(None, z, y, SIDE, beside, small)
    own(0)
    w = z * 2 + y
    copies = []
    for p in range(3):
        copies.append(pltpu.make_async_copy(shards[p], fulls[p].at[pl.ds(pl.multiple_of(w * rows, rows), rows)], own_sem.at[p]))
    copies.append(pltpu.make_async_copy(small, small_full.at[w], own_sem.at[3]))
    for copy in copies:
        copy.start()
    for d in range(1, 4):
        small_z(d)
    order = [
        lambda: z_step(0, 1), lambda: own(1), lambda: y_step(0, 0), lambda: z_step(0, 2), lambda: y_step(0, 1), lambda: x_step(0, 0), lambda: z_step(0, 3),
        lambda: y_step(0, 2), lambda: x_step(0, 1), lambda: z_step(1, 1), lambda: own(2), lambda: y_step(0, 3), lambda: x_step(0, 2), lambda: z_step(1, 2), lambda: y_step(1, 0), lambda: x_step(0, 3), lambda: z_step(1, 3),
        lambda: y_step(1, 1), lambda: x_step(1, 0), lambda: z_step(2, 1), lambda: y_step(1, 2), lambda: x_step(1, 1), lambda: z_step(2, 2), lambda: y_step(1, 3), lambda: x_step(1, 2), lambda: z_step(2, 3),
        lambda: y_step(2, 0), lambda: x_step(1, 3), lambda: y_step(2, 1), lambda: x_step(2, 0), lambda: y_step(2, 2), lambda: x_step(2, 1), lambda: y_step(2, 3), lambda: x_step(2, 2), lambda: x_step(2, 3),
    ]
    for step in order:
        step()
    for d in range(4):
        for cond, zz in (((None, z),) if d == 0 else ((z - d >= 0, z - d), (z + d <= 3, z + d))):
            small_arrive(cond, zz, flip(y))
    for p in range(3):
        for d in range(4):
            last(p, d)
    sends.finish()
    for copy in copies:
        copy.wait()


def gather(attn, up, down, small):
    rows, cols = attn.shape
    full = jax.ShapeDtypeStruct((8 * rows, cols), attn.dtype)
    anywhere = pl.BlockSpec(memory_space=pl.ANY)
    return pl.pallas_call(
        functools.partial(gather_kernel, rows, cols),
        out_shape=(full, full, full, jax.ShapeDtypeStruct((8,) + small.shape, small.dtype)),
        in_specs=[anywhere] * 4,
        out_specs=(anywhere,) * 4,
        scratch_shapes=[
            pltpu.SemaphoreType.DMA((6, 3, 8)),
            pltpu.SemaphoreType.DMA((3, 8, 3)),
            pltpu.SemaphoreType.DMA((3, 8)),
            pltpu.SemaphoreType.DMA((8,)),
            pltpu.SemaphoreType.DMA((4,)),
        ],
        compiler_params=pltpu.CompilerParams(collective_id=0, has_side_effects=True),
    )(attn, up, down, small)


E = 768
M = 1536
SLAB = 32
ORDER = (3, 0, 2, 1)


def slabs(rows, body):
    @pl.loop(0, rows // SLAB)
    def _(i):
        body(pl.ds(pl.multiple_of(i * SLAB, SLAB), SLAB))


def f32(v):
    return v.astype(jnp.float32)


def reduce_kernel(rows, g_a, g_b, g_c, small, out, small_out, sib, xs, xr, acc, yr, zu, zd, mr,
                  sib_s, sib_r, x_s, x_r, y_s, y_r, z_s, z_r, m_s, m_r, f_s, f_r,
                  ssib, sx, sy, szu, szd, sacc, sm_s, sm_r, phases=3):
    z, y, x, c = place()
    edge = x == c
    mid = jnp.logical_not(edge)
    grads = (g_a, g_b, g_c)
    sends = Sends()
    me = dev(z, y, x, c)
    above, below, beside = dev(z + 1, y, x, c), dev(z - 1, y, x, c), dev(z, flip(y), x, c)
    over, near, diag = dev(z, y, flip(x), c), dev(z, y, x, flip(c)), dev(z, y, flip(x), flip(c))
    ecol = pl.multiple_of(x * 2304, 768)
    pair = rows * 2

    def zrows(zz):
        return pl.ds(zz * pair, pair)

    def wrows(zz, yy):
        return pl.ds(pl.multiple_of((zz * 2 + yy) * rows, rows), rows)

    def copy(src, dst, ss, rs, to):
        return pltpu.make_async_remote_copy(src_ref=src, dst_ref=dst, send_sem=ss, recv_sem=rs, device_id=to, device_id_type=MESH)

    def wait(cond, dst, rs):
        when(cond, lambda: copy(dst, dst, rs, rs, me).wait_recv())

    meet(z, y, x, c, True)

    for p in range(phases):
        for zz in ORDER:
            sends.start(edge, lambda p=p, zz=zz: copy(
                grads[p].at[zrows(zz), pl.ds(pl.multiple_of(768 * flip(x), 768), 2304)], sib.at[p, zrows(zz)], sib_s.at[p, zz], sib_r.at[p, zz], near))
            sends.start(mid, lambda p=p, zz=zz: copy(
                grads[p].at[zrows(zz), pl.ds(ecol, E)], sib.at[p, zrows(zz), pl.ds(0, E)], sib_s.at[p, zz], sib_r.at[p, zz], near))

    sends.start(None, lambda: copy(small, ssib, sm_s.at[0], sm_r.at[0], near))
    wait(None, ssib, sm_r.at[0])
    sacc[...] = small[...] + ssib[...]
    sends.start(None, lambda: copy(sacc, sx, sm_s.at[1], sm_r.at[1], over))

    moff = 768 * x
    ooff = 1536 * flip(x)

    def first(p, zz):
        @pl.when(mid)
        def _():
            wait(None, sib.at[p, zrows(zz)], sib_r.at[p, zz])

            def one(r):
                r = pl.ds(zz * pair + r.start, SLAB)
                xs[p, r, :] = (f32(grads[p][r, pl.ds(pl.multiple_of(2304 * flip(x), 768), E)]) + f32(sib[p, r, pl.ds(pl.multiple_of(ooff, 768), E)])).astype(jnp.bfloat16)
                acc[p, r, :] = (f32(grads[p][r, pl.ds(768, M)]) + f32(sib[p, r, pl.ds(pl.multiple_of(moff, 768), M)])).astype(jnp.bfloat16)

            slabs(pair, one)

        sends.start(mid, lambda: copy(xs.at[p, zrows(zz)], xr.at[p, zrows(zz)], x_s.at[p, zz], x_r.at[p, zz], over))

        @pl.when(edge)
        def _():
            wait(None, sib.at[p, zrows(zz), pl.ds(0, E)], sib_r.at[p, zz])
            wait(None, xr.at[p, zrows(zz)], x_r.at[p, zz])

            def one(r):
                r = pl.ds(zz * pair + r.start, SLAB)
                acc[p, r, pl.ds(0, E)] = (f32(grads[p][r, pl.ds(ecol, E)]) + f32(sib[p, r, pl.ds(0, E)]) + f32(xr[p, r, :])).astype(jnp.bfloat16)

            slabs(pair, one)

        for cond, width in ((edge, E), (mid, M)):
            sends.start(cond, lambda width=width: copy(
                acc.at[p, wrows(zz, flip(y)), pl.ds(0, width)], yr.at[p, zz, :, pl.ds(0, width)], y_s.at[p, zz], y_r.at[p, zz], beside))

    def add_into(cond, p, zz, buffer, sem):
        for role, width in ((edge, E), (mid, M)):
            @pl.when(both(cond, role))
            def _():
                wait(None, buffer.at[p, zz, :, pl.ds(0, width)], sem)
                base = (zz * 2 + y) * rows

                def one(r):
                    here = pl.ds(pl.multiple_of(base + r.start, SLAB), SLAB)
                    acc[p, here, pl.ds(0, width)] = (f32(acc[p, here, pl.ds(0, width)]) + f32(buffer[p, zz, r, pl.ds(0, width)])).astype(jnp.bfloat16)

                slabs(rows, one)

    def z_push(cond, p, zz, buffer, k, to):
        for role, width in ((edge, E), (mid, M)):
            sends.start(both(cond, role), lambda width=width: copy(
                acc.at[p, wrows(zz, y), pl.ds(0, width)], buffer.at[p, zz, :, pl.ds(0, width)], z_s.at[k, p, zz], z_r.at[k, p, zz], to))

    def second(p, zz):
        add_into(None, p, zz, yr, y_r.at[p, zz])

    def line(p, t):
        up = both(z <= t, z < 3)
        zz = jnp.where(up, 3 + z - t, 0)
        add_into(both(up, z > 0), p, zz, zu, z_r.at[0, p, zz])
        z_push(up, p, zz, zu, 0, above)
        down = both(3 - z <= t, z > 0)
        zz = jnp.where(down, z + t - 3, 0)
        add_into(both(down, z < 3), p, zz, zd, z_r.at[1, p, zz])
        z_push(down, p, zz, zd, 1, below)

    def owner(p):
        add_into(z > 0, p, z, zu, z_r.at[0, p, z])
        add_into(z < 3, p, z, zd, z_r.at[1, p, z])

    def third(p):
        mine = wrows(z, y)
        sends.start(mid, lambda: copy(acc.at[p, mine], mr.at[p], m_s.at[p], m_r.at[p], diag))

        @pl.when(edge)
        def _():
            base = (z * 2 + y) * rows

            def one(r):
                here = pl.ds(pl.multiple_of(base + r.start, SLAB), SLAB)
                out[p, r, pl.ds(ecol, E)] = acc[p, here, pl.ds(0, E)]

            slabs(rows, one)

        for k, to in enumerate((near, over, diag)):
            sends.start(edge, lambda k=k, to=to: copy(
                out.at[p, :, pl.ds(ecol, E)], out.at[p, :, pl.ds(ecol, E)], f_s.at[p, k], f_r.at[p, x], to))

        @pl.when(mid)
        def _():
            wait(None, mr.at[p], m_r.at[p])
            base = (z * 2 + y) * rows

            def one(r):
                here = pl.ds(pl.multiple_of(base + r.start, SLAB), SLAB)
                out[p, r, pl.ds(E, M)] = (f32(acc[p, here, :]) + f32(mr[p, r, :])).astype(jnp.bfloat16)

            slabs(rows, one)

        sends.start(mid, lambda: copy(out.at[p, :, pl.ds(E, M)], out.at[p, :, pl.ds(E, M)], f_s.at[p, 0], f_r.at[p, 2], near))

    def last(p):
        for xx in range(2):
            wait(jnp.logical_not(both(edge, x == xx)), out.at[p, :, pl.ds(2304 * xx, E)], f_r.at[p, xx])
        wait(edge, out.at[p, :, pl.ds(E, M)], f_r.at[p, 2])

    def small_rest():
        wait(None, sx, sm_r.at[1])
        ssib[...] = sacc[...] + sx[...]

    def small_y():
        small_rest()
        for zz in range(4):
            sends.start(None, lambda zz=zz: copy(ssib.at[zz * 2 + flip(y)], sy.at[zz], sm_s.at[2 + zz], sm_r.at[2 + zz], beside))

    def small_add():
        for zz in range(4):
            wait(None, sy.at[zz], sm_r.at[2 + zz])
            sy[zz] = sy[zz] + ssib[zz * 2 + y]

    def small_line():
        for zz in ORDER:
            @pl.when(both(z <= zz, z > 0))
            def _():
                wait(None, szu.at[zz], sm_r.at[6 + zz])
                sy[zz] = sy[zz] + szu[zz]
            sends.start(z < zz, lambda zz=zz: copy(sy.at[zz], szu.at[zz], sm_s.at[6 + zz], sm_r.at[6 + zz], above))

            @pl.when(both(z >= zz, z < 3))
            def _():
                wait(None, szd.at[zz], sm_r.at[10 + zz])
                sy[zz] = sy[zz] + szd[zz]
            sends.start(z > zz, lambda zz=zz: copy(sy.at[zz], szd.at[zz], sm_s.at[10 + zz], sm_r.at[10 + zz], below))

    def F(p):
        for zz in ORDER:
            first(p, zz)

    def S(p):
        for zz in ORDER:
            second(p, zz)

    def L(p):
        for t in range(3):
            line(p, t)
        owner(p)

    F(0)
    small_y()
    F(1)
    S(0)
    small_add()
    F(2)
    L(0)
    small_line()
    S(1)
    L(1)
    third(0)
    S(2)
    L(2)
    third(1)
    third(2)
    small_out[...] = sy[z]
    for p in range(phases):
        last(p)
    sends.finish()


def reduce(g_a, g_b, g_c, small):
    total, cols = g_a.shape
    rows = total // 8
    b = jnp.bfloat16
    f = jnp.float32
    dma = pltpu.SemaphoreType.DMA
    vm = pl.BlockSpec(memory_space=pltpu.VMEM)
    one = small.shape[1:]
    return pl.pallas_call(
        functools.partial(reduce_kernel, rows),
        out_shape=(jax.ShapeDtypeStruct((3, rows, cols), b), jax.ShapeDtypeStruct(one, f)),
        in_specs=[vm] * 4,
        out_specs=(vm, vm),
        scratch_shapes=[
            pltpu.VMEM((3, total, 2304), b),
            pltpu.VMEM((3, total, E), b),
            pltpu.VMEM((3, total, E), b),
            pltpu.VMEM((3, total, M), b),
            pltpu.VMEM((3, 4, rows, M), b),
            pltpu.VMEM((3, 4, rows, M), b),
            pltpu.VMEM((3, 4, rows, M), b),
            pltpu.VMEM((3, rows, M), b),
            dma((3, 4)), dma((3, 4)), dma((3, 4)), dma((3, 4)), dma((3, 4)), dma((3, 4)),
            dma((2, 3, 4)), dma((2, 3, 4)), dma((3,)), dma((3,)), dma((3, 3)), dma((3, 3)),
            pltpu.VMEM((8,) + one, f), pltpu.VMEM((8,) + one, f),
            pltpu.VMEM((4,) + one, f), pltpu.VMEM((4,) + one, f), pltpu.VMEM((4,) + one, f),
            pltpu.VMEM((8,) + one, f),
            dma((14,)), dma((14,)),
        ],
        compiler_params=pltpu.CompilerParams(collective_id=1, has_side_effects=True, vmem_limit_bytes=60 * 2**20),
    )(g_a, g_b, g_c, small)


def layer_norm(values, gain, shift):
    center = values - jnp.mean(values, axis=-1, keepdims=True)
    inverse = lax.rsqrt(jnp.mean(center * center, axis=-1, keepdims=True) + LN_EPS)
    normed = center * inverse
    return (normed * gain + shift, normed, inverse)


def norm_back(incoming, normed, inverse, gain):
    dgain = jnp.sum(incoming * normed, axis=0)
    dshift = jnp.sum(incoming, axis=0)
    scaled = incoming * gain
    dvalues = inverse * (
        scaled
        - jnp.mean(scaled, axis=-1, keepdims=True)
        - normed * jnp.mean(scaled * normed, axis=-1, keepdims=True)
    )
    return (dvalues, dgain, dshift)


def mm(a, b, dims, out=jnp.float32):
    return lax.dot_general(a, b, (dims, ((), ())), preferred_element_type=jnp.float32).astype(out)


NN = ((1,), (0,))
NT = ((1,), (1,))
TN = ((0,), (0,))


def split_heads(values, seqs, length):
    return values.reshape(seqs, length, HEADS, HEAD_DIM)


def attend(pieces):
    query, key, value = pieces
    raw = jnp.einsum("qhe,khe->hqk", query, key, preferred_element_type=jnp.float32) * HEAD_DIM ** (
        -0.5
    )
    peak = jnp.max(raw, axis=-1, keepdims=True)
    expo = jnp.exp(raw - peak)
    total = jnp.sum(expo, axis=-1, keepdims=True)
    probs = (expo / total).astype(jnp.bfloat16)
    mixed = jnp.einsum("hqk,khe->qhe", probs, value, preferred_element_type=jnp.float32)
    return mixed.astype(jnp.bfloat16)


def attend_back(pieces):
    query, key, value, dmixed = pieces
    scale = HEAD_DIM ** (-0.5)
    raw = jnp.einsum("qhe,khe->hqk", query, key, preferred_element_type=jnp.float32) * scale
    probs = jax.nn.softmax(raw, axis=-1)
    dprobs = jnp.einsum("qhe,khe->hqk", dmixed, value, preferred_element_type=jnp.float32)
    dscore = probs * (dprobs - jnp.sum(dprobs * probs, axis=-1, keepdims=True))
    dscore = (dscore * scale).astype(jnp.bfloat16)
    dquery = jnp.einsum("hqk,khe->qhe", dscore, key, preferred_element_type=jnp.float32)
    dkey = jnp.einsum("hqk,qhe->khe", dscore, query, preferred_element_type=jnp.float32)
    dvalue = jnp.einsum(
        "hqk,qhe->khe", probs.astype(jnp.bfloat16), dmixed, preferred_element_type=jnp.float32
    )
    return (dquery, dkey, dvalue)


def adam_step(weight, first, second, grad, factor, decay, rate):
    grad = grad * factor
    first_new = BETA_ONE * first + (1.0 - BETA_ONE) * grad
    second_new = BETA_TWO * second + (1.0 - BETA_TWO) * grad * grad
    mean_hat = first_new / (1.0 - BETA_ONE**STEP)
    square_hat = second_new / (1.0 - BETA_TWO**STEP)
    weight_new = weight - rate * (mean_hat / (jnp.sqrt(square_hat) + ADAM_EPS) + decay * weight)
    return (weight_new, first_new, second_new)


def collect(tailored, qkv, out, up, down, vectors, bias):
    low = jnp.bfloat16
    attn = jnp.concatenate([qkv[0], qkv[1], qkv[2], out.T], axis=1).astype(low)
    up, down = up.astype(low), down.T.astype(low)
    if tailored:
        rows = attn.shape[0]
        small = jnp.concatenate(
            [jnp.pad(vectors, ((0, 0), (0, 128 - rows))), bias.reshape(-1, 128), jnp.zeros((5, 128))]
        ).astype(low)
        attn, up, down, small = gather(attn, up, down, small)
        vectors = jnp.swapaxes(small[:, :8, :rows], 0, 1).reshape(8, -1)
        bias = small[:, 8:11].reshape(-1)
    else:
        attn, up, down = (lax.all_gather(v, "wide", axis=0, tiled=True) for v in (attn, up, down))
        vectors = lax.all_gather(vectors.astype(low), "wide", axis=1, tiled=True)
        bias = lax.all_gather(bias.astype(low), "wide", axis=0, tiled=True)
    return attn, up, down, vectors.astype(jnp.float32), bias.astype(jnp.float32)


def total(tailored, attn, up, down, vectors, bias):
    if tailored:
        rows = attn.shape[0] // 8
        small = jnp.concatenate(
            [
                jnp.pad(jnp.swapaxes(vectors.reshape(8, 8, rows), 0, 1), ((0, 0), (0, 0), (0, 128 - rows))),
                bias.reshape(8, 3, 128),
                jnp.zeros((8, 5, 128)),
            ],
            axis=1,
        )
        own, small = reduce(attn, up, down, small)
        own = own.astype(jnp.float32)
        return own[0], own[1], own[2], small[:8, :rows], small[8:11].reshape(-1)
    attn, up, down = (
        lax.psum(lax.psum_scatter(v.astype(jnp.float32), "wide", scatter_dimension=0, tiled=True), "narrow")
        for v in (attn, up, down)
    )
    vectors = lax.psum(lax.psum_scatter(vectors, "wide", scatter_dimension=1, tiled=True), "narrow")
    bias = lax.psum(lax.psum_scatter(bias, "wide", scatter_dimension=0, tiled=True), "narrow")
    return attn, up, down, vectors, bias


def shards(
    tailored,
    tokens,
    mask_place,
    mask_count,
    masked_output_gradient,
    query_key_value_weight,
    qkv_first,
    qkv_second,
    out_weight,
    out_first,
    out_second,
    up_weight,
    up_first,
    up_second,
    down_weight,
    down_first,
    down_second_moment,
    vectors,
    vectors_first,
    vectors_second,
    up_bias,
    up_bias_first,
    up_bias_second,
):
    low = jnp.bfloat16
    seqs, length, width = tokens.shape
    slots = mask_place.shape[1]
    padded = -(-slots // 16) * 16
    flat = tokens.reshape(seqs * length, width)
    attn_w, up_w, down_w, vec, bias = collect(
        tailored, query_key_value_weight, out_weight, up_weight, down_weight, vectors, up_bias
    )
    wq, wk, wv, wo = (attn_w[:, k * width : (k + 1) * width] for k in range(4))

    query = (mm(flat, wq, NN) + vec[0]).astype(low)
    key = mm(flat, wk, NN, low)
    value = (mm(flat, wv, NN) + vec[1]).astype(low)
    query, key, value = (split_heads(v, seqs, length) for v in (query, key, value))
    mixed = lax.map(attend, (query, key, value)).reshape(seqs * length, width)

    def middle(rows, mixed):
        pre_one = rows.astype(jnp.float32) + (mm(mixed, wo, NT) + vec[2])
        hidden, normed, inverse = layer_norm(pre_one, vec[3], vec[4])
        hidden_low = hidden.astype(low)
        upper = mm(hidden_low, up_w, NN) + bias
        cumul = 0.5 * (1.0 + lax.erf(upper * SQRT_HALF))
        active = (upper * cumul).astype(low)
        pre_two = hidden + (mm(active, down_w, NT) + vec[5])
        return layer_norm(pre_two, vec[6], vec[7]), normed, inverse, hidden_low, upper, cumul, active

    layer_out = middle(flat, mixed)[0][0].astype(low).reshape(seqs, length, width)

    live = jnp.arange(padded)[None, :] < mask_count[:, None]
    spots = jnp.pad(mask_place, ((0, 0), (0, padded - slots)), constant_values=-1)
    pick = ((spots[:, :, None] == jnp.arange(length)[None, None, :]) & live[:, :, None]).astype(low)

    def take(values):
        return jnp.einsum("sil,sld->sid", pick, values.reshape(seqs, length, width), preferred_element_type=jnp.float32).astype(low)

    rows_m = take(flat).reshape(seqs * padded, width)
    mixed_m = take(mixed).reshape(seqs * padded, width)
    query_m = split_heads(take(query), seqs, padded)
    (_, normed_two, inverse_two), normed_one, inverse_one, hidden_m, upper, cumul, active = middle(rows_m, mixed_m)
    incoming = jnp.pad(masked_output_gradient.astype(jnp.float32), ((0, 0), (0, padded - slots), (0, 0)))
    incoming = jnp.where(live[:, :, None], incoming, 0.0).reshape(seqs * padded, width)
    dpre_two, dgain_two, dshift_two = norm_back(incoming, normed_two, inverse_two, vec[6])
    dbias_two = jnp.sum(dpre_two, axis=0)
    dtwo_low = dpre_two.astype(low)
    ddown = mm(dtwo_low, active, TN, low)
    dactive = mm(dtwo_low, down_w, NN)
    density = jnp.exp(-0.5 * upper * upper) * INV_ROOT_TWO_PI
    dupper = dactive * (cumul + upper * density)
    dup_bias = jnp.sum(dupper, axis=0)
    dupper_low = dupper.astype(low)
    dup = mm(hidden_m, dupper_low, TN, low)
    dhidden = dpre_two + mm(dupper_low, up_w, NT)
    dpre_one, dgain_one, dshift_one = norm_back(dhidden, normed_one, inverse_one, vec[3])
    dbias_out = jnp.sum(dpre_one, axis=0)
    done_low = dpre_one.astype(low)
    dout = mm(done_low, mixed_m, TN, low)
    dmixed = split_heads(mm(done_low, wo, NN, low), seqs, padded)
    dquery, dkey, dvalue = lax.map(attend_back, (query_m, key, value, dmixed))
    dquery = dquery.reshape(seqs * padded, width)
    dkey = dkey.reshape(seqs * length, width)
    dvalue = dvalue.reshape(seqs * length, width)
    dbias_query = jnp.sum(dquery, axis=0)
    dbias_value = jnp.sum(dvalue, axis=0)
    dquery, dkey, dvalue = dquery.astype(low), dkey.astype(low), dvalue.astype(low)
    dattn = jnp.concatenate([mm(rows_m, dquery, TN, low), mm(flat, dkey, TN, low), mm(flat, dvalue, TN, low), dout], axis=1)
    masked_part = dpre_one + mm(dquery, wq, NT)
    dtokens = jnp.einsum(
        "sil,sid->sld",
        pick.astype(jnp.float32),
        masked_part.reshape(seqs, padded, width),
        precision=lax.Precision.HIGHEST,
        preferred_element_type=jnp.float32,
    ).reshape(seqs * length, width)
    dtokens = dtokens + mm(dkey, wk, NT) + mm(dvalue, wv, NT)
    dvectors = jnp.stack(
        [dbias_query, dbias_value, dbias_out, dgain_one, dshift_one, dbias_two, dgain_two, dshift_two]
    )
    own_attn, own_up, own_down, own_vectors, own_bias = total(tailored, dattn, dup, ddown, dvectors, dup_bias)

    squares = [jnp.sum(v * v) for v in (own_attn, own_up, own_down, own_vectors, own_bias)]
    grad_norm = jnp.sqrt(lax.psum(sum(squares), "wide"))
    factor = CLIP_LIMIT / jnp.maximum(grad_norm, CLIP_LIMIT)
    own_qkv = jnp.swapaxes(own_attn[:, : 3 * width].reshape(-1, 3, width), 0, 1)
    own_out = own_attn[:, 3 * width :].T
    steps = (
        adam_step(query_key_value_weight, qkv_first, qkv_second, own_qkv, factor, DECAY_RATE, LEARN_RATE),
        adam_step(out_weight, out_first, out_second, own_out, factor, DECAY_RATE, OUTPUT_RATE),
        adam_step(up_weight, up_first, up_second, own_up, factor, DECAY_RATE, LEARN_RATE),
        adam_step(down_weight, down_first, down_second_moment, own_down.T, factor, DECAY_RATE, LEARN_RATE),
        adam_step(vectors, vectors_first, vectors_second, own_vectors, factor, 0.0, VECTOR_RATE),
        adam_step(up_bias, up_bias_first, up_bias_second, own_bias, factor, 0.0, BIAS_RATE),
    )
    return (layer_out, dtokens.reshape(seqs, length, width), grad_norm) + tuple(v for step in steps for v in step)


def solution(mesh):
    tailored = mesh.shape["wide"] == 8 and mesh.shape["narrow"] == 4
    data = P(("wide", "narrow"))
    rows = P("wide")
    columns = P(None, "wide")
    weights = (columns,) * 6 + (rows,) * 3 + (columns,) * 6 + (rows,) * 3
    return jax.shard_map(
        functools.partial(shards, tailored),
        mesh=mesh,
        in_specs=(data,) * 4 + weights,
        out_specs=(data, data, P()) + weights,
        check_vma=False,
    )
```

```python
import functools

import jax
import jax.numpy as jnp
from jax import lax
from jax.experimental import pallas as pl
from jax.experimental.pallas import tpu as pltpu
from jax.sharding import PartitionSpec as P

HEADS = 12
HEAD_DIM = 64
STEP = 10

LN_EPS = 1e-06
SQRT_HALF = 0.7071067811865476
INV_ROOT_TWO_PI = 0.3989422804014327
CLIP_LIMIT = 1.0
BETA_ONE = 0.9
BETA_TWO = 0.999
LEARN_RATE = 0.05
OUTPUT_RATE = 0.2
VECTOR_RATE = 0.5
BIAS_RATE = 0.3
DECAY_RATE = 0.01
ADAM_EPS = 1e-08

MESH = pl.DeviceIdType.MESH


def when(cond, body):
    if cond is None:
        body()
    else:
        pl.when(cond)(body)


class Sends:
    def __init__(self):
        self.started = []

    def start(self, cond, make):
        when(cond, lambda: make().start())
        self.started.append((cond, make))

    def finish(self):
        for cond, make in self.started:
            when(cond, lambda make=make: make().wait_send())


def both(a, b):
    return b if a is None else (a if b is None else jnp.logical_and(a, b))


def place():
    w, n = lax.axis_index("wide"), lax.axis_index("narrow")
    return w // 2, lax.rem(w, 2), n // 2, lax.rem(n, 2)


def flip(v):
    return 1 - v


def dev(z, y, x, c):
    return (z * 2 + y, x * 2 + c)


def meet(z, y, x, c, diagonal):
    bar = pltpu.get_barrier_semaphore()
    peers = [(None, dev(z, flip(y), x, c)), (None, dev(z, y, flip(x), c)), (None, dev(z, y, x, flip(c)))]
    if diagonal:
        peers.append((None, dev(z, y, flip(x), flip(c))))
    peers += [(z > 0, dev(z - 1, y, x, c)), (z < 3, dev(z + 1, y, x, c))]
    for cond, peer in peers:
        when(cond, lambda peer=peer: pl.semaphore_signal(bar, inc=1, device_id=peer, device_id_type=MESH))
    inner = jnp.logical_and(z > 0, z < 3)
    count = 4 if diagonal else 3
    pl.semaphore_wait(bar, count + 1 + jnp.where(inner, 1, 0))


def gather_kernel(rows, cols, attn, up, down, small, attn_full, up_full, down_full, small_full, send_sem, recv_sem, small_send, small_recv, own_sem):
    z, y, x, c = place()
    edge = x == c
    third = cols // 3
    mine, across = x + c, 2 * flip(x)
    fulls = (attn_full, up_full, down_full)
    shards = (attn, up, down)
    sends = Sends()
    zl, zh = z > 0, z < 3

    def spot(p, zz, yy, t):
        return fulls[p].at[pl.ds(pl.multiple_of((zz * 2 + yy) * rows, rows), rows), pl.ds(pl.multiple_of(t * third, third), third)]

    def push(cond, p, zz, yy, t, kind, to, src=None):
        def make():
            w = zz * 2 + yy
            where = spot(p, zz, yy, t)
            return pltpu.make_async_remote_copy(
                src_ref=where if src is None else src,
                dst_ref=where,
                send_sem=send_sem.at[kind, p, w],
                recv_sem=recv_sem.at[p, w, t],
                device_id=to,
                device_id_type=MESH,
            )

        sends.start(cond, make)

    def small_push(cond, zz, yy, kind, to, src=None):
        def make():
            w = zz * 2 + yy
            where = small_full.at[w]
            return pltpu.make_async_remote_copy(
                src_ref=where if src is None else src,
                dst_ref=where,
                send_sem=small_send.at[kind, w],
                recv_sem=small_recv.at[w],
                device_id=to,
                device_id_type=MESH,
            )

        sends.start(cond, make)

    def arrive(cond, p, zz, yy, t):
        def body():
            where = spot(p, zz, yy, t)
            w = zz * 2 + yy
            pltpu.make_async_remote_copy(where, where, send_sem.at[0, p, w], recv_sem.at[p, w, t], dev(z, y, x, c), device_id_type=MESH).wait_recv()

        when(cond, body)

    def small_arrive(cond, zz, yy):
        def body():
            w = zz * 2 + yy
            pltpu.make_async_remote_copy(small_full.at[w], small_full.at[w], small_send.at[0, w], small_recv.at[w], dev(z, y, x, c), device_id_type=MESH).wait_recv()

        when(cond, body)

    UP, DOWN, SIDE, OVER, NEAR, PASS = range(6)
    above, below, beside = dev(z + 1, y, x, c), dev(z - 1, y, x, c), dev(z, flip(y), x, c)
    over, near = dev(z, y, flip(x), c), dev(z, y, x, flip(c))

    def own(p):
        src = shards[p].at[:, pl.ds(pl.multiple_of(mine * third, third), third)]
        push(zh, p, z, y, mine, UP, above, src)
        push(zl, p, z, y, mine, DOWN, below, src)
        push(None, p, z, y, mine, SIDE, beside, src)

    def z_step(p, d):
        for cond, zz, onward, kind, to in ((z - d >= 0, z - d, zh, UP, above), (z + d <= 3, z + d, zl, DOWN, below)):
            arrive(cond, p, zz, y, mine)
            push(both(cond, onward), p, zz, y, mine, kind, to)
            push(cond, p, zz, y, mine, SIDE, beside)
            push(both(cond, edge), p, zz, y, mine, OVER, over)
            push(cond, p, zz, y, mine, NEAR, near)

    def y_step(p, d):
        steps = ((None, z),) if d == 0 else ((z - d >= 0, z - d), (z + d <= 3, z + d))
        for cond, zz in steps:
            arrive(cond, p, zz, flip(y), mine)
            push(both(cond, edge), p, zz, flip(y), mine, OVER, over)
            push(cond, p, zz, flip(y), mine, NEAR, near)

    def x_step(p, d):
        mid = jnp.logical_not(edge)
        for yy in (y, flip(y)):
            if d == 0:
                steps = () if yy is y else ((None, z),)
            else:
                steps = ((z - d >= 0, z - d), (z + d <= 3, z + d))
            for cond, zz in steps:
                cond = both(cond, mid)
                arrive(cond, p, zz, yy, across)
                push(cond, p, zz, yy, across, PASS, near)

    def last(p, d):
        for yy in (y, flip(y)):
            if d == 0:
                steps = () if yy is y else ((None, z),)
            else:
                steps = ((z - d >= 0, z - d), (z + d <= 3, z + d))
            for cond, zz in steps:
                arrive(cond, p, zz, yy, x + flip(c))
                arrive(both(cond, edge), p, zz, yy, across)

    def small_z(d):
        for cond, zz, onward, kind, to in ((z - d >= 0, z - d, zh, UP, above), (z + d <= 3, z + d, zl, DOWN, below)):
            small_arrive(cond, zz, y)
            small_push(both(cond, onward), zz, y, kind, to)
            small_push(cond, zz, y, SIDE, beside)

    meet(z, y, x, c, False)
    small_push(zh, z, y, UP, above, small)
    small_push(zl, z, y, DOWN, below, small)
    small_push(None, z, y, SIDE, beside, small)
    own(0)
    w = z * 2 + y
    copies = []
    for p in range(3):
        copies.append(pltpu.make_async_copy(shards[p], fulls[p].at[pl.ds(pl.multiple_of(w * rows, rows), rows)], own_sem.at[p]))
    copies.append(pltpu.make_async_copy(small, small_full.at[w], own_sem.at[3]))
    for copy in copies:
        copy.start()
    for d in range(1, 4):
        small_z(d)
    order = [
        lambda: z_step(0, 1), lambda: own(1), lambda: y_step(0, 0), lambda: z_step(0, 2), lambda: y_step(0, 1), lambda: x_step(0, 0), lambda: z_step(0, 3),
        lambda: y_step(0, 2), lambda: x_step(0, 1), lambda: z_step(1, 1), lambda: own(2), lambda: y_step(0, 3), lambda: x_step(0, 2), lambda: z_step(1, 2), lambda: y_step(1, 0), lambda: x_step(0, 3), lambda: z_step(1, 3),
        lambda: y_step(1, 1), lambda: x_step(1, 0), lambda: z_step(2, 1), lambda: y_step(1, 2), lambda: x_step(1, 1), lambda: z_step(2, 2), lambda: y_step(1, 3), lambda: x_step(1, 2), lambda: z_step(2, 3),
        lambda: y_step(2, 0), lambda: x_step(1, 3), lambda: y_step(2, 1), lambda: x_step(2, 0), lambda: y_step(2, 2), lambda: x_step(2, 1), lambda: y_step(2, 3), lambda: x_step(2, 2), lambda: x_step(2, 3),
    ]
    for step in order:
        step()
    for d in range(4):
        for cond, zz in (((None, z),) if d == 0 else ((z - d >= 0, z - d), (z + d <= 3, z + d))):
            small_arrive(cond, zz, flip(y))
    for p in range(3):
        for d in range(4):
            last(p, d)
    sends.finish()
    for copy in copies:
        copy.wait()


def gather(attn, up, down, small):
    rows, cols = attn.shape
    full = jax.ShapeDtypeStruct((8 * rows, cols), attn.dtype)
    anywhere = pl.BlockSpec(memory_space=pl.ANY)
    return pl.pallas_call(
        functools.partial(gather_kernel, rows, cols),
        out_shape=(full, full, full, jax.ShapeDtypeStruct((8,) + small.shape, small.dtype)),
        in_specs=[anywhere] * 4,
        out_specs=(anywhere,) * 4,
        scratch_shapes=[
            pltpu.SemaphoreType.DMA((6, 3, 8)),
            pltpu.SemaphoreType.DMA((3, 8, 3)),
            pltpu.SemaphoreType.DMA((3, 8)),
            pltpu.SemaphoreType.DMA((8,)),
            pltpu.SemaphoreType.DMA((4,)),
        ],
        compiler_params=pltpu.CompilerParams(collective_id=0, has_side_effects=True),
    )(attn, up, down, small)


E = 768
M = 1536
SLAB = 32
ORDER = (3, 0, 2, 1)


def slabs(rows, body):
    @pl.loop(0, rows // SLAB)
    def _(i):
        body(pl.ds(pl.multiple_of(i * SLAB, SLAB), SLAB))


def f32(v):
    return v.astype(jnp.float32)


def reduce_kernel(rows, g_a, g_b, g_c, small, out, small_out, sib, xs, xr, acc, yr, zu, zd, mr,
                  sib_s, sib_r, x_s, x_r, y_s, y_r, z_s, z_r, m_s, m_r, f_s, f_r,
                  ssib, sx, sy, szu, szd, sacc, sm_s, sm_r, phases=3):
    z, y, x, c = place()
    edge = x == c
    mid = jnp.logical_not(edge)
    grads = (g_a, g_b, g_c)
    sends = Sends()
    me = dev(z, y, x, c)
    above, below, beside = dev(z + 1, y, x, c), dev(z - 1, y, x, c), dev(z, flip(y), x, c)
    over, near, diag = dev(z, y, flip(x), c), dev(z, y, x, flip(c)), dev(z, y, flip(x), flip(c))
    ecol = pl.multiple_of(x * 2304, 768)
    pair = rows * 2

    def zrows(zz):
        return pl.ds(zz * pair, pair)

    def wrows(zz, yy):
        return pl.ds(pl.multiple_of((zz * 2 + yy) * rows, rows), rows)

    def copy(src, dst, ss, rs, to):
        return pltpu.make_async_remote_copy(src_ref=src, dst_ref=dst, send_sem=ss, recv_sem=rs, device_id=to, device_id_type=MESH)

    def wait(cond, dst, rs):
        when(cond, lambda: copy(dst, dst, rs, rs, me).wait_recv())

    meet(z, y, x, c, True)

    for p in range(phases):
        for zz in ORDER:
            sends.start(edge, lambda p=p, zz=zz: copy(
                grads[p].at[zrows(zz), pl.ds(pl.multiple_of(768 * flip(x), 768), 2304)], sib.at[p, zrows(zz)], sib_s.at[p, zz], sib_r.at[p, zz], near))
            sends.start(mid, lambda p=p, zz=zz: copy(
                grads[p].at[zrows(zz), pl.ds(ecol, E)], sib.at[p, zrows(zz), pl.ds(0, E)], sib_s.at[p, zz], sib_r.at[p, zz], near))

    sends.start(None, lambda: copy(small, ssib, sm_s.at[0], sm_r.at[0], near))
    wait(None, ssib, sm_r.at[0])
    sacc[...] = small[...] + ssib[...]
    sends.start(None, lambda: copy(sacc, sx, sm_s.at[1], sm_r.at[1], over))

    moff = 768 * x
    ooff = 1536 * flip(x)

    def first(p, zz):
        @pl.when(mid)
        def _():
            wait(None, sib.at[p, zrows(zz)], sib_r.at[p, zz])

            def one(r):
                r = pl.ds(zz * pair + r.start, SLAB)
                xs[p, r, :] = (f32(grads[p][r, pl.ds(pl.multiple_of(2304 * flip(x), 768), E)]) + f32(sib[p, r, pl.ds(pl.multiple_of(ooff, 768), E)])).astype(jnp.bfloat16)
                acc[p, r, :] = (f32(grads[p][r, pl.ds(768, M)]) + f32(sib[p, r, pl.ds(pl.multiple_of(moff, 768), M)])).astype(jnp.bfloat16)

            slabs(pair, one)

        sends.start(mid, lambda: copy(xs.at[p, zrows(zz)], xr.at[p, zrows(zz)], x_s.at[p, zz], x_r.at[p, zz], over))

        @pl.when(edge)
        def _():
            wait(None, sib.at[p, zrows(zz), pl.ds(0, E)], sib_r.at[p, zz])
            wait(None, xr.at[p, zrows(zz)], x_r.at[p, zz])

            def one(r):
                r = pl.ds(zz * pair + r.start, SLAB)
                acc[p, r, pl.ds(0, E)] = (f32(grads[p][r, pl.ds(ecol, E)]) + f32(sib[p, r, pl.ds(0, E)]) + f32(xr[p, r, :])).astype(jnp.bfloat16)

            slabs(pair, one)

        for cond, width in ((edge, E), (mid, M)):
            sends.start(cond, lambda width=width: copy(
                acc.at[p, wrows(zz, flip(y)), pl.ds(0, width)], yr.at[p, zz, :, pl.ds(0, width)], y_s.at[p, zz], y_r.at[p, zz], beside))

    def add_into(cond, p, zz, buffer, sem):
        for role, width in ((edge, E), (mid, M)):
            @pl.when(both(cond, role))
            def _():
                wait(None, buffer.at[p, zz, :, pl.ds(0, width)], sem)
                base = (zz * 2 + y) * rows

                def one(r):
                    here = pl.ds(pl.multiple_of(base + r.start, SLAB), SLAB)
                    acc[p, here, pl.ds(0, width)] = (f32(acc[p, here, pl.ds(0, width)]) + f32(buffer[p, zz, r, pl.ds(0, width)])).astype(jnp.bfloat16)

                slabs(rows, one)

    def z_push(cond, p, zz, buffer, k, to):
        for role, width in ((edge, E), (mid, M)):
            sends.start(both(cond, role), lambda width=width: copy(
                acc.at[p, wrows(zz, y), pl.ds(0, width)], buffer.at[p, zz, :, pl.ds(0, width)], z_s.at[k, p, zz], z_r.at[k, p, zz], to))

    def second(p, zz):
        add_into(None, p, zz, yr, y_r.at[p, zz])

    def line(p, t):
        up = both(z <= t, z < 3)
        zz = jnp.where(up, 3 + z - t, 0)
        add_into(both(up, z > 0), p, zz, zu, z_r.at[0, p, zz])
        z_push(up, p, zz, zu, 0, above)
        down = both(3 - z <= t, z > 0)
        zz = jnp.where(down, z + t - 3, 0)
        add_into(both(down, z < 3), p, zz, zd, z_r.at[1, p, zz])
        z_push(down, p, zz, zd, 1, below)

    def owner(p):
        add_into(z > 0, p, z, zu, z_r.at[0, p, z])
        add_into(z < 3, p, z, zd, z_r.at[1, p, z])

    def third(p):
        mine = wrows(z, y)
        sends.start(mid, lambda: copy(acc.at[p, mine], mr.at[p], m_s.at[p], m_r.at[p], diag))

        @pl.when(edge)
        def _():
            base = (z * 2 + y) * rows

            def one(r):
                here = pl.ds(pl.multiple_of(base + r.start, SLAB), SLAB)
                out[p, r, pl.ds(ecol, E)] = acc[p, here, pl.ds(0, E)]

            slabs(rows, one)

        for k, to in enumerate((near, over, diag)):
            sends.start(edge, lambda k=k, to=to: copy(
                out.at[p, :, pl.ds(ecol, E)], out.at[p, :, pl.ds(ecol, E)], f_s.at[p, k], f_r.at[p, x], to))

        @pl.when(mid)
        def _():
            wait(None, mr.at[p], m_r.at[p])
            base = (z * 2 + y) * rows

            def one(r):
                here = pl.ds(pl.multiple_of(base + r.start, SLAB), SLAB)
                out[p, r, pl.ds(E, M)] = (f32(acc[p, here, :]) + f32(mr[p, r, :])).astype(jnp.bfloat16)

            slabs(rows, one)

        sends.start(mid, lambda: copy(out.at[p, :, pl.ds(E, M)], out.at[p, :, pl.ds(E, M)], f_s.at[p, 0], f_r.at[p, 2], near))

    def last(p):
        for xx in range(2):
            wait(jnp.logical_not(both(edge, x == xx)), out.at[p, :, pl.ds(2304 * xx, E)], f_r.at[p, xx])
        wait(edge, out.at[p, :, pl.ds(E, M)], f_r.at[p, 2])

    def small_rest():
        wait(None, sx, sm_r.at[1])
        ssib[...] = sacc[...] + sx[...]

    def small_y():
        small_rest()
        for zz in range(4):
            sends.start(None, lambda zz=zz: copy(ssib.at[zz * 2 + flip(y)], sy.at[zz], sm_s.at[2 + zz], sm_r.at[2 + zz], beside))

    def small_add():
        for zz in range(4):
            wait(None, sy.at[zz], sm_r.at[2 + zz])
            sy[zz] = sy[zz] + ssib[zz * 2 + y]

    def small_line():
        for zz in ORDER:
            @pl.when(both(z <= zz, z > 0))
            def _():
                wait(None, szu.at[zz], sm_r.at[6 + zz])
                sy[zz] = sy[zz] + szu[zz]
            sends.start(z < zz, lambda zz=zz: copy(sy.at[zz], szu.at[zz], sm_s.at[6 + zz], sm_r.at[6 + zz], above))

            @pl.when(both(z >= zz, z < 3))
            def _():
                wait(None, szd.at[zz], sm_r.at[10 + zz])
                sy[zz] = sy[zz] + szd[zz]
            sends.start(z > zz, lambda zz=zz: copy(sy.at[zz], szd.at[zz], sm_s.at[10 + zz], sm_r.at[10 + zz], below))

    def F(p):
        for zz in ORDER:
            first(p, zz)

    def S(p):
        for zz in ORDER:
            second(p, zz)

    def L(p):
        for t in range(3):
            line(p, t)
        owner(p)

    F(0)
    small_y()
    F(1)
    S(0)
    small_add()
    F(2)
    L(0)
    small_line()
    S(1)
    L(1)
    third(0)
    S(2)
    L(2)
    third(1)
    third(2)
    small_out[...] = sy[z]
    for p in range(phases):
        last(p)
    sends.finish()


def reduce(g_a, g_b, g_c, small):
    total, cols = g_a.shape
    rows = total // 8
    b = jnp.bfloat16
    f = jnp.float32
    dma = pltpu.SemaphoreType.DMA
    vm = pl.BlockSpec(memory_space=pltpu.VMEM)
    one = small.shape[1:]
    return pl.pallas_call(
        functools.partial(reduce_kernel, rows),
        out_shape=(jax.ShapeDtypeStruct((3, rows, cols), b), jax.ShapeDtypeStruct(one, f)),
        in_specs=[vm] * 4,
        out_specs=(vm, vm),
        scratch_shapes=[
            pltpu.VMEM((3, total, 2304), b),
            pltpu.VMEM((3, total, E), b),
            pltpu.VMEM((3, total, E), b),
            pltpu.VMEM((3, total, M), b),
            pltpu.VMEM((3, 4, rows, M), b),
            pltpu.VMEM((3, 4, rows, M), b),
            pltpu.VMEM((3, 4, rows, M), b),
            pltpu.VMEM((3, rows, M), b),
            dma((3, 4)), dma((3, 4)), dma((3, 4)), dma((3, 4)), dma((3, 4)), dma((3, 4)),
            dma((2, 3, 4)), dma((2, 3, 4)), dma((3,)), dma((3,)), dma((3, 3)), dma((3, 3)),
            pltpu.VMEM((8,) + one, f), pltpu.VMEM((8,) + one, f),
            pltpu.VMEM((4,) + one, f), pltpu.VMEM((4,) + one, f), pltpu.VMEM((4,) + one, f),
            pltpu.VMEM((8,) + one, f),
            dma((14,)), dma((14,)),
        ],
        compiler_params=pltpu.CompilerParams(collective_id=1, has_side_effects=True, vmem_limit_bytes=60 * 2**20),
    )(g_a, g_b, g_c, small)


def layer_norm(values, gain, shift):
    center = values - jnp.mean(values, axis=-1, keepdims=True)
    inverse = lax.rsqrt(jnp.mean(center * center, axis=-1, keepdims=True) + LN_EPS)
    normed = center * inverse
    return (normed * gain + shift, normed, inverse)


def norm_back(incoming, normed, inverse, gain):
    dgain = jnp.sum(incoming * normed, axis=0)
    dshift = jnp.sum(incoming, axis=0)
    scaled = incoming * gain
    dvalues = inverse * (
        scaled
        - jnp.mean(scaled, axis=-1, keepdims=True)
        - normed * jnp.mean(scaled * normed, axis=-1, keepdims=True)
    )
    return (dvalues, dgain, dshift)


def mm(a, b, dims, out=jnp.float32):
    return lax.dot_general(a, b, (dims, ((), ())), preferred_element_type=jnp.float32).astype(out)


NN = ((1,), (0,))
NT = ((1,), (1,))
TN = ((0,), (0,))


def split_heads(values, seqs, length):
    return values.reshape(seqs, length, HEADS, HEAD_DIM)


def attend(pieces):
    query, key, value = pieces
    raw = jnp.einsum("qhe,khe->hqk", query, key, preferred_element_type=jnp.float32) * HEAD_DIM ** (
        -0.5
    )
    peak = jnp.max(raw, axis=-1, keepdims=True)
    expo = jnp.exp(raw - peak)
    total = jnp.sum(expo, axis=-1, keepdims=True)
    probs = (expo / total).astype(jnp.bfloat16)
    mixed = jnp.einsum("hqk,khe->qhe", probs, value, preferred_element_type=jnp.float32)
    return mixed.astype(jnp.bfloat16)


def attend_back(pieces):
    query, key, value, dmixed = pieces
    scale = HEAD_DIM ** (-0.5)
    raw = jnp.einsum("qhe,khe->hqk", query, key, preferred_element_type=jnp.float32) * scale
    probs = jax.nn.softmax(raw, axis=-1)
    dprobs = jnp.einsum("qhe,khe->hqk", dmixed, value, preferred_element_type=jnp.float32)
    dscore = probs * (dprobs - jnp.sum(dprobs * probs, axis=-1, keepdims=True))
    dscore = (dscore * scale).astype(jnp.bfloat16)
    dquery = jnp.einsum("hqk,khe->qhe", dscore, key, preferred_element_type=jnp.float32)
    dkey = jnp.einsum("hqk,qhe->khe", dscore, query, preferred_element_type=jnp.float32)
    dvalue = jnp.einsum(
        "hqk,qhe->khe", probs.astype(jnp.bfloat16), dmixed, preferred_element_type=jnp.float32
    )
    return (dquery, dkey, dvalue)


def adam_step(weight, first, second, grad, factor, decay, rate):
    grad = grad * factor
    first_new = BETA_ONE * first + (1.0 - BETA_ONE) * grad
    second_new = BETA_TWO * second + (1.0 - BETA_TWO) * grad * grad
    mean_hat = first_new / (1.0 - BETA_ONE**STEP)
    square_hat = second_new / (1.0 - BETA_TWO**STEP)
    weight_new = weight - rate * (mean_hat / (jnp.sqrt(square_hat) + ADAM_EPS) + decay * weight)
    return (weight_new, first_new, second_new)


def dot(a, b, dims):
    return lax.dot_general(a, b, (dims, ((), ())), preferred_element_type=jnp.float32)


NN = ((1,), (0,))
NT = ((1,), (1,))
TN = ((0,), (0,))
LOW = jnp.bfloat16


def norm(values, gain, shift):
    center = values - jnp.mean(values, axis=-1, keepdims=True)
    inverse = lax.rsqrt(jnp.mean(center * center, axis=-1, keepdims=True) + LN_EPS)
    normed = center * inverse
    return normed * gain + shift, normed, inverse


def norm_pull(incoming, normed, inverse, gain):
    dgain = jnp.sum(incoming * normed, axis=0, keepdims=True)
    dshift = jnp.sum(incoming, axis=0, keepdims=True)
    scaled = incoming * gain
    return (
        inverse * (scaled - jnp.mean(scaled, axis=-1, keepdims=True) - normed * jnp.mean(scaled * normed, axis=-1, keepdims=True)),
        dgain,
        dshift,
    )


def forward_kernel(
    rows, seqs, length, padded,
    attn, up, down, small, tokens, pick, grad,
    attn_o, up_o, down_o, vec_o, bias_o, kv_o, hidden_o, query_o, rows_o, mixed_o, hid_o, act_o, slope_o, dtwo_o, dlow_o, normed_o, inv_o, dvec_o,
    attn_full, up_full, down_full, small_full,
    qkv, mixed, hidden, vec, qbias, bias, query_m, rows_m, mixed_m, hid_m, act_m, slope, ytwo, dtwo, dlow, dvec, hid_f, normed_one, inverse_one,
    send_sem, recv_sem, small_send, small_recv, own_sem, save_sem, pair_send, pair_recv,
):
    z, y, x, c = place()
    width = tokens.shape[1]
    cols = attn.shape[1]
    edge = x == c
    third = cols // 3
    mine, across = x + c, 2 * flip(x)
    fulls = (attn_full, up_full, down_full)
    shards = (attn, up, down)
    sends = Sends()
    zl, zh = z > 0, z < 3
    count = seqs * padded

    def spot(p, zz, yy, t):
        return fulls[p].at[pl.ds(pl.multiple_of((zz * 2 + yy) * rows, rows), rows), pl.ds(pl.multiple_of(t * third, third), third)]

    def push(cond, p, zz, yy, t, kind, to, src=None):
        def make():
            w = zz * 2 + yy
            where = spot(p, zz, yy, t)
            return pltpu.make_async_remote_copy(
                src_ref=where if src is None else src,
                dst_ref=where,
                send_sem=send_sem.at[kind, p, w],
                recv_sem=recv_sem.at[p, w, t],
                device_id=to,
                device_id_type=MESH,
            )

        sends.start(cond, make)

    def small_push(cond, zz, yy, kind, to, src=None):
        def make():
            w = zz * 2 + yy
            where = small_full.at[w]
            return pltpu.make_async_remote_copy(
                src_ref=where if src is None else src,
                dst_ref=where,
                send_sem=small_send.at[kind, w],
                recv_sem=small_recv.at[w],
                device_id=to,
                device_id_type=MESH,
            )

        sends.start(cond, make)

    def arrive(cond, p, zz, yy, t):
        def body():
            where = spot(p, zz, yy, t)
            w = zz * 2 + yy
            pltpu.make_async_remote_copy(where, where, send_sem.at[0, p, w], recv_sem.at[p, w, t], dev(z, y, x, c), device_id_type=MESH).wait_recv()

        when(cond, body)

    def small_arrive(cond, zz, yy):
        def body():
            w = zz * 2 + yy
            pltpu.make_async_remote_copy(small_full.at[w], small_full.at[w], small_send.at[0, w], small_recv.at[w], dev(z, y, x, c), device_id_type=MESH).wait_recv()

        when(cond, body)

    UP, DOWN, SIDE, OVER, NEAR, PASS = range(6)
    above, below, beside = dev(z + 1, y, x, c), dev(z - 1, y, x, c), dev(z, flip(y), x, c)
    over, near = dev(z, y, flip(x), c), dev(z, y, x, flip(c))

    def around(d):
        return ((None, z),) if d == 0 else ((z - d >= 0, z - d), (z + d <= 3, z + d))

    def own(p):
        src = shards[p].at[:, pl.ds(pl.multiple_of(mine * third, third), third)]
        push(zh, p, z, y, mine, UP, above, src)
        push(zl, p, z, y, mine, DOWN, below, src)
        push(None, p, z, y, mine, SIDE, beside, src)

    def z_step(p, d):
        for cond, zz, onward, kind, to in ((z - d >= 0, z - d, zh, UP, above), (z + d <= 3, z + d, zl, DOWN, below)):
            arrive(cond, p, zz, y, mine)
            push(both(cond, onward), p, zz, y, mine, kind, to)
            push(cond, p, zz, y, mine, SIDE, beside)
            push(both(cond, edge), p, zz, y, mine, OVER, over)
            push(cond, p, zz, y, mine, NEAR, near)

    def y_step(p, d):
        for cond, zz in around(d):
            arrive(cond, p, zz, flip(y), mine)
            push(both(cond, edge), p, zz, flip(y), mine, OVER, over)
            push(cond, p, zz, flip(y), mine, NEAR, near)

    def x_step(p, d):
        mid = jnp.logical_not(edge)
        for yy in (y, flip(y)):
            for cond, zz in () if d == 0 and yy is y else around(d):
                cond = both(cond, mid)
                arrive(cond, p, zz, yy, across)
                push(cond, p, zz, yy, across, PASS, near)

    def last(p):
        for d in range(4):
            for yy in (y, flip(y)):
                for cond, zz in () if d == 0 and yy is y else around(d):
                    arrive(cond, p, zz, yy, x + flip(c))
                    arrive(both(cond, edge), p, zz, yy, across)
        copies[p].wait()
        keep(fulls[p], (attn_o, up_o, down_o)[p], p)

    def small_z(d):
        for cond, zz, onward, kind, to in ((z - d >= 0, z - d, zh, UP, above), (z + d <= 3, z + d, zl, DOWN, below)):
            small_arrive(cond, zz, y)
            small_push(both(cond, onward), zz, y, kind, to)
            small_push(cond, zz, y, SIDE, beside)

    saves = []

    def keep(src, dst, k):
        copy = pltpu.make_async_copy(src, dst, save_sem.at[k])
        copy.start()
        saves.append(copy)

    swaps = []

    def swap(ref, k):
        def make():
            return pltpu.make_async_remote_copy(ref.at[0], ref.at[1], pair_send.at[k], pair_recv.at[k], near, device_id_type=MESH)

        make().start()
        swaps.append((make, ref))

    def vectors():
        for d in range(4):
            for cond, zz in around(d):
                small_arrive(cond, zz, flip(y))
        copies[3].wait()
        at = lax.broadcasted_iota(jnp.int32, (128, width), 0)
        to = lax.broadcasted_iota(jnp.int32, (128, width), 1)
        total = jnp.zeros((16, width), jnp.float32)
        for w in range(8):
            place_w = jnp.logical_and(at + w * rows == to, at < rows).astype(jnp.float32).astype(LOW)
            total += dot(small_full[w], place_w, NN)
            for r in range(3):
                bias[:, pl.ds(w * 384 + r * 128, 128)] = small_full[w, 8 + r : 9 + r, :].astype(jnp.float32)
        vec[...] = total[:8]
        qbias[0] = total[0:1]
        qbias[1] = jnp.zeros((1, width), jnp.float32)
        qbias[2] = total[1:2]

    def project(i):
        r = pl.ds(i * 256, 256)

        @pl.loop(0, 3)
        def _(k):
            value = dot(tokens[r, :], attn_full[:, pl.ds(pl.multiple_of(k * width, width), width)], NN) + qbias[k]
            qkv[k, r, :] = (value * jnp.where(k == 0, 0.125, 1.0)).astype(LOW)

    def attend(s, j):
        lane = lax.broadcasted_iota(jnp.int32, (length, 128), 1) < 64
        cs = pl.ds(j * 128, 128)
        rs = pl.ds(s * length, length)
        key, value = qkv[1, rs, cs], qkv[2, rs, cs]
        zero, one = jnp.zeros_like(key), jnp.ones_like(key)
        keys = (jnp.where(lane, key, zero), jnp.where(lane, zero, key))
        values = (jnp.where(lane, value, one), jnp.where(lane, one, value))
        for q in range(length // 256):
            r = pl.ds(s * length + q * 256, 256)
            query = qkv[0, r, cs]
            parts = []
            for h in range(2):
                score = dot(query, keys[h], NT)
                expo = jnp.exp(score - jnp.max(score, axis=-1, keepdims=True))
                parts.append(dot(expo.astype(LOW), values[h], NN))
            left = lane[:256]
            top = jnp.where(left, parts[0], parts[1])
            under = pltpu.roll(jnp.where(left, parts[1], parts[0]), 64, 1)
            mixed[r, cs] = (top / under).astype(LOW)

    def middle(i):
        r = pl.ds(i * 256, 256)
        pre = tokens[r, :].astype(jnp.float32) + (dot(mixed[r, :], attn_full[:, pl.ds(3 * width, width)], NT) + vec[2:3, :])
        hidden[r, :] = norm(pre, vec[3:4, :], vec[4:5, :])[0]

    def masked_rows():
        for s in range(seqs):
            r = pl.ds(s * padded, padded)
            rs = pl.ds(s * length, length)
            rows_m[0, r, :] = dot(pick[s], tokens[rs, :], NN).astype(LOW)
            mixed_m[0, r, :] = dot(pick[s], mixed[rs, :], NN).astype(LOW)
            query_m[r, :] = dot(pick[s], qkv[0, rs, :], NN).astype(LOW)
        pre = rows_m[0].astype(jnp.float32) + (dot(mixed_m[0], attn_full[:, pl.ds(3 * width, width)], NT) + vec[2:3, :])
        value, normed, inverse = norm(pre, vec[3:4, :], vec[4:5, :])
        hid_f[...] = value
        hid_m[0] = value.astype(LOW)
        normed_one[...] = normed
        inverse_one[...] = jnp.broadcast_to(inverse, inverse_one.shape)
        swap(rows_m, 0)
        swap(mixed_m, 1)
        swap(hid_m, 2)
        keep(query_m, query_o, 3)
        keep(normed_one, normed_o, 4)
        keep(inverse_one, inv_o, 5)

    def upper(k):
        f = pl.ds(k * 768, 768)
        u = dot(hid_m[0], up_full[:, f], NN) + bias[:, f]
        cumul = 0.5 * (1.0 + lax.erf(u * SQRT_HALF))
        act_m[0, :, f] = (u * cumul).astype(LOW)
        slope[:, f] = cumul + u * (jnp.exp(-0.5 * u * u) * INV_ROOT_TWO_PI)

    def after_upper():
        swap(act_m, 3)
        keep(slope, slope_o, 6)

    def lower():
        @pl.loop(0, 3)
        def _(k):
            n = pl.ds(pl.multiple_of(k * 256, 256), 256)
            ytwo[:, n] = dot(act_m[0], down_full[n, :], NT)

        pre = hid_f[...] + (ytwo[...] + vec[5:6, :])
        _, normed, inverse = norm(pre, vec[6:7, :], vec[7:8, :])
        value, dgain, dshift = norm_pull(grad[...].astype(jnp.float32), normed, inverse, vec[6:7, :])
        dtwo[...] = value
        dlow[0] = value.astype(LOW)
        dvec[...] = jnp.zeros_like(dvec)
        dvec[5:6, :] = jnp.sum(value, axis=0, keepdims=True)
        dvec[6:7, :] = dgain
        dvec[7:8, :] = dshift
        swap(dlow, 4)
        keep(dtwo, dtwo_o, 7)
        keep(dvec, dvec_o, 8)

    meet(z, y, x, c, False)
    small_push(zh, z, y, UP, above, small)
    small_push(zl, z, y, DOWN, below, small)
    small_push(None, z, y, SIDE, beside, small)
    own(0)
    w = z * 2 + y
    copies = []
    for p in range(3):
        copies.append(pltpu.make_async_copy(shards[p], fulls[p].at[pl.ds(pl.multiple_of(w * rows, rows), rows)], own_sem.at[p]))
    copies.append(pltpu.make_async_copy(small, small_full.at[w], own_sem.at[3]))
    for copy in copies:
        copy.start()
    for d in range(1, 4):
        small_z(d)

    def save_hidden():
        keep(hidden, hidden_o, 9)
        keep(qkv.at[pl.ds(1, 2)], kv_o, 10)

    head = [
        lambda: z_step(0, 1), lambda: own(1), lambda: y_step(0, 0), lambda: z_step(0, 2), lambda: y_step(0, 1), lambda: x_step(0, 0), lambda: z_step(0, 3),
        lambda: y_step(0, 2), lambda: x_step(0, 1), vectors, lambda: z_step(1, 1), lambda: own(2), lambda: y_step(0, 3), lambda: x_step(0, 2), lambda: z_step(1, 2), lambda: y_step(1, 0), lambda: x_step(0, 3), lambda: z_step(1, 3),
        lambda: last(0),
    ]
    links = [
        lambda: y_step(1, 1), lambda: x_step(1, 0), lambda: z_step(2, 1), lambda: y_step(1, 2), lambda: x_step(1, 1), lambda: z_step(2, 2), lambda: y_step(1, 3), lambda: x_step(1, 2), lambda: z_step(2, 3),
        lambda: y_step(2, 0), lambda: x_step(1, 3), lambda: y_step(2, 1), lambda: x_step(2, 0), lambda: y_step(2, 2),
    ]
    work = [functools.partial(project, i) for i in range(4)]
    work += [functools.partial(attend, s, j) for s in range(seqs) for j in range(width // 128)]
    work += [functools.partial(middle, i) for i in range(4)]
    work += [masked_rows]
    for step in head:
        step()
    done = 0
    for k, step in enumerate(links):
        upto = len(work) * (k + 1) // len(links)
        for piece in work[done:upto]:
            piece()
        done = upto
        step()
    save_hidden()
    last(1)
    for k in range(4):
        upper(k)
        (lambda: x_step(2, 1), lambda: y_step(2, 3), lambda: x_step(2, 2), lambda: x_step(2, 3))[k]()
    after_upper()
    last(2)
    lower()
    keep(vec, vec_o, 11)
    keep(bias, bias_o, 12)
    for make, ref in swaps:
        make().wait_recv()
    for k, (ref, dst) in enumerate(((rows_m, rows_o), (mixed_m, mixed_o), (hid_m, hid_o), (act_m, act_o), (dlow, dlow_o))):
        keep(ref, dst, 13 + k)
    for make, ref in swaps:
        make().wait_send()
    sends.finish()
    for copy in saves:
        copy.wait()


def forward(attn, up, down, small, tokens, pick, grad):
    rows, cols = attn.shape
    width = tokens.shape[1]
    seqs, padded, length = pick.shape
    total = tokens.shape[0]
    count = seqs * padded
    shape = jax.ShapeDtypeStruct
    f = jnp.float32
    full = shape((8 * rows, cols), LOW)
    anywhere = pl.BlockSpec(memory_space=pl.ANY)
    vm = pl.BlockSpec(memory_space=pltpu.VMEM)
    dma = pltpu.SemaphoreType.DMA
    outs = (
        full, full, full, shape((8, width), f), shape((1, cols), f), shape((2, total, width), LOW), shape((total, width), f),
        shape((count, width), LOW), shape((2, count, width), LOW), shape((2, count, width), LOW), shape((2, count, width), LOW),
        shape((2, count, cols), LOW), shape((count, cols), f), shape((count, width), f), shape((2, count, width), LOW),
        shape((count, width), f), shape((count, 128), f), shape((8, width), f),
    )
    v = pltpu.VMEM
    return pl.pallas_call(
        functools.partial(forward_kernel, rows, seqs, length, padded),
        out_shape=outs,
        in_specs=[anywhere] * 4 + [vm] * 3,
        out_specs=(anywhere,) * len(outs),
        scratch_shapes=[
            v((8 * rows, cols), LOW), v((8 * rows, cols), LOW), v((8 * rows, cols), LOW), v((8, 16, 128), LOW),
            v((3, total, width), LOW), v((total, width), LOW), v((total, width), f), v((8, width), f), v((3, 1, width), f), v((1, cols), f),
            v((count, width), LOW), v((2, count, width), LOW), v((2, count, width), LOW), v((2, count, width), LOW), v((2, count, cols), LOW),
            v((count, cols), f), v((count, width), f), v((count, width), f), v((2, count, width), LOW), v((8, width), f),
            v((count, width), f), v((count, width), f), v((count, 128), f),
            dma((6, 3, 8)), dma((3, 8, 3)), dma((3, 8)), dma((8,)), dma((4,)), dma((18,)), dma((5,)), dma((5,)),
        ],
        compiler_params=pltpu.CompilerParams(collective_id=0, has_side_effects=True, vmem_limit_bytes=60 * 2**20),
    )(attn, up, down, small, tokens, pick, grad)


def masks(mask_place, mask_count, gradient, length):
    seqs, slots = mask_place.shape
    padded = -(-slots // 16) * 16
    live = jnp.arange(padded)[None, :] < mask_count[:, None]
    spots = jnp.pad(mask_place, ((0, 0), (0, padded - slots)), constant_values=-1)
    pick = (spots[:, :, None] == jnp.arange(length)[None, None, :]) & live[:, :, None]
    gradient = jnp.pad(gradient, ((0, 0), (0, padded - slots), (0, 0)))
    gradient = jnp.where(live[:, :, None], gradient, jnp.zeros_like(gradient))
    return pick, gradient.reshape(seqs * padded, -1)


def update(weights, moments, grads, grad_norm):
    factor = CLIP_LIMIT / jnp.maximum(grad_norm, CLIP_LIMIT)
    rates = (LEARN_RATE, OUTPUT_RATE, LEARN_RATE, LEARN_RATE, VECTOR_RATE, BIAS_RATE)
    out = ()
    for k in range(6):
        out += adam_step(weights[k], *moments[k], grads[k], factor, DECAY_RATE if k < 4 else 0.0, rates[k])
    return out


def natural(own_attn, own_up, own_down, own_vectors, own_bias):
    width = own_up.shape[1] // 4
    own_qkv = jnp.swapaxes(own_attn[:, : 3 * width].reshape(-1, 3, width), 0, 1)
    return own_qkv, own_attn[:, 3 * width :].T, own_up, own_down.T, own_vectors, own_bias


def finish(weights, moments, grads):
    grad_norm = jnp.sqrt(lax.psum(sum(jnp.sum(v * v) for v in grads), "wide"))
    return (grad_norm,) + update(weights, moments, natural(*grads), grad_norm)


def pack(qkv, out, up, down):
    attn = jnp.concatenate([qkv[0], qkv[1], qkv[2], out.T], axis=1)
    return attn.astype(jnp.bfloat16), up.astype(jnp.bfloat16), down.T.astype(jnp.bfloat16)


def small_pack(vectors, bias):
    rows = vectors.shape[1]
    return jnp.concatenate([jnp.pad(vectors, ((0, 0), (0, 128 - rows))), bias.reshape(-1, 128), jnp.zeros((5, 128))])


def plain(tokens, pick, gradient, weights):
    low = jnp.bfloat16
    seqs, length, width = tokens.shape
    padded = pick.shape[1]
    flat = tokens.reshape(seqs * length, width)
    attn_w, up_w, down_w = (lax.all_gather(v, "wide", axis=0, tiled=True) for v in pack(*weights[:4]))
    vec = lax.all_gather(weights[4].astype(low), "wide", axis=1, tiled=True).astype(jnp.float32)
    bias = lax.all_gather(weights[5].astype(low), "wide", axis=0, tiled=True).astype(jnp.float32)
    wq, wk, wv, wo = (attn_w[:, k * width : (k + 1) * width] for k in range(4))
    query = (mm(flat, wq, NN) + vec[0]).astype(low)
    key = mm(flat, wk, NN, low)
    value = (mm(flat, wv, NN) + vec[1]).astype(low)
    query, key, value = (split_heads(v, seqs, length) for v in (query, key, value))
    mixed = lax.map(attend, (query, key, value)).reshape(seqs * length, width)

    def middle(rows, mixed):
        pre_one = rows.astype(jnp.float32) + (mm(mixed, wo, NT) + vec[2])
        hidden, normed, inverse = layer_norm(pre_one, vec[3], vec[4])
        hidden_low = hidden.astype(low)
        upper = mm(hidden_low, up_w, NN) + bias
        cumul = 0.5 * (1.0 + lax.erf(upper * SQRT_HALF))
        active = (upper * cumul).astype(low)
        pre_two = hidden + (mm(active, down_w, NT) + vec[5])
        return layer_norm(pre_two, vec[6], vec[7]), normed, inverse, hidden_low, upper, cumul, active

    layer_out = middle(flat, mixed)[0][0].astype(low)
    pick_low = pick.astype(low)

    def take(values):
        values = values.reshape(seqs, length, width)
        return jnp.einsum("sil,sld->sid", pick_low, values, preferred_element_type=jnp.float32).astype(low)

    rows_m = take(flat).reshape(seqs * padded, width)
    mixed_m = take(mixed).reshape(seqs * padded, width)
    query_m = split_heads(take(query), seqs, padded)
    (_, normed_two, inverse_two), normed_one, inverse_one, hidden_m, upper, cumul, active = middle(rows_m, mixed_m)
    dpre_two, dgain_two, dshift_two = norm_back(gradient.astype(jnp.float32), normed_two, inverse_two, vec[6])
    dbias_two = jnp.sum(dpre_two, axis=0)
    dtwo_low = dpre_two.astype(low)
    ddown = mm(dtwo_low, active, TN)
    dactive = mm(dtwo_low, down_w, NN)
    density = jnp.exp(-0.5 * upper * upper) * INV_ROOT_TWO_PI
    dupper = dactive * (cumul + upper * density)
    dup_bias = jnp.sum(dupper, axis=0)
    dupper_low = dupper.astype(low)
    dup = mm(hidden_m, dupper_low, TN)
    dhidden = dpre_two + mm(dupper_low, up_w, NT)
    dpre_one, dgain_one, dshift_one = norm_back(dhidden, normed_one, inverse_one, vec[3])
    dbias_out = jnp.sum(dpre_one, axis=0)
    done_low = dpre_one.astype(low)
    dout = mm(done_low, mixed_m, TN)
    dmixed = split_heads(mm(done_low, wo, NN, low), seqs, padded)
    dquery, dkey, dvalue = lax.map(attend_back, (query_m, key, value, dmixed))
    dquery = dquery.reshape(seqs * padded, width)
    dkey = dkey.reshape(seqs * length, width)
    dvalue = dvalue.reshape(seqs * length, width)
    dbias_query = jnp.sum(dquery, axis=0)
    dbias_value = jnp.sum(dvalue, axis=0)
    dquery, dkey, dvalue = dquery.astype(low), dkey.astype(low), dvalue.astype(low)
    dattn = jnp.concatenate([mm(rows_m, dquery, TN), mm(flat, dkey, TN), mm(flat, dvalue, TN), dout], axis=1)
    masked_part = dpre_one + mm(dquery, wq, NT)
    dtokens = spread(pick, masked_part) + mm(dkey, wk, NT) + mm(dvalue, wv, NT)
    dvectors = jnp.stack(
        [dbias_query, dbias_value, dbias_out, dgain_one, dshift_one, dbias_two, dgain_two, dshift_two]
    )

    def owned(value, dim):
        return lax.psum(lax.psum_scatter(value, "wide", scatter_dimension=dim, tiled=True), "narrow")

    grads = (owned(dattn, 0), owned(dup, 0), owned(ddown, 0), owned(dvectors, 1), owned(dup_bias, 0))
    return layer_out, dtokens, grads


def spread(pick, rows):
    seqs, padded, length = pick.shape
    return jnp.einsum(
        "sil,sid->sld",
        pick.astype(jnp.float32),
        rows.reshape(seqs, padded, -1),
        precision=lax.Precision.HIGHEST,
        preferred_element_type=jnp.float32,
    ).reshape(seqs * length, -1)


def tailored(tokens, pick, gradient, weights):
    low = jnp.bfloat16
    seqs, length, width = tokens.shape
    padded = pick.shape[1]
    flat = tokens.reshape(seqs * length, width)
    (
        attn_w, up_w, down_w, vec, bias, kv, hidden, query_m, rows_m, mixed_m, hidden_m, active, slope, dpre_two, dtwo_low, normed_one, inverse_one, dvec,
    ) = forward(*pack(*weights[:4]), small_pack(*weights[4:]).astype(low), flat, pick.astype(low), gradient)
    wq, wk, wv, wo = (attn_w[:, k * width : (k + 1) * width] for k in range(4))
    hidden_low = hidden.astype(low)
    upper = mm(hidden_low, up_w, NN) + bias
    cumul = 0.5 * (1.0 + lax.erf(upper * SQRT_HALF))
    pre_two = hidden + (mm((upper * cumul).astype(low), down_w, NT) + vec[5])
    layer_out = layer_norm(pre_two, vec[6], vec[7])[0].astype(low)

    ddown = mm(dtwo_low[0], active[0], TN, low)
    dupper = mm(dtwo_low[0], down_w, NN) * slope
    dup_bias = jnp.sum(dupper, axis=0)
    dupper_low = dupper.astype(low)
    dup = mm(hidden_m[0], dupper_low, TN, low)
    dhidden = dpre_two + mm(dupper_low, up_w, NT)
    dpre_one, dgain_one, dshift_one = norm_back(dhidden, normed_one, inverse_one[:, :1], vec[3])
    dbias_out = jnp.sum(dpre_one, axis=0)
    done_low = dpre_one.astype(low)
    dout = mm(done_low, mixed_m[0], TN, low)
    dmixed = split_heads(mm(done_low, wo, NN, low), seqs, padded)
    dquery, dkey, dvalue = lax.map(
        attend_back, (split_heads(query_m * 8, seqs, padded), split_heads(kv[0], seqs, length), split_heads(kv[1], seqs, length), dmixed)
    )
    dquery = dquery.reshape(seqs * padded, width)
    dkey = dkey.reshape(seqs * length, width)
    dvalue = dvalue.reshape(seqs * length, width)
    dbias_query = jnp.sum(dquery, axis=0)
    dbias_value = jnp.sum(dvalue, axis=0)
    dquery, dkey, dvalue = dquery.astype(low), dkey.astype(low), dvalue.astype(low)
    dattn = jnp.concatenate([mm(rows_m[0], dquery, TN, low), mm(flat, dkey, TN, low), mm(flat, dvalue, TN, low), dout], axis=1)
    masked_part = dpre_one + mm(dquery, wq, NT)
    dtokens = spread(pick, masked_part) + mm(dkey, wk, NT) + mm(dvalue, wv, NT)
    dvectors = jnp.stack([dbias_query, dbias_value, dbias_out, dgain_one, dshift_one, dvec[5], dvec[6], dvec[7]])
    rows = width // 8
    small = jnp.concatenate(
        [
            jnp.pad(jnp.swapaxes(dvectors.reshape(8, 8, rows), 0, 1), ((0, 0), (0, 0), (0, 128 - rows))),
            dup_bias.reshape(8, 3, 128),
            jnp.zeros((8, 5, 128)),
        ],
        axis=1,
    )
    own, small = reduce(dattn, dup, ddown, small)
    own = own.astype(jnp.float32)
    return layer_out, dtokens, (own[0], own[1], own[2], small[:8, :rows], small[8:11].reshape(-1))


def shards(body, tokens, mask_place, mask_count, masked_output_gradient, *parameters):
    seqs, length, width = tokens.shape
    weights = parameters[0::3]
    moments = tuple(zip(parameters[1::3], parameters[2::3]))
    pick, gradient = masks(mask_place, mask_count, masked_output_gradient, length)
    layer_out, dtokens, grads = body(tokens, pick, gradient, weights)
    return (layer_out.reshape(seqs, length, width), dtokens.reshape(seqs, length, width)) + finish(weights, moments, grads)


def solution(mesh):
    body = tailored if mesh.shape["wide"] == 8 and mesh.shape["narrow"] == 4 else plain
    data = P(("wide", "narrow"))
    rows = P("wide")
    columns = P(None, "wide")
    weights = (columns,) * 6 + (rows,) * 3 + (columns,) * 6 + (rows,) * 3
    return jax.shard_map(
        functools.partial(shards, body),
        mesh=mesh,
        in_specs=(data,) * 4 + weights,
        out_specs=(data, data, P()) + weights,
        check_vma=False,
    )
```

```python
import functools

import jax
import jax.numpy as jnp
from jax import lax
from jax.experimental import pallas as pl
from jax.experimental.pallas import tpu as pltpu
from jax.sharding import PartitionSpec as P

HEADS = 12
HEAD_DIM = 64
STEP = 10

LN_EPS = 1e-06
SQRT_HALF = 0.7071067811865476
INV_ROOT_TWO_PI = 0.3989422804014327
CLIP_LIMIT = 1.0
BETA_ONE = 0.9
BETA_TWO = 0.999
LEARN_RATE = 0.05
OUTPUT_RATE = 0.2
VECTOR_RATE = 0.5
BIAS_RATE = 0.3
DECAY_RATE = 0.01
ADAM_EPS = 1e-08

MESH = pl.DeviceIdType.MESH


def when(cond, body):
    if callable(cond):
        cond = cond()
    if cond is None:
        body()
    else:
        pl.when(cond)(body)


class Sends:
    def __init__(self):
        self.started = []

    def start(self, cond, make):
        when(cond, lambda: make().start())
        self.started.append((cond, make))

    def finish(self):
        for cond, make in self.started:
            when(cond, lambda make=make: make().wait_send())


def both(a, b):
    return b if a is None else (a if b is None else jnp.logical_and(a, b))


def place():
    w, n = lax.axis_index("wide"), lax.axis_index("narrow")
    return w // 2, lax.rem(w, 2), n // 2, lax.rem(n, 2)


def flip(v):
    return 1 - v


def dev(z, y, x, c):
    return (z * 2 + y, x * 2 + c)


def meet(z, y, x, c, diagonal):
    bar = pltpu.get_barrier_semaphore()
    peers = [(None, dev(z, flip(y), x, c)), (None, dev(z, y, flip(x), c)), (None, dev(z, y, x, flip(c)))]
    if diagonal:
        peers.append((None, dev(z, y, flip(x), flip(c))))
    peers += [(z > 0, dev(z - 1, y, x, c)), (z < 3, dev(z + 1, y, x, c))]
    for cond, peer in peers:
        when(cond, lambda peer=peer: pl.semaphore_signal(bar, inc=1, device_id=peer, device_id_type=MESH))
    inner = jnp.logical_and(z > 0, z < 3)
    count = 4 if diagonal else 3
    pl.semaphore_wait(bar, count + 1 + jnp.where(inner, 1, 0))


def gather_kernel(rows, cols, attn, up, down, small, attn_full, up_full, down_full, small_full, send_sem, recv_sem, small_send, small_recv, own_sem):
    z, y, x, c = place()
    edge = x == c
    third = cols // 3
    mine, across = x + c, 2 * flip(x)
    fulls = (attn_full, up_full, down_full)
    shards = (attn, up, down)
    sends = Sends()
    zl, zh = z > 0, z < 3

    def spot(p, zz, yy, t):
        return fulls[p].at[pl.ds(pl.multiple_of((zz * 2 + yy) * rows, rows), rows), pl.ds(pl.multiple_of(t * third, third), third)]

    def push(cond, p, zz, yy, t, kind, to, src=None):
        def make():
            w = zz * 2 + yy
            where = spot(p, zz, yy, t)
            return pltpu.make_async_remote_copy(
                src_ref=where if src is None else src,
                dst_ref=where,
                send_sem=send_sem.at[kind, p, w],
                recv_sem=recv_sem.at[p, w, t],
                device_id=to,
                device_id_type=MESH,
            )

        sends.start(cond, make)

    def small_push(cond, zz, yy, kind, to, src=None):
        def make():
            w = zz * 2 + yy
            where = small_full.at[w]
            return pltpu.make_async_remote_copy(
                src_ref=where if src is None else src,
                dst_ref=where,
                send_sem=small_send.at[kind, w],
                recv_sem=small_recv.at[w],
                device_id=to,
                device_id_type=MESH,
            )

        sends.start(cond, make)

    def arrive(cond, p, zz, yy, t):
        def body():
            where = spot(p, zz, yy, t)
            w = zz * 2 + yy
            pltpu.make_async_remote_copy(where, where, send_sem.at[0, p, w], recv_sem.at[p, w, t], dev(z, y, x, c), device_id_type=MESH).wait_recv()

        when(cond, body)

    def small_arrive(cond, zz, yy):
        def body():
            w = zz * 2 + yy
            pltpu.make_async_remote_copy(small_full.at[w], small_full.at[w], small_send.at[0, w], small_recv.at[w], dev(z, y, x, c), device_id_type=MESH).wait_recv()

        when(cond, body)

    UP, DOWN, SIDE, OVER, NEAR, PASS = range(6)
    above, below, beside = dev(z + 1, y, x, c), dev(z - 1, y, x, c), dev(z, flip(y), x, c)
    over, near = dev(z, y, flip(x), c), dev(z, y, x, flip(c))

    def own(p):
        src = shards[p].at[:, pl.ds(pl.multiple_of(mine * third, third), third)]
        push(zh, p, z, y, mine, UP, above, src)
        push(zl, p, z, y, mine, DOWN, below, src)
        push(None, p, z, y, mine, SIDE, beside, src)

    def z_step(p, d):
        for cond, zz, onward, kind, to in ((z - d >= 0, z - d, zh, UP, above), (z + d <= 3, z + d, zl, DOWN, below)):
            arrive(cond, p, zz, y, mine)
            push(both(cond, onward), p, zz, y, mine, kind, to)
            push(cond, p, zz, y, mine, SIDE, beside)
            push(both(cond, edge), p, zz, y, mine, OVER, over)
            push(cond, p, zz, y, mine, NEAR, near)

    def y_step(p, d):
        steps = ((None, z),) if d == 0 else ((z - d >= 0, z - d), (z + d <= 3, z + d))
        for cond, zz in steps:
            arrive(cond, p, zz, flip(y), mine)
            push(both(cond, edge), p, zz, flip(y), mine, OVER, over)
            push(cond, p, zz, flip(y), mine, NEAR, near)

    def x_step(p, d):
        mid = jnp.logical_not(edge)
        for yy in (y, flip(y)):
            if d == 0:
                steps = () if yy is y else ((None, z),)
            else:
                steps = ((z - d >= 0, z - d), (z + d <= 3, z + d))
            for cond, zz in steps:
                cond = both(cond, mid)
                arrive(cond, p, zz, yy, across)
                push(cond, p, zz, yy, across, PASS, near)

    def last(p, d):
        for yy in (y, flip(y)):
            if d == 0:
                steps = () if yy is y else ((None, z),)
            else:
                steps = ((z - d >= 0, z - d), (z + d <= 3, z + d))
            for cond, zz in steps:
                arrive(cond, p, zz, yy, x + flip(c))
                arrive(both(cond, edge), p, zz, yy, across)

    def small_z(d):
        for cond, zz, onward, kind, to in ((z - d >= 0, z - d, zh, UP, above), (z + d <= 3, z + d, zl, DOWN, below)):
            small_arrive(cond, zz, y)
            small_push(both(cond, onward), zz, y, kind, to)
            small_push(cond, zz, y, SIDE, beside)

    meet(z, y, x, c, False)
    small_push(zh, z, y, UP, above, small)
    small_push(zl, z, y, DOWN, below, small)
    small_push(None, z, y, SIDE, beside, small)
    own(0)
    w = z * 2 + y
    copies = []
    for p in range(3):
        copies.append(pltpu.make_async_copy(shards[p], fulls[p].at[pl.ds(pl.multiple_of(w * rows, rows), rows)], own_sem.at[p]))
    copies.append(pltpu.make_async_copy(small, small_full.at[w], own_sem.at[3]))
    for copy in copies:
        copy.start()
    for d in range(1, 4):
        small_z(d)
    order = [
        lambda: z_step(0, 1), lambda: own(1), lambda: y_step(0, 0), lambda: z_step(0, 2), lambda: y_step(0, 1), lambda: x_step(0, 0), lambda: z_step(0, 3),
        lambda: y_step(0, 2), lambda: x_step(0, 1), lambda: z_step(1, 1), lambda: own(2), lambda: y_step(0, 3), lambda: x_step(0, 2), lambda: z_step(1, 2), lambda: y_step(1, 0), lambda: x_step(0, 3), lambda: z_step(1, 3),
        lambda: y_step(1, 1), lambda: x_step(1, 0), lambda: z_step(2, 1), lambda: y_step(1, 2), lambda: x_step(1, 1), lambda: z_step(2, 2), lambda: y_step(1, 3), lambda: x_step(1, 2), lambda: z_step(2, 3),
        lambda: y_step(2, 0), lambda: x_step(1, 3), lambda: y_step(2, 1), lambda: x_step(2, 0), lambda: y_step(2, 2), lambda: x_step(2, 1), lambda: y_step(2, 3), lambda: x_step(2, 2), lambda: x_step(2, 3),
    ]
    for step in order:
        step()
    for d in range(4):
        for cond, zz in (((None, z),) if d == 0 else ((z - d >= 0, z - d), (z + d <= 3, z + d))):
            small_arrive(cond, zz, flip(y))
    for p in range(3):
        for d in range(4):
            last(p, d)
    sends.finish()
    for copy in copies:
        copy.wait()


def gather(attn, up, down, small):
    rows, cols = attn.shape
    full = jax.ShapeDtypeStruct((8 * rows, cols), attn.dtype)
    anywhere = pl.BlockSpec(memory_space=pl.ANY)
    return pl.pallas_call(
        functools.partial(gather_kernel, rows, cols),
        out_shape=(full, full, full, jax.ShapeDtypeStruct((8,) + small.shape, small.dtype)),
        in_specs=[anywhere] * 4,
        out_specs=(anywhere,) * 4,
        scratch_shapes=[
            pltpu.SemaphoreType.DMA((6, 3, 8)),
            pltpu.SemaphoreType.DMA((3, 8, 3)),
            pltpu.SemaphoreType.DMA((3, 8)),
            pltpu.SemaphoreType.DMA((8,)),
            pltpu.SemaphoreType.DMA((4,)),
        ],
        compiler_params=pltpu.CompilerParams(collective_id=0, has_side_effects=True),
    )(attn, up, down, small)


def layer_norm(values, gain, shift):
    center = values - jnp.mean(values, axis=-1, keepdims=True)
    inverse = lax.rsqrt(jnp.mean(center * center, axis=-1, keepdims=True) + LN_EPS)
    normed = center * inverse
    return (normed * gain + shift, normed, inverse)


def norm_back(incoming, normed, inverse, gain):
    dgain = jnp.sum(incoming * normed, axis=0)
    dshift = jnp.sum(incoming, axis=0)
    scaled = incoming * gain
    dvalues = inverse * (
        scaled
        - jnp.mean(scaled, axis=-1, keepdims=True)
        - normed * jnp.mean(scaled * normed, axis=-1, keepdims=True)
    )
    return (dvalues, dgain, dshift)


def mm(a, b, dims, out=jnp.float32):
    return lax.dot_general(a, b, (dims, ((), ())), preferred_element_type=jnp.float32).astype(out)


NN = ((1,), (0,))
NT = ((1,), (1,))
TN = ((0,), (0,))


def split_heads(values, seqs, length):
    return values.reshape(seqs, length, HEADS, HEAD_DIM)


def attend(pieces):
    query, key, value = pieces
    raw = jnp.einsum("qhe,khe->hqk", query, key, preferred_element_type=jnp.float32) * HEAD_DIM ** (
        -0.5
    )
    peak = jnp.max(raw, axis=-1, keepdims=True)
    expo = jnp.exp(raw - peak)
    total = jnp.sum(expo, axis=-1, keepdims=True)
    probs = (expo / total).astype(jnp.bfloat16)
    mixed = jnp.einsum("hqk,khe->qhe", probs, value, preferred_element_type=jnp.float32)
    return mixed.astype(jnp.bfloat16)


def attend_back(pieces):
    query, key, value, dmixed = pieces
    scale = HEAD_DIM ** (-0.5)
    raw = jnp.einsum("qhe,khe->hqk", query, key, preferred_element_type=jnp.float32) * scale
    probs = jax.nn.softmax(raw, axis=-1)
    dprobs = jnp.einsum("qhe,khe->hqk", dmixed, value, preferred_element_type=jnp.float32)
    dscore = probs * (dprobs - jnp.sum(dprobs * probs, axis=-1, keepdims=True))
    dscore = (dscore * scale).astype(jnp.bfloat16)
    dquery = jnp.einsum("hqk,khe->qhe", dscore, key, preferred_element_type=jnp.float32)
    dkey = jnp.einsum("hqk,qhe->khe", dscore, query, preferred_element_type=jnp.float32)
    dvalue = jnp.einsum(
        "hqk,qhe->khe", probs.astype(jnp.bfloat16), dmixed, preferred_element_type=jnp.float32
    )
    return (dquery, dkey, dvalue)


def adam_step(weight, first, second, grad, factor, decay, rate):
    grad = grad * factor
    first_new = BETA_ONE * first + (1.0 - BETA_ONE) * grad
    second_new = BETA_TWO * second + (1.0 - BETA_TWO) * grad * grad
    mean_hat = first_new / (1.0 - BETA_ONE**STEP)
    square_hat = second_new / (1.0 - BETA_TWO**STEP)
    weight_new = weight - rate * (mean_hat / (jnp.sqrt(square_hat) + ADAM_EPS) + decay * weight)
    return (weight_new, first_new, second_new)


def dot(a, b, dims):
    return lax.dot_general(a, b, (dims, ((), ())), preferred_element_type=jnp.float32)


NN = ((1,), (0,))
NT = ((1,), (1,))
TN = ((0,), (0,))
LOW = jnp.bfloat16


def norm(values, gain, shift):
    center = values - jnp.mean(values, axis=-1, keepdims=True)
    inverse = lax.rsqrt(jnp.mean(center * center, axis=-1, keepdims=True) + LN_EPS)
    normed = center * inverse
    return normed * gain + shift, normed, inverse


def norm_pull(incoming, normed, inverse, gain):
    dgain = jnp.sum(incoming * normed, axis=0, keepdims=True)
    dshift = jnp.sum(incoming, axis=0, keepdims=True)
    scaled = incoming * gain
    return (
        inverse * (scaled - jnp.mean(scaled, axis=-1, keepdims=True) - normed * jnp.mean(scaled * normed, axis=-1, keepdims=True)),
        dgain,
        dshift,
    )


def forward_kernel(
    rows, seqs, length, padded,
    attn, up, down, small, tokens, pick, grad,
    attn_o, up_o, down_o, vec_o, bias_o, kv_o, hidden_o, query_o, rows_o, mixed_o, hid_o, act_o, slope_o, dtwo_o, dlow_o, normed_o, inv_o, dvec_o,
    attn_full, up_full, down_full, small_full,
    qkv, mixed, hidden, vec, qbias, bias, query_m, rows_m, mixed_m, hid_m, act_m, slope, ytwo, dtwo, dlow, dvec, hid_f, normed_one, inverse_one,
    send_sem, recv_sem, small_send, small_recv, own_sem, save_sem, pair_send, pair_recv,
):
    z, y, x, c = place()
    width = tokens.shape[1]
    cols = attn.shape[1]
    edge = x == c
    third = cols // 3
    mine, across = x + c, 2 * flip(x)
    fulls = (attn_full, up_full, down_full)
    shards = (attn, up, down)
    sends = Sends()
    zl, zh = z > 0, z < 3
    count = seqs * padded

    def spot(p, zz, yy, t):
        return fulls[p].at[pl.ds(pl.multiple_of((zz * 2 + yy) * rows, rows), rows), pl.ds(pl.multiple_of(t * third, third), third)]

    def push(cond, p, zz, yy, t, kind, to, src=None):
        def make():
            w = zz * 2 + yy
            where = spot(p, zz, yy, t)
            return pltpu.make_async_remote_copy(
                src_ref=where if src is None else src,
                dst_ref=where,
                send_sem=send_sem.at[kind, p, w],
                recv_sem=recv_sem.at[p, w, t],
                device_id=to,
                device_id_type=MESH,
            )

        sends.start(cond, make)

    def small_push(cond, zz, yy, kind, to, src=None):
        def make():
            w = zz * 2 + yy
            where = small_full.at[w]
            return pltpu.make_async_remote_copy(
                src_ref=where if src is None else src,
                dst_ref=where,
                send_sem=small_send.at[kind, w],
                recv_sem=small_recv.at[w],
                device_id=to,
                device_id_type=MESH,
            )

        sends.start(cond, make)

    def arrive(cond, p, zz, yy, t):
        def body():
            where = spot(p, zz, yy, t)
            w = zz * 2 + yy
            pltpu.make_async_remote_copy(where, where, send_sem.at[0, p, w], recv_sem.at[p, w, t], dev(z, y, x, c), device_id_type=MESH).wait_recv()

        when(cond, body)

    def small_arrive(cond, zz, yy):
        def body():
            w = zz * 2 + yy
            pltpu.make_async_remote_copy(small_full.at[w], small_full.at[w], small_send.at[0, w], small_recv.at[w], dev(z, y, x, c), device_id_type=MESH).wait_recv()

        when(cond, body)

    UP, DOWN, SIDE, OVER, NEAR, PASS = range(6)
    above, below, beside = dev(z + 1, y, x, c), dev(z - 1, y, x, c), dev(z, flip(y), x, c)
    over, near = dev(z, y, flip(x), c), dev(z, y, x, flip(c))

    def around(d):
        return ((None, z),) if d == 0 else ((z - d >= 0, z - d), (z + d <= 3, z + d))

    def own(p):
        src = shards[p].at[:, pl.ds(pl.multiple_of(mine * third, third), third)]
        push(zh, p, z, y, mine, UP, above, src)
        push(zl, p, z, y, mine, DOWN, below, src)
        push(None, p, z, y, mine, SIDE, beside, src)

    def z_step(p, d):
        for cond, zz, onward, kind, to in ((z - d >= 0, z - d, zh, UP, above), (z + d <= 3, z + d, zl, DOWN, below)):
            arrive(cond, p, zz, y, mine)
            push(both(cond, onward), p, zz, y, mine, kind, to)
            push(cond, p, zz, y, mine, SIDE, beside)
            push(both(cond, edge), p, zz, y, mine, OVER, over)
            push(cond, p, zz, y, mine, NEAR, near)

    def y_step(p, d):
        for cond, zz in around(d):
            arrive(cond, p, zz, flip(y), mine)
            push(both(cond, edge), p, zz, flip(y), mine, OVER, over)
            push(cond, p, zz, flip(y), mine, NEAR, near)

    def x_step(p, d):
        mid = jnp.logical_not(edge)
        for yy in (y, flip(y)):
            for cond, zz in () if d == 0 and yy is y else around(d):
                cond = both(cond, mid)
                arrive(cond, p, zz, yy, across)
                push(cond, p, zz, yy, across, PASS, near)

    def last(p):
        for d in range(4):
            for yy in (y, flip(y)):
                for cond, zz in () if d == 0 and yy is y else around(d):
                    arrive(cond, p, zz, yy, x + flip(c))
                    arrive(both(cond, edge), p, zz, yy, across)
        copies[p].wait()
        keep(fulls[p], (attn_o, up_o, down_o)[p], p)

    def small_z(d):
        for cond, zz, onward, kind, to in ((z - d >= 0, z - d, zh, UP, above), (z + d <= 3, z + d, zl, DOWN, below)):
            small_arrive(cond, zz, y)
            small_push(both(cond, onward), zz, y, kind, to)
            small_push(cond, zz, y, SIDE, beside)

    saves = []

    def keep(src, dst, k):
        copy = pltpu.make_async_copy(src, dst, save_sem.at[k])
        copy.start()
        saves.append(copy)

    swaps = []

    def swap(ref, k):
        def make():
            return pltpu.make_async_remote_copy(ref.at[0], ref.at[1], pair_send.at[k], pair_recv.at[k], near, device_id_type=MESH)

        make().start()
        swaps.append((make, ref))

    def vectors():
        for d in range(4):
            for cond, zz in around(d):
                small_arrive(cond, zz, flip(y))
        copies[3].wait()
        at = lax.broadcasted_iota(jnp.int32, (128, width), 0)
        to = lax.broadcasted_iota(jnp.int32, (128, width), 1)
        total = jnp.zeros((16, width), jnp.float32)
        for w in range(8):
            place_w = jnp.logical_and(at + w * rows == to, at < rows).astype(jnp.float32).astype(LOW)
            total += dot(small_full[w], place_w, NN)
            for r in range(3):
                bias[:, pl.ds(w * 384 + r * 128, 128)] = small_full[w, 8 + r : 9 + r, :].astype(jnp.float32)
        vec[...] = total[:8]
        qbias[0] = total[0:1]
        qbias[1] = jnp.zeros((1, width), jnp.float32)
        qbias[2] = total[1:2]

    def project(i):
        r = pl.ds(i * 256, 256)

        @pl.loop(0, 3)
        def _(k):
            value = dot(tokens[r, :], attn_full[:, pl.ds(pl.multiple_of(k * width, width), width)], NN) + qbias[k]
            qkv[k, r, :] = (value * jnp.where(k == 0, 0.125, 1.0)).astype(LOW)

    def attend(s, j):
        lane = lax.broadcasted_iota(jnp.int32, (length, 128), 1) < 64
        cs = pl.ds(j * 128, 128)
        rs = pl.ds(s * length, length)
        key, value = qkv[1, rs, cs], qkv[2, rs, cs]
        zero, one = jnp.zeros_like(key), jnp.ones_like(key)
        keys = (jnp.where(lane, key, zero), jnp.where(lane, zero, key))
        values = (jnp.where(lane, value, one), jnp.where(lane, one, value))
        for q in range(length // 256):
            r = pl.ds(s * length + q * 256, 256)
            query = qkv[0, r, cs]
            parts = []
            for h in range(2):
                score = dot(query, keys[h], NT)
                expo = jnp.exp(score - jnp.max(score, axis=-1, keepdims=True))
                parts.append(dot(expo.astype(LOW), values[h], NN))
            left = lane[:256]
            top = jnp.where(left, parts[0], parts[1])
            under = pltpu.roll(jnp.where(left, parts[1], parts[0]), 64, 1)
            mixed[r, cs] = (top / under).astype(LOW)

    def middle(i):
        r = pl.ds(i * 256, 256)
        pre = tokens[r, :].astype(jnp.float32) + (dot(mixed[r, :], attn_full[:, pl.ds(3 * width, width)], NT) + vec[2:3, :])
        hidden[r, :] = norm(pre, vec[3:4, :], vec[4:5, :])[0]

    def masked_rows():
        for s in range(seqs):
            r = pl.ds(s * padded, padded)
            rs = pl.ds(s * length, length)
            rows_m[0, r, :] = dot(pick[s], tokens[rs, :], NN).astype(LOW)
            mixed_m[0, r, :] = dot(pick[s], mixed[rs, :], NN).astype(LOW)
            query_m[r, :] = dot(pick[s], qkv[0, rs, :], NN).astype(LOW)
        pre = rows_m[0].astype(jnp.float32) + (dot(mixed_m[0], attn_full[:, pl.ds(3 * width, width)], NT) + vec[2:3, :])
        value, normed, inverse = norm(pre, vec[3:4, :], vec[4:5, :])
        hid_f[...] = value
        hid_m[0] = value.astype(LOW)
        normed_one[...] = normed
        inverse_one[...] = jnp.broadcast_to(inverse, inverse_one.shape)
        swap(rows_m, 0)
        swap(mixed_m, 1)
        swap(hid_m, 2)
        keep(query_m, query_o, 3)
        keep(normed_one, normed_o, 4)
        keep(inverse_one, inv_o, 5)

    def upper(k):
        f = pl.ds(k * 768, 768)
        u = dot(hid_m[0], up_full[:, f], NN) + bias[:, f]
        cumul = 0.5 * (1.0 + lax.erf(u * SQRT_HALF))
        act_m[0, :, f] = (u * cumul).astype(LOW)
        slope[:, f] = cumul + u * (jnp.exp(-0.5 * u * u) * INV_ROOT_TWO_PI)

    def after_upper():
        swap(act_m, 3)
        keep(slope, slope_o, 6)

    def lower():
        @pl.loop(0, 3)
        def _(k):
            n = pl.ds(pl.multiple_of(k * 256, 256), 256)
            ytwo[:, n] = dot(act_m[0], down_full[n, :], NT)

        pre = hid_f[...] + (ytwo[...] + vec[5:6, :])
        _, normed, inverse = norm(pre, vec[6:7, :], vec[7:8, :])
        value, dgain, dshift = norm_pull(grad[...].astype(jnp.float32), normed, inverse, vec[6:7, :])
        dtwo[...] = value
        dlow[0] = value.astype(LOW)
        dvec[...] = jnp.zeros_like(dvec)
        dvec[5:6, :] = jnp.sum(value, axis=0, keepdims=True)
        dvec[6:7, :] = dgain
        dvec[7:8, :] = dshift
        swap(dlow, 4)
        keep(dtwo, dtwo_o, 7)
        keep(dvec, dvec_o, 8)

    meet(z, y, x, c, False)
    small_push(zh, z, y, UP, above, small)
    small_push(zl, z, y, DOWN, below, small)
    small_push(None, z, y, SIDE, beside, small)
    own(0)
    w = z * 2 + y
    copies = []
    for p in range(3):
        copies.append(pltpu.make_async_copy(shards[p], fulls[p].at[pl.ds(pl.multiple_of(w * rows, rows), rows)], own_sem.at[p]))
    copies.append(pltpu.make_async_copy(small, small_full.at[w], own_sem.at[3]))
    for copy in copies:
        copy.start()
    for d in range(1, 4):
        small_z(d)

    def save_hidden():
        keep(hidden, hidden_o, 9)
        keep(qkv.at[pl.ds(1, 2)], kv_o, 10)

    head = [
        lambda: z_step(0, 1), lambda: own(1), lambda: y_step(0, 0), lambda: z_step(0, 2), lambda: y_step(0, 1), lambda: x_step(0, 0), lambda: z_step(0, 3),
        lambda: y_step(0, 2), lambda: x_step(0, 1), vectors, lambda: z_step(1, 1), lambda: own(2), lambda: y_step(0, 3), lambda: x_step(0, 2), lambda: z_step(1, 2), lambda: y_step(1, 0), lambda: x_step(0, 3), lambda: z_step(1, 3),
        lambda: last(0),
    ]
    links = [
        lambda: y_step(1, 1), lambda: x_step(1, 0), lambda: z_step(2, 1), lambda: y_step(1, 2), lambda: x_step(1, 1), lambda: z_step(2, 2), lambda: y_step(1, 3), lambda: x_step(1, 2), lambda: z_step(2, 3),
        lambda: y_step(2, 0), lambda: x_step(1, 3), lambda: y_step(2, 1), lambda: x_step(2, 0), lambda: y_step(2, 2),
    ]
    work = [functools.partial(project, i) for i in range(4)]
    work += [functools.partial(attend, s, j) for s in range(seqs) for j in range(width // 128)]
    work += [functools.partial(middle, i) for i in range(4)]
    work += [masked_rows]
    for step in head:
        step()
    done = 0
    for k, step in enumerate(links):
        upto = len(work) * (k + 1) // len(links)
        for piece in work[done:upto]:
            piece()
        done = upto
        step()
    save_hidden()
    last(1)
    for k in range(4):
        upper(k)
        (lambda: x_step(2, 1), lambda: y_step(2, 3), lambda: x_step(2, 2), lambda: x_step(2, 3))[k]()
    after_upper()
    last(2)
    lower()
    keep(vec, vec_o, 11)
    keep(bias, bias_o, 12)
    for make, ref in swaps:
        make().wait_recv()
    for k, (ref, dst) in enumerate(((rows_m, rows_o), (mixed_m, mixed_o), (hid_m, hid_o), (act_m, act_o), (dlow, dlow_o))):
        keep(ref, dst, 13 + k)
    for make, ref in swaps:
        make().wait_send()
    sends.finish()
    for copy in saves:
        copy.wait()


def forward(attn, up, down, small, tokens, pick, grad):
    rows, cols = attn.shape
    width = tokens.shape[1]
    seqs, padded, length = pick.shape
    total = tokens.shape[0]
    count = seqs * padded
    shape = jax.ShapeDtypeStruct
    f = jnp.float32
    full = shape((8 * rows, cols), LOW)
    anywhere = pl.BlockSpec(memory_space=pl.ANY)
    vm = pl.BlockSpec(memory_space=pltpu.VMEM)
    dma = pltpu.SemaphoreType.DMA
    outs = (
        full, full, full, shape((8, width), f), shape((1, cols), f), shape((2, total, width), LOW), shape((total, width), f),
        shape((count, width), LOW), shape((2, count, width), LOW), shape((2, count, width), LOW), shape((2, count, width), LOW),
        shape((2, count, cols), LOW), shape((count, cols), f), shape((count, width), f), shape((2, count, width), LOW),
        shape((count, width), f), shape((count, 128), f), shape((8, width), f),
    )
    v = pltpu.VMEM
    return pl.pallas_call(
        functools.partial(forward_kernel, rows, seqs, length, padded),
        out_shape=outs,
        in_specs=[anywhere] * 4 + [vm] * 3,
        out_specs=(anywhere,) * len(outs),
        scratch_shapes=[
            v((8 * rows, cols), LOW), v((8 * rows, cols), LOW), v((8 * rows, cols), LOW), v((8, 16, 128), LOW),
            v((3, total, width), LOW), v((total, width), LOW), v((total, width), f), v((8, width), f), v((3, 1, width), f), v((1, cols), f),
            v((count, width), LOW), v((2, count, width), LOW), v((2, count, width), LOW), v((2, count, width), LOW), v((2, count, cols), LOW),
            v((count, cols), f), v((count, width), f), v((count, width), f), v((2, count, width), LOW), v((8, width), f),
            v((count, width), f), v((count, width), f), v((count, 128), f),
            dma((6, 3, 8)), dma((3, 8, 3)), dma((3, 8)), dma((8,)), dma((4,)), dma((18,)), dma((5,)), dma((5,)),
        ],
        compiler_params=pltpu.CompilerParams(collective_id=0, has_side_effects=True, vmem_limit_bytes=60 * 2**20),
    )(attn, up, down, small, tokens, pick, grad)


E = 768
M = 1536
SLAB = 32
ORDER = (3, 0, 2, 1)


def slabs(rows, body):
    @pl.loop(0, rows // SLAB)
    def _(i):
        body(pl.multiple_of(i * SLAB, SLAB))


def f32(v):
    return v.astype(jnp.float32)


def backward_kernel(
    rows, seqs, length, padded,
    attn_h, up_h, down_h, vec, bias, kv_h, hidden_h, query_h, rows_h, mixed_h, hid_h, act_h, slope_h, dtwo_h, dlow_h, normed_h, inv_h, dvec_h, tokens_h, spots,
    layer_h, dtokens_h, out, small_out, norm_out,
    attn, up, down, kv, query_m, rows_m, mixed_m, hid_m, act_m, slope, dtwo, dlow, normed, inverse, dvec, tokens,
    left, right, dupper, dbias, dhid, dpre, done, dmix, dquery, dkv, part, tokens_t,
    htile, ytile, ltile,
    acc, xb, yr, zr, mr,
    sall, sall2, ssib, sx, sy, szu, szd, norms,
    load_sem, tile_sem, out_sem, pair_s, pair_r, dup_s, dup_r, sib_s, sib_r, x_s, x_r, y_s, y_r, z_s, z_r, m_s, m_r, f_s, f_r, sm_s, sm_r, n_s, n_r,
):
    z, y, x, c = place()
    edge = x == c
    mid = jnp.logical_not(edge)
    width = E
    count = seqs * padded
    total = seqs * length
    pair = rows * 2
    sends = Sends()
    me = dev(z, y, x, c)
    above, below, beside = dev(z + 1, y, x, c), dev(z - 1, y, x, c), dev(z, flip(y), x, c)
    over, near, diag = dev(z, y, flip(x), c), dev(z, y, x, flip(c)), dev(z, y, flip(x), flip(c))
    ecol = pl.multiple_of(x * 2304, 768)
    ocol = pl.multiple_of(flip(x) * 2304, 768)

    loads = []
    for k, (src, dst) in enumerate((
        (dlow_h, dlow), (act_h, act_m), (down_h, down), (slope_h, slope), (hid_h, hid_m), (up_h, up), (dtwo_h, dtwo), (normed_h, normed),
        (inv_h, inverse), (dvec_h, dvec), (attn_h, attn), (mixed_h, mixed_m), (query_h, query_m), (kv_h, kv), (rows_h, rows_m), (tokens_h, tokens),
    )):
        loads.append(pltpu.make_async_copy(src, dst, load_sem.at[k]))
        loads[-1].start()
    (L_DLOW, L_ACT, L_DOWN, L_SLOPE, L_HID, L_UP, L_DTWO, L_NORMED, L_INV, L_DVEC, L_ATTN, L_MIXED, L_QUERY, L_KV, L_ROWS, L_TOKENS) = range(16)

    def need(*ks):
        for k in ks:
            loads[k].wait()

    def copy(src, dst, ss, rs, to):
        return pltpu.make_async_remote_copy(src_ref=src, dst_ref=dst, send_sem=ss, recv_sem=rs, device_id=to, device_id_type=MESH)

    def wait(cond, dst, rs):
        when(cond, lambda: copy(dst, dst, rs, rs, me).wait_recv())

    def zrows(zz):
        return pl.ds(zz * pair, pair)

    def wrows(zz, yy):
        return pl.ds(pl.multiple_of((zz * 2 + yy) * rows, rows), rows)

    def add_x(p, zz):
        @pl.when(edge)
        def _():
            wait(None, xb.at[p, zrows(zz)], x_r.at[p, zz])

            def one(i):
                r = pl.ds(zz * pair + i, SLAB)
                acc[p, r, pl.ds(0, E)] = (f32(acc[p, r, pl.ds(0, E)]) + f32(xb[p, r, :])).astype(LOW)

            slabs(pair, one)

        push_y(edge, p, zz, E)

    def push_x(p, zz):
        sends.start(mid, lambda: copy(xb.at[p, zrows(zz)], xb.at[p, zrows(zz)], x_s.at[p, zz], x_r.at[p, zz], over))

    def push_y(cond, p, zz, wide):
        sends.start(cond, lambda: copy(
            acc.at[p, wrows(zz, flip(y)), pl.ds(0, wide)], yr.at[p, zz, :, pl.ds(0, wide)], y_s.at[p, zz], y_r.at[p, zz], beside))

    def add_into(cond, p, zz, buffer, slot, sem):
        for role, wide in ((edge, E), (mid, M)):
            @pl.when(both(cond, role))
            def _():
                wait(None, buffer.at[p, slot, :, pl.ds(0, wide)], sem)
                base = (zz * 2 + y) * rows

                def one(i):
                    here = pl.ds(pl.multiple_of(base + i, SLAB), SLAB)
                    acc[p, here, pl.ds(0, wide)] = (f32(acc[p, here, pl.ds(0, wide)]) + f32(buffer[p, slot, pl.ds(i, SLAB), pl.ds(0, wide)])).astype(LOW)

                slabs(rows, one)

    def add_y(p, zz):
        add_into(None, p, zz, yr, zz, y_r.at[p, zz])

    def z_push(cond, p, spot, k, to):
        for role, wide in ((edge, E), (mid, M)):
            def make(wide=wide):
                zz, slot = spot()
                return copy(acc.at[p, wrows(zz, y), pl.ds(0, wide)], zr.at[p, slot, :, pl.ds(0, wide)], z_s.at[k, p, zz], z_r.at[k, p, zz], to)

            sends.start(lambda role=role: both(cond(), role), make)

    def line(p, t):
        def upward():
            return both(z <= t, z < 3)

        def up_spot():
            zz = jnp.where(upward(), 3 + z - t, 0)
            return zz, zz

        def downward():
            return both(3 - z <= t, z > 0)

        def down_spot():
            zz = jnp.where(downward(), z + t - 3, 0)
            return zz, jnp.where(zz == z - 1, 4, zz)

        zz = up_spot()[0]
        add_into(both(upward(), z > 0), p, zz, zr, zz, z_r.at[0, p, zz])
        z_push(upward, p, up_spot, 0, above)
        zz = down_spot()[0]
        add_into(both(downward(), z < 3), p, zz, zr, zz, z_r.at[1, p, zz])
        z_push(downward, p, down_spot, 1, below)

    def owner(p):
        add_into(z > 0, p, z, zr, z, z_r.at[0, p, z])
        add_into(z < 3, p, z, zr, 4, z_r.at[1, p, z])
        sends.start(mid, lambda: copy(acc.at[p, wrows(z, y)], mr.at[p], m_s.at[p], m_r.at[p], diag))
        base = (z * 2 + y) * rows

        @pl.when(edge)
        def _():
            def one(i):
                out[p, pl.ds(i, SLAB), pl.ds(ecol, E)] = acc[p, pl.ds(pl.multiple_of(base + i, SLAB), SLAB), pl.ds(0, E)]

            slabs(rows, one)

        for k, to in enumerate((near, over, diag)):
            sends.start(edge, lambda k=k, to=to: copy(
                out.at[p, :, pl.ds(ecol, E)], out.at[p, :, pl.ds(ecol, E)], f_s.at[p, k], f_r.at[p, x], to))

    def middle_x(p):
        base = (z * 2 + y) * rows

        @pl.when(mid)
        def _():
            wait(None, mr.at[p], m_r.at[p])

            def one(i):
                out[p, pl.ds(i, SLAB), pl.ds(E, M)] = (f32(acc[p, pl.ds(pl.multiple_of(base + i, SLAB), SLAB), :]) + f32(mr[p, pl.ds(i, SLAB), :])).astype(LOW)

            slabs(rows, one)

        sends.start(mid, lambda: copy(out.at[p, :, pl.ds(E, M)], out.at[p, :, pl.ds(E, M)], f_s.at[p, 0], f_r.at[p, 2], near))

    def arrived(p):
        for xx in range(2):
            wait(jnp.logical_not(both(edge, x == xx)), out.at[p, :, pl.ds(2304 * xx, E)], f_r.at[p, xx])
        wait(edge, out.at[p, :, pl.ds(E, M)], f_r.at[p, 2])

    swaps = []

    def swap(ref, k):
        def make():
            return copy(ref.at[0], ref.at[1], pair_s.at[k], pair_r.at[k], near)

        make().start()
        swaps.append(make)

    def transpose_into(ref):
        for k in range(2):
            left[k] = ref[k].T

    def product(zz, ref, cols):
        return (dot(left[0, zrows(zz), :], ref[0, :, cols], NN) + dot(left[1, zrows(zz), :], ref[1, :, cols], NN)).astype(LOW)

    def grads(p, zz, ref):
        @pl.when(mid)
        def _():
            xb[p, zrows(zz), :] = product(zz, ref, pl.ds(ocol, E))

        push_x(p, zz)

        @pl.when(mid)
        def _():
            for k in range(2):
                acc[p, zrows(zz), pl.ds(k * E, E)] = product(zz, ref, pl.ds(E + k * E, E))

        push_y(mid, p, zz, M)

        @pl.when(edge)
        def _():
            acc[p, zrows(zz), pl.ds(0, E)] = product(zz, ref, pl.ds(ecol, E))

    def dup_copy(k):
        f = pl.ds(k * 768, 768)
        return copy(dupper.at[0, :, f], dupper.at[1, :, f], dup_s.at[k], dup_r.at[k], near)

    def upper_back(k):
        f = pl.ds(k * 768, 768)
        value = dot(dlow[0], down[:, f], NN) * slope[:, f]
        dbias[:, f] = jnp.sum(value, axis=0, keepdims=True)
        dupper[0, :, f] = value.astype(LOW)
        dup_copy(k).start()

    def hidden_back():
        @pl.loop(0, 3)
        def _(k):
            n = pl.ds(pl.multiple_of(k * 256, 256), 256)
            dhid[:, n] = dot(dupper[0], up[n, :], NT)

        value, dgain, dshift = norm_pull(dtwo[...] + dhid[...], normed[...], inverse[:, :1], vec[3:4, :])
        dpre[...] = value
        done[0] = value.astype(LOW)
        swap(done, 0)
        dvec[2:3, :] = jnp.sum(value, axis=0, keepdims=True)
        dvec[3:4, :] = dgain
        dvec[4:5, :] = dshift
        dmix[...] = dot(done[0], attn[:, pl.ds(3 * width, width)], NN).astype(LOW)

    def attend_back(step):
        s, j = step // 6, lax.rem(step, 6)
        cs = pl.ds(pl.multiple_of(j * 128, 128), 128)
        rs = pl.ds(pl.multiple_of(s * length, length), length)
        ms = pl.ds(pl.multiple_of(s * padded, padded), padded)
        lane = lax.broadcasted_iota(jnp.int32, (padded, 128), 1) < 64

        def halves(v):
            zero = jnp.zeros_like(v)
            return jnp.concatenate([jnp.where(lane, v, zero), jnp.where(lane, zero, v)], axis=0)

        key, value = kv[0, rs, cs], kv[1, rs, cs]
        queries, mixes = halves(query_m[ms, cs]), halves(dmix[ms, cs])
        score = dot(key, queries, NT)
        expo = jnp.exp(score - jnp.max(score, axis=0, keepdims=True))
        probs = expo / jnp.sum(expo, axis=0, keepdims=True)
        dprobs = dot(value, mixes, NT)
        dscore = (probs * (dprobs - jnp.sum(dprobs * probs, axis=0, keepdims=True))).astype(LOW)
        dkv[0, rs, cs] = dot(dscore, queries, NN).astype(LOW)
        dvalue = dot(probs.astype(LOW), mixes, NN)
        dkv[1, rs, cs] = dvalue.astype(LOW)
        dq = dot(dscore, key, TN) * 0.125
        dq = jnp.where(lane, dq[:padded], dq[padded:])
        dquery[0, ms, cs] = dq.astype(LOW)
        first = s == 0
        sums = jnp.concatenate([jnp.sum(dq, axis=0, keepdims=True), jnp.sum(dvalue, axis=0, keepdims=True)], axis=0)
        dvec[0:2, cs] = sums + jnp.where(first, 0.0, dvec[0:2, cs])

    def key_value_grads():
        for i in range(total // 256):
            r = pl.ds(i * 256, 256)
            tokens_t[:, r] = tokens[r, :].T

        def fill(store):
            @pl.loop(0, 8)
            def _(i):
                k = lax.rem(i, 2)
                n = pl.ds(pl.multiple_of(i // 2 * pair, pair), pair)
                store(n, pl.ds(pl.multiple_of(k * E, E), E), dot(tokens_t[n, :], dkv[k], NN).astype(LOW))

        @pl.when(mid)
        def _():
            def store(n, cols, value):
                acc[2, n, cols] = value

            fill(store)

        @pl.when(edge)
        def _():
            def store(n, cols, value):
                part[n, cols] = value

            fill(store)

        for zz in ORDER:
            sends.start(edge, lambda zz=zz: copy(part.at[zrows(zz)], part.at[zrows(zz)], sib_s.at[zz], sib_r.at[zz], near))

    def attention_sides():
        for k in range(2):
            left[k] = jnp.where(c == 0, rows_m[k], done[k]).T
            right[k] = jnp.where(c == 0, dquery[k], mixed_m[k])

    def attention_grads(zz):
        @pl.when(mid)
        def _():
            xb[2, zrows(zz), :] = product(zz, right, pl.ds(0, E))

        push_x(2, zz)

        @pl.when(mid)
        def _():
            wait(None, part.at[zrows(zz)], sib_r.at[zz])

            def one(i):
                r = pl.ds(zz * pair + i, SLAB)
                acc[2, r, :] = (f32(acc[2, r, :]) + f32(part[r, :])).astype(LOW)

            slabs(pair, one)

        push_y(mid, 2, zz, M)

        @pl.when(edge)
        def _():
            acc[2, zrows(zz), pl.ds(0, E)] = product(zz, right, pl.ds(0, E))

    def tile_load(i):
        slot = lax.rem(i, 2)
        return pltpu.make_async_copy(hidden_h.at[pl.ds(pl.multiple_of(i * 256, 256), 256)], htile.at[slot], tile_sem.at[slot])

    def layer_store(i):
        slot = lax.rem(i, 2)
        return pltpu.make_async_copy(ltile.at[slot], layer_h.at[pl.ds(pl.multiple_of(i * 256, 256), 256)], out_sem.at[slot])

    def feed_forward(step):
        i, k = step // 4, lax.rem(step, 4)
        slot = lax.rem(i, 2)

        @pl.when(k == 0)
        def _():
            tile_load(i).wait()

            @pl.when(i + 1 < total // 256)
            def _():
                tile_load(i + 1).start()

        f = pl.ds(pl.multiple_of(k * 768, 768), 768)
        u = dot(htile[slot].astype(LOW), up[:, f], NN) + bias[:, f]
        a = (u * (0.5 * (1.0 + lax.erf(u * SQRT_HALF)))).astype(LOW)
        ytile[...] = dot(a, down[:, f], NT) + jnp.where(k == 0, htile[slot] + vec[5:6, :], ytile[...])

        @pl.when(k == 3)
        def _():
            @pl.when(i >= 2)
            def _():
                layer_store(i - 2).wait()

            ltile[slot] = norm(ytile[...], vec[6:7, :], vec[7:8, :])[0].astype(LOW)
            layer_store(i).start()

    def token_store(i):
        slot = lax.rem(i, 2)
        return pltpu.make_async_copy(htile.at[slot], dtokens_h.at[pl.ds(pl.multiple_of(i * 256, 256), 256)], out_sem.at[2 + slot])

    def masked_tokens():
        dpre[...] = dpre[...] + dot(dquery[0], attn[:, pl.ds(0, width)], NT)

    def tokens_back(i):
        slot = lax.rem(i, 2)

        @pl.when(i >= 2)
        def _():
            token_store(i - 2).wait()

        r = pl.ds(pl.multiple_of(i * 256, 256), 256)
        s = i // (length // 256)
        here = lax.broadcasted_iota(jnp.int32, (256, padded), 0) + lax.rem(i, length // 256) * 256
        pick = (here == spots[pl.ds(s, 1), :]).astype(jnp.float32).astype(LOW)
        value = dpre[pl.ds(pl.multiple_of(s * padded, padded), padded), :]
        high = value.astype(LOW)
        rest = (value - f32(high)).astype(LOW)
        htile[slot] = (
            dot(dkv[0, r, :], attn[:, pl.ds(width, width)], NT) + dot(dkv[1, r, :], attn[:, pl.ds(2 * width, width)], NT) + (dot(pick, high, NN) + dot(pick, rest, NN))
        )
        token_store(i).start()

    def small_start():
        for w in range(8):
            sall[w] = jnp.zeros((16, 128), jnp.float32)
            turned = dvec[...] if w == 0 else pltpu.roll(dvec[...], width - rows * w, 1)
            lane = lax.broadcasted_iota(jnp.int32, (8, 128), 1)
            sall[w, 0:8, :] = jnp.where(lane < rows, turned[:, :128], 0.0)
            for r in range(3):
                sall[w, 8 + r : 9 + r, :] = dbias[:, pl.ds(w * 384 + r * 128, 128)]
        sends.start(None, lambda: copy(sall, ssib, sm_s.at[0], sm_r.at[0], near))

    def small_x():
        wait(None, ssib, sm_r.at[0])
        ssib[...] = sall[...] + ssib[...]
        sends.start(None, lambda: copy(ssib, sx, sm_s.at[1], sm_r.at[1], over))

    def small_y():
        wait(None, sx, sm_r.at[1])
        sall2[...] = ssib[...] + sx[...]
        for zz in range(4):
            sends.start(None, lambda zz=zz: copy(sall2.at[zz * 2 + flip(y)], sy.at[zz], sm_s.at[2 + zz], sm_r.at[2 + zz], beside))

    def small_add():
        for zz in range(4):
            wait(None, sy.at[zz], sm_r.at[2 + zz])
            sy[zz] = sy[zz] + sall2[zz * 2 + y]

    def small_line():
        for zz in ORDER:
            @pl.when(both(z <= zz, z > 0))
            def _():
                wait(None, szu.at[zz], sm_r.at[6 + zz])
                sy[zz] = sy[zz] + szu[zz]

            sends.start(lambda zz=zz: z < zz, lambda zz=zz: copy(sy.at[zz], szu.at[zz], sm_s.at[6 + zz], sm_r.at[6 + zz], above))

            @pl.when(both(z >= zz, z < 3))
            def _():
                wait(None, szd.at[zz], sm_r.at[10 + zz])
                sy[zz] = sy[zz] + szd[zz]

            sends.start(lambda zz=zz: z > zz, lambda zz=zz: copy(sy.at[zz], szd.at[zz], sm_s.at[10 + zz], sm_r.at[10 + zz], below))

    w = z * 2 + y

    def peer(k):
        return lax.rem(w + k, 8)

    def square_sum():
        small_out[...] = sy[z]
        total_squares = jnp.sum(sy[z] * sy[z])
        for p in range(3):
            def body(i, sums):
                v = f32(out[p, pl.ds(pl.multiple_of(i * 16, 16), 16), :])
                return sums + jnp.sum(v * v)

            total_squares = lax.fori_loop(0, rows // 16, body, total_squares)
        norms[w] = jnp.full((8, 128), total_squares, jnp.float32)
        for k in range(1, 8):
            sends.start(None, lambda k=k: copy(norms.at[w], norms.at[w], n_s.at[k], n_r.at[w], (peer(k), x * 2 + c)))
        for k in range(1, 8):
            wait(None, norms.at[peer(k)], n_r.at[peer(k)])
        whole = norms[0]
        for k in range(1, 8):
            whole = whole + norms[k]
        norm_out[...] = jnp.sqrt(whole)

    def looped(n, body, steps):
        @pl.loop(0, n)
        def _(i):
            body(i)
            for k in sorted(steps):
                pl.when(i == k)(lambda k=k: [step() for step in steps[k]] and None)

    bar = pltpu.get_barrier_semaphore()
    for to in [near, over, diag] + [(peer(k), x * 2 + c) for k in range(1, 8)]:
        pl.semaphore_signal(bar, inc=1, device_id=to, device_id_type=MESH)
    pl.semaphore_wait(bar, 10)

    need(L_DLOW, L_ACT)
    transpose_into(dlow)
    for zz in ORDER:
        grads(0, zz, act_m)
    need(L_DOWN, L_SLOPE)
    for k in range(4):
        upper_back(k)
    need(L_HID)
    transpose_into(hid_m)
    for k in range(4):
        dup_copy(k).wait_recv()
    for zz in ORDER:
        grads(1, zz, dupper)
    need(L_UP, L_DTWO, L_NORMED, L_INV, L_ATTN, L_DVEC)
    hidden_back()
    need(L_QUERY, L_KV)
    P = functools.partial
    looped(seqs * 6, attend_back, {2: [P(add_x, 0, 3)], 5: [P(add_x, 0, 0)], 8: [P(add_x, 0, 2)], 11: [P(add_x, 0, 1)]})
    swap(dquery, 1)
    small_start()
    need(L_TOKENS, L_ROWS, L_MIXED)
    key_value_grads()
    for make in swaps:
        make().wait_recv()
    attention_sides()
    for zz in ORDER:
        attention_grads(zz)
    masked_tokens()
    tile = total // 256
    looped(tile, tokens_back, {0: [P(add_y, 0, 3), small_x], 1: [P(add_y, 0, 0)], 2: [P(add_y, 0, 2)], 3: [P(add_y, 0, 1), small_y]})
    for i in range(tile - 2, tile):
        token_store(i).wait()
    tile_load(0).start()
    looped(tile * 4, feed_forward, {
        0: [P(add_x, 1, 3), P(add_x, 1, 0)],
        1: [P(line, 0, 0), small_add],
        2: [P(add_x, 1, 2), P(add_x, 1, 1), P(line, 0, 1)],
        3: [P(line, 0, 2), small_line],
        4: [P(add_y, 1, 3), P(owner, 0)],
        5: [P(add_y, 1, 0)],
        6: [P(add_y, 1, 2), P(add_x, 2, 3)],
        7: [P(add_y, 1, 1), P(add_x, 2, 0)],
        8: [P(line, 1, 0), P(add_x, 2, 2)],
        9: [P(line, 1, 1), P(add_x, 2, 1)],
        10: [P(line, 1, 2), P(middle_x, 0)],
        11: [P(owner, 1)],
        12: [P(add_y, 2, 3)],
        13: [P(add_y, 2, 0)],
        14: [P(middle_x, 1)],
        15: [P(add_y, 2, 2)],
    })
    add_y(2, 1)
    for t in range(3):
        line(2, t)
    owner(2)
    middle_x(2)
    for i in range(tile - 2, tile):
        layer_store(i).wait()
    for p in range(3):
        arrived(p)
    square_sum()
    sends.finish()
    for make in swaps:
        make().wait_send()
    for k in range(4):
        dup_copy(k).wait_send()


def backward(attn, up, down, vec, bias, kv, hidden, query_m, rows_m, mixed_m, hid_m, act_m, slope, dtwo, dlow, normed, inverse, dvec, tokens, spots):
    total, width = hidden.shape
    cols = up.shape[1]
    rows = width // 8
    seqs, padded = spots.shape
    length = total // seqs
    count = seqs * padded
    shape = jax.ShapeDtypeStruct
    f = jnp.float32
    anywhere = pl.BlockSpec(memory_space=pl.ANY)
    vm = pl.BlockSpec(memory_space=pltpu.VMEM)
    dma = pltpu.SemaphoreType.DMA
    v = pltpu.VMEM
    inputs = (attn, up, down, vec, bias, kv, hidden, query_m, rows_m, mixed_m, hid_m, act_m, slope, dtwo, dlow, normed, inverse, dvec, tokens, spots)

    def like(a):
        return v(a.shape, a.dtype)

    one = (16, 128)
    scratch = [like(a) for a in (attn, up, down, kv, query_m, rows_m, mixed_m, hid_m, act_m, slope, dtwo, dlow, normed, inverse, dvec, tokens)]
    scratch += [
        v((2, width, count), LOW), v((2, count, width), LOW), v((2, count, cols), LOW), v((1, cols), f), v((count, width), f), v((count, width), f),
        v((2, count, width), LOW), v((count, width), LOW), v((2, count, width), LOW), v((2, total, width), LOW), v((width, M), LOW), v((width, total), LOW),
        v((2, 256, width), f), v((256, width), f), v((2, 256, width), LOW),
        v((3, width, M), LOW), v((3, width, E), LOW), v((3, 4, rows, M), LOW), v((3, 5, rows, M), LOW), v((3, rows, M), LOW),
        v((8,) + one, f), v((8,) + one, f), v((8,) + one, f), v((8,) + one, f), v((4,) + one, f), v((4,) + one, f), v((4,) + one, f), v((8, 8, 128), f),
        dma((16,)), dma((2,)), dma((4,)), dma((2,)), dma((2,)), dma((4,)), dma((4,)), dma((4,)), dma((4,)), dma((3, 4)), dma((3, 4)), dma((3, 4)), dma((3, 4)),
        dma((2, 3, 4)), dma((2, 3, 4)), dma((3,)), dma((3,)), dma((3, 3)), dma((3, 3)), dma((14,)), dma((14,)), dma((8,)), dma((8,)),
    ]
    specs = [anywhere] * len(inputs)
    specs[3] = specs[4] = specs[19] = vm
    return pl.pallas_call(
        functools.partial(backward_kernel, rows, seqs, length, padded),
        out_shape=(shape((total, width), LOW), shape((total, width), f), shape((3, rows, cols), LOW), shape(one, f), shape((8, 128), f)),
        in_specs=specs,
        out_specs=(anywhere, anywhere, vm, vm, vm),
        scratch_shapes=scratch,
        compiler_params=pltpu.CompilerParams(collective_id=1, has_side_effects=True, vmem_limit_bytes=64 * 2**20 - 2**16),
    )(*inputs)


def masks(mask_place, mask_count, gradient, length):
    seqs, slots = mask_place.shape
    padded = -(-slots // 16) * 16
    live = jnp.arange(padded)[None, :] < mask_count[:, None]
    spots = jnp.pad(mask_place, ((0, 0), (0, padded - slots)), constant_values=-1)
    pick = (spots[:, :, None] == jnp.arange(length)[None, None, :]) & live[:, :, None]
    gradient = jnp.pad(gradient, ((0, 0), (0, padded - slots), (0, 0)))
    gradient = jnp.where(live[:, :, None], gradient, jnp.zeros_like(gradient))
    return pick, jnp.where(live, spots, -1), gradient.reshape(seqs * padded, -1)


def update(weights, moments, grads, grad_norm):
    factor = CLIP_LIMIT / jnp.maximum(grad_norm, CLIP_LIMIT)
    rates = (LEARN_RATE, OUTPUT_RATE, LEARN_RATE, LEARN_RATE, VECTOR_RATE, BIAS_RATE)
    out = ()
    for k in range(6):
        out += adam_step(weights[k], *moments[k], grads[k], factor, DECAY_RATE if k < 4 else 0.0, rates[k])
    return out


def natural(own_attn, own_up, own_down, own_vectors, own_bias):
    width = own_up.shape[1] // 4
    own_qkv = jnp.swapaxes(own_attn[:, : 3 * width].reshape(-1, 3, width), 0, 1)
    return own_qkv, own_attn[:, 3 * width :].T, own_up, own_down.T, own_vectors, own_bias


def pack(qkv, out, up, down):
    attn = jnp.concatenate([qkv[0], qkv[1], qkv[2], out.T], axis=1)
    return attn.astype(jnp.bfloat16), up.astype(jnp.bfloat16), down.T.astype(jnp.bfloat16)


def small_pack(vectors, bias):
    rows = vectors.shape[1]
    return jnp.concatenate([jnp.pad(vectors, ((0, 0), (0, 128 - rows))), bias.reshape(-1, 128), jnp.zeros((5, 128))])


def plain(tokens, pick, spots, gradient, weights):
    low = jnp.bfloat16
    seqs, length, width = tokens.shape
    padded = pick.shape[1]
    flat = tokens.reshape(seqs * length, width)
    attn_w, up_w, down_w = (lax.all_gather(v, "wide", axis=0, tiled=True) for v in pack(*weights[:4]))
    vec = lax.all_gather(weights[4].astype(low), "wide", axis=1, tiled=True).astype(jnp.float32)
    bias = lax.all_gather(weights[5].astype(low), "wide", axis=0, tiled=True).astype(jnp.float32)
    wq, wk, wv, wo = (attn_w[:, k * width : (k + 1) * width] for k in range(4))
    query = (mm(flat, wq, NN) + vec[0]).astype(low)
    key = mm(flat, wk, NN, low)
    value = (mm(flat, wv, NN) + vec[1]).astype(low)
    query, key, value = (split_heads(v, seqs, length) for v in (query, key, value))
    mixed = lax.map(attend, (query, key, value)).reshape(seqs * length, width)

    def middle(rows, mixed):
        pre_one = rows.astype(jnp.float32) + (mm(mixed, wo, NT) + vec[2])
        hidden, normed, inverse = layer_norm(pre_one, vec[3], vec[4])
        hidden_low = hidden.astype(low)
        upper = mm(hidden_low, up_w, NN) + bias
        cumul = 0.5 * (1.0 + lax.erf(upper * SQRT_HALF))
        active = (upper * cumul).astype(low)
        pre_two = hidden + (mm(active, down_w, NT) + vec[5])
        return layer_norm(pre_two, vec[6], vec[7]), normed, inverse, hidden_low, upper, cumul, active

    layer_out = middle(flat, mixed)[0][0].astype(low)
    pick_low = pick.astype(low)

    def take(values):
        values = values.reshape(seqs, length, width)
        return jnp.einsum("sil,sld->sid", pick_low, values, preferred_element_type=jnp.float32).astype(low)

    rows_m = take(flat).reshape(seqs * padded, width)
    mixed_m = take(mixed).reshape(seqs * padded, width)
    query_m = split_heads(take(query), seqs, padded)
    (_, normed_two, inverse_two), normed_one, inverse_one, hidden_m, upper, cumul, active = middle(rows_m, mixed_m)
    dpre_two, dgain_two, dshift_two = norm_back(gradient.astype(jnp.float32), normed_two, inverse_two, vec[6])
    dbias_two = jnp.sum(dpre_two, axis=0)
    dtwo_low = dpre_two.astype(low)
    ddown = mm(dtwo_low, active, TN)
    dactive = mm(dtwo_low, down_w, NN)
    density = jnp.exp(-0.5 * upper * upper) * INV_ROOT_TWO_PI
    dupper = dactive * (cumul + upper * density)
    dup_bias = jnp.sum(dupper, axis=0)
    dupper_low = dupper.astype(low)
    dup = mm(hidden_m, dupper_low, TN)
    dhidden = dpre_two + mm(dupper_low, up_w, NT)
    dpre_one, dgain_one, dshift_one = norm_back(dhidden, normed_one, inverse_one, vec[3])
    dbias_out = jnp.sum(dpre_one, axis=0)
    done_low = dpre_one.astype(low)
    dout = mm(done_low, mixed_m, TN)
    dmixed = split_heads(mm(done_low, wo, NN, low), seqs, padded)
    dquery, dkey, dvalue = lax.map(attend_back, (query_m, key, value, dmixed))
    dquery = dquery.reshape(seqs * padded, width)
    dkey = dkey.reshape(seqs * length, width)
    dvalue = dvalue.reshape(seqs * length, width)
    dbias_query = jnp.sum(dquery, axis=0)
    dbias_value = jnp.sum(dvalue, axis=0)
    dquery, dkey, dvalue = dquery.astype(low), dkey.astype(low), dvalue.astype(low)
    dattn = jnp.concatenate([mm(rows_m, dquery, TN), mm(flat, dkey, TN), mm(flat, dvalue, TN), dout], axis=1)
    masked_part = dpre_one + mm(dquery, wq, NT)
    dtokens = spread(pick, masked_part) + mm(dkey, wk, NT) + mm(dvalue, wv, NT)
    dvectors = jnp.stack(
        [dbias_query, dbias_value, dbias_out, dgain_one, dshift_one, dbias_two, dgain_two, dshift_two]
    )

    def owned(value, dim):
        return lax.psum(lax.psum_scatter(value, "wide", scatter_dimension=dim, tiled=True), "narrow")

    grads = (owned(dattn, 0), owned(dup, 0), owned(ddown, 0), owned(dvectors, 1), owned(dup_bias, 0))
    grad_norm = jnp.sqrt(lax.psum(sum(jnp.sum(v * v) for v in grads), "wide"))
    return layer_out, dtokens, grads, grad_norm


def spread(pick, rows):
    seqs, padded, length = pick.shape
    return jnp.einsum(
        "sil,sid->sld",
        pick.astype(jnp.float32),
        rows.reshape(seqs, padded, -1),
        precision=lax.Precision.HIGHEST,
        preferred_element_type=jnp.float32,
    ).reshape(seqs * length, -1)


def tailored(tokens, pick, spots, gradient, weights):
    low = jnp.bfloat16
    seqs, length, width = tokens.shape
    flat = tokens.reshape(seqs * length, width)
    saved = forward(*pack(*weights[:4]), small_pack(*weights[4:]).astype(low), flat, pick.astype(low), gradient)
    layer_out, dtokens, own, small, grad_norm = backward(*saved, flat, spots)
    own = own.astype(jnp.float32)
    rows = own.shape[1]
    return layer_out, dtokens, (own[2], own[1], own[0], small[:8, :rows], small[8:11].reshape(-1)), grad_norm[0, 0]


def shards(body, tokens, mask_place, mask_count, masked_output_gradient, *parameters):
    seqs, length, width = tokens.shape
    weights = parameters[0::3]
    moments = tuple(zip(parameters[1::3], parameters[2::3]))
    pick, spots, gradient = masks(mask_place, mask_count, masked_output_gradient, length)
    layer_out, dtokens, grads, grad_norm = body(tokens, pick, spots, gradient, weights)
    layer_out, dtokens = (v.reshape(seqs, length, width) for v in (layer_out, dtokens))
    return (layer_out, dtokens, grad_norm) + update(weights, moments, natural(*grads), grad_norm)


def solution(mesh):
    body = tailored if mesh.shape["wide"] == 8 and mesh.shape["narrow"] == 4 else plain
    data = P(("wide", "narrow"))
    rows = P("wide")
    columns = P(None, "wide")
    weights = (columns,) * 6 + (rows,) * 3 + (columns,) * 6 + (rows,) * 3
    return jax.shard_map(
        functools.partial(shards, body),
        mesh=mesh,
        in_specs=(data,) * 4 + weights,
        out_specs=(data, data, P()) + weights,
        check_vma=False,
    )
```

```python
import functools

import jax
import jax.numpy as jnp
from jax import lax
from jax.experimental import pallas as pl
from jax.experimental.pallas import tpu as pltpu
from jax.sharding import PartitionSpec as P

HEADS = 12
HEAD_DIM = 64
STEP = 10

LN_EPS = 1e-06
SQRT_HALF = 0.7071067811865476
INV_ROOT_TWO_PI = 0.3989422804014327
CLIP_LIMIT = 1.0
BETA_ONE = 0.9
BETA_TWO = 0.999
LEARN_RATE = 0.05
OUTPUT_RATE = 0.2
VECTOR_RATE = 0.5
BIAS_RATE = 0.3
DECAY_RATE = 0.01
ADAM_EPS = 1e-08

MESH = pl.DeviceIdType.MESH


def when(cond, body):
    if callable(cond):
        cond = cond()
    if cond is None:
        body()
    else:
        pl.when(cond)(body)


class Sends:
    def __init__(self):
        self.started = []

    def start(self, cond, make):
        when(cond, lambda: make().start())
        self.started.append((cond, make))

    def finish(self):
        for cond, make in self.started:
            when(cond, lambda make=make: make().wait_send())


def both(a, b):
    return b if a is None else (a if b is None else jnp.logical_and(a, b))


def place():
    w, n = lax.axis_index("wide"), lax.axis_index("narrow")
    return w // 2, lax.rem(w, 2), n // 2, lax.rem(n, 2)


def flip(v):
    return 1 - v


def dev(z, y, x, c):
    return (z * 2 + y, x * 2 + c)


def meet(z, y, x, c, diagonal):
    bar = pltpu.get_barrier_semaphore()
    peers = [(None, dev(z, flip(y), x, c)), (None, dev(z, y, flip(x), c)), (None, dev(z, y, x, flip(c)))]
    if diagonal:
        peers.append((None, dev(z, y, flip(x), flip(c))))
    peers += [(z > 0, dev(z - 1, y, x, c)), (z < 3, dev(z + 1, y, x, c))]
    for cond, peer in peers:
        when(cond, lambda peer=peer: pl.semaphore_signal(bar, inc=1, device_id=peer, device_id_type=MESH))
    inner = jnp.logical_and(z > 0, z < 3)
    count = 4 if diagonal else 3
    pl.semaphore_wait(bar, count + 1 + jnp.where(inner, 1, 0))


def gather_kernel(rows, cols, attn, up, down, small, attn_full, up_full, down_full, small_full, send_sem, recv_sem, small_send, small_recv, own_sem):
    z, y, x, c = place()
    edge = x == c
    third = cols // 3
    mine, across = x + c, 2 * flip(x)
    fulls = (attn_full, up_full, down_full)
    shards = (attn, up, down)
    sends = Sends()
    zl, zh = z > 0, z < 3

    def spot(p, zz, yy, t):
        return fulls[p].at[pl.ds(pl.multiple_of((zz * 2 + yy) * rows, rows), rows), pl.ds(pl.multiple_of(t * third, third), third)]

    def push(cond, p, zz, yy, t, kind, to, src=None):
        def make():
            w = zz * 2 + yy
            where = spot(p, zz, yy, t)
            return pltpu.make_async_remote_copy(
                src_ref=where if src is None else src,
                dst_ref=where,
                send_sem=send_sem.at[kind, p, w],
                recv_sem=recv_sem.at[p, w, t],
                device_id=to,
                device_id_type=MESH,
            )

        sends.start(cond, make)

    def small_push(cond, zz, yy, kind, to, src=None):
        def make():
            w = zz * 2 + yy
            where = small_full.at[w]
            return pltpu.make_async_remote_copy(
                src_ref=where if src is None else src,
                dst_ref=where,
                send_sem=small_send.at[kind, w],
                recv_sem=small_recv.at[w],
                device_id=to,
                device_id_type=MESH,
            )

        sends.start(cond, make)

    def arrive(cond, p, zz, yy, t):
        def body():
            where = spot(p, zz, yy, t)
            w = zz * 2 + yy
            pltpu.make_async_remote_copy(where, where, send_sem.at[0, p, w], recv_sem.at[p, w, t], dev(z, y, x, c), device_id_type=MESH).wait_recv()

        when(cond, body)

    def small_arrive(cond, zz, yy):
        def body():
            w = zz * 2 + yy
            pltpu.make_async_remote_copy(small_full.at[w], small_full.at[w], small_send.at[0, w], small_recv.at[w], dev(z, y, x, c), device_id_type=MESH).wait_recv()

        when(cond, body)

    UP, DOWN, SIDE, OVER, NEAR, PASS = range(6)
    above, below, beside = dev(z + 1, y, x, c), dev(z - 1, y, x, c), dev(z, flip(y), x, c)
    over, near = dev(z, y, flip(x), c), dev(z, y, x, flip(c))

    def own(p):
        src = shards[p].at[:, pl.ds(pl.multiple_of(mine * third, third), third)]
        push(zh, p, z, y, mine, UP, above, src)
        push(zl, p, z, y, mine, DOWN, below, src)
        push(None, p, z, y, mine, SIDE, beside, src)

    def z_step(p, d):
        for cond, zz, onward, kind, to in ((z - d >= 0, z - d, zh, UP, above), (z + d <= 3, z + d, zl, DOWN, below)):
            arrive(cond, p, zz, y, mine)
            push(both(cond, onward), p, zz, y, mine, kind, to)
            push(cond, p, zz, y, mine, SIDE, beside)
            push(both(cond, edge), p, zz, y, mine, OVER, over)
            push(cond, p, zz, y, mine, NEAR, near)

    def y_step(p, d):
        steps = ((None, z),) if d == 0 else ((z - d >= 0, z - d), (z + d <= 3, z + d))
        for cond, zz in steps:
            arrive(cond, p, zz, flip(y), mine)
            push(both(cond, edge), p, zz, flip(y), mine, OVER, over)
            push(cond, p, zz, flip(y), mine, NEAR, near)

    def x_step(p, d):
        mid = jnp.logical_not(edge)
        for yy in (y, flip(y)):
            if d == 0:
                steps = () if yy is y else ((None, z),)
            else:
                steps = ((z - d >= 0, z - d), (z + d <= 3, z + d))
            for cond, zz in steps:
                cond = both(cond, mid)
                arrive(cond, p, zz, yy, across)
                push(cond, p, zz, yy, across, PASS, near)

    def last(p, d):
        for yy in (y, flip(y)):
            if d == 0:
                steps = () if yy is y else ((None, z),)
            else:
                steps = ((z - d >= 0, z - d), (z + d <= 3, z + d))
            for cond, zz in steps:
                arrive(cond, p, zz, yy, x + flip(c))
                arrive(both(cond, edge), p, zz, yy, across)

    def small_z(d):
        for cond, zz, onward, kind, to in ((z - d >= 0, z - d, zh, UP, above), (z + d <= 3, z + d, zl, DOWN, below)):
            small_arrive(cond, zz, y)
            small_push(both(cond, onward), zz, y, kind, to)
            small_push(cond, zz, y, SIDE, beside)

    meet(z, y, x, c, False)
    small_push(zh, z, y, UP, above, small)
    small_push(zl, z, y, DOWN, below, small)
    small_push(None, z, y, SIDE, beside, small)
    own(0)
    w = z * 2 + y
    copies = []
    for p in range(3):
        copies.append(pltpu.make_async_copy(shards[p], fulls[p].at[pl.ds(pl.multiple_of(w * rows, rows), rows)], own_sem.at[p]))
    copies.append(pltpu.make_async_copy(small, small_full.at[w], own_sem.at[3]))
    for copy in copies:
        copy.start()
    for d in range(1, 4):
        small_z(d)
    order = [
        lambda: z_step(0, 1), lambda: own(1), lambda: y_step(0, 0), lambda: z_step(0, 2), lambda: y_step(0, 1), lambda: x_step(0, 0), lambda: z_step(0, 3),
        lambda: y_step(0, 2), lambda: x_step(0, 1), lambda: z_step(1, 1), lambda: own(2), lambda: y_step(0, 3), lambda: x_step(0, 2), lambda: z_step(1, 2), lambda: y_step(1, 0), lambda: x_step(0, 3), lambda: z_step(1, 3),
        lambda: y_step(1, 1), lambda: x_step(1, 0), lambda: z_step(2, 1), lambda: y_step(1, 2), lambda: x_step(1, 1), lambda: z_step(2, 2), lambda: y_step(1, 3), lambda: x_step(1, 2), lambda: z_step(2, 3),
        lambda: y_step(2, 0), lambda: x_step(1, 3), lambda: y_step(2, 1), lambda: x_step(2, 0), lambda: y_step(2, 2), lambda: x_step(2, 1), lambda: y_step(2, 3), lambda: x_step(2, 2), lambda: x_step(2, 3),
    ]
    for step in order:
        step()
    for d in range(4):
        for cond, zz in (((None, z),) if d == 0 else ((z - d >= 0, z - d), (z + d <= 3, z + d))):
            small_arrive(cond, zz, flip(y))
    for p in range(3):
        for d in range(4):
            last(p, d)
    sends.finish()
    for copy in copies:
        copy.wait()


def gather(attn, up, down, small):
    rows, cols = attn.shape
    full = jax.ShapeDtypeStruct((8 * rows, cols), attn.dtype)
    anywhere = pl.BlockSpec(memory_space=pl.ANY)
    return pl.pallas_call(
        functools.partial(gather_kernel, rows, cols),
        out_shape=(full, full, full, jax.ShapeDtypeStruct((8,) + small.shape, small.dtype)),
        in_specs=[anywhere] * 4,
        out_specs=(anywhere,) * 4,
        scratch_shapes=[
            pltpu.SemaphoreType.DMA((6, 3, 8)),
            pltpu.SemaphoreType.DMA((3, 8, 3)),
            pltpu.SemaphoreType.DMA((3, 8)),
            pltpu.SemaphoreType.DMA((8,)),
            pltpu.SemaphoreType.DMA((4,)),
        ],
        compiler_params=pltpu.CompilerParams(collective_id=0, has_side_effects=True),
    )(attn, up, down, small)


def layer_norm(values, gain, shift):
    center = values - jnp.mean(values, axis=-1, keepdims=True)
    inverse = lax.rsqrt(jnp.mean(center * center, axis=-1, keepdims=True) + LN_EPS)
    normed = center * inverse
    return (normed * gain + shift, normed, inverse)


def norm_back(incoming, normed, inverse, gain):
    dgain = jnp.sum(incoming * normed, axis=0)
    dshift = jnp.sum(incoming, axis=0)
    scaled = incoming * gain
    dvalues = inverse * (
        scaled
        - jnp.mean(scaled, axis=-1, keepdims=True)
        - normed * jnp.mean(scaled * normed, axis=-1, keepdims=True)
    )
    return (dvalues, dgain, dshift)


def mm(a, b, dims, out=jnp.float32):
    return lax.dot_general(a, b, (dims, ((), ())), preferred_element_type=jnp.float32).astype(out)


NN = ((1,), (0,))
NT = ((1,), (1,))
TN = ((0,), (0,))


def split_heads(values, seqs, length):
    return values.reshape(seqs, length, HEADS, HEAD_DIM)


def attend(pieces):
    query, key, value = pieces
    raw = jnp.einsum("qhe,khe->hqk", query, key, preferred_element_type=jnp.float32) * HEAD_DIM ** (
        -0.5
    )
    peak = jnp.max(raw, axis=-1, keepdims=True)
    expo = jnp.exp(raw - peak)
    total = jnp.sum(expo, axis=-1, keepdims=True)
    probs = (expo / total).astype(jnp.bfloat16)
    mixed = jnp.einsum("hqk,khe->qhe", probs, value, preferred_element_type=jnp.float32)
    return mixed.astype(jnp.bfloat16)


def attend_back(pieces):
    query, key, value, dmixed = pieces
    scale = HEAD_DIM ** (-0.5)
    raw = jnp.einsum("qhe,khe->hqk", query, key, preferred_element_type=jnp.float32) * scale
    probs = jax.nn.softmax(raw, axis=-1)
    dprobs = jnp.einsum("qhe,khe->hqk", dmixed, value, preferred_element_type=jnp.float32)
    dscore = probs * (dprobs - jnp.sum(dprobs * probs, axis=-1, keepdims=True))
    dscore = (dscore * scale).astype(jnp.bfloat16)
    dquery = jnp.einsum("hqk,khe->qhe", dscore, key, preferred_element_type=jnp.float32)
    dkey = jnp.einsum("hqk,qhe->khe", dscore, query, preferred_element_type=jnp.float32)
    dvalue = jnp.einsum(
        "hqk,qhe->khe", probs.astype(jnp.bfloat16), dmixed, preferred_element_type=jnp.float32
    )
    return (dquery, dkey, dvalue)


def adam_step(weight, first, second, grad, factor, decay, rate):
    grad = grad * factor
    first_new = BETA_ONE * first + (1.0 - BETA_ONE) * grad
    second_new = BETA_TWO * second + (1.0 - BETA_TWO) * grad * grad
    mean_hat = first_new / (1.0 - BETA_ONE**STEP)
    square_hat = second_new / (1.0 - BETA_TWO**STEP)
    weight_new = weight - rate * (mean_hat / (jnp.sqrt(square_hat) + ADAM_EPS) + decay * weight)
    return (weight_new, first_new, second_new)


def dot(a, b, dims):
    return lax.dot_general(a, b, (dims, ((), ())), preferred_element_type=jnp.float32)


NN = ((1,), (0,))
NT = ((1,), (1,))
TN = ((0,), (0,))
LOW = jnp.bfloat16


def norm(values, gain, shift):
    center = values - jnp.mean(values, axis=-1, keepdims=True)
    inverse = lax.rsqrt(jnp.mean(center * center, axis=-1, keepdims=True) + LN_EPS)
    normed = center * inverse
    return normed * gain + shift, normed, inverse


def norm_pull(incoming, normed, inverse, gain):
    dgain = jnp.sum(incoming * normed, axis=0, keepdims=True)
    dshift = jnp.sum(incoming, axis=0, keepdims=True)
    scaled = incoming * gain
    return (
        inverse * (scaled - jnp.mean(scaled, axis=-1, keepdims=True) - normed * jnp.mean(scaled * normed, axis=-1, keepdims=True)),
        dgain,
        dshift,
    )


def forward_kernel(
    rows, seqs, length, padded,
    qkv_h, out_h, up_h, down_h, vectors, up_bias, tokens_h, place_m, count_m, grad_m,
    attn_o, up_o, down_o, vec_o, bias_o, kv_o, hidden_o, query_o, rows_o, mixed_o, hid_o, act_o, slope_o, dtwo_o, dlow_o, normed_o, inv_o, dvec_o, pick_o,
    attn_full, up_full, down_full, small_full, small_f, qkv_f, out_f, up_f, down_f, tokens, pick, pick_t, grad,
    qkv, mixed, hidden, vec, qbias, bias, query_m, rows_m, mixed_m, hid_m, act_m, slope, ytwo, dtwo, dlow, dvec, hid_f, normed_one, inverse_one,
    send_sem, recv_sem, small_send, small_recv, load_sem, save_sem, pair_send, pair_recv,
):
    z, y, x, c = place()
    width = tokens.shape[1]
    cols = up_h.shape[1]
    edge = x == c
    third = cols // 3
    mine, across = x + c, 2 * flip(x)
    fulls = (attn_full, up_full, down_full)
    w = z * 2 + y
    mine_rows = pl.ds(pl.multiple_of(w * rows, 32), rows)
    sends = Sends()
    zl, zh = z > 0, z < 3
    count = seqs * padded

    def spot(p, zz, yy, t):
        return fulls[p].at[pl.ds(pl.multiple_of((zz * 2 + yy) * rows, rows), rows), pl.ds(pl.multiple_of(t * third, third), third)]

    def push(cond, p, zz, yy, t, kind, to):
        def make():
            whose = zz * 2 + yy
            where = spot(p, zz, yy, t)
            return pltpu.make_async_remote_copy(
                src_ref=where,
                dst_ref=where,
                send_sem=send_sem.at[kind, p, whose],
                recv_sem=recv_sem.at[p, whose, t],
                device_id=to,
                device_id_type=MESH,
            )

        sends.start(cond, make)

    def arrive(cond, p, zz, yy, t):
        def body():
            where = spot(p, zz, yy, t)
            whose = zz * 2 + yy
            pltpu.make_async_remote_copy(where, where, send_sem.at[0, p, whose], recv_sem.at[p, whose, t], dev(z, y, x, c), device_id_type=MESH).wait_recv()

        when(cond, body)

    UP, DOWN, SIDE, OVER, NEAR, PASS = range(6)
    above, below, beside = dev(z + 1, y, x, c), dev(z - 1, y, x, c), dev(z, flip(y), x, c)
    over, near = dev(z, y, flip(x), c), dev(z, y, x, flip(c))

    def around(d):
        return ((None, z),) if d == 0 else ((z - d >= 0, z - d), (z + d <= 3, z + d))

    def own(p):
        push(zh, p, z, y, mine, UP, above)
        push(zl, p, z, y, mine, DOWN, below)
        push(None, p, z, y, mine, SIDE, beside)

    def z_step(p, d):
        for cond, zz, onward, kind, to in ((z - d >= 0, z - d, zh, UP, above), (z + d <= 3, z + d, zl, DOWN, below)):
            arrive(cond, p, zz, y, mine)
            push(both(cond, onward), p, zz, y, mine, kind, to)
            push(cond, p, zz, y, mine, SIDE, beside)
            push(both(cond, edge), p, zz, y, mine, OVER, over)
            push(cond, p, zz, y, mine, NEAR, near)

    def y_step(p, d):
        for cond, zz in around(d):
            arrive(cond, p, zz, flip(y), mine)
            push(both(cond, edge), p, zz, flip(y), mine, OVER, over)
            push(cond, p, zz, flip(y), mine, NEAR, near)

    def x_step(p, d):
        mid = jnp.logical_not(edge)
        for yy in (y, flip(y)):
            for cond, zz in () if d == 0 and yy is y else around(d):
                cond = both(cond, mid)
                arrive(cond, p, zz, yy, across)
                push(cond, p, zz, yy, across, PASS, near)

    def last(p):
        for d in range(4):
            for yy in (y, flip(y)):
                for cond, zz in () if d == 0 and yy is y else around(d):
                    arrive(cond, p, zz, yy, x + flip(c))
                    arrive(both(cond, edge), p, zz, yy, across)
        keep(fulls[p], (attn_o, up_o, down_o)[p], p)

    saves = []

    def keep(src, dst, k):
        copy = pltpu.make_async_copy(src, dst, save_sem.at[k])
        copy.start()
        saves.append(copy)

    swaps = []

    def swap(ref, k):
        def make():
            return pltpu.make_async_remote_copy(ref.at[0], ref.at[1], pair_send.at[k], pair_recv.at[k], near, device_id_type=MESH)

        make().start()
        swaps.append((make, ref))

    def peer(k):
        return lax.rem(w + k, 8)

    def small_copy(k, whose):
        return pltpu.make_async_remote_copy(
            small_full.at[whose], small_full.at[whose], small_send.at[k], small_recv.at[whose], (peer(k), x * 2 + c), device_id_type=MESH
        )

    def small_out():
        small_f[...] = jnp.zeros_like(small_f)
        small_f[0:8, 0:rows] = vectors[...]
        for r in range(3):
            small_f[8 + r : 9 + r, :] = up_bias[pl.ds(r * 128, 128)].reshape(1, 128)
        small_full[w] = small_f[...].astype(LOW)
        for k in range(1, 8):
            sends.start(None, lambda k=k: small_copy(k, w))

    def attn_shard():
        loads[0].wait()
        loads[1].wait()
        for k in range(3):
            attn_full[mine_rows, pl.ds(k * width, width)] = qkv_f[k].astype(LOW)
        attn_full[mine_rows, pl.ds(3 * width, width)] = out_f[...].astype(LOW)

    def up_shard():
        loads[2].wait()
        up_full[mine_rows, :] = up_f[...].astype(LOW)

    def down_shard():
        loads[3].wait()
        down_full[mine_rows, :] = down_f[...].astype(LOW)

    def masks():
        slots = place_m.shape[1]
        for s in range(seqs):
            hit = lax.broadcasted_iota(jnp.int32, (length, slots), 0) == place_m[s : s + 1, :]
            live = lax.broadcasted_iota(jnp.int32, (length, slots), 1) < count_m[s]
            hit = jnp.logical_and(hit, live).astype(jnp.float32).astype(LOW)
            row = lax.broadcasted_iota(jnp.int32, (padded, slots), 0)
            slot = lax.broadcasted_iota(jnp.int32, (padded, slots), 1)
            same = (row == slot).astype(jnp.float32).astype(LOW)
            kept = jnp.logical_and(row == slot, slot < count_m[s]).astype(jnp.float32).astype(LOW)
            pick[s] = dot(same, hit, NT).astype(LOW)
            pick_t[s] = dot(hit, same, NT).astype(LOW)
            grad[pl.ds(s * padded, padded), :] = dot(kept, grad_m[s], NN)
        keep(pick_t, pick_o, 18)

    def vectors_in():
        for k in range(1, 8):
            small_copy(k, peer(k)).wait_recv()
        at = lax.broadcasted_iota(jnp.int32, (128, width), 0)
        to = lax.broadcasted_iota(jnp.int32, (128, width), 1)
        total = jnp.zeros((16, width), jnp.float32)
        for k in range(8):
            place_k = jnp.logical_and(at + k * rows == to, at < rows).astype(jnp.float32).astype(LOW)
            total += dot(small_full[k], place_k, NN)
            for r in range(3):
                bias[:, pl.ds(k * 384 + r * 128, 128)] = small_full[k, 8 + r : 9 + r, :].astype(jnp.float32)
        vec[...] = total[:8]
        qbias[0] = total[0:1]
        qbias[1] = jnp.zeros((1, width), jnp.float32)
        qbias[2] = total[1:2]

    def project(i):
        r = pl.ds(i * 256, 256)

        @pl.loop(0, 3)
        def _(k):
            value = dot(tokens[r, :], attn_full[:, pl.ds(pl.multiple_of(k * width, width), width)], NN) + qbias[k]
            qkv[k, r, :] = (value * jnp.where(k == 0, 0.125, 1.0)).astype(LOW)

    def attend(s, j):
        lane = lax.broadcasted_iota(jnp.int32, (length, 128), 1) < 64
        cs = pl.ds(j * 128, 128)
        rs = pl.ds(s * length, length)
        key, value = qkv[1, rs, cs], qkv[2, rs, cs]
        zero, one = jnp.zeros_like(key), jnp.ones_like(key)
        keys = (jnp.where(lane, key, zero), jnp.where(lane, zero, key))
        values = (jnp.where(lane, value, one), jnp.where(lane, one, value))
        for q in range(length // 256):
            r = pl.ds(s * length + q * 256, 256)
            query = qkv[0, r, cs]
            parts = []
            for h in range(2):
                score = dot(query, keys[h], NT)
                expo = jnp.exp(score - jnp.max(score, axis=-1, keepdims=True))
                parts.append(dot(expo.astype(LOW), values[h], NN))
            left = lane[:256]
            top = jnp.where(left, parts[0], parts[1])
            under = pltpu.roll(jnp.where(left, parts[1], parts[0]), 64, 1)
            mixed[r, cs] = (top / under).astype(LOW)

    def middle(i):
        r = pl.ds(i * 256, 256)
        pre = tokens[r, :].astype(jnp.float32) + (dot(mixed[r, :], attn_full[:, pl.ds(3 * width, width)], NT) + vec[2:3, :])
        hidden[r, :] = norm(pre, vec[3:4, :], vec[4:5, :])[0]

    def masked_rows():
        for s in range(seqs):
            r = pl.ds(s * padded, padded)
            rs = pl.ds(s * length, length)
            rows_m[0, r, :] = dot(pick[s], tokens[rs, :], NN).astype(LOW)
            mixed_m[0, r, :] = dot(pick[s], mixed[rs, :], NN).astype(LOW)
            query_m[r, :] = dot(pick[s], qkv[0, rs, :], NN).astype(LOW)
        pre = rows_m[0].astype(jnp.float32) + (dot(mixed_m[0], attn_full[:, pl.ds(3 * width, width)], NT) + vec[2:3, :])
        value, normed, inverse = norm(pre, vec[3:4, :], vec[4:5, :])
        hid_f[...] = value
        hid_m[0] = value.astype(LOW)
        normed_one[...] = normed
        inverse_one[...] = jnp.broadcast_to(inverse, inverse_one.shape)
        swap(rows_m, 0)
        swap(mixed_m, 1)
        swap(hid_m, 2)
        keep(query_m, query_o, 3)
        keep(normed_one, normed_o, 4)
        keep(inverse_one, inv_o, 5)

    def upper(k):
        f = pl.ds(k * 768, 768)
        u = dot(hid_m[0], up_full[:, f], NN) + bias[:, f]
        cumul = 0.5 * (1.0 + lax.erf(u * SQRT_HALF))
        act_m[0, :, f] = (u * cumul).astype(LOW)
        slope[:, f] = cumul + u * (jnp.exp(-0.5 * u * u) * INV_ROOT_TWO_PI)

    def after_upper():
        swap(act_m, 3)
        keep(slope, slope_o, 6)

    def lower():
        @pl.loop(0, 3)
        def _(k):
            n = pl.ds(pl.multiple_of(k * 256, 256), 256)
            ytwo[:, n] = dot(act_m[0], down_full[n, :], NT)

        pre = hid_f[...] + (ytwo[...] + vec[5:6, :])
        _, normed, inverse = norm(pre, vec[6:7, :], vec[7:8, :])
        value, dgain, dshift = norm_pull(grad[...], normed, inverse, vec[6:7, :])
        dtwo[...] = value
        dlow[0] = value.astype(LOW)
        dvec[...] = jnp.zeros_like(dvec)
        dvec[5:6, :] = jnp.sum(value, axis=0, keepdims=True)
        dvec[6:7, :] = dgain
        dvec[7:8, :] = dshift
        swap(dlow, 4)
        keep(dtwo, dtwo_o, 7)
        keep(dvec, dvec_o, 8)

    loads = []
    for k, (src, dst) in enumerate(((qkv_h, qkv_f), (out_h, out_f), (up_h, up_f), (down_h, down_f), (tokens_h, tokens))):
        loads.append(pltpu.make_async_copy(src, dst, load_sem.at[k]))
        loads[-1].start()
    bar = pltpu.get_barrier_semaphore()
    for to in [near, over] + [(peer(k), x * 2 + c) for k in range(1, 8)]:
        pl.semaphore_signal(bar, inc=1, device_id=to, device_id_type=MESH)
    attn_shard()
    pl.semaphore_wait(bar, 9)
    own(0)
    small_out()
    up_shard()
    down_shard()
    masks()

    def save_hidden():
        keep(hidden, hidden_o, 9)
        keep(qkv.at[pl.ds(1, 2)], kv_o, 10)

    Z, Y, X, L = z_step, y_step, x_step, last
    head = (
        (Z, 0, 1), (Y, 0, 0), (Z, 0, 2), (Y, 0, 1), (X, 0, 0), (Z, 0, 3), (own, 1), (Y, 0, 2), (X, 0, 1), (vectors_in,), (Y, 0, 3), (X, 0, 2), (Z, 1, 1), (X, 0, 3), (L, 0),
    )
    links = (
        (Y, 1, 0), (Z, 1, 2), (Y, 1, 1), (X, 1, 0), (Z, 1, 3), (own, 2), (Y, 1, 2), (X, 1, 1), (Y, 1, 3), (X, 1, 2), (Z, 2, 1), (X, 1, 3), (L, 1), (Y, 2, 0), (Z, 2, 2), (Y, 2, 1), (X, 2, 0), (Z, 2, 3),
    )
    ends = ((Y, 2, 2), (X, 2, 1), (Y, 2, 3), (X, 2, 2), (X, 2, 3))
    work = [functools.partial(project, i) for i in range(4)]
    work += [functools.partial(attend, s, j) for s in range(seqs) for j in range(width // 128)]
    work += [functools.partial(middle, i) for i in range(4)]
    work += [masked_rows, save_hidden]
    for step, *rest in head:
        step(*rest)
    loads[4].wait()
    done = 0
    for k, (step, *rest) in enumerate(links):
        upto = len(work) * (k + 1) // len(links)
        for piece in work[done:upto]:
            piece()
        done = upto
        step(*rest)
    for k in range(4):
        upper(k)
        step, *rest = ends[k]
        step(*rest)
    step, *rest = ends[4]
    step(*rest)
    after_upper()
    last(2)
    lower()
    keep(vec, vec_o, 11)
    keep(bias, bias_o, 12)
    for make, ref in swaps:
        make().wait_recv()
    for k, (ref, dst) in enumerate(((rows_m, rows_o), (mixed_m, mixed_o), (hid_m, hid_o), (act_m, act_o), (dlow, dlow_o))):
        keep(ref, dst, 13 + k)
    for make, ref in swaps:
        make().wait_send()
    sends.finish()
    for copy in saves:
        copy.wait()


def forward(qkv, out, up, down, vectors, up_bias, tokens, place_m, count_m, grad_m):
    rows, cols = up.shape
    out, down = out.T, down.T
    total, width = tokens.shape
    seqs, slots = place_m.shape
    length = total // seqs
    padded = -(-slots // 16) * 16
    count = seqs * padded
    shape = jax.ShapeDtypeStruct
    f = jnp.float32
    full = shape((8 * rows, cols), LOW)
    anywhere = pl.BlockSpec(memory_space=pl.ANY)
    vm = pl.BlockSpec(memory_space=pltpu.VMEM)
    dma = pltpu.SemaphoreType.DMA
    outs = (
        full, full, full, shape((8, width), f), shape((1, cols), f), shape((2, total, width), LOW), shape((total, width), f),
        shape((count, width), LOW), shape((2, count, width), LOW), shape((2, count, width), LOW), shape((2, count, width), LOW),
        shape((2, count, cols), LOW), shape((count, cols), f), shape((count, width), f), shape((2, count, width), LOW),
        shape((count, width), f), shape((count, 128), f), shape((8, width), f), shape((seqs, length, padded), LOW),
    )
    v = pltpu.VMEM
    return pl.pallas_call(
        functools.partial(forward_kernel, rows, seqs, length, padded),
        out_shape=outs,
        in_specs=[anywhere] * 4 + [vm] * 2 + [anywhere, vm, pl.BlockSpec(memory_space=pltpu.SMEM), vm],
        out_specs=(anywhere,) * len(outs),
        scratch_shapes=[
            v((8 * rows, cols), LOW), v((8 * rows, cols), LOW), v((8 * rows, cols), LOW), v((8, 16, 128), LOW), v((16, 128), f),
            v(qkv.shape, f), v(out.shape, f), v(up.shape, f), v(down.shape, f), v(tokens.shape, LOW), v((seqs, padded, length), LOW), v((seqs, length, padded), LOW), v((count, width), f),
            v((3, total, width), LOW), v((total, width), LOW), v((total, width), f), v((8, width), f), v((3, 1, width), f), v((1, cols), f),
            v((count, width), LOW), v((2, count, width), LOW), v((2, count, width), LOW), v((2, count, width), LOW), v((2, count, cols), LOW),
            v((count, cols), f), v((count, width), f), v((count, width), f), v((2, count, width), LOW), v((8, width), f),
            v((count, width), f), v((count, width), f), v((count, 128), f),
            dma((6, 3, 8)), dma((3, 8, 3)), dma((8,)), dma((8,)), dma((5,)), dma((19,)), dma((5,)), dma((5,)),
        ],
        compiler_params=pltpu.CompilerParams(collective_id=0, has_side_effects=True, vmem_limit_bytes=60 * 2**20),
    )(qkv, out, up, down, vectors, up_bias, tokens, place_m, count_m, grad_m)


E = 768
M = 1536
SLAB = 32
ORDER = (3, 0, 2, 1)
BESIDE_ATTENTION = {1: (("add_x", 0, 3), ("grads", 1, 3),), 3: (("grads", 1, 0),), 4: (("add_x", 0, 0),), 5: (("grads", 1, 2),), 7: (("add_x", 0, 2), ("grads", 1, 1),), 10: (("add_x", 0, 1),)}
BESIDE_KEYS = (("add_x", 1, 3), ("add_y", 0, 3), ("add_x", 1, 0),)
BESIDE_TOKENS = {0: (("add_x", 1, 2), ("add_y", 0, 0), ("line", 0, 0),), 1: (("attention_grads", 3),), 2: (("add_x", 1, 1),), 3: (("add_y", 0, 2), ("attention_grads", 0),)}
BESIDE_FEED_FORWARD = {0: (("add_x", 2, 3),), 1: (("attention_grads", 2),), 2: (("add_x", 2, 0), ("add_y", 0, 1), ("line", 0, 1),), 3: (("add_y", 1, 3), ("attention_grads", 1),), 4: (("add_x", 2, 2), ("add_y", 1, 0), ("line", 1, 0), ("add_y", 1, 2),), 6: (("line", 0, 2), ("add_x", 2, 1),), 8: (("add_y", 1, 1),), 9: (("line", 1, 1),), 12: (("add_y", 2, 3),), 13: (("owner", 0),)}
LAST = (("add_y", 2, 0), ("line", 2, 0), ("line", 1, 2), ("add_y", 2, 2), ("add_y", 2, 1), ("owner", 1), ("line", 2, 1), ("line", 2, 2), ("middle_x", 0), ("owner", 2), ("arrived", 0), ("middle_x", 1), ("arrived", 1), ("middle_x", 2), ("arrived", 2),)


def slabs(rows, body):
    @pl.loop(0, rows // SLAB)
    def _(i):
        body(pl.multiple_of(i * SLAB, SLAB))


def f32(v):
    return v.astype(jnp.float32)


def backward_kernel(
    rows, seqs, length, padded,
    attn_h, up_h, down_h, vec, bias, kv_h, hidden_h, query_h, rows_h, mixed_h, hid_h, act_h, slope_h, dtwo_h, dlow_h, normed_h, inv_h, dvec_h, pick_h, tokens_h,
    layer_h, dtokens_h, out, small_out, norm_out,
    attn, up, down, kv, query_m, rows_m, mixed_m, hid_m, act_m, slope, dtwo, dlow, normed, inverse, dvec, pick_t, tokens,
    left, right, dupper, dbias, dhid, dpre, done, dmix, dquery, dkv, part, tokens_t,
    htile, ytile, ltile,
    acc, xb, yr, zr, mr,
    sall, sall2, ssib, sx, sy, norms,
    load_sem, tile_sem, out_sem, pair_s, pair_r, dup_s, dup_r, sib_s, sib_r, x_s, x_r, y_s, y_r, z_s, z_r, m_s, m_r, f_s, f_r, sm_s, sm_r, sy_r, n_s, n_r,
):
    z, y, x, c = place()
    edge = x == c
    mid = jnp.logical_not(edge)
    width = E
    count = seqs * padded
    total = seqs * length
    pair = rows * 2
    sends = Sends()
    me = dev(z, y, x, c)
    above, below, beside = dev(z + 1, y, x, c), dev(z - 1, y, x, c), dev(z, flip(y), x, c)
    over, near, diag = dev(z, y, flip(x), c), dev(z, y, x, flip(c)), dev(z, y, flip(x), flip(c))
    ecol = pl.multiple_of(x * 2304, 768)
    ocol = pl.multiple_of(flip(x) * 2304, 768)

    loads = []
    for k, (src, dst) in enumerate((
        (dlow_h, dlow), (act_h, act_m), (down_h, down), (slope_h, slope), (hid_h, hid_m), (up_h, up), (dtwo_h, dtwo), (normed_h, normed),
        (inv_h, inverse), (dvec_h, dvec), (attn_h, attn), (mixed_h, mixed_m), (query_h, query_m), (kv_h, kv), (rows_h, rows_m), (tokens_h, tokens), (pick_h, pick_t),
    )):
        loads.append(pltpu.make_async_copy(src, dst, load_sem.at[k]))
        loads[-1].start()
    (L_DLOW, L_ACT, L_DOWN, L_SLOPE, L_HID, L_UP, L_DTWO, L_NORMED, L_INV, L_DVEC, L_ATTN, L_MIXED, L_QUERY, L_KV, L_ROWS, L_TOKENS, L_PICK) = range(17)

    def need(*ks):
        for k in ks:
            loads[k].wait()

    def copy(src, dst, ss, rs, to):
        return pltpu.make_async_remote_copy(src_ref=src, dst_ref=dst, send_sem=ss, recv_sem=rs, device_id=to, device_id_type=MESH)

    def wait(cond, dst, rs):
        when(cond, lambda: copy(dst, dst, rs, rs, me).wait_recv())

    def zrows(zz):
        return pl.ds(zz * pair, pair)

    def wrows(zz, yy):
        return pl.ds(pl.multiple_of((zz * 2 + yy) * rows, rows), rows)

    def add_x(p, zz):
        @pl.when(edge)
        def _():
            wait(None, xb.at[p, zrows(zz)], x_r.at[p, zz])

            def one(i):
                r = pl.ds(zz * pair + i, SLAB)
                acc[p, r, pl.ds(0, E)] = (f32(acc[p, r, pl.ds(0, E)]) + f32(xb[p, r, :])).astype(LOW)

            slabs(pair, one)

        push_y(edge, p, zz, E)

    def push_x(p, zz):
        sends.start(mid, lambda: copy(xb.at[p, zrows(zz)], xb.at[p, zrows(zz)], x_s.at[p, zz], x_r.at[p, zz], over))

    def push_y(cond, p, zz, wide):
        sends.start(cond, lambda: copy(
            acc.at[p, wrows(zz, flip(y)), pl.ds(0, wide)], yr.at[p, zz, :, pl.ds(0, wide)], y_s.at[p, zz], y_r.at[p, zz], beside))

    def add_into(cond, p, zz, buffer, slot, sem):
        for role, wide in ((edge, E), (mid, M)):
            @pl.when(both(cond, role))
            def _():
                wait(None, buffer.at[p, slot, :, pl.ds(0, wide)], sem)
                base = (zz * 2 + y) * rows

                def one(i):
                    here = pl.ds(pl.multiple_of(base + i, SLAB), SLAB)
                    acc[p, here, pl.ds(0, wide)] = (f32(acc[p, here, pl.ds(0, wide)]) + f32(buffer[p, slot, pl.ds(i, SLAB), pl.ds(0, wide)])).astype(LOW)

                slabs(rows, one)

    def add_y(p, zz):
        add_into(None, p, zz, yr, zz, y_r.at[p, zz])

    def z_push(cond, p, spot, k, to):
        for role, wide in ((edge, E), (mid, M)):
            def make(wide=wide):
                zz, slot = spot()
                return copy(acc.at[p, wrows(zz, y), pl.ds(0, wide)], zr.at[p, slot, :, pl.ds(0, wide)], z_s.at[k, p, zz], z_r.at[k, p, zz], to)

            sends.start(lambda role=role: both(cond(), role), make)

    def line(p, t):
        def upward():
            return both(z <= t, z < 3)

        def up_spot():
            zz = jnp.where(upward(), 3 + z - t, 0)
            return zz, zz

        def downward():
            return both(3 - z <= t, z > 0)

        def down_spot():
            zz = jnp.where(downward(), z + t - 3, 0)
            return zz, jnp.where(zz == z - 1, 4, zz)

        zz = up_spot()[0]
        add_into(both(upward(), z > 0), p, zz, zr, zz, z_r.at[0, p, zz])
        z_push(upward, p, up_spot, 0, above)
        zz = down_spot()[0]
        add_into(both(downward(), z < 3), p, zz, zr, zz, z_r.at[1, p, zz])
        z_push(downward, p, down_spot, 1, below)

    def owner(p):
        add_into(z > 0, p, z, zr, z, z_r.at[0, p, z])
        add_into(z < 3, p, z, zr, 4, z_r.at[1, p, z])
        sends.start(mid, lambda: copy(acc.at[p, wrows(z, y)], mr.at[p], m_s.at[p], m_r.at[p], diag))
        base = (z * 2 + y) * rows

        @pl.when(edge)
        def _():
            def one(i):
                out[p, pl.ds(i, SLAB), pl.ds(ecol, E)] = acc[p, pl.ds(pl.multiple_of(base + i, SLAB), SLAB), pl.ds(0, E)]

            slabs(rows, one)

        for k, to in enumerate((near, over, diag)):
            sends.start(edge, lambda k=k, to=to: copy(
                out.at[p, :, pl.ds(ecol, E)], out.at[p, :, pl.ds(ecol, E)], f_s.at[p, k], f_r.at[p, x], to))

    def middle_x(p):
        base = (z * 2 + y) * rows

        @pl.when(mid)
        def _():
            wait(None, mr.at[p], m_r.at[p])

            def one(i):
                out[p, pl.ds(i, SLAB), pl.ds(E, M)] = (f32(acc[p, pl.ds(pl.multiple_of(base + i, SLAB), SLAB), :]) + f32(mr[p, pl.ds(i, SLAB), :])).astype(LOW)

            slabs(rows, one)

        sends.start(mid, lambda: copy(out.at[p, :, pl.ds(E, M)], out.at[p, :, pl.ds(E, M)], f_s.at[p, 0], f_r.at[p, 2], near))

    def arrived(p):
        for xx in range(2):
            wait(jnp.logical_not(both(edge, x == xx)), out.at[p, :, pl.ds(2304 * xx, E)], f_r.at[p, xx])
        wait(edge, out.at[p, :, pl.ds(E, M)], f_r.at[p, 2])

    swaps = []

    def swap(ref, k):
        def make():
            return copy(ref.at[0], ref.at[1], pair_s.at[k], pair_r.at[k], near)

        make().start()
        swaps.append(make)

    def transpose_into(ref):
        for k in range(2):
            left[k] = ref[k].T

    def product(zz, ref, cols):
        return (dot(left[0, zrows(zz), :], ref[0, :, cols], NN) + dot(left[1, zrows(zz), :], ref[1, :, cols], NN)).astype(LOW)

    def grads(p, zz, ref):
        @pl.when(mid)
        def _():
            xb[p, zrows(zz), :] = product(zz, ref, pl.ds(ocol, E))

        push_x(p, zz)

        @pl.when(mid)
        def _():
            for k in range(2):
                acc[p, zrows(zz), pl.ds(k * E, E)] = product(zz, ref, pl.ds(E + k * E, E))

        push_y(mid, p, zz, M)

        @pl.when(edge)
        def _():
            acc[p, zrows(zz), pl.ds(0, E)] = product(zz, ref, pl.ds(ecol, E))

    def dup_copy(k):
        f = pl.ds(k * 768, 768)
        return copy(dupper.at[0, :, f], dupper.at[1, :, f], dup_s.at[k], dup_r.at[k], near)

    def upper_back(k):
        f = pl.ds(k * 768, 768)
        value = dot(dlow[0], down[:, f], NN) * slope[:, f]
        dbias[:, f] = jnp.sum(value, axis=0, keepdims=True)
        dupper[0, :, f] = value.astype(LOW)
        dup_copy(k).start()

    def hidden_back():
        @pl.loop(0, 3)
        def _(k):
            n = pl.ds(pl.multiple_of(k * 256, 256), 256)
            dhid[:, n] = dot(dupper[0], up[n, :], NT)

        value, dgain, dshift = norm_pull(dtwo[...] + dhid[...], normed[...], inverse[:, :1], vec[3:4, :])
        dpre[...] = value
        done[0] = value.astype(LOW)
        swap(done, 0)
        dvec[2:3, :] = jnp.sum(value, axis=0, keepdims=True)
        dvec[3:4, :] = dgain
        dvec[4:5, :] = dshift
        dmix[...] = dot(done[0], attn[:, pl.ds(3 * width, width)], NN).astype(LOW)

    def attend_back(step):
        s, j = step // 6, lax.rem(step, 6)
        cs = pl.ds(pl.multiple_of(j * 128, 128), 128)
        rs = pl.ds(pl.multiple_of(s * length, length), length)
        ms = pl.ds(pl.multiple_of(s * padded, padded), padded)
        lane = lax.broadcasted_iota(jnp.int32, (padded, 128), 1) < 64

        def halves(v):
            zero = jnp.zeros_like(v)
            return jnp.concatenate([jnp.where(lane, v, zero), jnp.where(lane, zero, v)], axis=0)

        key, value = kv[0, rs, cs], kv[1, rs, cs]
        queries, mixes = halves(query_m[ms, cs]), halves(dmix[ms, cs])
        score = dot(key, queries, NT)
        expo = jnp.exp(score - jnp.max(score, axis=0, keepdims=True))
        probs = expo / jnp.sum(expo, axis=0, keepdims=True)
        dprobs = dot(value, mixes, NT)
        dscore = (probs * (dprobs - jnp.sum(dprobs * probs, axis=0, keepdims=True))).astype(LOW)
        dkv[0, rs, cs] = dot(dscore, queries, NN).astype(LOW)
        dvalue = dot(probs.astype(LOW), mixes, NN)
        dkv[1, rs, cs] = dvalue.astype(LOW)
        dq = dot(dscore, key, TN) * 0.125
        dq = jnp.where(lane, dq[:padded], dq[padded:])
        dquery[0, ms, cs] = dq.astype(LOW)
        first = s == 0
        sums = jnp.concatenate([jnp.sum(dq, axis=0, keepdims=True), jnp.sum(dvalue, axis=0, keepdims=True)], axis=0)
        dvec[0:2, cs] = sums + jnp.where(first, 0.0, dvec[0:2, cs])

    def key_value_grads():
        for i in range(total // 256):
            r = pl.ds(i * 256, 256)
            tokens_t[:, r] = tokens[r, :].T

        def fill(store):
            @pl.loop(0, 8)
            def _(i):
                k = lax.rem(i, 2)
                n = pl.ds(pl.multiple_of(i // 2 * pair, pair), pair)
                store(n, pl.ds(pl.multiple_of(k * E, E), E), dot(tokens_t[n, :], dkv[k], NN).astype(LOW))

        @pl.when(mid)
        def _():
            def store(n, cols, value):
                acc[2, n, cols] = value

            fill(store)

        @pl.when(edge)
        def _():
            def store(n, cols, value):
                part[n, cols] = value

            fill(store)

        for zz in ORDER:
            sends.start(edge, lambda zz=zz: copy(part.at[zrows(zz)], part.at[zrows(zz)], sib_s.at[zz], sib_r.at[zz], near))

    def attention_sides():
        for k in range(2):
            left[k] = jnp.where(c == 0, rows_m[k], done[k]).T
            right[k] = jnp.where(c == 0, dquery[k], mixed_m[k])

    def attention_grads(zz):
        @pl.when(mid)
        def _():
            xb[2, zrows(zz), :] = product(zz, right, pl.ds(0, E))

        push_x(2, zz)

        @pl.when(mid)
        def _():
            wait(None, part.at[zrows(zz)], sib_r.at[zz])

            def one(i):
                r = pl.ds(zz * pair + i, SLAB)
                acc[2, r, :] = (f32(acc[2, r, :]) + f32(part[r, :])).astype(LOW)

            slabs(pair, one)

        push_y(mid, 2, zz, M)

        @pl.when(edge)
        def _():
            acc[2, zrows(zz), pl.ds(0, E)] = product(zz, right, pl.ds(0, E))

    def tile_load(i):
        slot = lax.rem(i, 2)
        return pltpu.make_async_copy(hidden_h.at[pl.ds(pl.multiple_of(i * 256, 256), 256)], htile.at[slot], tile_sem.at[slot])

    def layer_store(i):
        slot = lax.rem(i, 2)
        return pltpu.make_async_copy(ltile.at[slot], layer_h.at[pl.ds(pl.multiple_of(i * 256, 256), 256)], out_sem.at[slot])

    def feed_forward(step):
        i, k = step // 4, lax.rem(step, 4)
        slot = lax.rem(i, 2)

        @pl.when(k == 0)
        def _():
            tile_load(i).wait()

            @pl.when(i + 1 < total // 256)
            def _():
                tile_load(i + 1).start()

        f = pl.ds(pl.multiple_of(k * 768, 768), 768)
        u = dot(htile[slot].astype(LOW), up[:, f], NN) + bias[:, f]
        a = (u * (0.5 * (1.0 + lax.erf(u * SQRT_HALF)))).astype(LOW)
        ytile[...] = dot(a, down[:, f], NT) + jnp.where(k == 0, htile[slot] + vec[5:6, :], ytile[...])

        @pl.when(k == 3)
        def _():
            @pl.when(i >= 2)
            def _():
                layer_store(i - 2).wait()

            ltile[slot] = norm(ytile[...], vec[6:7, :], vec[7:8, :])[0].astype(LOW)
            layer_store(i).start()

    def token_store(i):
        slot = lax.rem(i, 2)
        return pltpu.make_async_copy(htile.at[slot], dtokens_h.at[pl.ds(pl.multiple_of(i * 256, 256), 256)], out_sem.at[2 + slot])

    def masked_tokens():
        dpre[...] = dpre[...] + dot(dquery[0], attn[:, pl.ds(0, width)], NT)

    def tokens_back(i):
        slot = lax.rem(i, 2)

        @pl.when(i >= 2)
        def _():
            token_store(i - 2).wait()

        r = pl.ds(pl.multiple_of(i * 256, 256), 256)
        s = i // (length // 256)
        pick = pick_t[s, pl.ds(pl.multiple_of(lax.rem(i, length // 256) * 256, 256), 256), :]
        value = dpre[pl.ds(pl.multiple_of(s * padded, padded), padded), :]
        high = value.astype(LOW)
        rest = (value - f32(high)).astype(LOW)
        htile[slot] = (
            dot(dkv[0, r, :], attn[:, pl.ds(width, width)], NT) + dot(dkv[1, r, :], attn[:, pl.ds(2 * width, width)], NT) + (dot(pick, high, NN) + dot(pick, rest, NN))
        )
        token_store(i).start()

    def small_start():
        for w in range(8):
            sall[w] = jnp.zeros((16, 128), jnp.float32)
            turned = dvec[...] if w == 0 else pltpu.roll(dvec[...], width - rows * w, 1)
            lane = lax.broadcasted_iota(jnp.int32, (8, 128), 1)
            sall[w, 0:8, :] = jnp.where(lane < rows, turned[:, :128], 0.0)
            for r in range(3):
                sall[w, 8 + r : 9 + r, :] = dbias[:, pl.ds(w * 384 + r * 128, 128)]
        sends.start(None, lambda: copy(sall, ssib, sm_s.at[0], sm_r.at[0], near))

    def small_x():
        wait(None, ssib, sm_r.at[0])
        ssib[...] = sall[...] + ssib[...]
        sends.start(None, lambda: copy(ssib, sx, sm_s.at[1], sm_r.at[1], over))

    w = z * 2 + y

    def peer(k):
        return lax.rem(w + k, 8)

    def small_y():
        wait(None, sx, sm_r.at[1])
        sall2[...] = ssib[...] + sx[...]
        for k in range(1, 8):
            sends.start(None, lambda k=k: copy(sall2.at[peer(k)], sy.at[w], sm_s.at[1 + k], sy_r.at[w], (peer(k), x * 2 + c)))
        sy[w] = sall2[w]

    def small_add():
        for k in range(1, 8):
            wait(None, sy.at[peer(k)], sy_r.at[peer(k)])
        value = sy[0]
        for k in range(1, 8):
            value = value + sy[k]
        small_out[...] = value

    def square_sum():
        value = small_out[...]
        squares = value * value
        for p in range(3):
            def body(i, sums):
                v = f32(out[p, pl.ds(pl.multiple_of(i * 16, 16), 16), :])
                v = v * v
                for k in range(v.shape[1] // 128):
                    sums = sums + v[:, k * 128 : (k + 1) * 128]
                return sums

            squares = lax.fori_loop(0, rows // 16, body, squares)
        norms[w] = jnp.full((8, 128), jnp.sum(squares), jnp.float32)
        for k in range(1, 8):
            sends.start(None, lambda k=k: copy(norms.at[w], norms.at[w], n_s.at[k], n_r.at[w], (peer(k), x * 2 + c)))
        for k in range(1, 8):
            wait(None, norms.at[peer(k)], n_r.at[peer(k)])
        whole = norms[0]
        for k in range(1, 8):
            whole = whole + norms[k]
        norm_out[...] = jnp.sqrt(whole)

    moves = {
        "add_x": add_x, "add_y": add_y, "line": line, "owner": owner, "middle_x": middle_x, "arrived": arrived,
        "grads": lambda p, zz: grads(p, zz, dupper), "attention_grads": lambda zz: attention_grads(zz),
    }
    small_moves = {("add_y", 1, 3): small_y, ("owner", 1): small_add}

    def run(steps):
        for name, *rest in steps:
            moves[name](*rest)
            small_moves.get((name, *rest), lambda: None)()

    def looped(n, body, table):
        @pl.loop(0, n)
        def _(i):
            body(i)
            for k in sorted(table):
                pl.when(i == k)(lambda k=k: run(table[k]))

    bar = pltpu.get_barrier_semaphore()
    for to in [near, over, diag] + [(peer(k), x * 2 + c) for k in range(1, 8)]:
        pl.semaphore_signal(bar, inc=1, device_id=to, device_id_type=MESH)
    pl.semaphore_wait(bar, 10)

    need(L_DLOW, L_ACT)
    transpose_into(dlow)
    for zz in ORDER:
        grads(0, zz, act_m)
    need(L_DOWN, L_SLOPE)
    for k in range(4):
        upper_back(k)
    need(L_HID)
    transpose_into(hid_m)
    need(L_UP, L_DTWO, L_NORMED, L_INV, L_ATTN, L_DVEC)
    hidden_back()
    for k in range(4):
        dup_copy(k).wait_recv()
    need(L_QUERY, L_KV)
    looped(seqs * 6, attend_back, BESIDE_ATTENTION)
    swap(dquery, 1)
    small_start()
    need(L_TOKENS, L_ROWS, L_MIXED, L_PICK)
    key_value_grads()
    small_x()
    run(BESIDE_KEYS)
    for make in swaps:
        make().wait_recv()
    attention_sides()
    masked_tokens()
    tile = total // 256
    looped(tile, tokens_back, BESIDE_TOKENS)
    for i in range(tile - 2, tile):
        token_store(i).wait()
    tile_load(0).start()
    looped(tile * 4, feed_forward, BESIDE_FEED_FORWARD)
    run(LAST)
    for i in range(tile - 2, tile):
        layer_store(i).wait()
    square_sum()
    sends.finish()
    for make in swaps:
        make().wait_send()
    for k in range(4):
        dup_copy(k).wait_send()


def backward(attn, up, down, vec, bias, kv, hidden, query_m, rows_m, mixed_m, hid_m, act_m, slope, dtwo, dlow, normed, inverse, dvec, pick_t, tokens):
    total, width = hidden.shape
    cols = up.shape[1]
    rows = width // 8
    seqs, length, padded = pick_t.shape
    count = seqs * padded
    shape = jax.ShapeDtypeStruct
    f = jnp.float32
    anywhere = pl.BlockSpec(memory_space=pl.ANY)
    vm = pl.BlockSpec(memory_space=pltpu.VMEM)
    dma = pltpu.SemaphoreType.DMA
    v = pltpu.VMEM
    inputs = (attn, up, down, vec, bias, kv, hidden, query_m, rows_m, mixed_m, hid_m, act_m, slope, dtwo, dlow, normed, inverse, dvec, pick_t, tokens)

    def like(a):
        return v(a.shape, a.dtype)

    one = (16, 128)
    scratch = [like(a) for a in (attn, up, down, kv, query_m, rows_m, mixed_m, hid_m, act_m, slope, dtwo, dlow, normed, inverse, dvec, pick_t, tokens)]
    scratch += [
        v((2, width, count), LOW), v((2, count, width), LOW), v((2, count, cols), LOW), v((1, cols), f), v((count, width), f), v((count, width), f),
        v((2, count, width), LOW), v((count, width), LOW), v((2, count, width), LOW), v((2, total, width), LOW), v((width, M), LOW), v((width, total), LOW),
        v((2, 256, width), f), v((256, width), f), v((2, 256, width), LOW),
        v((3, width, M), LOW), v((3, width, E), LOW), v((3, 4, rows, M), LOW), v((3, 5, rows, M), LOW), v((3, rows, M), LOW),
        v((8,) + one, f), v((8,) + one, f), v((8,) + one, f), v((8,) + one, f), v((8,) + one, f), v((8, 8, 128), f),
        dma((17,)), dma((2,)), dma((4,)), dma((2,)), dma((2,)), dma((4,)), dma((4,)), dma((4,)), dma((4,)), dma((3, 4)), dma((3, 4)), dma((3, 4)), dma((3, 4)),
        dma((2, 3, 4)), dma((2, 3, 4)), dma((3,)), dma((3,)), dma((3, 3)), dma((3, 3)), dma((9,)), dma((2,)), dma((8,)), dma((8,)), dma((8,)),
    ]
    specs = [anywhere] * len(inputs)
    specs[3] = specs[4] = vm
    return pl.pallas_call(
        functools.partial(backward_kernel, rows, seqs, length, padded),
        out_shape=(shape((total, width), LOW), shape((total, width), f), shape((3, rows, cols), LOW), shape(one, f), shape((8, 128), f)),
        in_specs=specs,
        out_specs=(anywhere, anywhere, vm, vm, vm),
        scratch_shapes=scratch,
        compiler_params=pltpu.CompilerParams(collective_id=1, has_side_effects=True, vmem_limit_bytes=64 * 2**20 - 2**16),
    )(*inputs)


def adam_kernel(layer, dtokens, norm, own, small, *refs):
    weights, firsts, seconds = refs[0:6], refs[6:12], refs[12:18]
    outs = refs[18:36]
    layer_o, dtokens_o, norm_o, layer_v, dtokens_v, sem = refs[36:]
    step_id = pl.program_id(0)
    copies_in = [pltpu.make_async_copy(layer, layer_v, sem.at[0]), pltpu.make_async_copy(dtokens, dtokens_v, sem.at[1])]
    copies_out = [pltpu.make_async_copy(layer_v, layer_o, sem.at[2]), pltpu.make_async_copy(dtokens_v, dtokens_o, sem.at[3])]

    @pl.when(step_id == 0)
    def _():
        for copy in copies_in:
            copy.start()
        norm_o[0, 0] = jnp.max(norm[...])

    @pl.when(step_id == 2)
    def _():
        for first, then in zip(copies_in, copies_out):
            first.wait()
            then.start()

    factor = CLIP_LIMIT / jnp.maximum(norm[0:1, 0:1], CLIP_LIMIT)

    def step(k, where, grad, decay, rate):
        grad = grad * factor.reshape((1,) * grad.ndim)
        weight = weights[k][where]
        first = BETA_ONE * firsts[k][where] + (1.0 - BETA_ONE) * grad
        second = BETA_TWO * seconds[k][where] + (1.0 - BETA_TWO) * grad * grad
        mean_hat = first * (1.0 / (1.0 - BETA_ONE**STEP))
        square_hat = second * (1.0 / (1.0 - BETA_TWO**STEP))
        outs[3 * k][where] = weight - rate * (mean_hat / (jnp.sqrt(square_hat) + ADAM_EPS) + decay * weight)
        outs[3 * k + 1][where] = first
        outs[3 * k + 2][where] = second

    width = weights[1].shape[1]
    for k in range(3):
        step(0, (k,), f32(own[2, :, pl.ds(k * width, width)]), DECAY_RATE, LEARN_RATE)
    everything = (slice(None), slice(None))
    step(1, everything, f32(own[2, :, pl.ds(3 * width, width)]), DECAY_RATE, OUTPUT_RATE)
    for k in range(4):
        cols = (slice(None), pl.ds(k * width, width))
        step(2, cols, f32(own[1, :, pl.ds(k * width, width)]), DECAY_RATE, LEARN_RATE)
        step(3, cols, f32(own[0, :, pl.ds(k * width, width)]), DECAY_RATE, LEARN_RATE)

    @pl.when(step_id == pl.num_programs(0) - 1)
    def _():
        for copy in copies_out:
            copy.wait()

    @pl.when(step_id == 0)
    def _():
        lanes = weights[4].shape[1]
        step(4, everything, small[0:8, 0:lanes], 0.0, VECTOR_RATE)
        step(5, everything, small[8:11, :], 0.0, BIAS_RATE)


def adam(layer, dtokens, norm, own, small, weights, moments):
    def turn(values):
        a, b, c, d, e, g = values
        return a, b.T, c, d.T, e, g.reshape(3, 128)

    arrays = turn(weights) + turn([m[0] for m in moments]) + turn([m[1] for m in moments])
    rows, cols = arrays[2].shape
    width = cols // 4
    slab = 16
    anywhere = pl.BlockSpec(memory_space=pl.ANY)
    specs = [
        pl.BlockSpec((3, slab, width), lambda i: (0, i, 0)),
        pl.BlockSpec((slab, width), lambda i: (i, 0)),
        pl.BlockSpec((slab, cols), lambda i: (i, 0)),
        pl.BlockSpec((slab, cols), lambda i: (i, 0)),
        pl.BlockSpec(arrays[4].shape, lambda i: (0, 0)),
        pl.BlockSpec(arrays[5].shape, lambda i: (0, 0)),
    ]
    outs = pl.pallas_call(
        adam_kernel,
        grid=(rows // slab,),
        out_shape=tuple(jax.ShapeDtypeStruct(a.shape, a.dtype) for a in arrays[:6] for _ in range(3))
        + (jax.ShapeDtypeStruct(layer.shape, layer.dtype), jax.ShapeDtypeStruct(dtokens.shape, dtokens.dtype), jax.ShapeDtypeStruct((1, 1), jnp.float32)),
        in_specs=[
            anywhere,
            anywhere,
            pl.BlockSpec(norm.shape, lambda i: (0, 0)),
            pl.BlockSpec((3, slab, cols), lambda i: (0, i, 0)),
            pl.BlockSpec(small.shape, lambda i: (0, 0)),
        ] + specs * 3,
        out_specs=tuple(s for s in specs for _ in range(3)) + (anywhere, anywhere, pl.BlockSpec(memory_space=pltpu.SMEM)),
        scratch_shapes=[pltpu.VMEM(layer.shape, layer.dtype), pltpu.VMEM(dtokens.shape, dtokens.dtype), pltpu.SemaphoreType.DMA((4,))],
        compiler_params=pltpu.CompilerParams(vmem_limit_bytes=64 * 2**20 - 2**16),
    )(layer, dtokens, norm, own, small, *arrays)

    def back(k, v):
        return v.T if k in (1, 3) else v.reshape(-1) if k == 5 else v

    return (outs[18], outs[19], outs[20].reshape(())) + tuple(back(i // 3, v) for i, v in enumerate(outs[:18]))


def masks(mask_place, mask_count, gradient, length):
    seqs, slots = mask_place.shape
    padded = -(-slots // 16) * 16
    live = jnp.arange(padded)[None, :] < mask_count[:, None]
    spots = jnp.pad(mask_place, ((0, 0), (0, padded - slots)), constant_values=-1)
    pick = (spots[:, :, None] == jnp.arange(length)[None, None, :]) & live[:, :, None]
    gradient = jnp.pad(gradient, ((0, 0), (0, padded - slots), (0, 0)))
    gradient = jnp.where(live[:, :, None], gradient, jnp.zeros_like(gradient))
    return pick, gradient.reshape(seqs * padded, -1)


def update(weights, moments, grads, grad_norm):
    factor = CLIP_LIMIT / jnp.maximum(grad_norm, CLIP_LIMIT)
    rates = (LEARN_RATE, OUTPUT_RATE, LEARN_RATE, LEARN_RATE, VECTOR_RATE, BIAS_RATE)
    out = ()
    for k in range(6):
        out += adam_step(weights[k], *moments[k], grads[k], factor, DECAY_RATE if k < 4 else 0.0, rates[k])
    return out


def natural(own_attn, own_up, own_down, own_vectors, own_bias):
    width = own_up.shape[1] // 4
    own_qkv = jnp.swapaxes(own_attn[:, : 3 * width].reshape(-1, 3, width), 0, 1)
    return own_qkv, own_attn[:, 3 * width :].T, own_up, own_down.T, own_vectors, own_bias


def pack(qkv, out, up, down):
    attn = jnp.concatenate([qkv[0], qkv[1], qkv[2], out.T], axis=1)
    return attn.astype(jnp.bfloat16), up.astype(jnp.bfloat16), down.T.astype(jnp.bfloat16)


def plain(tokens, mask_place, mask_count, gradient, weights, moments):
    low = jnp.bfloat16
    seqs, length, width = tokens.shape
    pick, gradient = masks(mask_place, mask_count, gradient, length)
    padded = pick.shape[1]
    flat = tokens.reshape(seqs * length, width)
    attn_w, up_w, down_w = (lax.all_gather(v, "wide", axis=0, tiled=True) for v in pack(*weights[:4]))
    vec = lax.all_gather(weights[4].astype(low), "wide", axis=1, tiled=True).astype(jnp.float32)
    bias = lax.all_gather(weights[5].astype(low), "wide", axis=0, tiled=True).astype(jnp.float32)
    wq, wk, wv, wo = (attn_w[:, k * width : (k + 1) * width] for k in range(4))
    query = (mm(flat, wq, NN) + vec[0]).astype(low)
    key = mm(flat, wk, NN, low)
    value = (mm(flat, wv, NN) + vec[1]).astype(low)
    query, key, value = (split_heads(v, seqs, length) for v in (query, key, value))
    mixed = lax.map(attend, (query, key, value)).reshape(seqs * length, width)

    def middle(rows, mixed):
        pre_one = rows.astype(jnp.float32) + (mm(mixed, wo, NT) + vec[2])
        hidden, normed, inverse = layer_norm(pre_one, vec[3], vec[4])
        hidden_low = hidden.astype(low)
        upper = mm(hidden_low, up_w, NN) + bias
        cumul = 0.5 * (1.0 + lax.erf(upper * SQRT_HALF))
        active = (upper * cumul).astype(low)
        pre_two = hidden + (mm(active, down_w, NT) + vec[5])
        return layer_norm(pre_two, vec[6], vec[7]), normed, inverse, hidden_low, upper, cumul, active

    layer_out = middle(flat, mixed)[0][0].astype(low)
    pick_low = pick.astype(low)

    def take(values):
        values = values.reshape(seqs, length, width)
        return jnp.einsum("sil,sld->sid", pick_low, values, preferred_element_type=jnp.float32).astype(low)

    rows_m = take(flat).reshape(seqs * padded, width)
    mixed_m = take(mixed).reshape(seqs * padded, width)
    query_m = split_heads(take(query), seqs, padded)
    (_, normed_two, inverse_two), normed_one, inverse_one, hidden_m, upper, cumul, active = middle(rows_m, mixed_m)
    dpre_two, dgain_two, dshift_two = norm_back(gradient.astype(jnp.float32), normed_two, inverse_two, vec[6])
    dbias_two = jnp.sum(dpre_two, axis=0)
    dtwo_low = dpre_two.astype(low)
    ddown = mm(dtwo_low, active, TN)
    dactive = mm(dtwo_low, down_w, NN)
    density = jnp.exp(-0.5 * upper * upper) * INV_ROOT_TWO_PI
    dupper = dactive * (cumul + upper * density)
    dup_bias = jnp.sum(dupper, axis=0)
    dupper_low = dupper.astype(low)
    dup = mm(hidden_m, dupper_low, TN)
    dhidden = dpre_two + mm(dupper_low, up_w, NT)
    dpre_one, dgain_one, dshift_one = norm_back(dhidden, normed_one, inverse_one, vec[3])
    dbias_out = jnp.sum(dpre_one, axis=0)
    done_low = dpre_one.astype(low)
    dout = mm(done_low, mixed_m, TN)
    dmixed = split_heads(mm(done_low, wo, NN, low), seqs, padded)
    dquery, dkey, dvalue = lax.map(attend_back, (query_m, key, value, dmixed))
    dquery = dquery.reshape(seqs * padded, width)
    dkey = dkey.reshape(seqs * length, width)
    dvalue = dvalue.reshape(seqs * length, width)
    dbias_query = jnp.sum(dquery, axis=0)
    dbias_value = jnp.sum(dvalue, axis=0)
    dquery, dkey, dvalue = dquery.astype(low), dkey.astype(low), dvalue.astype(low)
    dattn = jnp.concatenate([mm(rows_m, dquery, TN), mm(flat, dkey, TN), mm(flat, dvalue, TN), dout], axis=1)
    masked_part = dpre_one + mm(dquery, wq, NT)
    dtokens = spread(pick, masked_part) + mm(dkey, wk, NT) + mm(dvalue, wv, NT)
    dvectors = jnp.stack(
        [dbias_query, dbias_value, dbias_out, dgain_one, dshift_one, dbias_two, dgain_two, dshift_two]
    )

    def owned(value, dim):
        return lax.psum(lax.psum_scatter(value, "wide", scatter_dimension=dim, tiled=True), "narrow")

    grads = (owned(dattn, 0), owned(dup, 0), owned(ddown, 0), owned(dvectors, 1), owned(dup_bias, 0))
    grad_norm = jnp.sqrt(lax.psum(sum(jnp.sum(v * v) for v in grads), "wide"))
    return (layer_out, dtokens, grad_norm) + update(weights, moments, natural(*grads), grad_norm)


def spread(pick, rows):
    seqs, padded, length = pick.shape
    return jnp.einsum(
        "sil,sid->sld",
        pick.astype(jnp.float32),
        rows.reshape(seqs, padded, -1),
        precision=lax.Precision.HIGHEST,
        preferred_element_type=jnp.float32,
    ).reshape(seqs * length, -1)


def tailored(tokens, mask_place, mask_count, gradient, weights, moments):
    seqs, length, width = tokens.shape
    flat = tokens.reshape(seqs * length, width)
    saved = forward(*weights, flat, mask_place, mask_count, gradient)
    layer_out, dtokens, own, small, grad_norm = backward(*saved, flat)
    return adam(layer_out, dtokens, grad_norm, own, small, weights, moments)


def shards(body, tokens, mask_place, mask_count, masked_output_gradient, *parameters):
    seqs, length, width = tokens.shape
    weights = parameters[0::3]
    moments = tuple(zip(parameters[1::3], parameters[2::3]))
    layer_out, dtokens, *rest = body(tokens, mask_place, mask_count, masked_output_gradient, weights, moments)
    return (layer_out.reshape(seqs, length, width), dtokens.reshape(seqs, length, width), *rest)


def solution(mesh):
    body = tailored if mesh.shape["wide"] == 8 and mesh.shape["narrow"] == 4 else plain
    data = P(("wide", "narrow"))
    rows = P("wide")
    columns = P(None, "wide")
    weights = (columns,) * 6 + (rows,) * 3 + (columns,) * 6 + (rows,) * 3
    return jax.shard_map(
        functools.partial(shards, body),
        mesh=mesh,
        in_specs=(data,) * 4 + weights,
        out_specs=(data, data, P()) + weights,
        check_vma=False,
    )
```

```python
import functools

import jax
import jax.numpy as jnp
from jax import lax
from jax.experimental import pallas as pl
from jax.experimental.pallas import tpu as pltpu
from jax.sharding import PartitionSpec as P

HEADS = 12
HEAD_DIM = 64
STEP = 10

LN_EPS = 1e-06
SQRT_HALF = 0.7071067811865476
INV_ROOT_TWO_PI = 0.3989422804014327
CLIP_LIMIT = 1.0
BETA_ONE = 0.9
BETA_TWO = 0.999
LEARN_RATE = 0.05
OUTPUT_RATE = 0.2
VECTOR_RATE = 0.5
BIAS_RATE = 0.3
DECAY_RATE = 0.01
ADAM_EPS = 1e-08

MESH = pl.DeviceIdType.MESH


def when(cond, body):
    if callable(cond):
        cond = cond()
    if cond is None:
        body()
    else:
        pl.when(cond)(body)


class Sends:
    def __init__(self):
        self.started = []

    def start(self, cond, make):
        when(cond, lambda: make().start())
        self.started.append((cond, make))

    def finish(self):
        for cond, make in self.started:
            when(cond, lambda make=make: make().wait_send())


def both(a, b):
    return b if a is None else (a if b is None else jnp.logical_and(a, b))


def place():
    w, n = lax.axis_index("wide"), lax.axis_index("narrow")
    return w // 2, lax.rem(w, 2), n // 2, lax.rem(n, 2)


def flip(v):
    return 1 - v


def dev(z, y, x, c):
    return (z * 2 + y, x * 2 + c)


def meet(z, y, x, c, diagonal):
    bar = pltpu.get_barrier_semaphore()
    peers = [(None, dev(z, flip(y), x, c)), (None, dev(z, y, flip(x), c)), (None, dev(z, y, x, flip(c)))]
    if diagonal:
        peers.append((None, dev(z, y, flip(x), flip(c))))
    peers += [(z > 0, dev(z - 1, y, x, c)), (z < 3, dev(z + 1, y, x, c))]
    for cond, peer in peers:
        when(cond, lambda peer=peer: pl.semaphore_signal(bar, inc=1, device_id=peer, device_id_type=MESH))
    inner = jnp.logical_and(z > 0, z < 3)
    count = 4 if diagonal else 3
    pl.semaphore_wait(bar, count + 1 + jnp.where(inner, 1, 0))


def gather_kernel(rows, cols, attn, up, down, small, attn_full, up_full, down_full, small_full, send_sem, recv_sem, small_send, small_recv, own_sem):
    z, y, x, c = place()
    edge = x == c
    third = cols // 3
    mine, across = x + c, 2 * flip(x)
    fulls = (attn_full, up_full, down_full)
    shards = (attn, up, down)
    sends = Sends()
    zl, zh = z > 0, z < 3

    def spot(p, zz, yy, t):
        return fulls[p].at[pl.ds(pl.multiple_of((zz * 2 + yy) * rows, rows), rows), pl.ds(pl.multiple_of(t * third, third), third)]

    def push(cond, p, zz, yy, t, kind, to, src=None):
        def make():
            w = zz * 2 + yy
            where = spot(p, zz, yy, t)
            return pltpu.make_async_remote_copy(
                src_ref=where if src is None else src,
                dst_ref=where,
                send_sem=send_sem.at[kind, p, w],
                recv_sem=recv_sem.at[p, w, t],
                device_id=to,
                device_id_type=MESH,
            )

        sends.start(cond, make)

    def small_push(cond, zz, yy, kind, to, src=None):
        def make():
            w = zz * 2 + yy
            where = small_full.at[w]
            return pltpu.make_async_remote_copy(
                src_ref=where if src is None else src,
                dst_ref=where,
                send_sem=small_send.at[kind, w],
                recv_sem=small_recv.at[w],
                device_id=to,
                device_id_type=MESH,
            )

        sends.start(cond, make)

    def arrive(cond, p, zz, yy, t):
        def body():
            where = spot(p, zz, yy, t)
            w = zz * 2 + yy
            pltpu.make_async_remote_copy(where, where, send_sem.at[0, p, w], recv_sem.at[p, w, t], dev(z, y, x, c), device_id_type=MESH).wait_recv()

        when(cond, body)

    def small_arrive(cond, zz, yy):
        def body():
            w = zz * 2 + yy
            pltpu.make_async_remote_copy(small_full.at[w], small_full.at[w], small_send.at[0, w], small_recv.at[w], dev(z, y, x, c), device_id_type=MESH).wait_recv()

        when(cond, body)

    UP, DOWN, SIDE, OVER, NEAR, PASS = range(6)
    above, below, beside = dev(z + 1, y, x, c), dev(z - 1, y, x, c), dev(z, flip(y), x, c)
    over, near = dev(z, y, flip(x), c), dev(z, y, x, flip(c))

    def own(p):
        src = shards[p].at[:, pl.ds(pl.multiple_of(mine * third, third), third)]
        push(zh, p, z, y, mine, UP, above, src)
        push(zl, p, z, y, mine, DOWN, below, src)
        push(None, p, z, y, mine, SIDE, beside, src)

    def z_step(p, d):
        for cond, zz, onward, kind, to in ((z - d >= 0, z - d, zh, UP, above), (z + d <= 3, z + d, zl, DOWN, below)):
            arrive(cond, p, zz, y, mine)
            push(both(cond, onward), p, zz, y, mine, kind, to)
            push(cond, p, zz, y, mine, SIDE, beside)
            push(both(cond, edge), p, zz, y, mine, OVER, over)
            push(cond, p, zz, y, mine, NEAR, near)

    def y_step(p, d):
        steps = ((None, z),) if d == 0 else ((z - d >= 0, z - d), (z + d <= 3, z + d))
        for cond, zz in steps:
            arrive(cond, p, zz, flip(y), mine)
            push(both(cond, edge), p, zz, flip(y), mine, OVER, over)
            push(cond, p, zz, flip(y), mine, NEAR, near)

    def x_step(p, d):
        mid = jnp.logical_not(edge)
        for yy in (y, flip(y)):
            if d == 0:
                steps = () if yy is y else ((None, z),)
            else:
                steps = ((z - d >= 0, z - d), (z + d <= 3, z + d))
            for cond, zz in steps:
                cond = both(cond, mid)
                arrive(cond, p, zz, yy, across)
                push(cond, p, zz, yy, across, PASS, near)

    def last(p, d):
        for yy in (y, flip(y)):
            if d == 0:
                steps = () if yy is y else ((None, z),)
            else:
                steps = ((z - d >= 0, z - d), (z + d <= 3, z + d))
            for cond, zz in steps:
                arrive(cond, p, zz, yy, x + flip(c))
                arrive(both(cond, edge), p, zz, yy, across)

    def small_z(d):
        for cond, zz, onward, kind, to in ((z - d >= 0, z - d, zh, UP, above), (z + d <= 3, z + d, zl, DOWN, below)):
            small_arrive(cond, zz, y)
            small_push(both(cond, onward), zz, y, kind, to)
            small_push(cond, zz, y, SIDE, beside)

    meet(z, y, x, c, False)
    small_push(zh, z, y, UP, above, small)
    small_push(zl, z, y, DOWN, below, small)
    small_push(None, z, y, SIDE, beside, small)
    own(0)
    w = z * 2 + y
    copies = []
    for p in range(3):
        copies.append(pltpu.make_async_copy(shards[p], fulls[p].at[pl.ds(pl.multiple_of(w * rows, rows), rows)], own_sem.at[p]))
    copies.append(pltpu.make_async_copy(small, small_full.at[w], own_sem.at[3]))
    for copy in copies:
        copy.start()
    for d in range(1, 4):
        small_z(d)
    order = [
        lambda: z_step(0, 1), lambda: own(1), lambda: y_step(0, 0), lambda: z_step(0, 2), lambda: y_step(0, 1), lambda: x_step(0, 0), lambda: z_step(0, 3),
        lambda: y_step(0, 2), lambda: x_step(0, 1), lambda: z_step(1, 1), lambda: own(2), lambda: y_step(0, 3), lambda: x_step(0, 2), lambda: z_step(1, 2), lambda: y_step(1, 0), lambda: x_step(0, 3), lambda: z_step(1, 3),
        lambda: y_step(1, 1), lambda: x_step(1, 0), lambda: z_step(2, 1), lambda: y_step(1, 2), lambda: x_step(1, 1), lambda: z_step(2, 2), lambda: y_step(1, 3), lambda: x_step(1, 2), lambda: z_step(2, 3),
        lambda: y_step(2, 0), lambda: x_step(1, 3), lambda: y_step(2, 1), lambda: x_step(2, 0), lambda: y_step(2, 2), lambda: x_step(2, 1), lambda: y_step(2, 3), lambda: x_step(2, 2), lambda: x_step(2, 3),
    ]
    for step in order:
        step()
    for d in range(4):
        for cond, zz in (((None, z),) if d == 0 else ((z - d >= 0, z - d), (z + d <= 3, z + d))):
            small_arrive(cond, zz, flip(y))
    for p in range(3):
        for d in range(4):
            last(p, d)
    sends.finish()
    for copy in copies:
        copy.wait()


def gather(attn, up, down, small):
    rows, cols = attn.shape
    full = jax.ShapeDtypeStruct((8 * rows, cols), attn.dtype)
    anywhere = pl.BlockSpec(memory_space=pl.ANY)
    return pl.pallas_call(
        functools.partial(gather_kernel, rows, cols),
        out_shape=(full, full, full, jax.ShapeDtypeStruct((8,) + small.shape, small.dtype)),
        in_specs=[anywhere] * 4,
        out_specs=(anywhere,) * 4,
        scratch_shapes=[
            pltpu.SemaphoreType.DMA((6, 3, 8)),
            pltpu.SemaphoreType.DMA((3, 8, 3)),
            pltpu.SemaphoreType.DMA((3, 8)),
            pltpu.SemaphoreType.DMA((8,)),
            pltpu.SemaphoreType.DMA((4,)),
        ],
        compiler_params=pltpu.CompilerParams(collective_id=0, has_side_effects=True),
    )(attn, up, down, small)


def layer_norm(values, gain, shift):
    center = values - jnp.mean(values, axis=-1, keepdims=True)
    inverse = lax.rsqrt(jnp.mean(center * center, axis=-1, keepdims=True) + LN_EPS)
    normed = center * inverse
    return (normed * gain + shift, normed, inverse)


def norm_back(incoming, normed, inverse, gain):
    dgain = jnp.sum(incoming * normed, axis=0)
    dshift = jnp.sum(incoming, axis=0)
    scaled = incoming * gain
    dvalues = inverse * (
        scaled
        - jnp.mean(scaled, axis=-1, keepdims=True)
        - normed * jnp.mean(scaled * normed, axis=-1, keepdims=True)
    )
    return (dvalues, dgain, dshift)


def mm(a, b, dims, out=jnp.float32):
    return lax.dot_general(a, b, (dims, ((), ())), preferred_element_type=jnp.float32).astype(out)


NN = ((1,), (0,))
NT = ((1,), (1,))
TN = ((0,), (0,))


def split_heads(values, seqs, length):
    return values.reshape(seqs, length, HEADS, HEAD_DIM)


def attend(pieces):
    query, key, value = pieces
    raw = jnp.einsum("qhe,khe->hqk", query, key, preferred_element_type=jnp.float32) * HEAD_DIM ** (
        -0.5
    )
    peak = jnp.max(raw, axis=-1, keepdims=True)
    expo = jnp.exp(raw - peak)
    total = jnp.sum(expo, axis=-1, keepdims=True)
    probs = (expo / total).astype(jnp.bfloat16)
    mixed = jnp.einsum("hqk,khe->qhe", probs, value, preferred_element_type=jnp.float32)
    return mixed.astype(jnp.bfloat16)


def attend_back(pieces):
    query, key, value, dmixed = pieces
    scale = HEAD_DIM ** (-0.5)
    raw = jnp.einsum("qhe,khe->hqk", query, key, preferred_element_type=jnp.float32) * scale
    probs = jax.nn.softmax(raw, axis=-1)
    dprobs = jnp.einsum("qhe,khe->hqk", dmixed, value, preferred_element_type=jnp.float32)
    dscore = probs * (dprobs - jnp.sum(dprobs * probs, axis=-1, keepdims=True))
    dscore = (dscore * scale).astype(jnp.bfloat16)
    dquery = jnp.einsum("hqk,khe->qhe", dscore, key, preferred_element_type=jnp.float32)
    dkey = jnp.einsum("hqk,qhe->khe", dscore, query, preferred_element_type=jnp.float32)
    dvalue = jnp.einsum(
        "hqk,qhe->khe", probs.astype(jnp.bfloat16), dmixed, preferred_element_type=jnp.float32
    )
    return (dquery, dkey, dvalue)


def adam_step(weight, first, second, grad, factor, decay, rate):
    grad = grad * factor
    first_new = BETA_ONE * first + (1.0 - BETA_ONE) * grad
    second_new = BETA_TWO * second + (1.0 - BETA_TWO) * grad * grad
    mean_hat = first_new / (1.0 - BETA_ONE**STEP)
    square_hat = second_new / (1.0 - BETA_TWO**STEP)
    weight_new = weight - rate * (mean_hat / (jnp.sqrt(square_hat) + ADAM_EPS) + decay * weight)
    return (weight_new, first_new, second_new)


GATHER_ORDER = (
    ("z_step", 0, 1), ("y_step", 0, 0), ("z_step", 0, 2), ("y_step", 0, 1), ("z_step", 0, 3), ("own", 1),
    ("x_step", 0, 1), ("y_step", 0, 2), ("y_step", 0, 3), ("x_step", 0, 0), ("z_step", 1, 1), ("vectors_in",),
    ("x_step", 0, 2), ("x_step", 0, 3), ("y_step", 1, 0), ("z_step", 1, 2), ("last", 0), ("project", 0),
    ("project", 1), ("project", 2), ("own", 2), ("z_step", 1, 3), ("project", 3), ("x_step", 1, 0),
    ("attend", 0), ("y_step", 1, 1), ("attend", 1), ("attend", 2), ("z_step", 2, 1), ("attend", 3),
    ("y_step", 1, 2), ("attend", 4), ("attend", 5), ("attend", 6), ("x_step", 1, 1), ("y_step", 1, 3),
    ("attend", 7), ("z_step", 2, 2), ("y_step", 2, 0), ("attend", 8), ("attend", 9), ("attend", 10),
    ("x_step", 1, 2), ("attend", 11), ("x_step", 1, 3), ("z_step", 2, 3), ("middle", 0), ("middle", 1),
    ("y_step", 2, 1), ("middle", 2), ("middle", 3), ("masked",), ("x_step", 2, 1), ("x_step", 2, 0),
    ("y_step", 2, 2), ("save_hidden",), ("last", 1), ("upper", 0), ("y_step", 2, 3), ("upper", 1),
    ("x_step", 2, 2), ("upper", 2), ("x_step", 2, 3), ("upper", 3), ("last", 2),
)


def dot(a, b, dims):
    return lax.dot_general(a, b, (dims, ((), ())), preferred_element_type=jnp.float32)


NN = ((1,), (0,))
NT = ((1,), (1,))
TN = ((0,), (0,))
LOW = jnp.bfloat16


def norm(values, gain, shift):
    center = values - jnp.mean(values, axis=-1, keepdims=True)
    inverse = lax.rsqrt(jnp.mean(center * center, axis=-1, keepdims=True) + LN_EPS)
    normed = center * inverse
    return normed * gain + shift, normed, inverse


def norm_pull(incoming, normed, inverse, gain):
    dgain = jnp.sum(incoming * normed, axis=0, keepdims=True)
    dshift = jnp.sum(incoming, axis=0, keepdims=True)
    scaled = incoming * gain
    return (
        inverse * (scaled - jnp.mean(scaled, axis=-1, keepdims=True) - normed * jnp.mean(scaled * normed, axis=-1, keepdims=True)),
        dgain,
        dshift,
    )


def forward_kernel(
    rows, seqs, length, padded,
    qkv_h, out_h, up_h, down_h, vectors, up_bias, tokens_h, place_m, count_m, grad_m,
    attn_o, up_o, down_o, vec_o, bias_o, kv_o, hidden_o, query_o, rows_o, mixed_o, hid_o, act_o, slope_o, dtwo_o, dlow_o, normed_o, inv_o, dvec_o, pick_o,
    attn_full, up_full, down_full, small_full, small_f, qkv_f, out_f, up_f, down_f, tokens, pick, pick_t, grad,
    qkv, mixed, hidden, vec, qbias, bias, query_m, rows_m, mixed_m, hid_m, act_m, slope, ytwo, dtwo, dlow, dvec, hid_f, normed_one, inverse_one,
    send_sem, recv_sem, small_send, small_recv, load_sem, save_sem, pair_send, pair_recv,
):
    z, y, x, c = place()
    width = tokens.shape[1]
    cols = up_h.shape[1]
    edge = x == c
    third = cols // 3
    mine, across = x + c, 2 * flip(x)
    fulls = (attn_full, up_full, down_full)
    w = z * 2 + y
    mine_rows = pl.ds(pl.multiple_of(w * rows, 32), rows)
    sends = Sends()
    zl, zh = z > 0, z < 3
    count = seqs * padded

    def spot(p, zz, yy, t):
        return fulls[p].at[pl.ds(pl.multiple_of((zz * 2 + yy) * rows, rows), rows), pl.ds(pl.multiple_of(t * third, third), third)]

    def push(cond, p, zz, yy, t, kind, to):
        def make():
            whose = zz * 2 + yy
            where = spot(p, zz, yy, t)
            return pltpu.make_async_remote_copy(
                src_ref=where,
                dst_ref=where,
                send_sem=send_sem.at[kind, p, whose],
                recv_sem=recv_sem.at[p, whose, t],
                device_id=to,
                device_id_type=MESH,
            )

        sends.start(cond, make)

    def arrive(cond, p, zz, yy, t):
        def body():
            where = spot(p, zz, yy, t)
            whose = zz * 2 + yy
            pltpu.make_async_remote_copy(where, where, send_sem.at[0, p, whose], recv_sem.at[p, whose, t], dev(z, y, x, c), device_id_type=MESH).wait_recv()

        when(cond, body)

    UP, DOWN, SIDE, OVER, NEAR, PASS = range(6)
    above, below, beside = dev(z + 1, y, x, c), dev(z - 1, y, x, c), dev(z, flip(y), x, c)
    over, near = dev(z, y, flip(x), c), dev(z, y, x, flip(c))

    def around(d):
        return ((None, z),) if d == 0 else ((z - d >= 0, z - d), (z + d <= 3, z + d))

    def own(p):
        push(zh, p, z, y, mine, UP, above)
        push(zl, p, z, y, mine, DOWN, below)
        push(None, p, z, y, mine, SIDE, beside)

    def z_step(p, d):
        for cond, zz, onward, kind, to in ((z - d >= 0, z - d, zh, UP, above), (z + d <= 3, z + d, zl, DOWN, below)):
            arrive(cond, p, zz, y, mine)
            push(both(cond, onward), p, zz, y, mine, kind, to)
            push(cond, p, zz, y, mine, SIDE, beside)
            push(both(cond, edge), p, zz, y, mine, OVER, over)
            push(cond, p, zz, y, mine, NEAR, near)

    def y_step(p, d):
        for cond, zz in around(d):
            arrive(cond, p, zz, flip(y), mine)
            push(both(cond, edge), p, zz, flip(y), mine, OVER, over)
            push(cond, p, zz, flip(y), mine, NEAR, near)

    def x_step(p, d):
        mid = jnp.logical_not(edge)
        for yy in (y, flip(y)):
            for cond, zz in () if d == 0 and yy is y else around(d):
                cond = both(cond, mid)
                arrive(cond, p, zz, yy, across)
                push(cond, p, zz, yy, across, PASS, near)

    def last(p):
        for d in range(4):
            for yy in (y, flip(y)):
                for cond, zz in () if d == 0 and yy is y else around(d):
                    arrive(cond, p, zz, yy, x + flip(c))
                    arrive(both(cond, edge), p, zz, yy, across)
        keep(fulls[p], (attn_o, up_o, down_o)[p], p)

    saves = []

    def keep(src, dst, k):
        copy = pltpu.make_async_copy(src, dst, save_sem.at[k])
        copy.start()
        saves.append(copy)

    swaps = []

    def swap(ref, k):
        def make():
            return pltpu.make_async_remote_copy(ref.at[0], ref.at[1], pair_send.at[k], pair_recv.at[k], near, device_id_type=MESH)

        make().start()
        swaps.append((make, ref))

    def peer(k):
        return lax.rem(w + k, 8)

    def small_copy(k, whose):
        return pltpu.make_async_remote_copy(
            small_full.at[whose], small_full.at[whose], small_send.at[k], small_recv.at[whose], (peer(k), x * 2 + c), device_id_type=MESH
        )

    def small_out():
        small_f[...] = jnp.zeros_like(small_f)
        small_f[0:8, 0:rows] = vectors[...]
        for r in range(3):
            small_f[8 + r : 9 + r, :] = up_bias[pl.ds(r * 128, 128)].reshape(1, 128)
        small_full[w] = small_f[...].astype(LOW)
        for k in range(1, 8):
            sends.start(None, lambda k=k: small_copy(k, w))

    def attn_shard():
        loads[0].wait()
        loads[1].wait()
        for k in range(3):
            attn_full[mine_rows, pl.ds(k * width, width)] = qkv_f[k].astype(LOW)
        attn_full[mine_rows, pl.ds(3 * width, width)] = out_f[...].astype(LOW)

    def up_shard():
        loads[2].wait()
        up_full[mine_rows, :] = up_f[...].astype(LOW)

    def down_shard():
        loads[3].wait()
        down_full[mine_rows, :] = down_f[...].astype(LOW)

    def masks():
        slots = place_m.shape[1]
        for s in range(seqs):
            hit = lax.broadcasted_iota(jnp.int32, (length, slots), 0) == place_m[s : s + 1, :]
            live = lax.broadcasted_iota(jnp.int32, (length, slots), 1) < count_m[s]
            hit = jnp.logical_and(hit, live).astype(jnp.float32).astype(LOW)
            row = lax.broadcasted_iota(jnp.int32, (padded, slots), 0)
            slot = lax.broadcasted_iota(jnp.int32, (padded, slots), 1)
            same = (row == slot).astype(jnp.float32).astype(LOW)
            kept = jnp.logical_and(row == slot, slot < count_m[s]).astype(jnp.float32).astype(LOW)
            pick[s] = dot(same, hit, NT).astype(LOW)
            pick_t[s] = dot(hit, same, NT).astype(LOW)
            grad[pl.ds(s * padded, padded), :] = dot(kept, f32(grad_m[...])[:, s, :].astype(LOW), NN)
        keep(pick_t, pick_o, 18)

    def vectors_in():
        loads[4].wait()
        for k in range(1, 8):
            small_copy(k, peer(k)).wait_recv()
        at = lax.broadcasted_iota(jnp.int32, (128, width), 0)
        to = lax.broadcasted_iota(jnp.int32, (128, width), 1)
        total = jnp.zeros((16, width), jnp.float32)
        for k in range(8):
            place_k = jnp.logical_and(at + k * rows == to, at < rows).astype(jnp.float32).astype(LOW)
            total += dot(small_full[k], place_k, NN)
            for r in range(3):
                bias[:, pl.ds(k * 384 + r * 128, 128)] = small_full[k, 8 + r : 9 + r, :].astype(jnp.float32)
        vec[...] = total[:8]
        qbias[0] = total[0:1]
        qbias[1] = jnp.zeros((1, width), jnp.float32)
        qbias[2] = total[1:2]

    def project(i):
        r = pl.ds(i * 256, 256)

        @pl.loop(0, 3)
        def _(k):
            value = dot(tokens[r, :], attn_full[:, pl.ds(pl.multiple_of(k * width, width), width)], NN) + qbias[k]
            qkv[k, r, :] = (value * jnp.where(k == 0, 0.125, 1.0)).astype(LOW)

    def attend(s, j):
        lane = lax.broadcasted_iota(jnp.int32, (length, 128), 1) < 64
        cs = pl.ds(j * 128, 128)
        rs = pl.ds(s * length, length)
        key, value = qkv[1, rs, cs], qkv[2, rs, cs]
        zero, one = jnp.zeros_like(key), jnp.ones_like(key)
        keys = (jnp.where(lane, key, zero), jnp.where(lane, zero, key))
        values = (jnp.where(lane, value, one), jnp.where(lane, one, value))
        for q in range(length // 256):
            r = pl.ds(s * length + q * 256, 256)
            query = qkv[0, r, cs]
            parts = []
            for h in range(2):
                score = dot(query, keys[h], NT)
                expo = jnp.exp(score - jnp.max(score, axis=-1, keepdims=True))
                parts.append(dot(expo.astype(LOW), values[h], NN))
            left = lane[:256]
            top = jnp.where(left, parts[0], parts[1])
            under = pltpu.roll(jnp.where(left, parts[1], parts[0]), 64, 1)
            mixed[r, cs] = (top / under).astype(LOW)

    def middle(i):
        r = pl.ds(i * 256, 256)
        pre = tokens[r, :].astype(jnp.float32) + (dot(mixed[r, :], attn_full[:, pl.ds(3 * width, width)], NT) + vec[2:3, :])
        hidden[r, :] = norm(pre, vec[3:4, :], vec[4:5, :])[0]

    def masked_rows():
        for s in range(seqs):
            r = pl.ds(s * padded, padded)
            rs = pl.ds(s * length, length)
            rows_m[0, r, :] = dot(pick[s], tokens[rs, :], NN).astype(LOW)
            mixed_m[0, r, :] = dot(pick[s], mixed[rs, :], NN).astype(LOW)
            query_m[r, :] = dot(pick[s], qkv[0, rs, :], NN).astype(LOW)
        pre = rows_m[0].astype(jnp.float32) + (dot(mixed_m[0], attn_full[:, pl.ds(3 * width, width)], NT) + vec[2:3, :])
        value, normed, inverse = norm(pre, vec[3:4, :], vec[4:5, :])
        hid_f[...] = value
        hid_m[0] = value.astype(LOW)
        normed_one[...] = normed
        inverse_one[...] = jnp.broadcast_to(inverse, inverse_one.shape)
        swap(rows_m, 0)
        swap(mixed_m, 1)
        swap(hid_m, 2)
        keep(query_m, query_o, 3)
        keep(normed_one, normed_o, 4)
        keep(inverse_one, inv_o, 5)

    def upper(k):
        f = pl.ds(k * 768, 768)
        u = dot(hid_m[0], up_full[:, f], NN) + bias[:, f]
        cumul = 0.5 * (1.0 + lax.erf(u * SQRT_HALF))
        act_m[0, :, f] = (u * cumul).astype(LOW)
        slope[:, f] = cumul + u * (jnp.exp(-0.5 * u * u) * INV_ROOT_TWO_PI)

    def after_upper():
        swap(act_m, 3)
        keep(slope, slope_o, 6)

    def lower():
        @pl.loop(0, 3)
        def _(k):
            n = pl.ds(pl.multiple_of(k * 256, 256), 256)
            ytwo[:, n] = dot(act_m[0], down_full[n, :], NT)

        pre = hid_f[...] + (ytwo[...] + vec[5:6, :])
        _, normed, inverse = norm(pre, vec[6:7, :], vec[7:8, :])
        value, dgain, dshift = norm_pull(grad[...], normed, inverse, vec[6:7, :])
        dtwo[...] = value
        dlow[0] = value.astype(LOW)
        dvec[...] = jnp.zeros_like(dvec)
        dvec[5:6, :] = jnp.sum(value, axis=0, keepdims=True)
        dvec[6:7, :] = dgain
        dvec[7:8, :] = dshift
        swap(dlow, 4)
        keep(dtwo, dtwo_o, 7)
        keep(dvec, dvec_o, 8)

    loads = []
    for k, (src, dst) in enumerate(((qkv_h, qkv_f), (out_h, out_f), (up_h, up_f), (down_h, down_f), (tokens_h, tokens))):
        loads.append(pltpu.make_async_copy(src, dst, load_sem.at[k]))
        loads[-1].start()
    bar = pltpu.get_barrier_semaphore()
    for to in [near, over] + [(peer(k), x * 2 + c) for k in range(1, 8)]:
        pl.semaphore_signal(bar, inc=1, device_id=to, device_id_type=MESH)
    attn_shard()
    pl.semaphore_wait(bar, 9)
    own(0)
    small_out()
    up_shard()
    down_shard()
    masks()

    def save_hidden():
        keep(hidden, hidden_o, 9)
        keep(qkv.at[pl.ds(1, 2)], kv_o, 10)

    steps = {
        "z_step": z_step, "y_step": y_step, "x_step": x_step, "own": own, "last": last, "vectors_in": vectors_in, "project": project,
        "attend": lambda i: attend(i // (width // 128), i % (width // 128)), "middle": middle, "masked": masked_rows, "save_hidden": save_hidden, "upper": upper,
    }
    for name, *rest in GATHER_ORDER:
        steps[name](*rest)
    after_upper()
    lower()
    keep(vec, vec_o, 11)
    keep(bias, bias_o, 12)
    for make, ref in swaps:
        make().wait_recv()
    for k, (ref, dst) in enumerate(((rows_m, rows_o), (mixed_m, mixed_o), (hid_m, hid_o), (act_m, act_o), (dlow, dlow_o))):
        keep(ref, dst, 13 + k)
    for make, ref in swaps:
        make().wait_send()
    sends.finish()
    for copy in saves:
        copy.wait()


def forward(qkv, out, up, down, vectors, up_bias, tokens, place_m, count_m, grad_m):
    rows, cols = up.shape
    out, down, grad_m = out.T, down.T, jnp.swapaxes(grad_m, 0, 1)
    total, width = tokens.shape
    seqs, slots = place_m.shape
    length = total // seqs
    padded = -(-slots // 16) * 16
    count = seqs * padded
    shape = jax.ShapeDtypeStruct
    f = jnp.float32
    full = shape((8 * rows, cols), LOW)
    anywhere = pl.BlockSpec(memory_space=pl.ANY)
    vm = pl.BlockSpec(memory_space=pltpu.VMEM)
    dma = pltpu.SemaphoreType.DMA
    outs = (
        full, full, full, shape((8, width), f), shape((1, cols), f), shape((2, total, width), LOW), shape((total, width), f),
        shape((count, width), LOW), shape((2, count, width), LOW), shape((2, count, width), LOW), shape((2, count, width), LOW),
        shape((2, count, cols), LOW), shape((count, cols), f), shape((count, width), f), shape((2, count, width), LOW),
        shape((count, width), f), shape((count, 128), f), shape((8, width), f), shape((seqs, length, padded), LOW),
    )
    v = pltpu.VMEM
    return pl.pallas_call(
        functools.partial(forward_kernel, rows, seqs, length, padded),
        out_shape=outs,
        in_specs=[anywhere] * 4 + [vm] * 2 + [anywhere, vm, pl.BlockSpec(memory_space=pltpu.SMEM), vm],
        out_specs=(anywhere,) * len(outs),
        scratch_shapes=[
            v((8 * rows, cols), LOW), v((8 * rows, cols), LOW), v((8 * rows, cols), LOW), v((8, 16, 128), LOW), v((16, 128), f),
            v(qkv.shape, f), v(out.shape, f), v(up.shape, f), v(down.shape, f), v(tokens.shape, LOW), v((seqs, padded, length), LOW), v((seqs, length, padded), LOW), v((count, width), f),
            v((3, total, width), LOW), v((total, width), LOW), v((total, width), f), v((8, width), f), v((3, 1, width), f), v((1, cols), f),
            v((count, width), LOW), v((2, count, width), LOW), v((2, count, width), LOW), v((2, count, width), LOW), v((2, count, cols), LOW),
            v((count, cols), f), v((count, width), f), v((count, width), f), v((2, count, width), LOW), v((8, width), f),
            v((count, width), f), v((count, width), f), v((count, 128), f),
            dma((6, 3, 8)), dma((3, 8, 3)), dma((8,)), dma((8,)), dma((5,)), dma((19,)), dma((5,)), dma((5,)),
        ],
        compiler_params=pltpu.CompilerParams(collective_id=0, has_side_effects=True, vmem_limit_bytes=60 * 2**20),
    )(qkv, out, up, down, vectors, up_bias, tokens, place_m, count_m, grad_m)


E = 768
M = 1536
SLAB = 32
ORDER = (0, 1, 2, 3)
BESIDE_ATTENTION = {2: (("add_x", 0, 0), ("add_x", 0, 1),), 4: (("grads", 1, 0), ("grads", 1, 2), ("add_x", 0, 2),), 10: (("add_y", 0, 0), ("add_x", 0, 3),)}
BESIDE_KEYS = (("line", 0, 0), ("grads", 1, 1), ("add_y", 0, 1), ("grads", 1, 3), ("add_x", 1, 0), ("line", 0, 1), ("add_x", 1, 1), ("add_y", 0, 2),)
BESIDE_TOKENS = {2: (("attention_grads", 0), ("line", 0, 2),), 3: (("add_x", 1, 3), ("add_y", 0, 3),)}
BESIDE_FEED_FORWARD = {2: (("add_y", 1, 0), ("line", 1, 0),), 3: (("attention_grads", 1),), 4: (("add_x", 1, 2),), 5: (("add_y", 1, 1), ("line", 1, 1),), 6: (("add_x", 2, 0), ("add_x", 2, 1),), 7: (("owner", 0),), 9: (("add_y", 2, 0), ("line", 2, 0), ("add_y", 1, 2), ("attention_grads", 3), ("attention_grads", 2), ("line", 1, 2),), 12: (("add_y", 2, 1),), 13: (("line", 2, 1),), 14: (("add_x", 2, 3), ("add_y", 1, 3), ("add_x", 2, 2), ("owner", 1),)}
LAST = (("add_y", 2, 3), ("add_y", 2, 2), ("line", 2, 2), ("middle_x", 0), ("middle_x", 1), ("owner", 2), ("arrived", 0), ("arrived", 1), ("middle_x", 2), ("arrived", 2),)


def slabs(rows, body):
    @pl.loop(0, rows // SLAB)
    def _(i):
        body(pl.multiple_of(i * SLAB, SLAB))


def f32(v):
    return v.astype(jnp.float32)


def backward_kernel(
    rows, seqs, length, padded,
    attn_h, up_h, down_h, vec, bias, kv_h, hidden_h, query_h, rows_h, mixed_h, hid_h, act_h, slope_h, dtwo_h, dlow_h, normed_h, inv_h, dvec_h, pick_h, tokens_h,
    layer_h, dtokens_h, out, small_out, norm_out,
    attn, up, down, kv, query_m, rows_m, mixed_m, hid_m, act_m, slope, dtwo, dlow, normed, inverse, dvec, pick_t, tokens,
    left, right, dupper, dbias, dhid, dpre, done, dmix, dquery, dkv, part, tokens_t,
    htile, ytile, ltile,
    acc, xb, yr, zr, mr,
    sall, sall2, ssib, sx, sy, norms,
    load_sem, tile_sem, out_sem, pair_s, pair_r, dup_s, dup_r, sib_s, sib_r, x_s, x_r, y_s, y_r, z_s, z_r, m_s, m_r, f_s, f_r, sm_s, sm_r, sy_r, n_s, n_r,
):
    z, y, x, c = place()
    edge = x == c
    mid = jnp.logical_not(edge)
    width = E
    count = seqs * padded
    total = seqs * length
    pair = rows * 2
    sends = Sends()
    me = dev(z, y, x, c)
    above, below, beside = dev(z + 1, y, x, c), dev(z - 1, y, x, c), dev(z, flip(y), x, c)
    over, near, diag = dev(z, y, flip(x), c), dev(z, y, x, flip(c)), dev(z, y, flip(x), flip(c))
    ecol = pl.multiple_of(x * 2304, 768)
    ocol = pl.multiple_of(flip(x) * 2304, 768)

    loads = []
    for k, (src, dst) in enumerate((
        (dlow_h, dlow), (act_h, act_m), (down_h, down), (slope_h, slope), (hid_h, hid_m), (up_h, up), (dtwo_h, dtwo), (normed_h, normed),
        (inv_h, inverse), (dvec_h, dvec), (attn_h, attn), (mixed_h, mixed_m), (query_h, query_m), (kv_h, kv), (rows_h, rows_m), (tokens_h, tokens), (pick_h, pick_t),
    )):
        loads.append(pltpu.make_async_copy(src, dst, load_sem.at[k]))
        loads[-1].start()
    (L_DLOW, L_ACT, L_DOWN, L_SLOPE, L_HID, L_UP, L_DTWO, L_NORMED, L_INV, L_DVEC, L_ATTN, L_MIXED, L_QUERY, L_KV, L_ROWS, L_TOKENS, L_PICK) = range(17)

    def need(*ks):
        for k in ks:
            loads[k].wait()

    def copy(src, dst, ss, rs, to):
        return pltpu.make_async_remote_copy(src_ref=src, dst_ref=dst, send_sem=ss, recv_sem=rs, device_id=to, device_id_type=MESH)

    def wait(cond, dst, rs):
        when(cond, lambda: copy(dst, dst, rs, rs, me).wait_recv())

    def turn(k):
        picks = ((3, 3, 0, 0), (2, 0, 3, 1), (1, 2, 1, 2), (0, 1, 2, 3))[k]
        value = jnp.int32(picks[0])
        for zv in range(1, 4):
            value = jnp.where(z == zv, picks[zv], value)
        return value

    def zrows(k):
        return pl.ds(pl.multiple_of(turn(k) * pair, pair), pair)

    def wrows(zz, yy):
        return pl.ds(pl.multiple_of((zz * 2 + yy) * rows, rows), rows)

    def add_x(p, zz):
        @pl.when(edge)
        def _():
            wait(None, xb.at[p, zrows(zz)], x_r.at[p, zz])

            base = turn(zz) * pair

            def one(i):
                r = pl.ds(pl.multiple_of(base + i, SLAB), SLAB)
                acc[p, r, pl.ds(0, E)] = (f32(acc[p, r, pl.ds(0, E)]) + f32(xb[p, r, :])).astype(LOW)

            slabs(pair, one)

        push_y(edge, p, zz, E)

    def push_x(p, zz):
        sends.start(mid, lambda: copy(xb.at[p, zrows(zz)], xb.at[p, zrows(zz)], x_s.at[p, zz], x_r.at[p, zz], over))

    def push_y(cond, p, zz, wide):
        sends.start(cond, lambda: copy(
            acc.at[p, wrows(turn(zz), flip(y)), pl.ds(0, wide)], yr.at[p, zz, :, pl.ds(0, wide)], y_s.at[p, zz], y_r.at[p, zz], beside))

    def add_into(cond, p, zz, buffer, slot, sem):
        for role, wide in ((edge, E), (mid, M)):
            @pl.when(both(cond, role))
            def _():
                wait(None, buffer.at[p, slot, :, pl.ds(0, wide)], sem)
                base = (zz * 2 + y) * rows

                def one(i):
                    here = pl.ds(pl.multiple_of(base + i, SLAB), SLAB)
                    acc[p, here, pl.ds(0, wide)] = (f32(acc[p, here, pl.ds(0, wide)]) + f32(buffer[p, slot, pl.ds(i, SLAB), pl.ds(0, wide)])).astype(LOW)

                slabs(rows, one)

    def add_y(p, zz):
        add_into(None, p, turn(zz), yr, zz, y_r.at[p, zz])

    def z_push(cond, p, spot, k, to):
        for role, wide in ((edge, E), (mid, M)):
            def make(wide=wide):
                zz, slot = spot()
                return copy(acc.at[p, wrows(zz, y), pl.ds(0, wide)], zr.at[p, slot, :, pl.ds(0, wide)], z_s.at[k, p, zz], z_r.at[k, p, zz], to)

            sends.start(lambda role=role: both(cond(), role), make)

    def line(p, t):
        def upward():
            return both(z <= t, z < 3)

        def up_spot():
            zz = jnp.where(upward(), 3 + z - t, 0)
            return zz, zz

        def downward():
            return both(3 - z <= t, z > 0)

        def down_spot():
            zz = jnp.where(downward(), z + t - 3, 0)
            return zz, jnp.where(zz == z - 1, 4, zz)

        zz = up_spot()[0]
        add_into(both(upward(), z > 0), p, zz, zr, zz, z_r.at[0, p, zz])
        z_push(upward, p, up_spot, 0, above)
        zz = down_spot()[0]
        add_into(both(downward(), z < 3), p, zz, zr, zz, z_r.at[1, p, zz])
        z_push(downward, p, down_spot, 1, below)

    def owner(p):
        add_into(z > 0, p, z, zr, z, z_r.at[0, p, z])
        add_into(z < 3, p, z, zr, 4, z_r.at[1, p, z])
        sends.start(mid, lambda: copy(acc.at[p, wrows(z, y)], mr.at[p], m_s.at[p], m_r.at[p], diag))
        base = (z * 2 + y) * rows

        @pl.when(edge)
        def _():
            def one(i):
                out[p, pl.ds(i, SLAB), pl.ds(ecol, E)] = acc[p, pl.ds(pl.multiple_of(base + i, SLAB), SLAB), pl.ds(0, E)]

            slabs(rows, one)

        for k, to in enumerate((near, over, diag)):
            sends.start(edge, lambda k=k, to=to: copy(
                out.at[p, :, pl.ds(ecol, E)], out.at[p, :, pl.ds(ecol, E)], f_s.at[p, k], f_r.at[p, x], to))

    def middle_x(p):
        base = (z * 2 + y) * rows

        @pl.when(mid)
        def _():
            wait(None, mr.at[p], m_r.at[p])

            def one(i):
                out[p, pl.ds(i, SLAB), pl.ds(E, M)] = (f32(acc[p, pl.ds(pl.multiple_of(base + i, SLAB), SLAB), :]) + f32(mr[p, pl.ds(i, SLAB), :])).astype(LOW)

            slabs(rows, one)

        sends.start(mid, lambda: copy(out.at[p, :, pl.ds(E, M)], out.at[p, :, pl.ds(E, M)], f_s.at[p, 0], f_r.at[p, 2], near))

    def arrived(p):
        for xx in range(2):
            wait(jnp.logical_not(both(edge, x == xx)), out.at[p, :, pl.ds(2304 * xx, E)], f_r.at[p, xx])
        wait(edge, out.at[p, :, pl.ds(E, M)], f_r.at[p, 2])

    swaps = []

    def swap(ref, k):
        def make():
            return copy(ref.at[0], ref.at[1], pair_s.at[k], pair_r.at[k], near)

        make().start()
        swaps.append(make)

    def transpose_into(ref):
        for k in range(2):
            left[k] = ref[k].T

    def product(zz, ref, cols):
        return (dot(left[0, zrows(zz), :], ref[0, :, cols], NN) + dot(left[1, zrows(zz), :], ref[1, :, cols], NN)).astype(LOW)

    def grads(p, zz, ref):
        @pl.when(mid)
        def _():
            xb[p, zrows(zz), :] = product(zz, ref, pl.ds(ocol, E))

        push_x(p, zz)

        @pl.when(mid)
        def _():
            for k in range(2):
                acc[p, zrows(zz), pl.ds(k * E, E)] = product(zz, ref, pl.ds(E + k * E, E))

        push_y(mid, p, zz, M)

        @pl.when(edge)
        def _():
            acc[p, zrows(zz), pl.ds(0, E)] = product(zz, ref, pl.ds(ecol, E))

    def dup_copy(k):
        f = pl.ds(k * 768, 768)
        return copy(dupper.at[0, :, f], dupper.at[1, :, f], dup_s.at[k], dup_r.at[k], near)

    def upper_back(k):
        f = pl.ds(k * 768, 768)
        value = dot(dlow[0], down[:, f], NN) * slope[:, f]
        dbias[:, f] = jnp.sum(value, axis=0, keepdims=True)
        dupper[0, :, f] = value.astype(LOW)
        dup_copy(k).start()

    def hidden_back():
        @pl.loop(0, 3)
        def _(k):
            n = pl.ds(pl.multiple_of(k * 256, 256), 256)
            dhid[:, n] = dot(dupper[0], up[n, :], NT)

        value, dgain, dshift = norm_pull(dtwo[...] + dhid[...], normed[...], inverse[:, :1], vec[3:4, :])
        dpre[...] = value
        done[0] = value.astype(LOW)
        swap(done, 0)
        dvec[2:3, :] = jnp.sum(value, axis=0, keepdims=True)
        dvec[3:4, :] = dgain
        dvec[4:5, :] = dshift
        dmix[...] = dot(done[0], attn[:, pl.ds(3 * width, width)], NN).astype(LOW)

    def attend_back(step):
        s, j = step // 6, lax.rem(step, 6)
        cs = pl.ds(pl.multiple_of(j * 128, 128), 128)
        rs = pl.ds(pl.multiple_of(s * length, length), length)
        ms = pl.ds(pl.multiple_of(s * padded, padded), padded)
        lane = lax.broadcasted_iota(jnp.int32, (padded, 128), 1) < 64

        def halves(v):
            zero = jnp.zeros_like(v)
            return jnp.concatenate([jnp.where(lane, v, zero), jnp.where(lane, zero, v)], axis=0)

        key, value = kv[0, rs, cs], kv[1, rs, cs]
        queries, mixes = halves(query_m[ms, cs]), halves(dmix[ms, cs])
        score = dot(key, queries, NT)
        expo = jnp.exp(score - jnp.max(score, axis=0, keepdims=True))
        probs = expo / jnp.sum(expo, axis=0, keepdims=True)
        dprobs = dot(value, mixes, NT)
        dscore = (probs * (dprobs - jnp.sum(dprobs * probs, axis=0, keepdims=True))).astype(LOW)
        dkv[0, rs, cs] = dot(dscore, queries, NN).astype(LOW)
        dvalue = dot(probs.astype(LOW), mixes, NN)
        dkv[1, rs, cs] = dvalue.astype(LOW)
        dq = dot(dscore, key, TN) * 0.125
        dq = jnp.where(lane, dq[:padded], dq[padded:])
        dquery[0, ms, cs] = dq.astype(LOW)
        first = s == 0
        sums = jnp.concatenate([jnp.sum(dq, axis=0, keepdims=True), jnp.sum(dvalue, axis=0, keepdims=True)], axis=0)
        dvec[0:2, cs] = sums + jnp.where(first, 0.0, dvec[0:2, cs])

    def key_value_grads():
        for i in range(total // 256):
            r = pl.ds(i * 256, 256)
            tokens_t[:, r] = tokens[r, :].T

        def fill(store):
            @pl.loop(0, 8)
            def _(i):
                k = lax.rem(i, 2)
                n = pl.ds(pl.multiple_of(i // 2 * pair, pair), pair)
                store(n, pl.ds(pl.multiple_of(k * E, E), E), dot(tokens_t[n, :], dkv[k], NN).astype(LOW))

        @pl.when(mid)
        def _():
            def store(n, cols, value):
                acc[2, n, cols] = value

            fill(store)

        @pl.when(edge)
        def _():
            def store(n, cols, value):
                part[n, cols] = value

            fill(store)

        for zz in ORDER:
            sends.start(edge, lambda zz=zz: copy(part.at[zrows(zz)], part.at[zrows(zz)], sib_s.at[zz], sib_r.at[zz], near))

    def attention_sides():
        for k in range(2):
            left[k] = jnp.where(c == 0, rows_m[k], done[k]).T
            right[k] = jnp.where(c == 0, dquery[k], mixed_m[k])

    def attention_grads(zz):
        @pl.when(mid)
        def _():
            xb[2, zrows(zz), :] = product(zz, right, pl.ds(0, E))

        push_x(2, zz)

        @pl.when(mid)
        def _():
            wait(None, part.at[zrows(zz)], sib_r.at[zz])

            base = turn(zz) * pair

            def one(i):
                r = pl.ds(pl.multiple_of(base + i, SLAB), SLAB)
                acc[2, r, :] = (f32(acc[2, r, :]) + f32(part[r, :])).astype(LOW)

            slabs(pair, one)

        push_y(mid, 2, zz, M)

        @pl.when(edge)
        def _():
            acc[2, zrows(zz), pl.ds(0, E)] = product(zz, right, pl.ds(0, E))

    def tile_load(i):
        slot = lax.rem(i, 2)
        return pltpu.make_async_copy(hidden_h.at[pl.ds(pl.multiple_of(i * 256, 256), 256)], htile.at[slot], tile_sem.at[slot])

    def layer_store(i):
        slot = lax.rem(i, 2)
        return pltpu.make_async_copy(ltile.at[slot], layer_h.at[pl.ds(pl.multiple_of(i * 256, 256), 256)], out_sem.at[slot])

    def feed_forward(step):
        i, k = step // 4, lax.rem(step, 4)
        slot = lax.rem(i, 2)

        @pl.when(k == 0)
        def _():
            tile_load(i).wait()

            @pl.when(i + 1 < total // 256)
            def _():
                tile_load(i + 1).start()

        f = pl.ds(pl.multiple_of(k * 768, 768), 768)
        u = dot(htile[slot].astype(LOW), up[:, f], NN) + bias[:, f]
        a = (u * (0.5 * (1.0 + lax.erf(u * SQRT_HALF)))).astype(LOW)
        ytile[...] = dot(a, down[:, f], NT) + jnp.where(k == 0, htile[slot] + vec[5:6, :], ytile[...])

        @pl.when(k == 3)
        def _():
            @pl.when(i >= 2)
            def _():
                layer_store(i - 2).wait()

            ltile[slot] = norm(ytile[...], vec[6:7, :], vec[7:8, :])[0].astype(LOW)
            layer_store(i).start()

    def token_store(i):
        slot = lax.rem(i, 2)
        return pltpu.make_async_copy(htile.at[slot], dtokens_h.at[pl.ds(pl.multiple_of(i * 256, 256), 256)], out_sem.at[2 + slot])

    def masked_tokens():
        dpre[...] = dpre[...] + dot(dquery[0], attn[:, pl.ds(0, width)], NT)

    def tokens_back(i):
        slot = lax.rem(i, 2)

        @pl.when(i >= 2)
        def _():
            token_store(i - 2).wait()

        r = pl.ds(pl.multiple_of(i * 256, 256), 256)
        s = i // (length // 256)
        pick = pick_t[s, pl.ds(pl.multiple_of(lax.rem(i, length // 256) * 256, 256), 256), :]
        value = dpre[pl.ds(pl.multiple_of(s * padded, padded), padded), :]
        high = value.astype(LOW)
        rest = (value - f32(high)).astype(LOW)
        htile[slot] = (
            dot(dkv[0, r, :], attn[:, pl.ds(width, width)], NT) + dot(dkv[1, r, :], attn[:, pl.ds(2 * width, width)], NT) + (dot(pick, high, NN) + dot(pick, rest, NN))
        )
        token_store(i).start()

    def small_start():
        for w in range(8):
            sall[w] = jnp.zeros((16, 128), jnp.float32)
            turned = dvec[...] if w == 0 else pltpu.roll(dvec[...], width - rows * w, 1)
            lane = lax.broadcasted_iota(jnp.int32, (8, 128), 1)
            sall[w, 0:8, :] = jnp.where(lane < rows, turned[:, :128], 0.0)
            for r in range(3):
                sall[w, 8 + r : 9 + r, :] = dbias[:, pl.ds(w * 384 + r * 128, 128)]
        sends.start(None, lambda: copy(sall, ssib, sm_s.at[0], sm_r.at[0], near))

    def small_x():
        wait(None, ssib, sm_r.at[0])
        ssib[...] = sall[...] + ssib[...]
        sends.start(None, lambda: copy(ssib, sx, sm_s.at[1], sm_r.at[1], over))

    w = z * 2 + y

    def peer(k):
        return lax.rem(w + k, 8)

    def small_y():
        wait(None, sx, sm_r.at[1])
        sall2[...] = ssib[...] + sx[...]
        for k in range(1, 8):
            sends.start(None, lambda k=k: copy(sall2.at[peer(k)], sy.at[w], sm_s.at[1 + k], sy_r.at[w], (peer(k), x * 2 + c)))
        sy[w] = sall2[w]

    def small_add():
        for k in range(1, 8):
            wait(None, sy.at[peer(k)], sy_r.at[peer(k)])
        value = sy[0]
        for k in range(1, 8):
            value = value + sy[k]
        small_out[...] = value

    def square_sum():
        value = small_out[...]
        squares = value * value
        for p in range(3):
            def body(i, sums):
                v = f32(out[p, pl.ds(pl.multiple_of(i * 16, 16), 16), :])
                v = v * v
                for k in range(v.shape[1] // 128):
                    sums = sums + v[:, k * 128 : (k + 1) * 128]
                return sums

            squares = lax.fori_loop(0, rows // 16, body, squares)
        norms[w] = jnp.full((8, 128), jnp.sum(squares), jnp.float32)
        for k in range(1, 8):
            sends.start(None, lambda k=k: copy(norms.at[w], norms.at[w], n_s.at[k], n_r.at[w], (peer(k), x * 2 + c)))
        for k in range(1, 8):
            wait(None, norms.at[peer(k)], n_r.at[peer(k)])
        whole = norms[0]
        for k in range(1, 8):
            whole = whole + norms[k]
        norm_out[...] = jnp.sqrt(whole)

    moves = {
        "add_x": add_x, "add_y": add_y, "line": line, "owner": owner, "middle_x": middle_x, "arrived": arrived,
        "grads": lambda p, zz: grads(p, zz, dupper), "attention_grads": lambda zz: attention_grads(zz),
    }
    small_moves = {("add_y", 1, 0): small_y, ("owner", 1): small_add}

    def run(steps):
        for name, *rest in steps:
            moves[name](*rest)
            small_moves.get((name, *rest), lambda: None)()

    def looped(n, body, table):
        @pl.loop(0, n)
        def _(i):
            body(i)
            for k in sorted(table):
                pl.when(i == k)(lambda k=k: run(table[k]))

    bar = pltpu.get_barrier_semaphore()
    for to in [near, over, diag] + [(peer(k), x * 2 + c) for k in range(1, 8)]:
        pl.semaphore_signal(bar, inc=1, device_id=to, device_id_type=MESH)
    pl.semaphore_wait(bar, 10)

    need(L_DLOW, L_ACT)
    transpose_into(dlow)
    for zz in ORDER:
        grads(0, zz, act_m)
    need(L_DOWN, L_SLOPE)
    for k in range(4):
        upper_back(k)
    need(L_HID)
    transpose_into(hid_m)
    need(L_UP, L_DTWO, L_NORMED, L_INV, L_ATTN, L_DVEC)
    hidden_back()
    for k in range(4):
        dup_copy(k).wait_recv()
    need(L_QUERY, L_KV)
    looped(seqs * 6, attend_back, BESIDE_ATTENTION)
    swap(dquery, 1)
    small_start()
    need(L_TOKENS, L_ROWS, L_MIXED, L_PICK)
    key_value_grads()
    small_x()
    run(BESIDE_KEYS)
    for make in swaps:
        make().wait_recv()
    attention_sides()
    masked_tokens()
    tile = total // 256
    looped(tile, tokens_back, BESIDE_TOKENS)
    for i in range(tile - 2, tile):
        token_store(i).wait()
    tile_load(0).start()
    looped(tile * 4, feed_forward, BESIDE_FEED_FORWARD)
    run(LAST)
    for i in range(tile - 2, tile):
        layer_store(i).wait()
    square_sum()
    sends.finish()
    for make in swaps:
        make().wait_send()
    for k in range(4):
        dup_copy(k).wait_send()


def backward(attn, up, down, vec, bias, kv, hidden, query_m, rows_m, mixed_m, hid_m, act_m, slope, dtwo, dlow, normed, inverse, dvec, pick_t, tokens):
    total, width = hidden.shape
    cols = up.shape[1]
    rows = width // 8
    seqs, length, padded = pick_t.shape
    count = seqs * padded
    shape = jax.ShapeDtypeStruct
    f = jnp.float32
    anywhere = pl.BlockSpec(memory_space=pl.ANY)
    vm = pl.BlockSpec(memory_space=pltpu.VMEM)
    dma = pltpu.SemaphoreType.DMA
    v = pltpu.VMEM
    inputs = (attn, up, down, vec, bias, kv, hidden, query_m, rows_m, mixed_m, hid_m, act_m, slope, dtwo, dlow, normed, inverse, dvec, pick_t, tokens)

    def like(a):
        return v(a.shape, a.dtype)

    one = (16, 128)
    scratch = [like(a) for a in (attn, up, down, kv, query_m, rows_m, mixed_m, hid_m, act_m, slope, dtwo, dlow, normed, inverse, dvec, pick_t, tokens)]
    scratch += [
        v((2, width, count), LOW), v((2, count, width), LOW), v((2, count, cols), LOW), v((1, cols), f), v((count, width), f), v((count, width), f),
        v((2, count, width), LOW), v((count, width), LOW), v((2, count, width), LOW), v((2, total, width), LOW), v((width, M), LOW), v((width, total), LOW),
        v((2, 256, width), f), v((256, width), f), v((2, 256, width), LOW),
        v((3, width, M), LOW), v((3, width, E), LOW), v((3, 4, rows, M), LOW), v((3, 5, rows, M), LOW), v((3, rows, M), LOW),
        v((8,) + one, f), v((8,) + one, f), v((8,) + one, f), v((8,) + one, f), v((8,) + one, f), v((8, 8, 128), f),
        dma((17,)), dma((2,)), dma((4,)), dma((2,)), dma((2,)), dma((4,)), dma((4,)), dma((4,)), dma((4,)), dma((3, 4)), dma((3, 4)), dma((3, 4)), dma((3, 4)),
        dma((2, 3, 4)), dma((2, 3, 4)), dma((3,)), dma((3,)), dma((3, 3)), dma((3, 3)), dma((9,)), dma((2,)), dma((8,)), dma((8,)), dma((8,)),
    ]
    specs = [anywhere] * len(inputs)
    specs[3] = specs[4] = vm
    return pl.pallas_call(
        functools.partial(backward_kernel, rows, seqs, length, padded),
        out_shape=(shape((total, width), LOW), shape((total, width), f), shape((3, rows, cols), LOW), shape(one, f), shape((8, 128), f)),
        in_specs=specs,
        out_specs=(anywhere, anywhere, vm, vm, vm),
        scratch_shapes=scratch,
        compiler_params=pltpu.CompilerParams(collective_id=1, has_side_effects=True, vmem_limit_bytes=64 * 2**20 - 2**16),
    )(*inputs)


def adam_kernel(layer, dtokens, norm, own, small, *refs):
    weights, firsts, seconds = refs[0:6], refs[6:12], refs[12:18]
    outs = refs[18:36]
    layer_o, dtokens_o, norm_o, layer_v, dtokens_v, sem = refs[36:]
    step_id = pl.program_id(0)
    copies_in = [pltpu.make_async_copy(layer, layer_v, sem.at[0]), pltpu.make_async_copy(dtokens, dtokens_v, sem.at[1])]
    copies_out = [pltpu.make_async_copy(layer_v, layer_o, sem.at[2]), pltpu.make_async_copy(dtokens_v, dtokens_o, sem.at[3])]

    @pl.when(step_id == 0)
    def _():
        for copy in copies_in:
            copy.start()
        norm_o[0, 0] = jnp.max(norm[...])

    @pl.when(step_id == 2)
    def _():
        for first, then in zip(copies_in, copies_out):
            first.wait()
            then.start()

    factor = CLIP_LIMIT / jnp.maximum(norm[0:1, 0:1], CLIP_LIMIT)

    def step(k, where, grad, decay, rate):
        grad = grad * factor.reshape((1,) * grad.ndim)
        weight = weights[k][where]
        first = BETA_ONE * firsts[k][where] + (1.0 - BETA_ONE) * grad
        second = BETA_TWO * seconds[k][where] + (1.0 - BETA_TWO) * grad * grad
        mean_hat = first * (1.0 / (1.0 - BETA_ONE**STEP))
        square_hat = second * (1.0 / (1.0 - BETA_TWO**STEP))
        outs[3 * k][where] = weight - rate * (mean_hat / (jnp.sqrt(square_hat) + ADAM_EPS) + decay * weight)
        outs[3 * k + 1][where] = first
        outs[3 * k + 2][where] = second

    width = weights[1].shape[1]
    for k in range(3):
        step(0, (k,), f32(own[2, :, pl.ds(k * width, width)]), DECAY_RATE, LEARN_RATE)
    everything = (slice(None), slice(None))
    step(1, everything, f32(own[2, :, pl.ds(3 * width, width)]), DECAY_RATE, OUTPUT_RATE)
    for k in range(4):
        cols = (slice(None), pl.ds(k * width, width))
        step(2, cols, f32(own[1, :, pl.ds(k * width, width)]), DECAY_RATE, LEARN_RATE)
        step(3, cols, f32(own[0, :, pl.ds(k * width, width)]), DECAY_RATE, LEARN_RATE)

    @pl.when(step_id == pl.num_programs(0) - 1)
    def _():
        for copy in copies_out:
            copy.wait()

    @pl.when(step_id == 0)
    def _():
        lanes = weights[4].shape[1]
        step(4, everything, small[0:8, 0:lanes], 0.0, VECTOR_RATE)
        step(5, everything, small[8:11, :], 0.0, BIAS_RATE)


def adam(layer, dtokens, norm, own, small, weights, moments):
    def turn(values):
        a, b, c, d, e, g = values
        return a, b.T, c, d.T, e, g.reshape(3, 128)

    arrays = turn(weights) + turn([m[0] for m in moments]) + turn([m[1] for m in moments])
    rows, cols = arrays[2].shape
    width = cols // 4
    slab = 16
    anywhere = pl.BlockSpec(memory_space=pl.ANY)
    specs = [
        pl.BlockSpec((3, slab, width), lambda i: (0, i, 0)),
        pl.BlockSpec((slab, width), lambda i: (i, 0)),
        pl.BlockSpec((slab, cols), lambda i: (i, 0)),
        pl.BlockSpec((slab, cols), lambda i: (i, 0)),
        pl.BlockSpec(arrays[4].shape, lambda i: (0, 0)),
        pl.BlockSpec(arrays[5].shape, lambda i: (0, 0)),
    ]
    outs = pl.pallas_call(
        adam_kernel,
        grid=(rows // slab,),
        out_shape=tuple(jax.ShapeDtypeStruct(a.shape, a.dtype) for a in arrays[:6] for _ in range(3))
        + (jax.ShapeDtypeStruct(layer.shape, layer.dtype), jax.ShapeDtypeStruct(dtokens.shape, dtokens.dtype), jax.ShapeDtypeStruct((1, 1), jnp.float32)),
        in_specs=[
            anywhere,
            anywhere,
            pl.BlockSpec(norm.shape, lambda i: (0, 0)),
            pl.BlockSpec((3, slab, cols), lambda i: (0, i, 0)),
            pl.BlockSpec(small.shape, lambda i: (0, 0)),
        ] + specs * 3,
        out_specs=tuple(s for s in specs for _ in range(3)) + (anywhere, anywhere, pl.BlockSpec(memory_space=pltpu.SMEM)),
        scratch_shapes=[pltpu.VMEM(layer.shape, layer.dtype), pltpu.VMEM(dtokens.shape, dtokens.dtype), pltpu.SemaphoreType.DMA((4,))],
        compiler_params=pltpu.CompilerParams(vmem_limit_bytes=64 * 2**20 - 2**16),
    )(layer, dtokens, norm, own, small, *arrays)

    def back(k, v):
        return v.T if k in (1, 3) else v.reshape(-1) if k == 5 else v

    return (outs[18], outs[19], outs[20].reshape(())) + tuple(back(i // 3, v) for i, v in enumerate(outs[:18]))


def masks(mask_place, mask_count, gradient, length):
    seqs, slots = mask_place.shape
    padded = -(-slots // 16) * 16
    live = jnp.arange(padded)[None, :] < mask_count[:, None]
    spots = jnp.pad(mask_place, ((0, 0), (0, padded - slots)), constant_values=-1)
    pick = (spots[:, :, None] == jnp.arange(length)[None, None, :]) & live[:, :, None]
    gradient = jnp.pad(gradient, ((0, 0), (0, padded - slots), (0, 0)))
    gradient = jnp.where(live[:, :, None], gradient, jnp.zeros_like(gradient))
    return pick, gradient.reshape(seqs * padded, -1)


def update(weights, moments, grads, grad_norm):
    factor = CLIP_LIMIT / jnp.maximum(grad_norm, CLIP_LIMIT)
    rates = (LEARN_RATE, OUTPUT_RATE, LEARN_RATE, LEARN_RATE, VECTOR_RATE, BIAS_RATE)
    out = ()
    for k in range(6):
        out += adam_step(weights[k], *moments[k], grads[k], factor, DECAY_RATE if k < 4 else 0.0, rates[k])
    return out


def natural(own_attn, own_up, own_down, own_vectors, own_bias):
    width = own_up.shape[1] // 4
    own_qkv = jnp.swapaxes(own_attn[:, : 3 * width].reshape(-1, 3, width), 0, 1)
    return own_qkv, own_attn[:, 3 * width :].T, own_up, own_down.T, own_vectors, own_bias


def pack(qkv, out, up, down):
    attn = jnp.concatenate([qkv[0], qkv[1], qkv[2], out.T], axis=1)
    return attn.astype(jnp.bfloat16), up.astype(jnp.bfloat16), down.T.astype(jnp.bfloat16)


def plain(tokens, mask_place, mask_count, gradient, weights, moments):
    low = jnp.bfloat16
    seqs, length, width = tokens.shape
    pick, gradient = masks(mask_place, mask_count, gradient, length)
    padded = pick.shape[1]
    flat = tokens.reshape(seqs * length, width)
    attn_w, up_w, down_w = (lax.all_gather(v, "wide", axis=0, tiled=True) for v in pack(*weights[:4]))
    vec = lax.all_gather(weights[4].astype(low), "wide", axis=1, tiled=True).astype(jnp.float32)
    bias = lax.all_gather(weights[5].astype(low), "wide", axis=0, tiled=True).astype(jnp.float32)
    wq, wk, wv, wo = (attn_w[:, k * width : (k + 1) * width] for k in range(4))
    query = (mm(flat, wq, NN) + vec[0]).astype(low)
    key = mm(flat, wk, NN, low)
    value = (mm(flat, wv, NN) + vec[1]).astype(low)
    query, key, value = (split_heads(v, seqs, length) for v in (query, key, value))
    mixed = lax.map(attend, (query, key, value)).reshape(seqs * length, width)

    def middle(rows, mixed):
        pre_one = rows.astype(jnp.float32) + (mm(mixed, wo, NT) + vec[2])
        hidden, normed, inverse = layer_norm(pre_one, vec[3], vec[4])
        hidden_low = hidden.astype(low)
        upper = mm(hidden_low, up_w, NN) + bias
        cumul = 0.5 * (1.0 + lax.erf(upper * SQRT_HALF))
        active = (upper * cumul).astype(low)
        pre_two = hidden + (mm(active, down_w, NT) + vec[5])
        return layer_norm(pre_two, vec[6], vec[7]), normed, inverse, hidden_low, upper, cumul, active

    layer_out = middle(flat, mixed)[0][0].astype(low)
    pick_low = pick.astype(low)

    def take(values):
        values = values.reshape(seqs, length, width)
        return jnp.einsum("sil,sld->sid", pick_low, values, preferred_element_type=jnp.float32).astype(low)

    rows_m = take(flat).reshape(seqs * padded, width)
    mixed_m = take(mixed).reshape(seqs * padded, width)
    query_m = split_heads(take(query), seqs, padded)
    (_, normed_two, inverse_two), normed_one, inverse_one, hidden_m, upper, cumul, active = middle(rows_m, mixed_m)
    dpre_two, dgain_two, dshift_two = norm_back(gradient.astype(jnp.float32), normed_two, inverse_two, vec[6])
    dbias_two = jnp.sum(dpre_two, axis=0)
    dtwo_low = dpre_two.astype(low)
    ddown = mm(dtwo_low, active, TN)
    dactive = mm(dtwo_low, down_w, NN)
    density = jnp.exp(-0.5 * upper * upper) * INV_ROOT_TWO_PI
    dupper = dactive * (cumul + upper * density)
    dup_bias = jnp.sum(dupper, axis=0)
    dupper_low = dupper.astype(low)
    dup = mm(hidden_m, dupper_low, TN)
    dhidden = dpre_two + mm(dupper_low, up_w, NT)
    dpre_one, dgain_one, dshift_one = norm_back(dhidden, normed_one, inverse_one, vec[3])
    dbias_out = jnp.sum(dpre_one, axis=0)
    done_low = dpre_one.astype(low)
    dout = mm(done_low, mixed_m, TN)
    dmixed = split_heads(mm(done_low, wo, NN, low), seqs, padded)
    dquery, dkey, dvalue = lax.map(attend_back, (query_m, key, value, dmixed))
    dquery = dquery.reshape(seqs * padded, width)
    dkey = dkey.reshape(seqs * length, width)
    dvalue = dvalue.reshape(seqs * length, width)
    dbias_query = jnp.sum(dquery, axis=0)
    dbias_value = jnp.sum(dvalue, axis=0)
    dquery, dkey, dvalue = dquery.astype(low), dkey.astype(low), dvalue.astype(low)
    dattn = jnp.concatenate([mm(rows_m, dquery, TN), mm(flat, dkey, TN), mm(flat, dvalue, TN), dout], axis=1)
    masked_part = dpre_one + mm(dquery, wq, NT)
    dtokens = spread(pick, masked_part) + mm(dkey, wk, NT) + mm(dvalue, wv, NT)
    dvectors = jnp.stack(
        [dbias_query, dbias_value, dbias_out, dgain_one, dshift_one, dbias_two, dgain_two, dshift_two]
    )

    def owned(value, dim):
        return lax.psum(lax.psum_scatter(value, "wide", scatter_dimension=dim, tiled=True), "narrow")

    grads = (owned(dattn, 0), owned(dup, 0), owned(ddown, 0), owned(dvectors, 1), owned(dup_bias, 0))
    grad_norm = jnp.sqrt(lax.psum(sum(jnp.sum(v * v) for v in grads), "wide"))
    return (layer_out, dtokens, grad_norm) + update(weights, moments, natural(*grads), grad_norm)


def spread(pick, rows):
    seqs, padded, length = pick.shape
    return jnp.einsum(
        "sil,sid->sld",
        pick.astype(jnp.float32),
        rows.reshape(seqs, padded, -1),
        precision=lax.Precision.HIGHEST,
        preferred_element_type=jnp.float32,
    ).reshape(seqs * length, -1)


def tailored(tokens, mask_place, mask_count, gradient, weights, moments):
    seqs, length, width = tokens.shape
    flat = tokens.reshape(seqs * length, width)
    saved = forward(*weights, flat, mask_place, mask_count, gradient)
    layer_out, dtokens, own, small, grad_norm = backward(*saved, flat)
    return adam(layer_out, dtokens, grad_norm, own, small, weights, moments)


def shards(body, tokens, mask_place, mask_count, masked_output_gradient, *parameters):
    seqs, length, width = tokens.shape
    weights = parameters[0::3]
    moments = tuple(zip(parameters[1::3], parameters[2::3]))
    layer_out, dtokens, *rest = body(tokens, mask_place, mask_count, masked_output_gradient, weights, moments)
    return (layer_out.reshape(seqs, length, width), dtokens.reshape(seqs, length, width), *rest)


def solution(mesh):
    body = tailored if mesh.shape["wide"] == 8 and mesh.shape["narrow"] == 4 else plain
    data = P(("wide", "narrow"))
    rows = P("wide")
    columns = P(None, "wide")
    weights = (columns,) * 6 + (rows,) * 3 + (columns,) * 6 + (rows,) * 3
    return jax.shard_map(
        functools.partial(shards, body),
        mesh=mesh,
        in_specs=(data,) * 4 + weights,
        out_specs=(data, data, P()) + weights,
        check_vma=False,
    )
```

```python
import functools

import jax
import jax.numpy as jnp
from jax import lax
from jax.experimental import pallas as pl
from jax.experimental.pallas import tpu as pltpu
from jax.sharding import PartitionSpec as P

HEADS = 12
HEAD_DIM = 64
STEP = 10

LN_EPS = 1e-06
SQRT_HALF = 0.7071067811865476
INV_ROOT_TWO_PI = 0.3989422804014327
CLIP_LIMIT = 1.0
BETA_ONE = 0.9
BETA_TWO = 0.999
LEARN_RATE = 0.05
OUTPUT_RATE = 0.2
VECTOR_RATE = 0.5
BIAS_RATE = 0.3
DECAY_RATE = 0.01
ADAM_EPS = 1e-08

MESH = pl.DeviceIdType.MESH


def when(cond, body):
    if callable(cond):
        cond = cond()
    if cond is None:
        body()
    else:
        pl.when(cond)(body)


class Sends:
    def __init__(self):
        self.started = []

    def start(self, cond, make):
        when(cond, lambda: make().start())
        self.started.append((cond, make))

    def finish(self):
        for cond, make in self.started:
            when(cond, lambda make=make: make().wait_send())


def both(a, b):
    return b if a is None else (a if b is None else jnp.logical_and(a, b))


def place():
    w, n = lax.axis_index("wide"), lax.axis_index("narrow")
    return w // 2, lax.rem(w, 2), n // 2, lax.rem(n, 2)


def flip(v):
    return 1 - v


def dev(z, y, x, c):
    return (z * 2 + y, x * 2 + c)


def meet(z, y, x, c, diagonal):
    bar = pltpu.get_barrier_semaphore()
    peers = [(None, dev(z, flip(y), x, c)), (None, dev(z, y, flip(x), c)), (None, dev(z, y, x, flip(c)))]
    if diagonal:
        peers.append((None, dev(z, y, flip(x), flip(c))))
    peers += [(z > 0, dev(z - 1, y, x, c)), (z < 3, dev(z + 1, y, x, c))]
    for cond, peer in peers:
        when(cond, lambda peer=peer: pl.semaphore_signal(bar, inc=1, device_id=peer, device_id_type=MESH))
    inner = jnp.logical_and(z > 0, z < 3)
    count = 4 if diagonal else 3
    pl.semaphore_wait(bar, count + 1 + jnp.where(inner, 1, 0))


def gather_kernel(rows, cols, attn, up, down, small, attn_full, up_full, down_full, small_full, send_sem, recv_sem, small_send, small_recv, own_sem):
    z, y, x, c = place()
    edge = x == c
    third = cols // 3
    mine, across = x + c, 2 * flip(x)
    fulls = (attn_full, up_full, down_full)
    shards = (attn, up, down)
    sends = Sends()
    zl, zh = z > 0, z < 3

    def spot(p, zz, yy, t):
        return fulls[p].at[pl.ds(pl.multiple_of((zz * 2 + yy) * rows, rows), rows), pl.ds(pl.multiple_of(t * third, third), third)]

    def push(cond, p, zz, yy, t, kind, to, src=None):
        def make():
            w = zz * 2 + yy
            where = spot(p, zz, yy, t)
            return pltpu.make_async_remote_copy(
                src_ref=where if src is None else src,
                dst_ref=where,
                send_sem=send_sem.at[kind, p, w],
                recv_sem=recv_sem.at[p, w, t],
                device_id=to,
                device_id_type=MESH,
            )

        sends.start(cond, make)

    def small_push(cond, zz, yy, kind, to, src=None):
        def make():
            w = zz * 2 + yy
            where = small_full.at[w]
            return pltpu.make_async_remote_copy(
                src_ref=where if src is None else src,
                dst_ref=where,
                send_sem=small_send.at[kind, w],
                recv_sem=small_recv.at[w],
                device_id=to,
                device_id_type=MESH,
            )

        sends.start(cond, make)

    def arrive(cond, p, zz, yy, t):
        def body():
            where = spot(p, zz, yy, t)
            w = zz * 2 + yy
            pltpu.make_async_remote_copy(where, where, send_sem.at[0, p, w], recv_sem.at[p, w, t], dev(z, y, x, c), device_id_type=MESH).wait_recv()

        when(cond, body)

    def small_arrive(cond, zz, yy):
        def body():
            w = zz * 2 + yy
            pltpu.make_async_remote_copy(small_full.at[w], small_full.at[w], small_send.at[0, w], small_recv.at[w], dev(z, y, x, c), device_id_type=MESH).wait_recv()

        when(cond, body)

    UP, DOWN, SIDE, OVER, NEAR, PASS = range(6)
    above, below, beside = dev(z + 1, y, x, c), dev(z - 1, y, x, c), dev(z, flip(y), x, c)
    over, near = dev(z, y, flip(x), c), dev(z, y, x, flip(c))

    def own(p):
        src = shards[p].at[:, pl.ds(pl.multiple_of(mine * third, third), third)]
        push(zh, p, z, y, mine, UP, above, src)
        push(zl, p, z, y, mine, DOWN, below, src)
        push(None, p, z, y, mine, SIDE, beside, src)

    def z_step(p, d):
        for cond, zz, onward, kind, to in ((z - d >= 0, z - d, zh, UP, above), (z + d <= 3, z + d, zl, DOWN, below)):
            arrive(cond, p, zz, y, mine)
            push(both(cond, onward), p, zz, y, mine, kind, to)
            push(cond, p, zz, y, mine, SIDE, beside)
            push(both(cond, edge), p, zz, y, mine, OVER, over)
            push(cond, p, zz, y, mine, NEAR, near)

    def y_step(p, d):
        steps = ((None, z),) if d == 0 else ((z - d >= 0, z - d), (z + d <= 3, z + d))
        for cond, zz in steps:
            arrive(cond, p, zz, flip(y), mine)
            push(both(cond, edge), p, zz, flip(y), mine, OVER, over)
            push(cond, p, zz, flip(y), mine, NEAR, near)

    def x_step(p, d):
        mid = jnp.logical_not(edge)
        for yy in (y, flip(y)):
            if d == 0:
                steps = () if yy is y else ((None, z),)
            else:
                steps = ((z - d >= 0, z - d), (z + d <= 3, z + d))
            for cond, zz in steps:
                cond = both(cond, mid)
                arrive(cond, p, zz, yy, across)
                push(cond, p, zz, yy, across, PASS, near)

    def last(p, d):
        for yy in (y, flip(y)):
            if d == 0:
                steps = () if yy is y else ((None, z),)
            else:
                steps = ((z - d >= 0, z - d), (z + d <= 3, z + d))
            for cond, zz in steps:
                arrive(cond, p, zz, yy, x + flip(c))
                arrive(both(cond, edge), p, zz, yy, across)

    def small_z(d):
        for cond, zz, onward, kind, to in ((z - d >= 0, z - d, zh, UP, above), (z + d <= 3, z + d, zl, DOWN, below)):
            small_arrive(cond, zz, y)
            small_push(both(cond, onward), zz, y, kind, to)
            small_push(cond, zz, y, SIDE, beside)

    meet(z, y, x, c, False)
    small_push(zh, z, y, UP, above, small)
    small_push(zl, z, y, DOWN, below, small)
    small_push(None, z, y, SIDE, beside, small)
    own(0)
    w = z * 2 + y
    copies = []
    for p in range(3):
        copies.append(pltpu.make_async_copy(shards[p], fulls[p].at[pl.ds(pl.multiple_of(w * rows, rows), rows)], own_sem.at[p]))
    copies.append(pltpu.make_async_copy(small, small_full.at[w], own_sem.at[3]))
    for copy in copies:
        copy.start()
    for d in range(1, 4):
        small_z(d)
    order = [
        lambda: z_step(0, 1), lambda: own(1), lambda: y_step(0, 0), lambda: z_step(0, 2), lambda: y_step(0, 1), lambda: x_step(0, 0), lambda: z_step(0, 3),
        lambda: y_step(0, 2), lambda: x_step(0, 1), lambda: z_step(1, 1), lambda: own(2), lambda: y_step(0, 3), lambda: x_step(0, 2), lambda: z_step(1, 2), lambda: y_step(1, 0), lambda: x_step(0, 3), lambda: z_step(1, 3),
        lambda: y_step(1, 1), lambda: x_step(1, 0), lambda: z_step(2, 1), lambda: y_step(1, 2), lambda: x_step(1, 1), lambda: z_step(2, 2), lambda: y_step(1, 3), lambda: x_step(1, 2), lambda: z_step(2, 3),
        lambda: y_step(2, 0), lambda: x_step(1, 3), lambda: y_step(2, 1), lambda: x_step(2, 0), lambda: y_step(2, 2), lambda: x_step(2, 1), lambda: y_step(2, 3), lambda: x_step(2, 2), lambda: x_step(2, 3),
    ]
    for step in order:
        step()
    for d in range(4):
        for cond, zz in (((None, z),) if d == 0 else ((z - d >= 0, z - d), (z + d <= 3, z + d))):
            small_arrive(cond, zz, flip(y))
    for p in range(3):
        for d in range(4):
            last(p, d)
    sends.finish()
    for copy in copies:
        copy.wait()


def gather(attn, up, down, small):
    rows, cols = attn.shape
    full = jax.ShapeDtypeStruct((8 * rows, cols), attn.dtype)
    anywhere = pl.BlockSpec(memory_space=pl.ANY)
    return pl.pallas_call(
        functools.partial(gather_kernel, rows, cols),
        out_shape=(full, full, full, jax.ShapeDtypeStruct((8,) + small.shape, small.dtype)),
        in_specs=[anywhere] * 4,
        out_specs=(anywhere,) * 4,
        scratch_shapes=[
            pltpu.SemaphoreType.DMA((6, 3, 8)),
            pltpu.SemaphoreType.DMA((3, 8, 3)),
            pltpu.SemaphoreType.DMA((3, 8)),
            pltpu.SemaphoreType.DMA((8,)),
            pltpu.SemaphoreType.DMA((4,)),
        ],
        compiler_params=pltpu.CompilerParams(collective_id=0, has_side_effects=True),
    )(attn, up, down, small)


def layer_norm(values, gain, shift):
    center = values - jnp.mean(values, axis=-1, keepdims=True)
    inverse = lax.rsqrt(jnp.mean(center * center, axis=-1, keepdims=True) + LN_EPS)
    normed = center * inverse
    return (normed * gain + shift, normed, inverse)


def norm_back(incoming, normed, inverse, gain):
    dgain = jnp.sum(incoming * normed, axis=0)
    dshift = jnp.sum(incoming, axis=0)
    scaled = incoming * gain
    dvalues = inverse * (
        scaled
        - jnp.mean(scaled, axis=-1, keepdims=True)
        - normed * jnp.mean(scaled * normed, axis=-1, keepdims=True)
    )
    return (dvalues, dgain, dshift)


def mm(a, b, dims, out=jnp.float32):
    return lax.dot_general(a, b, (dims, ((), ())), preferred_element_type=jnp.float32).astype(out)


NN = ((1,), (0,))
NT = ((1,), (1,))
TN = ((0,), (0,))


def split_heads(values, seqs, length):
    return values.reshape(seqs, length, HEADS, HEAD_DIM)


def attend(pieces):
    query, key, value = pieces
    raw = jnp.einsum("qhe,khe->hqk", query, key, preferred_element_type=jnp.float32) * HEAD_DIM ** (
        -0.5
    )
    peak = jnp.max(raw, axis=-1, keepdims=True)
    expo = jnp.exp(raw - peak)
    total = jnp.sum(expo, axis=-1, keepdims=True)
    probs = (expo / total).astype(jnp.bfloat16)
    mixed = jnp.einsum("hqk,khe->qhe", probs, value, preferred_element_type=jnp.float32)
    return mixed.astype(jnp.bfloat16)


def attend_back(pieces):
    query, key, value, dmixed = pieces
    scale = HEAD_DIM ** (-0.5)
    raw = jnp.einsum("qhe,khe->hqk", query, key, preferred_element_type=jnp.float32) * scale
    probs = jax.nn.softmax(raw, axis=-1)
    dprobs = jnp.einsum("qhe,khe->hqk", dmixed, value, preferred_element_type=jnp.float32)
    dscore = probs * (dprobs - jnp.sum(dprobs * probs, axis=-1, keepdims=True))
    dscore = (dscore * scale).astype(jnp.bfloat16)
    dquery = jnp.einsum("hqk,khe->qhe", dscore, key, preferred_element_type=jnp.float32)
    dkey = jnp.einsum("hqk,qhe->khe", dscore, query, preferred_element_type=jnp.float32)
    dvalue = jnp.einsum(
        "hqk,qhe->khe", probs.astype(jnp.bfloat16), dmixed, preferred_element_type=jnp.float32
    )
    return (dquery, dkey, dvalue)


def adam_step(weight, first, second, grad, factor, decay, rate):
    grad = grad * factor
    first_new = BETA_ONE * first + (1.0 - BETA_ONE) * grad
    second_new = BETA_TWO * second + (1.0 - BETA_TWO) * grad * grad
    mean_hat = first_new / (1.0 - BETA_ONE**STEP)
    square_hat = second_new / (1.0 - BETA_TWO**STEP)
    weight_new = weight - rate * (mean_hat / (jnp.sqrt(square_hat) + ADAM_EPS) + decay * weight)
    return (weight_new, first_new, second_new)


GATHER_ORDER = (
    ("z_step", 0, 1), ("y_step", 0, 0), ("z_step", 0, 2), ("y_step", 0, 1), ("z_step", 0, 3), ("own", 1),
    ("x_step", 0, 1), ("y_step", 0, 2), ("y_step", 0, 3), ("x_step", 0, 0), ("z_step", 1, 1), ("vectors_in",),
    ("x_step", 0, 2), ("x_step", 0, 3), ("y_step", 1, 0), ("z_step", 1, 2), ("last", 0), ("project", 0),
    ("project", 1), ("project", 2), ("own", 2), ("z_step", 1, 3), ("project", 3), ("x_step", 1, 0),
    ("attend", 0), ("y_step", 1, 1), ("attend", 1), ("attend", 2), ("z_step", 2, 1), ("attend", 3),
    ("y_step", 1, 2), ("attend", 4), ("attend", 5), ("attend", 6), ("x_step", 1, 1), ("y_step", 1, 3),
    ("attend", 7), ("z_step", 2, 2), ("y_step", 2, 0), ("attend", 8), ("attend", 9), ("attend", 10),
    ("x_step", 1, 2), ("attend", 11), ("x_step", 1, 3), ("z_step", 2, 3), ("middle", 0), ("middle", 1),
    ("y_step", 2, 1), ("middle", 2), ("middle", 3), ("masked",), ("x_step", 2, 1), ("x_step", 2, 0),
    ("y_step", 2, 2), ("save_hidden",), ("last", 1), ("upper", 0), ("y_step", 2, 3), ("upper", 1),
    ("x_step", 2, 2), ("upper", 2), ("x_step", 2, 3), ("upper", 3), ("last", 2),
)


def dot(a, b, dims):
    return lax.dot_general(a, b, (dims, ((), ())), preferred_element_type=jnp.float32)


NN = ((1,), (0,))
NT = ((1,), (1,))
TN = ((0,), (0,))
LOW = jnp.bfloat16


def norm(values, gain, shift):
    center = values - jnp.mean(values, axis=-1, keepdims=True)
    inverse = lax.rsqrt(jnp.mean(center * center, axis=-1, keepdims=True) + LN_EPS)
    normed = center * inverse
    return normed * gain + shift, normed, inverse


def norm_pull(incoming, normed, inverse, gain):
    dgain = jnp.sum(incoming * normed, axis=0, keepdims=True)
    dshift = jnp.sum(incoming, axis=0, keepdims=True)
    scaled = incoming * gain
    return (
        inverse * (scaled - jnp.mean(scaled, axis=-1, keepdims=True) - normed * jnp.mean(scaled * normed, axis=-1, keepdims=True)),
        dgain,
        dshift,
    )


def forward_part(
    rows, seqs, length, padded, sends,
    qkv_h, out_h, up_h, down_h, vectors, up_bias, tokens_h, place_m, count_m, grad_m, hidden_o,
    attn_full, up_full, down_full, small_full, small_f, tokens, pick_t, kv, vec, qbias, bias,
    query_m, rows_m, mixed_m, hid_m, act_m, slope, dtwo, dlow, dvec, normed_one, inverse_one,
    send_sem, recv_sem, small_send, small_recv, load_sem, save_sem, pair_send, pair_recv,
):
    qkv_f = out_f = up_f = down_f = queries = mixed = hidden = pick = ytwo = hid_f = grad = None
    z, y, x, c = place()
    width = tokens.shape[1]
    total = tokens.shape[0]
    cols = up_h.shape[1]
    edge = x == c
    third = cols // 3
    mine, across = x + c, 2 * flip(x)
    fulls = (attn_full, up_full, down_full)
    w = z * 2 + y
    mine_rows = pl.ds(pl.multiple_of(w * rows, 32), rows)
    zl, zh = z > 0, z < 3
    count = seqs * padded

    def spot(p, zz, yy, t):
        return fulls[p].at[pl.ds(pl.multiple_of((zz * 2 + yy) * rows, rows), rows), pl.ds(pl.multiple_of(t * third, third), third)]

    def push(cond, p, zz, yy, t, kind, to):
        def make():
            whose = zz * 2 + yy
            where = spot(p, zz, yy, t)
            return pltpu.make_async_remote_copy(
                src_ref=where,
                dst_ref=where,
                send_sem=send_sem.at[kind, p, whose],
                recv_sem=recv_sem.at[p, whose, t],
                device_id=to,
                device_id_type=MESH,
            )

        sends.start(cond, make)

    def arrive(cond, p, zz, yy, t):
        def body():
            where = spot(p, zz, yy, t)
            whose = zz * 2 + yy
            pltpu.make_async_remote_copy(where, where, send_sem.at[0, p, whose], recv_sem.at[p, whose, t], dev(z, y, x, c), device_id_type=MESH).wait_recv()

        when(cond, body)

    UP, DOWN, SIDE, OVER, NEAR, PASS = range(6)
    above, below, beside = dev(z + 1, y, x, c), dev(z - 1, y, x, c), dev(z, flip(y), x, c)
    over, near = dev(z, y, flip(x), c), dev(z, y, x, flip(c))

    other_y = flip(y)
    span = {d: ((z - d >= 0, z - d), (z + d <= 3, z + d)) for d in range(1, 4)}
    span[0] = ((None, z),)
    mid = jnp.logical_not(edge)

    def around(d):
        return span[d]

    def also(a, b):
        return lambda: both(a, b)

    def own(p):
        push(zh, p, z, y, mine, UP, above)
        push(zl, p, z, y, mine, DOWN, below)
        push(None, p, z, y, mine, SIDE, beside)

    def z_step(p, d):
        for (cond, zz), onward, kind, to in zip(span[d], (zh, zl), (UP, DOWN), (above, below)):
            arrive(cond, p, zz, y, mine)
            push(also(cond, onward), p, zz, y, mine, kind, to)
            push(cond, p, zz, y, mine, SIDE, beside)
            push(also(cond, edge), p, zz, y, mine, OVER, over)
            push(cond, p, zz, y, mine, NEAR, near)

    def y_step(p, d):
        for cond, zz in around(d):
            arrive(cond, p, zz, other_y, mine)
            push(also(cond, edge), p, zz, other_y, mine, OVER, over)
            push(cond, p, zz, other_y, mine, NEAR, near)

    def x_step(p, d):
        for yy in (y, other_y):
            for cond, zz in () if d == 0 and yy is y else around(d):
                arrive(also(cond, mid), p, zz, yy, across)
                push(also(cond, mid), p, zz, yy, across, PASS, near)

    def last(p):
        for d in range(4):
            for yy in (y, other_y):
                for cond, zz in () if d == 0 and yy is y else around(d):
                    arrive(cond, p, zz, yy, x + flip(c))
                    arrive(both(cond, edge), p, zz, yy, across)

    saves = []

    def keep(src, dst, k):
        copy = pltpu.make_async_copy(src, dst, save_sem.at[k])
        copy.start()
        saves.append(copy)

    swaps = []

    def swap(ref, k):
        def make():
            return pltpu.make_async_remote_copy(ref.at[0], ref.at[1], pair_send.at[k], pair_recv.at[k], near, device_id_type=MESH)

        sends.start(None, make)
        swaps.append(make)

    def peer(k):
        return lax.rem(w + k, 8)

    def small_copy(k, whose):
        return pltpu.make_async_remote_copy(
            small_full.at[whose], small_full.at[whose], small_send.at[k], small_recv.at[whose], (peer(k), x * 2 + c), device_id_type=MESH
        )

    def small_out():
        small_f[...] = jnp.zeros_like(small_f)
        small_f[0:8, 0:rows] = vectors[...]
        for r in range(3):
            small_f[8 + r : 9 + r, :] = up_bias[pl.ds(r * 128, 128)].reshape(1, 128)
        small_full[w] = small_f[...].astype(LOW)
        for k in range(1, 8):
            sends.start(None, lambda k=k: small_copy(k, w))

    def attn_shard():
        loads[1].wait()
        loads[2].wait()
        for k in range(3):
            attn_full[mine_rows, pl.ds(k * width, width)] = qkv_f[k].astype(LOW)
        attn_full[mine_rows, pl.ds(3 * width, width)] = out_f[...].astype(LOW)

    def up_shard():
        loads[3].wait()
        up_full[mine_rows, :] = up_f[...].astype(LOW)

    def down_shard():
        loads[4].wait()
        down_full[mine_rows, :] = down_f[...].astype(LOW)

    def masks():
        slots = place_m.shape[1]
        for s in range(seqs):
            hit = lax.broadcasted_iota(jnp.int32, (length, slots), 0) == place_m[s : s + 1, :]
            live = lax.broadcasted_iota(jnp.int32, (length, slots), 1) < count_m[s]
            hit = jnp.logical_and(hit, live).astype(jnp.float32).astype(LOW)
            row = lax.broadcasted_iota(jnp.int32, (padded, slots), 0)
            slot = lax.broadcasted_iota(jnp.int32, (padded, slots), 1)
            same = (row == slot).astype(jnp.float32).astype(LOW)
            kept = jnp.logical_and(row == slot, slot < count_m[s]).astype(jnp.float32).astype(LOW)
            pick[s] = dot(same, hit, NT).astype(LOW)
            pick_t[s] = dot(hit, same, NT).astype(LOW)
            grad[pl.ds(s * padded, padded), :] = dot(kept, f32(grad_m[...])[:, s, :].astype(LOW), NN)

    def vectors_in():
        loads[0].wait()
        for k in range(1, 8):
            small_copy(k, peer(k)).wait_recv()
        at = lax.broadcasted_iota(jnp.int32, (128, width), 0)
        to = lax.broadcasted_iota(jnp.int32, (128, width), 1)
        total = jnp.zeros((16, width), jnp.float32)
        for k in range(8):
            place_k = jnp.logical_and(at + k * rows == to, at < rows).astype(jnp.float32).astype(LOW)
            total += dot(small_full[k], place_k, NN)
            for r in range(3):
                bias[:, pl.ds(k * 384 + r * 128, 128)] = small_full[k, 8 + r : 9 + r, :].astype(jnp.float32)
        vec[...] = total[:8]
        qbias[0] = total[0:1]
        qbias[1] = jnp.zeros((1, width), jnp.float32)
        qbias[2] = total[1:2]

    def project(i):
        r = pl.ds(i * 256, 256)

        for k in range(3):
            value = dot(tokens[r, :], attn_full[:, pl.ds(k * width, width)], NN) + qbias[k]
            if k == 0:
                queries[r, :] = (value * 0.125).astype(LOW)
            else:
                kv[k - 1, r, :] = value.astype(LOW)

    def attend(s, j):
        lane = lax.broadcasted_iota(jnp.int32, (length, 128), 1) < 64
        cs = pl.ds(j * 128, 128)
        rs = pl.ds(s * length, length)
        key, value = kv[0, rs, cs], kv[1, rs, cs]
        zero, one = jnp.zeros_like(key), jnp.ones_like(key)
        keys = (jnp.where(lane, key, zero), jnp.where(lane, zero, key))
        values = (jnp.where(lane, value, one), jnp.where(lane, one, value))
        for q in range(length // 256):
            r = pl.ds(s * length + q * 256, 256)
            query = queries[r, cs]
            parts = []
            for h in range(2):
                score = dot(query, keys[h], NT)
                expo = jnp.exp(score - jnp.max(score, axis=-1, keepdims=True))
                parts.append(dot(expo.astype(LOW), values[h], NN))
            left = lane[:256]
            top = jnp.where(left, parts[0], parts[1])
            under = pltpu.roll(jnp.where(left, parts[1], parts[0]), 64, 1)
            mixed[r, cs] = (top / under).astype(LOW)

    def middle(i):
        r = pl.ds(i * 256, 256)
        pre = tokens[r, :].astype(jnp.float32) + (dot(mixed[r, :], attn_full[:, pl.ds(3 * width, width)], NT) + vec[2:3, :])
        hidden[r, :] = norm(pre, vec[3:4, :], vec[4:5, :])[0]

    def masked_rows():
        for s in range(seqs):
            r = pl.ds(s * padded, padded)
            rs = pl.ds(s * length, length)
            rows_m[0, r, :] = dot(pick[s], tokens[rs, :], NN).astype(LOW)
            mixed_m[0, r, :] = dot(pick[s], mixed[rs, :], NN).astype(LOW)
            query_m[r, :] = dot(pick[s], queries[rs, :], NN).astype(LOW)
        pre = rows_m[0].astype(jnp.float32) + (dot(mixed_m[0], attn_full[:, pl.ds(3 * width, width)], NT) + vec[2:3, :])
        value, normed, inverse = norm(pre, vec[3:4, :], vec[4:5, :])
        hid_f[...] = value
        hid_m[0] = value.astype(LOW)
        normed_one[...] = normed
        inverse_one[...] = jnp.broadcast_to(inverse, inverse_one.shape)
        swap(rows_m, 0)
        swap(mixed_m, 1)
        swap(hid_m, 2)

    def upper(k):
        f = pl.ds(k * 768, 768)
        u = dot(hid_m[0], up_full[:, f], NN) + bias[:, f]
        cumul = 0.5 * (1.0 + lax.erf(u * SQRT_HALF))
        act_m[0, :, f] = (u * cumul).astype(LOW)
        slope[:, f] = cumul + u * (jnp.exp(-0.5 * u * u) * INV_ROOT_TWO_PI)

    def after_upper():
        swap(act_m, 3)

    def lower():
        @pl.loop(0, 3)
        def _(k):
            n = pl.ds(pl.multiple_of(k * 256, 256), 256)
            ytwo[:, n] = dot(act_m[0], down_full[n, :], NT)

        pre = hid_f[...] + (ytwo[...] + vec[5:6, :])
        _, normed, inverse = norm(pre, vec[6:7, :], vec[7:8, :])
        value, dgain, dshift = norm_pull(grad[...], normed, inverse, vec[6:7, :])
        dtwo[...] = value
        dlow[0] = value.astype(LOW)
        dvec[...] = jnp.zeros_like(dvec)
        dvec[5:6, :] = jnp.sum(value, axis=0, keepdims=True)
        dvec[6:7, :] = dgain
        dvec[7:8, :] = dshift
        swap(dlow, 4)

    loads = [pltpu.make_async_copy(tokens_h, tokens, load_sem.at[4])]
    loads[0].start()

    def prepare(*refs):
        nonlocal qkv_f, out_f, up_f, down_f
        qkv_f, out_f, up_f, down_f = refs
        for k, src in enumerate((qkv_h, out_h, up_h, down_h)):
            loads.append(pltpu.make_async_copy(src, refs[k], load_sem.at[k]))
            loads[-1].start()
        bar = pltpu.get_barrier_semaphore()
        for to in [near, over, dev(z, y, flip(x), flip(c))] + [(peer(k), x * 2 + c) for k in range(1, 8)]:
            pl.semaphore_signal(bar, inc=1, device_id=to, device_id_type=MESH)
        attn_shard()
        pl.semaphore_wait(bar, 10)
        own(0)
        small_out()
        up_shard()
        down_shard()

    f = jnp.float32
    v = pltpu.VMEM
    pl.run_scoped(prepare, v(qkv_h.shape, f), v(out_h.shape, f), v(up_h.shape, f), v(down_h.shape, f))

    def save_hidden():
        keep(hidden, hidden_o, 0)

    steps = {
        "z_step": z_step, "y_step": y_step, "x_step": x_step, "own": own, "last": last, "vectors_in": vectors_in, "project": project,
        "attend": lambda i: attend(i // (width // 128), i % (width // 128)), "middle": middle, "masked": masked_rows, "save_hidden": save_hidden, "upper": upper,
    }

    def run(*refs):
        nonlocal queries, mixed, hidden, pick, ytwo, hid_f, grad
        queries, mixed, hidden, pick, ytwo, hid_f, grad = refs
        masks()
        for name, *rest in GATHER_ORDER:
            steps[name](*rest)
        after_upper()
        lower()
        for make in swaps:
            make().wait_recv()
        for copy in saves:
            copy.wait()

    pl.run_scoped(
        run, v((total, width), LOW), v((total, width), LOW), v((total, width), f), v((seqs, padded, length), LOW), v((count, width), f), v((count, width), f), v((count, width), f)
    )


E = 768
M = 1536
SLAB = 32
ORDER = (0, 1, 2, 3)
BESIDE_ATTENTION = {2: (("add_x", 0, 0), ("add_x", 0, 1),), 4: (("grads", 1, 0), ("grads", 1, 2), ("add_x", 0, 2),), 10: (("add_y", 0, 0), ("add_x", 0, 3),)}
BESIDE_KEYS = (("line", 0, 0), ("grads", 1, 1), ("add_y", 0, 1), ("grads", 1, 3), ("add_x", 1, 0), ("line", 0, 1), ("add_x", 1, 1), ("add_y", 0, 2),)
BESIDE_TOKENS = {2: (("attention_grads", 0), ("line", 0, 2),), 3: (("add_x", 1, 3), ("add_y", 0, 3),)}
BESIDE_FEED_FORWARD = {2: (("add_y", 1, 0), ("line", 1, 0),), 3: (("attention_grads", 1),), 4: (("add_x", 1, 2),), 5: (("add_y", 1, 1), ("line", 1, 1),), 6: (("add_x", 2, 0), ("add_x", 2, 1),), 7: (("owner", 0),), 9: (("add_y", 2, 0), ("line", 2, 0), ("add_y", 1, 2), ("attention_grads", 3), ("attention_grads", 2), ("line", 1, 2),), 12: (("add_y", 2, 1),), 13: (("line", 2, 1),), 14: (("add_x", 2, 3), ("add_y", 1, 3), ("add_x", 2, 2), ("owner", 1),)}
LAST = (("add_y", 2, 3), ("add_y", 2, 2), ("line", 2, 2), ("middle_x", 0), ("middle_x", 1), ("owner", 2), ("arrived", 0), ("arrived", 1), ("middle_x", 2), ("arrived", 2),)


def slabs(rows, body):
    @pl.loop(0, rows // SLAB)
    def _(i):
        body(pl.multiple_of(i * SLAB, SLAB))


def f32(v):
    return v.astype(jnp.float32)


def backward_part(
    rows, seqs, length, padded, sends,
    attn, up, down, vec, bias, kv, hidden_h, query_m, rows_m, mixed_m, hid_m, act_m, slope, dtwo, dlow, normed, inverse, dvec, pick_t, tokens,
    layer_h, dtokens_h, out, small_out, norm_out,
    dupper, dbias, done, dquery, part,
    acc, xb, yr, zr, mr,
    sall, sall2, ssib, sx, sy, norms,
    tile_sem, out_sem, pair_s, pair_r, dup_s, dup_r, sib_s, sib_r, x_s, x_r, y_s, y_r, z_s, z_r, m_s, m_r, f_s, f_r, sm_s, sm_r, sy_r, n_s, n_r,
):
    left = right = dhid = dpre = dmix = dkv = tokens_t = htile = ytile = ltile = None
    z, y, x, c = place()
    edge = x == c
    mid = jnp.logical_not(edge)
    width = E
    count = seqs * padded
    total = seqs * length
    pair = rows * 2
    me = dev(z, y, x, c)
    above, below, beside = dev(z + 1, y, x, c), dev(z - 1, y, x, c), dev(z, flip(y), x, c)
    over, near, diag = dev(z, y, flip(x), c), dev(z, y, x, flip(c)), dev(z, y, flip(x), flip(c))
    ecol = pl.multiple_of(x * 2304, 768)
    ocol = pl.multiple_of(flip(x) * 2304, 768)

    def copy(src, dst, ss, rs, to):
        return pltpu.make_async_remote_copy(src_ref=src, dst_ref=dst, send_sem=ss, recv_sem=rs, device_id=to, device_id_type=MESH)

    def wait(cond, dst, rs):
        when(cond, lambda: copy(dst, dst, rs, rs, me).wait_recv())

    def turn(k):
        picks = ((3, 3, 0, 0), (2, 0, 3, 1), (1, 2, 1, 2), (0, 1, 2, 3))[k]
        value = jnp.int32(picks[0])
        for zv in range(1, 4):
            value = jnp.where(z == zv, picks[zv], value)
        return value

    def zrows(k):
        return pl.ds(pl.multiple_of(turn(k) * pair, pair), pair)

    def wrows(zz, yy):
        return pl.ds(pl.multiple_of((zz * 2 + yy) * rows, rows), rows)

    def add_x(p, zz):
        @pl.when(edge)
        def _():
            wait(None, xb.at[p, zrows(zz)], x_r.at[p, zz])

            base = turn(zz) * pair

            def one(i):
                r = pl.ds(pl.multiple_of(base + i, SLAB), SLAB)
                acc[p, r, pl.ds(0, E)] = (f32(acc[p, r, pl.ds(0, E)]) + f32(xb[p, r, :])).astype(LOW)

            slabs(pair, one)

        push_y(edge, p, zz, E)

    def push_x(p, zz):
        sends.start(mid, lambda: copy(xb.at[p, zrows(zz)], xb.at[p, zrows(zz)], x_s.at[p, zz], x_r.at[p, zz], over))

    def push_y(cond, p, zz, wide):
        sends.start(cond, lambda: copy(
            acc.at[p, wrows(turn(zz), flip(y)), pl.ds(0, wide)], yr.at[p, zz, :, pl.ds(0, wide)], y_s.at[p, zz], y_r.at[p, zz], beside))

    def add_into(cond, p, zz, buffer, slot, sem):
        for role, wide in ((edge, E), (mid, M)):
            @pl.when(both(cond, role))
            def _():
                wait(None, buffer.at[p, slot, :, pl.ds(0, wide)], sem)
                base = (zz * 2 + y) * rows

                def one(i):
                    here = pl.ds(pl.multiple_of(base + i, SLAB), SLAB)
                    acc[p, here, pl.ds(0, wide)] = (f32(acc[p, here, pl.ds(0, wide)]) + f32(buffer[p, slot, pl.ds(i, SLAB), pl.ds(0, wide)])).astype(LOW)

                slabs(rows, one)

    def add_y(p, zz):
        add_into(None, p, turn(zz), yr, zz, y_r.at[p, zz])

    def z_push(cond, p, spot, k, to):
        for role, wide in ((edge, E), (mid, M)):
            def make(wide=wide):
                zz, slot = spot()
                return copy(acc.at[p, wrows(zz, y), pl.ds(0, wide)], zr.at[p, slot, :, pl.ds(0, wide)], z_s.at[k, p, zz], z_r.at[k, p, zz], to)

            sends.start(lambda role=role: both(cond(), role), make)

    def line(p, t):
        def upward():
            return both(z <= t, z < 3)

        def up_spot():
            zz = jnp.where(upward(), 3 + z - t, 0)
            return zz, zz

        def downward():
            return both(3 - z <= t, z > 0)

        def down_spot():
            zz = jnp.where(downward(), z + t - 3, 0)
            return zz, jnp.where(zz == z - 1, 4, zz)

        zz = up_spot()[0]
        add_into(both(upward(), z > 0), p, zz, zr, zz, z_r.at[0, p, zz])
        z_push(upward, p, up_spot, 0, above)
        zz = down_spot()[0]
        add_into(both(downward(), z < 3), p, zz, zr, zz, z_r.at[1, p, zz])
        z_push(downward, p, down_spot, 1, below)

    def owner(p):
        add_into(z > 0, p, z, zr, z, z_r.at[0, p, z])
        add_into(z < 3, p, z, zr, 4, z_r.at[1, p, z])
        sends.start(mid, lambda: copy(acc.at[p, wrows(z, y)], mr.at[p], m_s.at[p], m_r.at[p], diag))
        base = (z * 2 + y) * rows

        @pl.when(edge)
        def _():
            def one(i):
                out[p, pl.ds(i, SLAB), pl.ds(ecol, E)] = acc[p, pl.ds(pl.multiple_of(base + i, SLAB), SLAB), pl.ds(0, E)]

            slabs(rows, one)

        for k, to in enumerate((near, over, diag)):
            sends.start(edge, lambda k=k, to=to: copy(
                out.at[p, :, pl.ds(ecol, E)], out.at[p, :, pl.ds(ecol, E)], f_s.at[p, k], f_r.at[p, x], to))

    def middle_x(p):
        base = (z * 2 + y) * rows

        @pl.when(mid)
        def _():
            wait(None, mr.at[p], m_r.at[p])

            def one(i):
                out[p, pl.ds(i, SLAB), pl.ds(E, M)] = (f32(acc[p, pl.ds(pl.multiple_of(base + i, SLAB), SLAB), :]) + f32(mr[p, pl.ds(i, SLAB), :])).astype(LOW)

            slabs(rows, one)

        sends.start(mid, lambda: copy(out.at[p, :, pl.ds(E, M)], out.at[p, :, pl.ds(E, M)], f_s.at[p, 0], f_r.at[p, 2], near))

    def arrived(p):
        for xx in range(2):
            wait(jnp.logical_not(both(edge, x == xx)), out.at[p, :, pl.ds(2304 * xx, E)], f_r.at[p, xx])
        wait(edge, out.at[p, :, pl.ds(E, M)], f_r.at[p, 2])

    swaps = []

    def swap(ref, k):
        def make():
            return copy(ref.at[0], ref.at[1], pair_s.at[k], pair_r.at[k], near)

        make().start()
        swaps.append(make)

    def transpose_into(ref):
        for k in range(2):
            left[k] = ref[k].T

    def product(zz, ref, cols):
        return (dot(left[0, zrows(zz), :], ref[0, :, cols], NN) + dot(left[1, zrows(zz), :], ref[1, :, cols], NN)).astype(LOW)

    def grads(p, zz, ref):
        @pl.when(mid)
        def _():
            xb[p, zrows(zz), :] = product(zz, ref, pl.ds(ocol, E))

        push_x(p, zz)

        @pl.when(mid)
        def _():
            for k in range(2):
                acc[p, zrows(zz), pl.ds(k * E, E)] = product(zz, ref, pl.ds(E + k * E, E))

        push_y(mid, p, zz, M)

        @pl.when(edge)
        def _():
            acc[p, zrows(zz), pl.ds(0, E)] = product(zz, ref, pl.ds(ecol, E))

    def dup_copy(k):
        f = pl.ds(k * 768, 768)
        return copy(dupper.at[0, :, f], dupper.at[1, :, f], dup_s.at[k], dup_r.at[k], near)

    def upper_back(k):
        f = pl.ds(k * 768, 768)
        value = dot(dlow[0], down[:, f], NN) * slope[:, f]
        dbias[:, f] = jnp.sum(value, axis=0, keepdims=True)
        dupper[0, :, f] = value.astype(LOW)
        dup_copy(k).start()

    def hidden_back():
        @pl.loop(0, 3)
        def _(k):
            n = pl.ds(pl.multiple_of(k * 256, 256), 256)
            dhid[:, n] = dot(dupper[0], up[n, :], NT)

        value, dgain, dshift = norm_pull(dtwo[...] + dhid[...], normed[...], inverse[:, :1], vec[3:4, :])
        dpre[...] = value
        done[0] = value.astype(LOW)
        swap(done, 0)
        dvec[2:3, :] = jnp.sum(value, axis=0, keepdims=True)
        dvec[3:4, :] = dgain
        dvec[4:5, :] = dshift
        dmix[...] = dot(done[0], attn[:, pl.ds(3 * width, width)], NN).astype(LOW)

    def attend_back(step):
        s, j = step // 6, lax.rem(step, 6)
        cs = pl.ds(pl.multiple_of(j * 128, 128), 128)
        rs = pl.ds(pl.multiple_of(s * length, length), length)
        ms = pl.ds(pl.multiple_of(s * padded, padded), padded)
        lane = lax.broadcasted_iota(jnp.int32, (padded, 128), 1) < 64

        def halves(v):
            zero = jnp.zeros_like(v)
            return jnp.concatenate([jnp.where(lane, v, zero), jnp.where(lane, zero, v)], axis=0)

        key, value = kv[0, rs, cs], kv[1, rs, cs]
        queries, mixes = halves(query_m[ms, cs]), halves(dmix[ms, cs])
        score = dot(key, queries, NT)
        expo = jnp.exp(score - jnp.max(score, axis=0, keepdims=True))
        probs = expo / jnp.sum(expo, axis=0, keepdims=True)
        dprobs = dot(value, mixes, NT)
        dscore = (probs * (dprobs - jnp.sum(dprobs * probs, axis=0, keepdims=True))).astype(LOW)
        dkv[0, rs, cs] = dot(dscore, queries, NN).astype(LOW)
        dvalue = dot(probs.astype(LOW), mixes, NN)
        dkv[1, rs, cs] = dvalue.astype(LOW)
        dq = dot(dscore, key, TN) * 0.125
        dq = jnp.where(lane, dq[:padded], dq[padded:])
        dquery[0, ms, cs] = dq.astype(LOW)
        first = s == 0
        sums = jnp.concatenate([jnp.sum(dq, axis=0, keepdims=True), jnp.sum(dvalue, axis=0, keepdims=True)], axis=0)
        dvec[0:2, cs] = sums + jnp.where(first, 0.0, dvec[0:2, cs])

    def key_value_grads():
        for i in range(total // 256):
            r = pl.ds(i * 256, 256)
            tokens_t[:, r] = tokens[r, :].T

        def fill(store):
            @pl.loop(0, 8)
            def _(i):
                k = lax.rem(i, 2)
                n = pl.ds(pl.multiple_of(i // 2 * pair, pair), pair)
                store(n, pl.ds(pl.multiple_of(k * E, E), E), dot(tokens_t[n, :], dkv[k], NN).astype(LOW))

        @pl.when(mid)
        def _():
            def store(n, cols, value):
                acc[2, n, cols] = value

            fill(store)

        @pl.when(edge)
        def _():
            def store(n, cols, value):
                part[n, cols] = value

            fill(store)

        for zz in ORDER:
            sends.start(edge, lambda zz=zz: copy(part.at[zrows(zz)], part.at[zrows(zz)], sib_s.at[zz], sib_r.at[zz], near))

    def attention_sides():
        for k in range(2):
            left[k] = jnp.where(c == 0, rows_m[k], done[k]).T
            right[k] = jnp.where(c == 0, dquery[k], mixed_m[k])

    def attention_grads(zz):
        @pl.when(mid)
        def _():
            xb[2, zrows(zz), :] = product(zz, right, pl.ds(0, E))

        push_x(2, zz)

        @pl.when(mid)
        def _():
            wait(None, part.at[zrows(zz)], sib_r.at[zz])

            base = turn(zz) * pair

            def one(i):
                r = pl.ds(pl.multiple_of(base + i, SLAB), SLAB)
                acc[2, r, :] = (f32(acc[2, r, :]) + f32(part[r, :])).astype(LOW)

            slabs(pair, one)

        push_y(mid, 2, zz, M)

        @pl.when(edge)
        def _():
            acc[2, zrows(zz), pl.ds(0, E)] = product(zz, right, pl.ds(0, E))

    def tile_load(i):
        slot = lax.rem(i, 2)
        return pltpu.make_async_copy(hidden_h.at[pl.ds(pl.multiple_of(i * 256, 256), 256)], htile.at[slot], tile_sem.at[slot])

    def layer_store(i):
        slot = lax.rem(i, 2)
        return pltpu.make_async_copy(ltile.at[slot], layer_h.at[pl.ds(pl.multiple_of(i * 256, 256), 256)], out_sem.at[slot])

    def feed_forward(step):
        i, k = step // 4, lax.rem(step, 4)
        slot = lax.rem(i, 2)

        @pl.when(k == 0)
        def _():
            tile_load(i).wait()

            @pl.when(i + 1 < total // 256)
            def _():
                tile_load(i + 1).start()

        f = pl.ds(pl.multiple_of(k * 768, 768), 768)
        u = dot(htile[slot].astype(LOW), up[:, f], NN) + bias[:, f]
        a = (u * (0.5 * (1.0 + lax.erf(u * SQRT_HALF)))).astype(LOW)
        ytile[...] = dot(a, down[:, f], NT) + jnp.where(k == 0, htile[slot] + vec[5:6, :], ytile[...])

        @pl.when(k == 3)
        def _():
            @pl.when(i >= 2)
            def _():
                layer_store(i - 2).wait()

            ltile[slot] = norm(ytile[...], vec[6:7, :], vec[7:8, :])[0].astype(LOW)
            layer_store(i).start()

    def token_store(i):
        slot = lax.rem(i, 2)
        return pltpu.make_async_copy(htile.at[slot], dtokens_h.at[pl.ds(pl.multiple_of(i * 256, 256), 256)], out_sem.at[2 + slot])

    def masked_tokens():
        dpre[...] = dpre[...] + dot(dquery[0], attn[:, pl.ds(0, width)], NT)

    def tokens_back(i):
        slot = lax.rem(i, 2)

        @pl.when(i >= 2)
        def _():
            token_store(i - 2).wait()

        r = pl.ds(pl.multiple_of(i * 256, 256), 256)
        s = i // (length // 256)
        pick = pick_t[s, pl.ds(pl.multiple_of(lax.rem(i, length // 256) * 256, 256), 256), :]
        value = dpre[pl.ds(pl.multiple_of(s * padded, padded), padded), :]
        high = value.astype(LOW)
        rest = (value - f32(high)).astype(LOW)
        htile[slot] = (
            dot(dkv[0, r, :], attn[:, pl.ds(width, width)], NT) + dot(dkv[1, r, :], attn[:, pl.ds(2 * width, width)], NT) + (dot(pick, high, NN) + dot(pick, rest, NN))
        )
        token_store(i).start()

    def small_start():
        for w in range(8):
            sall[w] = jnp.zeros((16, 128), jnp.float32)
            turned = dvec[...] if w == 0 else pltpu.roll(dvec[...], width - rows * w, 1)
            lane = lax.broadcasted_iota(jnp.int32, (8, 128), 1)
            sall[w, 0:8, :] = jnp.where(lane < rows, turned[:, :128], 0.0)
            for r in range(3):
                sall[w, 8 + r : 9 + r, :] = dbias[:, pl.ds(w * 384 + r * 128, 128)]
        sends.start(None, lambda: copy(sall, ssib, sm_s.at[0], sm_r.at[0], near))

    def small_x():
        wait(None, ssib, sm_r.at[0])
        ssib[...] = sall[...] + ssib[...]
        sends.start(None, lambda: copy(ssib, sx, sm_s.at[1], sm_r.at[1], over))

    w = z * 2 + y

    def peer(k):
        return lax.rem(w + k, 8)

    def small_y():
        wait(None, sx, sm_r.at[1])
        sall2[...] = ssib[...] + sx[...]
        for k in range(1, 8):
            sends.start(None, lambda k=k: copy(sall2.at[peer(k)], sy.at[w], sm_s.at[1 + k], sy_r.at[w], (peer(k), x * 2 + c)))
        sy[w] = sall2[w]

    def small_add():
        for k in range(1, 8):
            wait(None, sy.at[peer(k)], sy_r.at[peer(k)])
        value = sy[0]
        for k in range(1, 8):
            value = value + sy[k]
        small_out[...] = value

    def square_sum():
        value = small_out[...]
        squares = value * value
        for p in range(3):
            def body(i, sums):
                v = f32(out[p, pl.ds(pl.multiple_of(i * 16, 16), 16), :])
                v = v * v
                for k in range(v.shape[1] // 128):
                    sums = sums + v[:, k * 128 : (k + 1) * 128]
                return sums

            squares = lax.fori_loop(0, rows // 16, body, squares)
        norms[w] = jnp.full((8, 128), jnp.sum(squares), jnp.float32)
        for k in range(1, 8):
            sends.start(None, lambda k=k: copy(norms.at[w], norms.at[w], n_s.at[k], n_r.at[w], (peer(k), x * 2 + c)))
        for k in range(1, 8):
            wait(None, norms.at[peer(k)], n_r.at[peer(k)])
        whole = norms[0]
        for k in range(1, 8):
            whole = whole + norms[k]
        norm_out[...] = jnp.sqrt(whole)

    moves = {
        "add_x": add_x, "add_y": add_y, "line": line, "owner": owner, "middle_x": middle_x, "arrived": arrived,
        "grads": lambda p, zz: grads(p, zz, dupper), "attention_grads": lambda zz: attention_grads(zz),
    }
    small_moves = {("add_y", 1, 0): small_y, ("owner", 1): small_add}

    def run(steps):
        for name, *rest in steps:
            moves[name](*rest)
            small_moves.get((name, *rest), lambda: None)()

    def looped(n, body, table):
        @pl.loop(0, n)
        def _(i):
            body(i)
            for k in sorted(table):
                pl.when(i == k)(lambda k=k: run(table[k]))

    tile = total // 256
    f = jnp.float32
    v = pltpu.VMEM

    def compute(*refs):
        nonlocal left, right, dhid, dpre, dmix, dkv, tokens_t, htile, ytile, ltile
        left, right, dhid, dpre, dmix, dkv, tokens_t, htile, ytile, ltile = refs
        transpose_into(dlow)
        for zz in ORDER:
            grads(0, zz, act_m)
        for k in range(4):
            upper_back(k)
        transpose_into(hid_m)
        hidden_back()
        for k in range(4):
            dup_copy(k).wait_recv()
        looped(seqs * 6, attend_back, BESIDE_ATTENTION)
        swap(dquery, 1)
        small_start()
        key_value_grads()
        small_x()
        run(BESIDE_KEYS)
        for make in swaps:
            make().wait_recv()
        attention_sides()
        masked_tokens()
        looped(tile, tokens_back, BESIDE_TOKENS)
        for i in range(tile - 2, tile):
            token_store(i).wait()
        tile_load(0).start()
        looped(tile * 4, feed_forward, BESIDE_FEED_FORWARD)
        for i in range(tile - 2, tile):
            layer_store(i).wait()

    pl.run_scoped(
        compute,
        v((2, width, count), LOW), v((2, count, width), LOW), v((count, width), f), v((count, width), f), v((count, width), LOW), v((2, total, width), LOW),
        v((width, total), LOW), v((2, 256, width), f), v((256, width), f), v((2, 256, width), LOW),
    )
    run(LAST)
    square_sum()
    for make in swaps:
        make().wait_send()
    for k in range(4):
        dup_copy(k).wait_send()


def step_kernel(rows, seqs, length, padded, *refs):
    refs = list(refs)

    def take(n):
        got, refs[:] = refs[:n], refs[n:]
        return got

    raw = take(10)
    layer_h, dtokens_h, out, small_out, norm_out, hidden_h = take(6)
    weights, (small_full, small_f, tokens, pick_t, kv, vec, qbias, bias) = take(3), take(8)
    masked = take(11)
    query_m, rows_m, mixed_m, hid_m, act_m, slope, dtwo, dlow, dvec, normed, inverse = masked
    sems = take(8)
    sends = Sends()
    forward_part(rows, seqs, length, padded, sends, *raw, hidden_h, *weights, small_full, small_f, tokens, pick_t, kv, vec, qbias, bias, *masked, *sems)
    backward_part(
        rows, seqs, length, padded, sends, *weights, vec, bias, kv, hidden_h, query_m, rows_m, mixed_m, hid_m, act_m, slope, dtwo, dlow, normed, inverse, dvec, pick_t, tokens,
        layer_h, dtokens_h, out, small_out, norm_out, *refs,
    )
    sends.finish()


def whole_step(qkv, out, up, down, vectors, up_bias, tokens, place_m, count_m, grad_m):
    rows, cols = up.shape
    out, down, grad_m = out.T, down.T, jnp.swapaxes(grad_m, 0, 1)
    total, width = tokens.shape
    seqs, slots = place_m.shape
    length = total // seqs
    padded = -(-slots // 16) * 16
    count = seqs * padded
    shape = jax.ShapeDtypeStruct
    f = jnp.float32
    anywhere = pl.BlockSpec(memory_space=pl.ANY)
    vm = pl.BlockSpec(memory_space=pltpu.VMEM)
    dma = pltpu.SemaphoreType.DMA
    v = pltpu.VMEM
    one = (16, 128)
    scratch = [
        v((width, cols), LOW), v((width, cols), LOW), v((width, cols), LOW),
        v((8,) + one, LOW), v(one, f), v((total, width), LOW), v((seqs, length, padded), LOW), v((2, total, width), LOW), v((8, width), f), v((3, 1, width), f), v((1, cols), f),
        v((count, width), LOW), v((2, count, width), LOW), v((2, count, width), LOW), v((2, count, width), LOW), v((2, count, cols), LOW),
        v((count, cols), f), v((count, width), f), v((2, count, width), LOW), v((8, width), f), v((count, width), f), v((count, 128), f),
        dma((6, 3, 8)), dma((3, 8, 3)), dma((8,)), dma((8,)), dma((5,)), dma((1,)), dma((5,)), dma((5,)),
        v((2, count, cols), LOW), v((1, cols), f), v((2, count, width), LOW), v((2, count, width), LOW), v((width, M), LOW),
        v((3, width, M), LOW), v((3, width, E), LOW), v((3, 4, rows, M), LOW), v((3, 5, rows, M), LOW), v((3, rows, M), LOW),
        v((8,) + one, f), v((8,) + one, f), v((8,) + one, f), v((8,) + one, f), v((8,) + one, f), v((8, 8, 128), f),
        dma((2,)), dma((4,)), dma((2,)), dma((2,)), dma((4,)), dma((4,)), dma((4,)), dma((4,)), dma((3, 4)), dma((3, 4)), dma((3, 4)), dma((3, 4)),
        dma((2, 3, 4)), dma((2, 3, 4)), dma((3,)), dma((3,)), dma((3, 3)), dma((3, 3)), dma((9,)), dma((2,)), dma((8,)), dma((8,)), dma((8,)),
    ]
    return pl.pallas_call(
        functools.partial(step_kernel, rows, seqs, length, padded),
        out_shape=(shape((total, width), LOW), shape((total, width), f), shape((3, rows, cols), LOW), shape(one, f), shape((8, 128), f), shape((total, width), f)),
        in_specs=[anywhere] * 4 + [vm] * 2 + [anywhere, vm, pl.BlockSpec(memory_space=pltpu.SMEM), vm],
        out_specs=(anywhere, anywhere, vm, vm, vm, anywhere),
        scratch_shapes=scratch,
        compiler_params=pltpu.CompilerParams(collective_id=0, has_side_effects=True, vmem_limit_bytes=64 * 2**20 - 2**16),
    )(qkv, out, up, down, vectors, up_bias, tokens, place_m, count_m, grad_m)[:5]


def adam_kernel(layer, dtokens, norm, own, small, *refs):
    weights, firsts, seconds = refs[0:6], refs[6:12], refs[12:18]
    outs = refs[18:36]
    layer_o, dtokens_o, norm_o, layer_v, dtokens_v, sem = refs[36:]
    step_id = pl.program_id(0)
    copies_in = [pltpu.make_async_copy(layer, layer_v, sem.at[0]), pltpu.make_async_copy(dtokens, dtokens_v, sem.at[1])]
    copies_out = [pltpu.make_async_copy(layer_v, layer_o, sem.at[2]), pltpu.make_async_copy(dtokens_v, dtokens_o, sem.at[3])]

    @pl.when(step_id == 0)
    def _():
        for copy in copies_in:
            copy.start()
        norm_o[0, 0] = jnp.max(norm[...])

    @pl.when(step_id == 2)
    def _():
        for first, then in zip(copies_in, copies_out):
            first.wait()
            then.start()

    factor = CLIP_LIMIT / jnp.maximum(norm[0:1, 0:1], CLIP_LIMIT)

    def step(k, where, grad, decay, rate):
        grad = grad * factor.reshape((1,) * grad.ndim)
        weight = weights[k][where]
        first = BETA_ONE * firsts[k][where] + (1.0 - BETA_ONE) * grad
        second = BETA_TWO * seconds[k][where] + (1.0 - BETA_TWO) * grad * grad
        mean_hat = first * (1.0 / (1.0 - BETA_ONE**STEP))
        square_hat = second * (1.0 / (1.0 - BETA_TWO**STEP))
        outs[3 * k][where] = weight - rate * (mean_hat / (jnp.sqrt(square_hat) + ADAM_EPS) + decay * weight)
        outs[3 * k + 1][where] = first
        outs[3 * k + 2][where] = second

    width = weights[1].shape[1]
    for k in range(3):
        step(0, (k,), f32(own[2, :, pl.ds(k * width, width)]), DECAY_RATE, LEARN_RATE)
    everything = (slice(None), slice(None))
    step(1, everything, f32(own[2, :, pl.ds(3 * width, width)]), DECAY_RATE, OUTPUT_RATE)
    for k in range(4):
        cols = (slice(None), pl.ds(k * width, width))
        step(2, cols, f32(own[1, :, pl.ds(k * width, width)]), DECAY_RATE, LEARN_RATE)
        step(3, cols, f32(own[0, :, pl.ds(k * width, width)]), DECAY_RATE, LEARN_RATE)

    @pl.when(step_id == pl.num_programs(0) - 1)
    def _():
        for copy in copies_out:
            copy.wait()

    @pl.when(step_id == 0)
    def _():
        lanes = weights[4].shape[1]
        step(4, everything, small[0:8, 0:lanes], 0.0, VECTOR_RATE)
        step(5, everything, small[8:11, :], 0.0, BIAS_RATE)


def adam(layer, dtokens, norm, own, small, weights, moments):
    def turn(values):
        a, b, c, d, e, g = values
        return a, b.T, c, d.T, e, g.reshape(3, 128)

    arrays = turn(weights) + turn([m[0] for m in moments]) + turn([m[1] for m in moments])
    rows, cols = arrays[2].shape
    width = cols // 4
    slab = 16
    anywhere = pl.BlockSpec(memory_space=pl.ANY)
    specs = [
        pl.BlockSpec((3, slab, width), lambda i: (0, i, 0)),
        pl.BlockSpec((slab, width), lambda i: (i, 0)),
        pl.BlockSpec((slab, cols), lambda i: (i, 0)),
        pl.BlockSpec((slab, cols), lambda i: (i, 0)),
        pl.BlockSpec(arrays[4].shape, lambda i: (0, 0)),
        pl.BlockSpec(arrays[5].shape, lambda i: (0, 0)),
    ]
    outs = pl.pallas_call(
        adam_kernel,
        grid=(rows // slab,),
        out_shape=tuple(jax.ShapeDtypeStruct(a.shape, a.dtype) for a in arrays[:6] for _ in range(3))
        + (jax.ShapeDtypeStruct(layer.shape, layer.dtype), jax.ShapeDtypeStruct(dtokens.shape, dtokens.dtype), jax.ShapeDtypeStruct((1, 1), jnp.float32)),
        in_specs=[
            anywhere,
            anywhere,
            pl.BlockSpec(norm.shape, lambda i: (0, 0)),
            pl.BlockSpec((3, slab, cols), lambda i: (0, i, 0)),
            pl.BlockSpec(small.shape, lambda i: (0, 0)),
        ] + specs * 3,
        out_specs=tuple(s for s in specs for _ in range(3)) + (anywhere, anywhere, pl.BlockSpec(memory_space=pltpu.SMEM)),
        scratch_shapes=[pltpu.VMEM(layer.shape, layer.dtype), pltpu.VMEM(dtokens.shape, dtokens.dtype), pltpu.SemaphoreType.DMA((4,))],
        compiler_params=pltpu.CompilerParams(vmem_limit_bytes=64 * 2**20 - 2**16),
    )(layer, dtokens, norm, own, small, *arrays)

    def back(k, v):
        return v.T if k in (1, 3) else v.reshape(-1) if k == 5 else v

    return (outs[18], outs[19], outs[20].reshape(())) + tuple(back(i // 3, v) for i, v in enumerate(outs[:18]))


def masks(mask_place, mask_count, gradient, length):
    seqs, slots = mask_place.shape
    padded = -(-slots // 16) * 16
    live = jnp.arange(padded)[None, :] < mask_count[:, None]
    spots = jnp.pad(mask_place, ((0, 0), (0, padded - slots)), constant_values=-1)
    pick = (spots[:, :, None] == jnp.arange(length)[None, None, :]) & live[:, :, None]
    gradient = jnp.pad(gradient, ((0, 0), (0, padded - slots), (0, 0)))
    gradient = jnp.where(live[:, :, None], gradient, jnp.zeros_like(gradient))
    return pick, gradient.reshape(seqs * padded, -1)


def update(weights, moments, grads, grad_norm):
    factor = CLIP_LIMIT / jnp.maximum(grad_norm, CLIP_LIMIT)
    rates = (LEARN_RATE, OUTPUT_RATE, LEARN_RATE, LEARN_RATE, VECTOR_RATE, BIAS_RATE)
    out = ()
    for k in range(6):
        out += adam_step(weights[k], *moments[k], grads[k], factor, DECAY_RATE if k < 4 else 0.0, rates[k])
    return out


def natural(own_attn, own_up, own_down, own_vectors, own_bias):
    width = own_up.shape[1] // 4
    own_qkv = jnp.swapaxes(own_attn[:, : 3 * width].reshape(-1, 3, width), 0, 1)
    return own_qkv, own_attn[:, 3 * width :].T, own_up, own_down.T, own_vectors, own_bias


def pack(qkv, out, up, down):
    attn = jnp.concatenate([qkv[0], qkv[1], qkv[2], out.T], axis=1)
    return attn.astype(jnp.bfloat16), up.astype(jnp.bfloat16), down.T.astype(jnp.bfloat16)


def plain(tokens, mask_place, mask_count, gradient, weights, moments):
    low = jnp.bfloat16
    seqs, length, width = tokens.shape
    pick, gradient = masks(mask_place, mask_count, gradient, length)
    padded = pick.shape[1]
    flat = tokens.reshape(seqs * length, width)
    attn_w, up_w, down_w = (lax.all_gather(v, "wide", axis=0, tiled=True) for v in pack(*weights[:4]))
    vec = lax.all_gather(weights[4].astype(low), "wide", axis=1, tiled=True).astype(jnp.float32)
    bias = lax.all_gather(weights[5].astype(low), "wide", axis=0, tiled=True).astype(jnp.float32)
    wq, wk, wv, wo = (attn_w[:, k * width : (k + 1) * width] for k in range(4))
    query = (mm(flat, wq, NN) + vec[0]).astype(low)
    key = mm(flat, wk, NN, low)
    value = (mm(flat, wv, NN) + vec[1]).astype(low)
    query, key, value = (split_heads(v, seqs, length) for v in (query, key, value))
    mixed = lax.map(attend, (query, key, value)).reshape(seqs * length, width)

    def middle(rows, mixed):
        pre_one = rows.astype(jnp.float32) + (mm(mixed, wo, NT) + vec[2])
        hidden, normed, inverse = layer_norm(pre_one, vec[3], vec[4])
        hidden_low = hidden.astype(low)
        upper = mm(hidden_low, up_w, NN) + bias
        cumul = 0.5 * (1.0 + lax.erf(upper * SQRT_HALF))
        active = (upper * cumul).astype(low)
        pre_two = hidden + (mm(active, down_w, NT) + vec[5])
        return layer_norm(pre_two, vec[6], vec[7]), normed, inverse, hidden_low, upper, cumul, active

    layer_out = middle(flat, mixed)[0][0].astype(low)
    pick_low = pick.astype(low)

    def take(values):
        values = values.reshape(seqs, length, width)
        return jnp.einsum("sil,sld->sid", pick_low, values, preferred_element_type=jnp.float32).astype(low)

    rows_m = take(flat).reshape(seqs * padded, width)
    mixed_m = take(mixed).reshape(seqs * padded, width)
    query_m = split_heads(take(query), seqs, padded)
    (_, normed_two, inverse_two), normed_one, inverse_one, hidden_m, upper, cumul, active = middle(rows_m, mixed_m)
    dpre_two, dgain_two, dshift_two = norm_back(gradient.astype(jnp.float32), normed_two, inverse_two, vec[6])
    dbias_two = jnp.sum(dpre_two, axis=0)
    dtwo_low = dpre_two.astype(low)
    ddown = mm(dtwo_low, active, TN)
    dactive = mm(dtwo_low, down_w, NN)
    density = jnp.exp(-0.5 * upper * upper) * INV_ROOT_TWO_PI
    dupper = dactive * (cumul + upper * density)
    dup_bias = jnp.sum(dupper, axis=0)
    dupper_low = dupper.astype(low)
    dup = mm(hidden_m, dupper_low, TN)
    dhidden = dpre_two + mm(dupper_low, up_w, NT)
    dpre_one, dgain_one, dshift_one = norm_back(dhidden, normed_one, inverse_one, vec[3])
    dbias_out = jnp.sum(dpre_one, axis=0)
    done_low = dpre_one.astype(low)
    dout = mm(done_low, mixed_m, TN)
    dmixed = split_heads(mm(done_low, wo, NN, low), seqs, padded)
    dquery, dkey, dvalue = lax.map(attend_back, (query_m, key, value, dmixed))
    dquery = dquery.reshape(seqs * padded, width)
    dkey = dkey.reshape(seqs * length, width)
    dvalue = dvalue.reshape(seqs * length, width)
    dbias_query = jnp.sum(dquery, axis=0)
    dbias_value = jnp.sum(dvalue, axis=0)
    dquery, dkey, dvalue = dquery.astype(low), dkey.astype(low), dvalue.astype(low)
    dattn = jnp.concatenate([mm(rows_m, dquery, TN), mm(flat, dkey, TN), mm(flat, dvalue, TN), dout], axis=1)
    masked_part = dpre_one + mm(dquery, wq, NT)
    dtokens = spread(pick, masked_part) + mm(dkey, wk, NT) + mm(dvalue, wv, NT)
    dvectors = jnp.stack(
        [dbias_query, dbias_value, dbias_out, dgain_one, dshift_one, dbias_two, dgain_two, dshift_two]
    )

    def owned(value, dim):
        return lax.psum(lax.psum_scatter(value, "wide", scatter_dimension=dim, tiled=True), "narrow")

    grads = (owned(dattn, 0), owned(dup, 0), owned(ddown, 0), owned(dvectors, 1), owned(dup_bias, 0))
    grad_norm = jnp.sqrt(lax.psum(sum(jnp.sum(v * v) for v in grads), "wide"))
    return (layer_out, dtokens, grad_norm) + update(weights, moments, natural(*grads), grad_norm)


def spread(pick, rows):
    seqs, padded, length = pick.shape
    return jnp.einsum(
        "sil,sid->sld",
        pick.astype(jnp.float32),
        rows.reshape(seqs, padded, -1),
        precision=lax.Precision.HIGHEST,
        preferred_element_type=jnp.float32,
    ).reshape(seqs * length, -1)


def tailored(tokens, mask_place, mask_count, gradient, weights, moments):
    seqs, length, width = tokens.shape
    flat = tokens.reshape(seqs * length, width)
    layer_out, dtokens, own, small, grad_norm = whole_step(*weights, flat, mask_place, mask_count, gradient)
    return adam(layer_out, dtokens, grad_norm, own, small, weights, moments)


def shards(body, tokens, mask_place, mask_count, masked_output_gradient, *parameters):
    seqs, length, width = tokens.shape
    weights = parameters[0::3]
    moments = tuple(zip(parameters[1::3], parameters[2::3]))
    layer_out, dtokens, *rest = body(tokens, mask_place, mask_count, masked_output_gradient, weights, moments)
    return (layer_out.reshape(seqs, length, width), dtokens.reshape(seqs, length, width), *rest)


def solution(mesh):
    body = tailored if mesh.shape["wide"] == 8 and mesh.shape["narrow"] == 4 else plain
    data = P(("wide", "narrow"))
    rows = P("wide")
    columns = P(None, "wide")
    weights = (columns,) * 6 + (rows,) * 3 + (columns,) * 6 + (rows,) * 3
    return jax.shard_map(
        functools.partial(shards, body),
        mesh=mesh,
        in_specs=(data,) * 4 + weights,
        out_specs=(data, data, P()) + weights,
        check_vma=False,
    )
```

```python
import functools

import jax
import jax.numpy as jnp
from jax import lax
from jax.experimental import pallas as pl
from jax.experimental.pallas import tpu as pltpu
from jax.sharding import PartitionSpec as P

HEADS = 12
HEAD_DIM = 64
STEP = 10

LN_EPS = 1e-06
SQRT_HALF = 0.7071067811865476
INV_ROOT_TWO_PI = 0.3989422804014327
CLIP_LIMIT = 1.0
BETA_ONE = 0.9
BETA_TWO = 0.999
LEARN_RATE = 0.05
OUTPUT_RATE = 0.2
VECTOR_RATE = 0.5
BIAS_RATE = 0.3
DECAY_RATE = 0.01
ADAM_EPS = 1e-08

MESH = pl.DeviceIdType.MESH


def when(cond, body):
    if callable(cond):
        cond = cond()
    if cond is None:
        body()
    else:
        pl.when(cond)(body)


class Sends:
    def __init__(self):
        self.started = []

    def start(self, cond, make):
        when(cond, lambda: make().start())
        self.started.append((cond, make))

    def finish(self):
        for cond, make in self.started:
            when(cond, lambda make=make: make().wait_send())


def both(a, b):
    return b if a is None else (a if b is None else jnp.logical_and(a, b))


def place():
    w, n = lax.axis_index("wide"), lax.axis_index("narrow")
    return w // 2, lax.rem(w, 2), n // 2, lax.rem(n, 2)


def flip(v):
    return 1 - v


def dev(z, y, x, c):
    return (z * 2 + y, x * 2 + c)


def meet(z, y, x, c, diagonal):
    bar = pltpu.get_barrier_semaphore()
    peers = [(None, dev(z, flip(y), x, c)), (None, dev(z, y, flip(x), c)), (None, dev(z, y, x, flip(c)))]
    if diagonal:
        peers.append((None, dev(z, y, flip(x), flip(c))))
    peers += [(z > 0, dev(z - 1, y, x, c)), (z < 3, dev(z + 1, y, x, c))]
    for cond, peer in peers:
        when(cond, lambda peer=peer: pl.semaphore_signal(bar, inc=1, device_id=peer, device_id_type=MESH))
    inner = jnp.logical_and(z > 0, z < 3)
    count = 4 if diagonal else 3
    pl.semaphore_wait(bar, count + 1 + jnp.where(inner, 1, 0))


def gather_kernel(rows, cols, attn, up, down, small, attn_full, up_full, down_full, small_full, send_sem, recv_sem, small_send, small_recv, own_sem):
    z, y, x, c = place()
    edge = x == c
    third = cols // 3
    mine, across = x + c, 2 * flip(x)
    fulls = (attn_full, up_full, down_full)
    shards = (attn, up, down)
    sends = Sends()
    zl, zh = z > 0, z < 3

    def spot(p, zz, yy, t):
        return fulls[p].at[pl.ds(pl.multiple_of((zz * 2 + yy) * rows, rows), rows), pl.ds(pl.multiple_of(t * third, third), third)]

    def push(cond, p, zz, yy, t, kind, to, src=None):
        def make():
            w = zz * 2 + yy
            where = spot(p, zz, yy, t)
            return pltpu.make_async_remote_copy(
                src_ref=where if src is None else src,
                dst_ref=where,
                send_sem=send_sem.at[kind, p, w],
                recv_sem=recv_sem.at[p, w, t],
                device_id=to,
                device_id_type=MESH,
            )

        sends.start(cond, make)

    def small_push(cond, zz, yy, kind, to, src=None):
        def make():
            w = zz * 2 + yy
            where = small_full.at[w]
            return pltpu.make_async_remote_copy(
                src_ref=where if src is None else src,
                dst_ref=where,
                send_sem=small_send.at[kind, w],
                recv_sem=small_recv.at[w],
                device_id=to,
                device_id_type=MESH,
            )

        sends.start(cond, make)

    def arrive(cond, p, zz, yy, t):
        def body():
            where = spot(p, zz, yy, t)
            w = zz * 2 + yy
            pltpu.make_async_remote_copy(where, where, send_sem.at[0, p, w], recv_sem.at[p, w, t], dev(z, y, x, c), device_id_type=MESH).wait_recv()

        when(cond, body)

    def small_arrive(cond, zz, yy):
        def body():
            w = zz * 2 + yy
            pltpu.make_async_remote_copy(small_full.at[w], small_full.at[w], small_send.at[0, w], small_recv.at[w], dev(z, y, x, c), device_id_type=MESH).wait_recv()

        when(cond, body)

    UP, DOWN, SIDE, OVER, NEAR, PASS = range(6)
    above, below, beside = dev(z + 1, y, x, c), dev(z - 1, y, x, c), dev(z, flip(y), x, c)
    over, near = dev(z, y, flip(x), c), dev(z, y, x, flip(c))

    def own(p):
        src = shards[p].at[:, pl.ds(pl.multiple_of(mine * third, third), third)]
        push(zh, p, z, y, mine, UP, above, src)
        push(zl, p, z, y, mine, DOWN, below, src)
        push(None, p, z, y, mine, SIDE, beside, src)

    def z_step(p, d):
        for cond, zz, onward, kind, to in ((z - d >= 0, z - d, zh, UP, above), (z + d <= 3, z + d, zl, DOWN, below)):
            arrive(cond, p, zz, y, mine)
            push(both(cond, onward), p, zz, y, mine, kind, to)
            push(cond, p, zz, y, mine, SIDE, beside)
            push(both(cond, edge), p, zz, y, mine, OVER, over)
            push(cond, p, zz, y, mine, NEAR, near)

    def y_step(p, d):
        steps = ((None, z),) if d == 0 else ((z - d >= 0, z - d), (z + d <= 3, z + d))
        for cond, zz in steps:
            arrive(cond, p, zz, flip(y), mine)
            push(both(cond, edge), p, zz, flip(y), mine, OVER, over)
            push(cond, p, zz, flip(y), mine, NEAR, near)

    def x_step(p, d):
        mid = jnp.logical_not(edge)
        for yy in (y, flip(y)):
            if d == 0:
                steps = () if yy is y else ((None, z),)
            else:
                steps = ((z - d >= 0, z - d), (z + d <= 3, z + d))
            for cond, zz in steps:
                cond = both(cond, mid)
                arrive(cond, p, zz, yy, across)
                push(cond, p, zz, yy, across, PASS, near)

    def last(p, d):
        for yy in (y, flip(y)):
            if d == 0:
                steps = () if yy is y else ((None, z),)
            else:
                steps = ((z - d >= 0, z - d), (z + d <= 3, z + d))
            for cond, zz in steps:
                arrive(cond, p, zz, yy, x + flip(c))
                arrive(both(cond, edge), p, zz, yy, across)

    def small_z(d):
        for cond, zz, onward, kind, to in ((z - d >= 0, z - d, zh, UP, above), (z + d <= 3, z + d, zl, DOWN, below)):
            small_arrive(cond, zz, y)
            small_push(both(cond, onward), zz, y, kind, to)
            small_push(cond, zz, y, SIDE, beside)

    meet(z, y, x, c, False)
    small_push(zh, z, y, UP, above, small)
    small_push(zl, z, y, DOWN, below, small)
    small_push(None, z, y, SIDE, beside, small)
    own(0)
    w = z * 2 + y
    copies = []
    for p in range(3):
        copies.append(pltpu.make_async_copy(shards[p], fulls[p].at[pl.ds(pl.multiple_of(w * rows, rows), rows)], own_sem.at[p]))
    copies.append(pltpu.make_async_copy(small, small_full.at[w], own_sem.at[3]))
    for copy in copies:
        copy.start()
    for d in range(1, 4):
        small_z(d)
    order = [
        lambda: z_step(0, 1), lambda: own(1), lambda: y_step(0, 0), lambda: z_step(0, 2), lambda: y_step(0, 1), lambda: x_step(0, 0), lambda: z_step(0, 3),
        lambda: y_step(0, 2), lambda: x_step(0, 1), lambda: z_step(1, 1), lambda: own(2), lambda: y_step(0, 3), lambda: x_step(0, 2), lambda: z_step(1, 2), lambda: y_step(1, 0), lambda: x_step(0, 3), lambda: z_step(1, 3),
        lambda: y_step(1, 1), lambda: x_step(1, 0), lambda: z_step(2, 1), lambda: y_step(1, 2), lambda: x_step(1, 1), lambda: z_step(2, 2), lambda: y_step(1, 3), lambda: x_step(1, 2), lambda: z_step(2, 3),
        lambda: y_step(2, 0), lambda: x_step(1, 3), lambda: y_step(2, 1), lambda: x_step(2, 0), lambda: y_step(2, 2), lambda: x_step(2, 1), lambda: y_step(2, 3), lambda: x_step(2, 2), lambda: x_step(2, 3),
    ]
    for step in order:
        step()
    for d in range(4):
        for cond, zz in (((None, z),) if d == 0 else ((z - d >= 0, z - d), (z + d <= 3, z + d))):
            small_arrive(cond, zz, flip(y))
    for p in range(3):
        for d in range(4):
            last(p, d)
    sends.finish()
    for copy in copies:
        copy.wait()


def gather(attn, up, down, small):
    rows, cols = attn.shape
    full = jax.ShapeDtypeStruct((8 * rows, cols), attn.dtype)
    anywhere = pl.BlockSpec(memory_space=pl.ANY)
    return pl.pallas_call(
        functools.partial(gather_kernel, rows, cols),
        out_shape=(full, full, full, jax.ShapeDtypeStruct((8,) + small.shape, small.dtype)),
        in_specs=[anywhere] * 4,
        out_specs=(anywhere,) * 4,
        scratch_shapes=[
            pltpu.SemaphoreType.DMA((6, 3, 8)),
            pltpu.SemaphoreType.DMA((3, 8, 3)),
            pltpu.SemaphoreType.DMA((3, 8)),
            pltpu.SemaphoreType.DMA((8,)),
            pltpu.SemaphoreType.DMA((4,)),
        ],
        compiler_params=pltpu.CompilerParams(collective_id=0, has_side_effects=True),
    )(attn, up, down, small)


def layer_norm(values, gain, shift):
    center = values - jnp.mean(values, axis=-1, keepdims=True)
    inverse = lax.rsqrt(jnp.mean(center * center, axis=-1, keepdims=True) + LN_EPS)
    normed = center * inverse
    return (normed * gain + shift, normed, inverse)


def norm_back(incoming, normed, inverse, gain):
    dgain = jnp.sum(incoming * normed, axis=0)
    dshift = jnp.sum(incoming, axis=0)
    scaled = incoming * gain
    dvalues = inverse * (
        scaled
        - jnp.mean(scaled, axis=-1, keepdims=True)
        - normed * jnp.mean(scaled * normed, axis=-1, keepdims=True)
    )
    return (dvalues, dgain, dshift)


def mm(a, b, dims, out=jnp.float32):
    return lax.dot_general(a, b, (dims, ((), ())), preferred_element_type=jnp.float32).astype(out)


NN = ((1,), (0,))
NT = ((1,), (1,))
TN = ((0,), (0,))


def split_heads(values, seqs, length):
    return values.reshape(seqs, length, HEADS, HEAD_DIM)


def attend(pieces):
    query, key, value = pieces
    raw = jnp.einsum("qhe,khe->hqk", query, key, preferred_element_type=jnp.float32) * HEAD_DIM ** (
        -0.5
    )
    peak = jnp.max(raw, axis=-1, keepdims=True)
    expo = jnp.exp(raw - peak)
    total = jnp.sum(expo, axis=-1, keepdims=True)
    probs = (expo / total).astype(jnp.bfloat16)
    mixed = jnp.einsum("hqk,khe->qhe", probs, value, preferred_element_type=jnp.float32)
    return mixed.astype(jnp.bfloat16)


def attend_back(pieces):
    query, key, value, dmixed = pieces
    scale = HEAD_DIM ** (-0.5)
    raw = jnp.einsum("qhe,khe->hqk", query, key, preferred_element_type=jnp.float32) * scale
    probs = jax.nn.softmax(raw, axis=-1)
    dprobs = jnp.einsum("qhe,khe->hqk", dmixed, value, preferred_element_type=jnp.float32)
    dscore = probs * (dprobs - jnp.sum(dprobs * probs, axis=-1, keepdims=True))
    dscore = (dscore * scale).astype(jnp.bfloat16)
    dquery = jnp.einsum("hqk,khe->qhe", dscore, key, preferred_element_type=jnp.float32)
    dkey = jnp.einsum("hqk,qhe->khe", dscore, query, preferred_element_type=jnp.float32)
    dvalue = jnp.einsum(
        "hqk,qhe->khe", probs.astype(jnp.bfloat16), dmixed, preferred_element_type=jnp.float32
    )
    return (dquery, dkey, dvalue)


def adam_step(weight, first, second, grad, factor, decay, rate):
    grad = grad * factor
    first_new = BETA_ONE * first + (1.0 - BETA_ONE) * grad
    second_new = BETA_TWO * second + (1.0 - BETA_TWO) * grad * grad
    mean_hat = first_new / (1.0 - BETA_ONE**STEP)
    square_hat = second_new / (1.0 - BETA_TWO**STEP)
    weight_new = weight - rate * (mean_hat / (jnp.sqrt(square_hat) + ADAM_EPS) + decay * weight)
    return (weight_new, first_new, second_new)


GATHER_ORDER = (
    ("z_step", 0, 1),
    ("y_step", 0, 0),
    ("z_step", 0, 2),
    ("own", 1),
    ("y_step", 0, 1),
    ("x_step", 0, 0),
    ("y_step", 0, 2),
    ("z_step", 0, 3),
    ("y_step", 0, 3),
    ("z_step", 1, 1),
    ("x_step", 0, 2),
    ("x_step", 0, 1),
    ("y_step", 1, 0),
    ("vectors_in",),
    ("z_step", 1, 2),
    ("x_step", 0, 3),
    ("last", 0),
    ("loop", "project", 4, {0: (("own", 2),), 1: (("y_step", 1, 1),)}),
    ("z_step", 1, 3),
    ("loop", "attend", 12, {0: (("y_step", 1, 2),), 2: (("z_step", 2, 1),), 4: (("y_step", 2, 0),), 5: (("y_step", 1, 3),), 7: (("x_step", 1, 1), ("z_step", 2, 2),), 9: (("y_step", 2, 1),)}),
    ("z_step", 2, 3),
    ("loop", "middle", 4, {0: (("y_step", 2, 2), ("x_step", 1, 2), ("x_step", 1, 0),), 1: (("x_step", 1, 3),)}),
    ("masked",),
    ("y_step", 2, 3),
    ("x_step", 2, 0),
    ("last", 1),
    ("save_hidden",),
    ("loop", "upper", 4, {1: (("x_step", 2, 1),), 2: (("x_step", 2, 2), ("x_step", 2, 3),)}),
    ("last", 2),
)


def dot(a, b, dims):
    return lax.dot_general(a, b, (dims, ((), ())), preferred_element_type=jnp.float32)


NN = ((1,), (0,))
NT = ((1,), (1,))
TN = ((0,), (0,))
LOW = jnp.bfloat16


def norm(values, gain, shift):
    center = values - jnp.mean(values, axis=-1, keepdims=True)
    inverse = lax.rsqrt(jnp.mean(center * center, axis=-1, keepdims=True) + LN_EPS)
    normed = center * inverse
    return normed * gain + shift, normed, inverse


def norm_pull(incoming, normed, inverse, gain):
    dgain = jnp.sum(incoming * normed, axis=0, keepdims=True)
    dshift = jnp.sum(incoming, axis=0, keepdims=True)
    scaled = incoming * gain
    return (
        inverse * (scaled - jnp.mean(scaled, axis=-1, keepdims=True) - normed * jnp.mean(scaled * normed, axis=-1, keepdims=True)),
        dgain,
        dshift,
    )


def forward_part(
    rows, seqs, length, padded, sends,
    qkv_h, out_h, up_h, down_h, vectors, up_bias, tokens_h, place_m, count_m, grad_m, hidden_o,
    attn_full, up_full, down_full, small_full, small_f, tokens, pick_t, kv, vec, qbias, bias,
    query_m, rows_m, mixed_m, hid_m, act_m, slope, dtwo, dlow, dvec, normed_one, inverse_one,
    send_sem, recv_sem, small_send, small_recv, load_sem, save_sem, pair_send, pair_recv,
):
    qkv_f = out_f = up_f = down_f = queries = mixed = hidden = pick = ytwo = hid_f = grad = None
    z, y, x, c = place()
    width = tokens.shape[1]
    total = tokens.shape[0]
    cols = up_h.shape[1]
    edge = x == c
    third = cols // 3
    mine, across = x + c, 2 * flip(x)
    fulls = (attn_full, up_full, down_full)
    w = z * 2 + y
    mine_rows = pl.ds(pl.multiple_of(w * rows, 32), rows)
    zl, zh = z > 0, z < 3
    count = seqs * padded

    def spot(p, zz, yy, t):
        return fulls[p].at[pl.ds(pl.multiple_of((zz * 2 + yy) * rows, rows), rows), pl.ds(pl.multiple_of(t * third, third), third)]

    def push(cond, p, zz, yy, t, kind, to):
        def make():
            whose = zz * 2 + yy
            where = spot(p, zz, yy, t)
            return pltpu.make_async_remote_copy(
                src_ref=where,
                dst_ref=where,
                send_sem=send_sem.at[kind, p, whose],
                recv_sem=recv_sem.at[p, whose, t],
                device_id=to,
                device_id_type=MESH,
            )

        sends.start(cond, make)

    def arrive(cond, p, zz, yy, t):
        def body():
            where = spot(p, zz, yy, t)
            whose = zz * 2 + yy
            pltpu.make_async_remote_copy(where, where, send_sem.at[0, p, whose], recv_sem.at[p, whose, t], dev(z, y, x, c), device_id_type=MESH).wait_recv()

        when(cond, body)

    UP, DOWN, SIDE, OVER, NEAR, PASS = range(6)
    above, below, beside = dev(z + 1, y, x, c), dev(z - 1, y, x, c), dev(z, flip(y), x, c)
    over, near = dev(z, y, flip(x), c), dev(z, y, x, flip(c))

    other_y = flip(y)
    span = {d: ((z - d >= 0, z - d), (z + d <= 3, z + d)) for d in range(1, 4)}
    span[0] = ((None, z),)
    mid = jnp.logical_not(edge)

    def around(d):
        return span[d]

    def also(a, b):
        return lambda: both(a, b)

    def own(p):
        push(zh, p, z, y, mine, UP, above)
        push(zl, p, z, y, mine, DOWN, below)
        push(None, p, z, y, mine, SIDE, beside)

    def z_step(p, d):
        for (cond, zz), onward, kind, to in zip(span[d], (zh, zl), (UP, DOWN), (above, below)):
            arrive(cond, p, zz, y, mine)
            push(also(cond, onward), p, zz, y, mine, kind, to)
            push(also(cond, edge) if d == 1 else cond, p, zz, y, mine, SIDE, beside)
            push(also(cond, edge), p, zz, y, mine, OVER, over)
            push(cond, p, zz, y, mine, NEAR, near)

    def y_step(p, d):
        for cond, zz in around(d):
            arrive(cond, p, zz, other_y, mine)
            if d == 0:
                push(also(zh, mid), p, zz, other_y, mine, UP, above)
                push(also(zl, mid), p, zz, other_y, mine, DOWN, below)
            push(also(cond, edge), p, zz, other_y, mine, OVER, over)
            push(cond, p, zz, other_y, mine, NEAR, near)

    def x_step(p, d):
        for yy in (y, other_y):
            for cond, zz in () if d == 0 and yy is y else around(d):
                arrive(also(cond, mid), p, zz, yy, across)
                push(also(cond, mid), p, zz, yy, across, PASS, near)

    def last(p):
        for d in range(4):
            for yy in (y, other_y):
                for cond, zz in () if d == 0 and yy is y else around(d):
                    arrive(cond, p, zz, yy, x + flip(c))
                    arrive(both(cond, edge), p, zz, yy, across)

    saves = []

    def keep(src, dst, k):
        copy = pltpu.make_async_copy(src, dst, save_sem.at[k])
        copy.start()
        saves.append(copy)

    swaps = []

    def swap(ref, k):
        def make():
            return pltpu.make_async_remote_copy(ref.at[0], ref.at[1], pair_send.at[k], pair_recv.at[k], near, device_id_type=MESH)

        sends.start(None, make)
        swaps.append(make)

    def peer(k):
        return lax.rem(w + k, 8)

    def small_copy(k, whose):
        return pltpu.make_async_remote_copy(
            small_full.at[whose], small_full.at[whose], small_send.at[k], small_recv.at[whose], (peer(k), x * 2 + c), device_id_type=MESH
        )

    def small_out():
        small_f[...] = jnp.zeros_like(small_f)
        small_f[0:8, 0:rows] = vectors[...]
        for r in range(3):
            small_f[8 + r : 9 + r, :] = up_bias[pl.ds(r * 128, 128)].reshape(1, 128)
        small_full[w] = small_f[...].astype(LOW)
        for k in range(1, 8):
            sends.start(None, lambda k=k: small_copy(k, w))

    def attn_shard():
        loads[1].wait()
        loads[2].wait()
        for k in range(3):
            attn_full[mine_rows, pl.ds(k * width, width)] = qkv_f[k].astype(LOW)
        attn_full[mine_rows, pl.ds(3 * width, width)] = out_f[...].astype(LOW)

    def up_shard():
        loads[3].wait()
        up_full[mine_rows, :] = up_f[...].astype(LOW)

    def down_shard():
        loads[4].wait()
        down_full[mine_rows, :] = down_f[...].astype(LOW)

    def masks():
        slots = place_m.shape[1]
        for s in range(seqs):
            hit = lax.broadcasted_iota(jnp.int32, (length, slots), 0) == place_m[s : s + 1, :]
            live = lax.broadcasted_iota(jnp.int32, (length, slots), 1) < count_m[s]
            hit = jnp.logical_and(hit, live).astype(jnp.float32).astype(LOW)
            row = lax.broadcasted_iota(jnp.int32, (padded, slots), 0)
            slot = lax.broadcasted_iota(jnp.int32, (padded, slots), 1)
            same = (row == slot).astype(jnp.float32).astype(LOW)
            kept = jnp.logical_and(row == slot, slot < count_m[s]).astype(jnp.float32).astype(LOW)
            pick[s] = dot(same, hit, NT).astype(LOW)
            pick_t[s] = dot(hit, same, NT).astype(LOW)
            grad[pl.ds(s * padded, padded), :] = dot(kept, f32(grad_m[...])[:, s, :].astype(LOW), NN)

    def vectors_in():
        loads[0].wait()
        for k in range(1, 8):
            small_copy(k, peer(k)).wait_recv()
        at = lax.broadcasted_iota(jnp.int32, (128, width), 0)
        to = lax.broadcasted_iota(jnp.int32, (128, width), 1)
        total = jnp.zeros((16, width), jnp.float32)
        for k in range(8):
            place_k = jnp.logical_and(at + k * rows == to, at < rows).astype(jnp.float32).astype(LOW)
            total += dot(small_full[k], place_k, NN)
            for r in range(3):
                bias[:, pl.ds(k * 384 + r * 128, 128)] = small_full[k, 8 + r : 9 + r, :].astype(jnp.float32)
        vec[...] = total[:8]
        qbias[0] = total[0:1]
        qbias[1] = jnp.zeros((1, width), jnp.float32)
        qbias[2] = total[1:2]

    def tile(i):
        return pl.ds(pl.multiple_of(i * 256, 256), 256)

    def project(i):
        r = tile(i)
        for k in range(3):
            value = dot(tokens[r, :], attn_full[:, pl.ds(k * width, width)], NN) + qbias[k]
            if k == 0:
                queries[r, :] = (value * 0.125).astype(LOW)
            else:
                kv[k - 1, r, :] = value.astype(LOW)

    def attend(step):
        s, j = step // (width // 128), lax.rem(step, width // 128)
        lane = lax.broadcasted_iota(jnp.int32, (length, 128), 1) < 64
        cs = pl.ds(pl.multiple_of(j * 128, 128), 128)
        rs = pl.ds(pl.multiple_of(s * length, length), length)
        key, value = kv[0, rs, cs], kv[1, rs, cs]
        zero, one = jnp.zeros_like(key), jnp.ones_like(key)
        keys = (jnp.where(lane, key, zero), jnp.where(lane, zero, key))
        values = (jnp.where(lane, value, one), jnp.where(lane, one, value))
        for q in range(length // 256):
            r = pl.ds(pl.multiple_of(s * length + q * 256, 256), 256)
            query = queries[r, cs]
            parts = []
            for h in range(2):
                score = dot(query, keys[h], NT)
                expo = jnp.exp(score - jnp.max(score, axis=-1, keepdims=True))
                parts.append(dot(expo.astype(LOW), values[h], NN))
            left = lane[:256]
            top = jnp.where(left, parts[0], parts[1])
            under = pltpu.roll(jnp.where(left, parts[1], parts[0]), 64, 1)
            mixed[r, cs] = (top / under).astype(LOW)

    def middle(i):
        r = tile(i)
        pre = tokens[r, :].astype(jnp.float32) + (dot(mixed[r, :], attn_full[:, pl.ds(3 * width, width)], NT) + vec[2:3, :])
        hidden[r, :] = norm(pre, vec[3:4, :], vec[4:5, :])[0]

    def masked_rows():
        for s in range(seqs):
            r = pl.ds(s * padded, padded)
            rs = pl.ds(s * length, length)
            rows_m[0, r, :] = dot(pick[s], tokens[rs, :], NN).astype(LOW)
            mixed_m[0, r, :] = dot(pick[s], mixed[rs, :], NN).astype(LOW)
            query_m[r, :] = dot(pick[s], queries[rs, :], NN).astype(LOW)
        pre = rows_m[0].astype(jnp.float32) + (dot(mixed_m[0], attn_full[:, pl.ds(3 * width, width)], NT) + vec[2:3, :])
        value, normed, inverse = norm(pre, vec[3:4, :], vec[4:5, :])
        hid_f[...] = value
        hid_m[0] = value.astype(LOW)
        normed_one[...] = normed
        inverse_one[...] = jnp.broadcast_to(inverse, inverse_one.shape)
        swap(rows_m, 0)
        swap(mixed_m, 1)
        swap(hid_m, 2)

    def upper(k):
        f = pl.ds(pl.multiple_of(k * 768, 768), 768)
        u = dot(hid_m[0], up_full[:, f], NN) + bias[:, f]
        cumul = 0.5 * (1.0 + lax.erf(u * SQRT_HALF))
        act_m[0, :, f] = (u * cumul).astype(LOW)
        slope[:, f] = cumul + u * (jnp.exp(-0.5 * u * u) * INV_ROOT_TWO_PI)

    def after_upper():
        swap(act_m, 3)

    def lower():
        @pl.loop(0, 3)
        def _(k):
            n = pl.ds(pl.multiple_of(k * 256, 256), 256)
            ytwo[:, n] = dot(act_m[0], down_full[n, :], NT)

        pre = hid_f[...] + (ytwo[...] + vec[5:6, :])
        _, normed, inverse = norm(pre, vec[6:7, :], vec[7:8, :])
        value, dgain, dshift = norm_pull(grad[...], normed, inverse, vec[6:7, :])
        dtwo[...] = value
        dlow[0] = value.astype(LOW)
        dvec[...] = jnp.zeros_like(dvec)
        dvec[5:6, :] = jnp.sum(value, axis=0, keepdims=True)
        dvec[6:7, :] = dgain
        dvec[7:8, :] = dshift
        swap(dlow, 4)

    loads = [pltpu.make_async_copy(tokens_h, tokens, load_sem.at[4])]
    loads[0].start()

    def prepare(*refs):
        nonlocal qkv_f, out_f, up_f, down_f
        qkv_f, out_f, up_f, down_f = refs
        for k, src in enumerate((qkv_h, out_h, up_h, down_h)):
            loads.append(pltpu.make_async_copy(src, refs[k], load_sem.at[k]))
            loads[-1].start()
        bar = pltpu.get_barrier_semaphore()
        for to in [near, over, dev(z, y, flip(x), flip(c))] + [(peer(k), x * 2 + c) for k in range(1, 8)]:
            pl.semaphore_signal(bar, inc=1, device_id=to, device_id_type=MESH)
        attn_shard()
        pl.semaphore_wait(bar, 10)
        own(0)
        small_out()
        up_shard()
        down_shard()

    f = jnp.float32
    v = pltpu.VMEM
    pl.run_scoped(prepare, v(qkv_h.shape, f), v(out_h.shape, f), v(up_h.shape, f), v(down_h.shape, f))

    def save_hidden():
        keep(hidden, hidden_o, 0)

    steps = {
        "z_step": z_step, "y_step": y_step, "x_step": x_step, "own": own, "last": last, "vectors_in": vectors_in,
        "masked": masked_rows, "save_hidden": save_hidden,
    }
    pieces = {"project": project, "attend": attend, "middle": middle, "upper": upper}

    def perform(plan):
        for name, *rest in plan:
            if name == "loop":
                piece, n, table = rest

                @pl.loop(0, n)
                def _(i):
                    pieces[piece](i)
                    for k in sorted(table):
                        pl.when(i == k)(lambda k=k: perform(table[k]))
            else:
                steps[name](*rest)

    def run(*refs):
        nonlocal queries, mixed, hidden, pick, ytwo, hid_f, grad
        queries, mixed, hidden, pick, ytwo, hid_f, grad = refs
        masks()
        perform(GATHER_ORDER)
        after_upper()
        lower()
        for make in swaps:
            make().wait_recv()
        for copy in saves:
            copy.wait()

    pl.run_scoped(
        run, v((total, width), LOW), v((total, width), LOW), v((total, width), f), v((seqs, padded, length), LOW), v((count, width), f), v((count, width), f), v((count, width), f)
    )


E = 768
M = 1536
SLAB = 32
ORDER = (0, 1, 2, 3)
BESIDE_ATTENTION = {2: (("add_x", 0, 0),), 3: (("grads", 1, 0),), 7: (("add_x", 0, 2), ("add_x", 0, 1),), 11: (("grads", 1, 3), ("add_y", 0, 0),)}
BESIDE_KEYS = (("line", 0, 0), ("grads", 1, 2), ("grads", 1, 1), ("add_y", 0, 1), ("add_x", 1, 0), ("line", 0, 1),)
BESIDE_TOKENS = {2: (("attention_grads", 0), ("add_y", 0, 2), ("line", 0, 2),)}
BESIDE_FEED_FORWARD = {0: (("add_x", 1, 1), ("add_y", 1, 0), ("add_x", 2, 0), ("add_x", 1, 2), ("line", 1, 0), ("add_x", 0, 3),), 4: (("attention_grads", 1),), 5: (("add_y", 2, 0), ("line", 2, 0), ("add_x", 2, 1), ("add_y", 1, 1), ("line", 1, 1),), 6: (("add_y", 1, 2),), 8: (("add_x", 1, 3), ("attention_grads", 2), ("add_y", 0, 3), ("attention_grads", 3),), 10: (("line", 1, 2), ("owner", 0), ("add_x", 2, 3), ("add_y", 2, 1), ("line", 2, 1), ("add_x", 2, 2),), 14: (("add_y", 1, 3),)}
LAST = (("owner", 1), ("add_y", 2, 2), ("line", 2, 2), ("add_y", 2, 3), ("middle_x", 0), ("middle_x", 1), ("relay", 0), ("owner", 2), ("relay", 1), ("arrived", 0), ("middle_x", 2), ("arrived", 1), ("relay", 2), ("arrived", 2),)


def slabs(rows, body):
    @pl.loop(0, rows // SLAB)
    def _(i):
        body(pl.multiple_of(i * SLAB, SLAB))


def f32(v):
    return v.astype(jnp.float32)


def backward_part(
    rows, seqs, length, padded, sends,
    attn, up, down, vec, bias, kv, hidden_h, query_m, rows_m, mixed_m, hid_m, act_m, slope, dtwo, dlow, normed, inverse, dvec, pick_t, tokens,
    layer_h, dtokens_h, out, small_out, norm_out,
    dupper, dbias, done, dquery, part,
    acc, xb, yr, zr, mr,
    sall, sall2, ssib, sx, sy, norms,
    tile_sem, out_sem, pair_s, pair_r, dup_s, dup_r, sib_s, sib_r, x_s, x_r, y_s, y_r, z_s, z_r, m_s, m_r, f_s, f_r, sm_s, sm_r, sy_r, n_s, n_r,
):
    left = right = dhid = dpre = dmix = dkv = tokens_t = htile = ytile = ltile = None
    z, y, x, c = place()
    edge = x == c
    mid = jnp.logical_not(edge)
    width = E
    count = seqs * padded
    total = seqs * length
    pair = rows * 2
    me = dev(z, y, x, c)
    above, below, beside = dev(z + 1, y, x, c), dev(z - 1, y, x, c), dev(z, flip(y), x, c)
    over, near, diag = dev(z, y, flip(x), c), dev(z, y, x, flip(c)), dev(z, y, flip(x), flip(c))
    ecol = pl.multiple_of(x * 2304, 768)
    ocol = pl.multiple_of(flip(x) * 2304, 768)

    def copy(src, dst, ss, rs, to):
        return pltpu.make_async_remote_copy(src_ref=src, dst_ref=dst, send_sem=ss, recv_sem=rs, device_id=to, device_id_type=MESH)

    def wait(cond, dst, rs):
        when(cond, lambda: copy(dst, dst, rs, rs, me).wait_recv())

    def turn(k):
        picks = ((3, 3, 0, 0), (2, 0, 3, 1), (1, 2, 1, 2), (0, 1, 2, 3))[k]
        value = jnp.int32(picks[0])
        for zv in range(1, 4):
            value = jnp.where(z == zv, picks[zv], value)
        return value

    def zrows(k):
        return pl.ds(pl.multiple_of(turn(k) * pair, pair), pair)

    def wrows(zz, yy):
        return pl.ds(pl.multiple_of((zz * 2 + yy) * rows, rows), rows)

    def add_x(p, zz):
        @pl.when(edge)
        def _():
            wait(None, xb.at[p, zrows(zz)], x_r.at[p, zz])

            base = turn(zz) * pair

            def one(i):
                r = pl.ds(pl.multiple_of(base + i, SLAB), SLAB)
                acc[p, r, pl.ds(0, E)] = (f32(acc[p, r, pl.ds(0, E)]) + f32(xb[p, r, :])).astype(LOW)

            slabs(pair, one)

        push_y(edge, p, zz, E)

    def push_x(p, zz):
        sends.start(mid, lambda: copy(xb.at[p, zrows(zz)], xb.at[p, zrows(zz)], x_s.at[p, zz], x_r.at[p, zz], over))

    def push_y(cond, p, zz, wide):
        sends.start(cond, lambda: copy(
            acc.at[p, wrows(turn(zz), flip(y)), pl.ds(0, wide)], yr.at[p, zz, :, pl.ds(0, wide)], y_s.at[p, zz], y_r.at[p, zz], beside))

    def add_into(cond, p, zz, buffer, slot, sem):
        for role, wide in ((edge, E), (mid, M)):
            @pl.when(both(cond, role))
            def _():
                wait(None, buffer.at[p, slot, :, pl.ds(0, wide)], sem)
                base = (zz * 2 + y) * rows

                def one(i):
                    here = pl.ds(pl.multiple_of(base + i, SLAB), SLAB)
                    acc[p, here, pl.ds(0, wide)] = (f32(acc[p, here, pl.ds(0, wide)]) + f32(buffer[p, slot, pl.ds(i, SLAB), pl.ds(0, wide)])).astype(LOW)

                slabs(rows, one)

    def add_y(p, zz):
        add_into(None, p, turn(zz), yr, zz, y_r.at[p, zz])

    def z_push(cond, p, spot, k, to):
        for role, wide in ((edge, E), (mid, M)):
            def make(wide=wide):
                zz, slot = spot()
                return copy(acc.at[p, wrows(zz, y), pl.ds(0, wide)], zr.at[p, slot, :, pl.ds(0, wide)], z_s.at[k, p, zz], z_r.at[k, p, zz], to)

            sends.start(lambda role=role: both(cond(), role), make)

    def line(p, t):
        def upward():
            return both(z <= t, z < 3)

        def up_spot():
            zz = jnp.where(upward(), 3 + z - t, 0)
            return zz, zz

        def downward():
            return both(3 - z <= t, z > 0)

        def down_spot():
            zz = jnp.where(downward(), z + t - 3, 0)
            return zz, jnp.where(zz == z - 1, 4, zz)

        zz = up_spot()[0]
        add_into(both(upward(), z > 0), p, zz, zr, zz, z_r.at[0, p, zz])
        z_push(upward, p, up_spot, 0, above)
        zz = down_spot()[0]
        add_into(both(downward(), z < 3), p, zz, zr, zz, z_r.at[1, p, zz])
        z_push(downward, p, down_spot, 1, below)

    def owner(p):
        add_into(z > 0, p, z, zr, z, z_r.at[0, p, z])
        add_into(z < 3, p, z, zr, 4, z_r.at[1, p, z])
        sends.start(mid, lambda: copy(acc.at[p, wrows(z, y)], mr.at[p], m_s.at[p], m_r.at[p], diag))
        base = (z * 2 + y) * rows

        @pl.when(edge)
        def _():
            def one(i):
                out[p, pl.ds(i, SLAB), pl.ds(ecol, E)] = acc[p, pl.ds(pl.multiple_of(base + i, SLAB), SLAB), pl.ds(0, E)]

            slabs(rows, one)

        for k, to in enumerate((near, over)):
            sends.start(edge, lambda k=k, to=to: copy(
                out.at[p, :, pl.ds(ecol, E)], out.at[p, :, pl.ds(ecol, E)], f_s.at[p, k], f_r.at[p, x], to))

    def middle_x(p):
        base = (z * 2 + y) * rows

        @pl.when(mid)
        def _():
            wait(None, mr.at[p], m_r.at[p])

            def one(i):
                out[p, pl.ds(i, SLAB), pl.ds(E, M)] = (f32(acc[p, pl.ds(pl.multiple_of(base + i, SLAB), SLAB), :]) + f32(mr[p, pl.ds(i, SLAB), :])).astype(LOW)

            slabs(rows, one)

        sends.start(mid, lambda: copy(out.at[p, :, pl.ds(E, M)], out.at[p, :, pl.ds(E, M)], f_s.at[p, 0], f_r.at[p, 2], near))

    def relay(p):
        wait(mid, out.at[p, :, pl.ds(ocol, E)], f_r.at[p, flip(x)])
        sends.start(mid, lambda: copy(out.at[p, :, pl.ds(ocol, E)], out.at[p, :, pl.ds(ocol, E)], f_s.at[p, 1], f_r.at[p, flip(x)], near))

    def arrived(p):
        wait(edge, out.at[p, :, pl.ds(ocol, E)], f_r.at[p, flip(x)])
        wait(mid, out.at[p, :, pl.ds(ecol, E)], f_r.at[p, x])
        wait(edge, out.at[p, :, pl.ds(E, M)], f_r.at[p, 2])

    swaps = []

    def swap(ref, k):
        def make():
            return copy(ref.at[0], ref.at[1], pair_s.at[k], pair_r.at[k], near)

        make().start()
        swaps.append(make)

    def transpose_into(ref):
        for k in range(2):
            left[k] = ref[k].T

    def product(zz, ref, cols):
        return (dot(left[0, zrows(zz), :], ref[0, :, cols], NN) + dot(left[1, zrows(zz), :], ref[1, :, cols], NN)).astype(LOW)

    def grads(p, zz, ref):
        @pl.when(mid)
        def _():
            xb[p, zrows(zz), :] = product(zz, ref, pl.ds(ocol, E))

        push_x(p, zz)

        @pl.when(mid)
        def _():
            for k in range(2):
                acc[p, zrows(zz), pl.ds(k * E, E)] = product(zz, ref, pl.ds(E + k * E, E))

        push_y(mid, p, zz, M)

        @pl.when(edge)
        def _():
            acc[p, zrows(zz), pl.ds(0, E)] = product(zz, ref, pl.ds(ecol, E))

    def dup_copy(k):
        f = pl.ds(k * 768, 768)
        return copy(dupper.at[0, :, f], dupper.at[1, :, f], dup_s.at[k], dup_r.at[k], near)

    def upper_back(k):
        f = pl.ds(k * 768, 768)
        value = dot(dlow[0], down[:, f], NN) * slope[:, f]
        dbias[:, f] = jnp.sum(value, axis=0, keepdims=True)
        dupper[0, :, f] = value.astype(LOW)
        dup_copy(k).start()

    def hidden_back():
        @pl.loop(0, 3)
        def _(k):
            n = pl.ds(pl.multiple_of(k * 256, 256), 256)
            dhid[:, n] = dot(dupper[0], up[n, :], NT)

        value, dgain, dshift = norm_pull(dtwo[...] + dhid[...], normed[...], inverse[:, :1], vec[3:4, :])
        dpre[...] = value
        done[0] = value.astype(LOW)
        swap(done, 0)
        dvec[2:3, :] = jnp.sum(value, axis=0, keepdims=True)
        dvec[3:4, :] = dgain
        dvec[4:5, :] = dshift
        dmix[...] = dot(done[0], attn[:, pl.ds(3 * width, width)], NN).astype(LOW)

    def attend_back(step):
        s, j = step // 6, lax.rem(step, 6)
        cs = pl.ds(pl.multiple_of(j * 128, 128), 128)
        rs = pl.ds(pl.multiple_of(s * length, length), length)
        ms = pl.ds(pl.multiple_of(s * padded, padded), padded)
        lane = lax.broadcasted_iota(jnp.int32, (padded, 128), 1) < 64

        def halves(v):
            zero = jnp.zeros_like(v)
            return jnp.concatenate([jnp.where(lane, v, zero), jnp.where(lane, zero, v)], axis=0)

        key, value = kv[0, rs, cs], kv[1, rs, cs]
        queries, mixes = halves(query_m[ms, cs]), halves(dmix[ms, cs])
        score = dot(key, queries, NT)
        expo = jnp.exp(score - jnp.max(score, axis=0, keepdims=True))
        probs = expo / jnp.sum(expo, axis=0, keepdims=True)
        dprobs = dot(value, mixes, NT)
        dscore = (probs * (dprobs - jnp.sum(dprobs * probs, axis=0, keepdims=True))).astype(LOW)
        dkv[0, rs, cs] = dot(dscore, queries, NN).astype(LOW)
        dvalue = dot(probs.astype(LOW), mixes, NN)
        dkv[1, rs, cs] = dvalue.astype(LOW)
        dq = dot(dscore, key, TN) * 0.125
        dq = jnp.where(lane, dq[:padded], dq[padded:])
        dquery[0, ms, cs] = dq.astype(LOW)
        first = s == 0
        sums = jnp.concatenate([jnp.sum(dq, axis=0, keepdims=True), jnp.sum(dvalue, axis=0, keepdims=True)], axis=0)
        dvec[0:2, cs] = sums + jnp.where(first, 0.0, dvec[0:2, cs])

    def key_value_grads():
        for i in range(total // 256):
            r = pl.ds(i * 256, 256)
            tokens_t[:, r] = tokens[r, :].T

        def fill(store):
            @pl.loop(0, 8)
            def _(i):
                k = lax.rem(i, 2)
                n = pl.ds(pl.multiple_of(i // 2 * pair, pair), pair)
                store(n, pl.ds(pl.multiple_of(k * E, E), E), dot(tokens_t[n, :], dkv[k], NN).astype(LOW))

        @pl.when(mid)
        def _():
            def store(n, cols, value):
                acc[2, n, cols] = value

            fill(store)

        @pl.when(edge)
        def _():
            def store(n, cols, value):
                part[n, cols] = value

            fill(store)

        for zz in ORDER:
            sends.start(edge, lambda zz=zz: copy(part.at[zrows(zz)], part.at[zrows(zz)], sib_s.at[zz], sib_r.at[zz], near))

    def attention_sides():
        for k in range(2):
            left[k] = jnp.where(c == 0, rows_m[k], done[k]).T
            right[k] = jnp.where(c == 0, dquery[k], mixed_m[k])

    def attention_grads(zz):
        @pl.when(mid)
        def _():
            xb[2, zrows(zz), :] = product(zz, right, pl.ds(0, E))

        push_x(2, zz)

        @pl.when(mid)
        def _():
            wait(None, part.at[zrows(zz)], sib_r.at[zz])

            base = turn(zz) * pair

            def one(i):
                r = pl.ds(pl.multiple_of(base + i, SLAB), SLAB)
                acc[2, r, :] = (f32(acc[2, r, :]) + f32(part[r, :])).astype(LOW)

            slabs(pair, one)

        push_y(mid, 2, zz, M)

        @pl.when(edge)
        def _():
            acc[2, zrows(zz), pl.ds(0, E)] = product(zz, right, pl.ds(0, E))

    def tile_load(i):
        slot = lax.rem(i, 2)
        return pltpu.make_async_copy(hidden_h.at[pl.ds(pl.multiple_of(i * 256, 256), 256)], htile.at[slot], tile_sem.at[slot])

    def layer_store(i):
        slot = lax.rem(i, 2)
        return pltpu.make_async_copy(ltile.at[slot], layer_h.at[pl.ds(pl.multiple_of(i * 256, 256), 256)], out_sem.at[slot])

    def feed_forward(step):
        i, k = step // 4, lax.rem(step, 4)
        slot = lax.rem(i, 2)

        @pl.when(k == 0)
        def _():
            tile_load(i).wait()

            @pl.when(i + 1 < total // 256)
            def _():
                tile_load(i + 1).start()

        f = pl.ds(pl.multiple_of(k * 768, 768), 768)
        u = dot(htile[slot].astype(LOW), up[:, f], NN) + bias[:, f]
        a = (u * (0.5 * (1.0 + lax.erf(u * SQRT_HALF)))).astype(LOW)
        ytile[...] = dot(a, down[:, f], NT) + jnp.where(k == 0, htile[slot] + vec[5:6, :], ytile[...])

        @pl.when(k == 3)
        def _():
            @pl.when(i >= 2)
            def _():
                layer_store(i - 2).wait()

            ltile[slot] = norm(ytile[...], vec[6:7, :], vec[7:8, :])[0].astype(LOW)
            layer_store(i).start()

    def token_store(i):
        slot = lax.rem(i, 2)
        return pltpu.make_async_copy(htile.at[slot], dtokens_h.at[pl.ds(pl.multiple_of(i * 256, 256), 256)], out_sem.at[2 + slot])

    def masked_tokens():
        dpre[...] = dpre[...] + dot(dquery[0], attn[:, pl.ds(0, width)], NT)

    def tokens_back(i):
        slot = lax.rem(i, 2)

        @pl.when(i >= 2)
        def _():
            token_store(i - 2).wait()

        r = pl.ds(pl.multiple_of(i * 256, 256), 256)
        s = i // (length // 256)
        pick = pick_t[s, pl.ds(pl.multiple_of(lax.rem(i, length // 256) * 256, 256), 256), :]
        value = dpre[pl.ds(pl.multiple_of(s * padded, padded), padded), :]
        high = value.astype(LOW)
        rest = (value - f32(high)).astype(LOW)
        htile[slot] = (
            dot(dkv[0, r, :], attn[:, pl.ds(width, width)], NT) + dot(dkv[1, r, :], attn[:, pl.ds(2 * width, width)], NT) + (dot(pick, high, NN) + dot(pick, rest, NN))
        )
        token_store(i).start()

    def small_start():
        for w in range(8):
            sall[w] = jnp.zeros((16, 128), jnp.float32)
            turned = dvec[...] if w == 0 else pltpu.roll(dvec[...], width - rows * w, 1)
            lane = lax.broadcasted_iota(jnp.int32, (8, 128), 1)
            sall[w, 0:8, :] = jnp.where(lane < rows, turned[:, :128], 0.0)
            for r in range(3):
                sall[w, 8 + r : 9 + r, :] = dbias[:, pl.ds(w * 384 + r * 128, 128)]
        sends.start(None, lambda: copy(sall, ssib, sm_s.at[0], sm_r.at[0], near))

    def small_x():
        wait(None, ssib, sm_r.at[0])
        ssib[...] = sall[...] + ssib[...]
        sends.start(None, lambda: copy(ssib, sx, sm_s.at[1], sm_r.at[1], over))

    w = z * 2 + y

    def peer(k):
        return lax.rem(w + k, 8)

    def small_y():
        wait(None, sx, sm_r.at[1])
        sall2[...] = ssib[...] + sx[...]
        for k in range(1, 8):
            sends.start(None, lambda k=k: copy(sall2.at[peer(k)], sy.at[w], sm_s.at[1 + k], sy_r.at[w], (peer(k), x * 2 + c)))
        sy[w] = sall2[w]

    def small_add():
        for k in range(1, 8):
            wait(None, sy.at[peer(k)], sy_r.at[peer(k)])
        value = sy[0]
        for k in range(1, 8):
            value = value + sy[k]
        small_out[...] = value

    def square_sum():
        value = small_out[...]
        squares = value * value
        for p in range(3):
            def body(i, sums):
                v = f32(out[p, pl.ds(pl.multiple_of(i * 16, 16), 16), :])
                v = v * v
                for k in range(v.shape[1] // 128):
                    sums = sums + v[:, k * 128 : (k + 1) * 128]
                return sums

            squares = lax.fori_loop(0, rows // 16, body, squares)
        norms[w] = jnp.full((8, 128), jnp.sum(squares), jnp.float32)
        for k in range(1, 8):
            sends.start(None, lambda k=k: copy(norms.at[w], norms.at[w], n_s.at[k], n_r.at[w], (peer(k), x * 2 + c)))
        for k in range(1, 8):
            wait(None, norms.at[peer(k)], n_r.at[peer(k)])
        whole = norms[0]
        for k in range(1, 8):
            whole = whole + norms[k]
        norm_out[...] = jnp.sqrt(whole)

    moves = {
        "add_x": add_x, "add_y": add_y, "line": line, "owner": owner, "middle_x": middle_x, "relay": relay, "arrived": arrived,
        "grads": lambda p, zz: grads(p, zz, dupper), "attention_grads": lambda zz: attention_grads(zz),
    }
    small_moves = {("add_y", 1, 0): small_y, ("owner", 1): small_add}

    def run(steps):
        for name, *rest in steps:
            moves[name](*rest)
            small_moves.get((name, *rest), lambda: None)()

    def looped(n, body, table):
        @pl.loop(0, n)
        def _(i):
            body(i)
            for k in sorted(table):
                pl.when(i == k)(lambda k=k: run(table[k]))

    tile = total // 256
    f = jnp.float32
    v = pltpu.VMEM

    def compute(*refs):
        nonlocal left, right, dhid, dpre, dmix, dkv, tokens_t, htile, ytile, ltile
        left, right, dhid, dpre, dmix, dkv, tokens_t, htile, ytile, ltile = refs
        transpose_into(dlow)
        for zz in ORDER:
            grads(0, zz, act_m)
        for k in range(4):
            upper_back(k)
        transpose_into(hid_m)
        hidden_back()
        for k in range(4):
            dup_copy(k).wait_recv()
        looped(seqs * 6, attend_back, BESIDE_ATTENTION)
        swap(dquery, 1)
        small_start()
        key_value_grads()
        small_x()
        run(BESIDE_KEYS)
        for make in swaps:
            make().wait_recv()
        attention_sides()
        masked_tokens()
        looped(tile, tokens_back, BESIDE_TOKENS)
        for i in range(tile - 2, tile):
            token_store(i).wait()
        tile_load(0).start()
        looped(tile * 4, feed_forward, BESIDE_FEED_FORWARD)
        for i in range(tile - 2, tile):
            layer_store(i).wait()

    pl.run_scoped(
        compute,
        v((2, width, count), LOW), v((2, count, width), LOW), v((count, width), f), v((count, width), f), v((count, width), LOW), v((2, total, width), LOW),
        v((width, total), LOW), v((2, 256, width), f), v((256, width), f), v((2, 256, width), LOW),
    )
    run(LAST)
    square_sum()
    for make in swaps:
        make().wait_send()
    for k in range(4):
        dup_copy(k).wait_send()


def step_kernel(rows, seqs, length, padded, *refs):
    refs = list(refs)

    def take(n):
        got, refs[:] = refs[:n], refs[n:]
        return got

    raw = take(10)
    layer_h, dtokens_h, out, small_out, norm_out, hidden_h = take(6)
    weights, (small_full, small_f, tokens, pick_t, kv, vec, qbias, bias) = take(3), take(8)
    masked = take(11)
    query_m, rows_m, mixed_m, hid_m, act_m, slope, dtwo, dlow, dvec, normed, inverse = masked
    sems = take(8)
    sends = Sends()
    forward_part(rows, seqs, length, padded, sends, *raw, hidden_h, *weights, small_full, small_f, tokens, pick_t, kv, vec, qbias, bias, *masked, *sems)
    backward_part(
        rows, seqs, length, padded, sends, *weights, vec, bias, kv, hidden_h, query_m, rows_m, mixed_m, hid_m, act_m, slope, dtwo, dlow, normed, inverse, dvec, pick_t, tokens,
        layer_h, dtokens_h, out, small_out, norm_out, *refs,
    )
    sends.finish()


def whole_step(qkv, out, up, down, vectors, up_bias, tokens, place_m, count_m, grad_m):
    rows, cols = up.shape
    out, down, grad_m = out.T, down.T, jnp.swapaxes(grad_m, 0, 1)
    total, width = tokens.shape
    seqs, slots = place_m.shape
    length = total // seqs
    padded = -(-slots // 16) * 16
    count = seqs * padded
    shape = jax.ShapeDtypeStruct
    f = jnp.float32
    anywhere = pl.BlockSpec(memory_space=pl.ANY)
    vm = pl.BlockSpec(memory_space=pltpu.VMEM)
    dma = pltpu.SemaphoreType.DMA
    v = pltpu.VMEM
    one = (16, 128)
    scratch = [
        v((width, cols), LOW), v((width, cols), LOW), v((width, cols), LOW),
        v((8,) + one, LOW), v(one, f), v((total, width), LOW), v((seqs, length, padded), LOW), v((2, total, width), LOW), v((8, width), f), v((3, 1, width), f), v((1, cols), f),
        v((count, width), LOW), v((2, count, width), LOW), v((2, count, width), LOW), v((2, count, width), LOW), v((2, count, cols), LOW),
        v((count, cols), f), v((count, width), f), v((2, count, width), LOW), v((8, width), f), v((count, width), f), v((count, 128), f),
        dma((6, 3, 8)), dma((3, 8, 3)), dma((8,)), dma((8,)), dma((5,)), dma((1,)), dma((5,)), dma((5,)),
        v((2, count, cols), LOW), v((1, cols), f), v((2, count, width), LOW), v((2, count, width), LOW), v((width, M), LOW),
        v((3, width, M), LOW), v((3, width, E), LOW), v((3, 4, rows, M), LOW), v((3, 5, rows, M), LOW), v((3, rows, M), LOW),
        v((8,) + one, f), v((8,) + one, f), v((8,) + one, f), v((8,) + one, f), v((8,) + one, f), v((8, 8, 128), f),
        dma((2,)), dma((4,)), dma((2,)), dma((2,)), dma((4,)), dma((4,)), dma((4,)), dma((4,)), dma((3, 4)), dma((3, 4)), dma((3, 4)), dma((3, 4)),
        dma((2, 3, 4)), dma((2, 3, 4)), dma((3,)), dma((3,)), dma((3, 3)), dma((3, 3)), dma((9,)), dma((2,)), dma((8,)), dma((8,)), dma((8,)),
    ]
    return pl.pallas_call(
        functools.partial(step_kernel, rows, seqs, length, padded),
        out_shape=(shape((total, width), LOW), shape((total, width), f), shape((3, rows, cols), LOW), shape(one, f), shape((8, 128), f), shape((total, width), f)),
        in_specs=[anywhere] * 4 + [vm] * 2 + [anywhere, vm, pl.BlockSpec(memory_space=pltpu.SMEM), vm],
        out_specs=(anywhere, anywhere, vm, vm, vm, anywhere),
        scratch_shapes=scratch,
        compiler_params=pltpu.CompilerParams(collective_id=0, has_side_effects=True, vmem_limit_bytes=64 * 2**20 - 2**16),
    )(qkv, out, up, down, vectors, up_bias, tokens, place_m, count_m, grad_m)[:5]


def adam_kernel(layer, dtokens, norm, own, small, *refs):
    weights, firsts, seconds = refs[0:6], refs[6:12], refs[12:18]
    outs = refs[18:36]
    layer_o, dtokens_o, norm_o, layer_v, dtokens_v, sem = refs[36:]
    step_id = pl.program_id(0)
    copies_in = [pltpu.make_async_copy(layer, layer_v, sem.at[0]), pltpu.make_async_copy(dtokens, dtokens_v, sem.at[1])]
    copies_out = [pltpu.make_async_copy(layer_v, layer_o, sem.at[2]), pltpu.make_async_copy(dtokens_v, dtokens_o, sem.at[3])]

    @pl.when(step_id == 0)
    def _():
        for copy in copies_in:
            copy.start()
        norm_o[0, 0] = jnp.max(norm[...])

    @pl.when(step_id == 2)
    def _():
        for first, then in zip(copies_in, copies_out):
            first.wait()
            then.start()

    factor = CLIP_LIMIT / jnp.maximum(norm[0:1, 0:1], CLIP_LIMIT)

    def step(k, where, grad, decay, rate):
        grad = grad * factor.reshape((1,) * grad.ndim)
        weight = weights[k][where]
        first = BETA_ONE * firsts[k][where] + (1.0 - BETA_ONE) * grad
        second = BETA_TWO * seconds[k][where] + (1.0 - BETA_TWO) * grad * grad
        mean_hat = first * (1.0 / (1.0 - BETA_ONE**STEP))
        square_hat = second * (1.0 / (1.0 - BETA_TWO**STEP))
        outs[3 * k][where] = weight - rate * (mean_hat / (jnp.sqrt(square_hat) + ADAM_EPS) + decay * weight)
        outs[3 * k + 1][where] = first
        outs[3 * k + 2][where] = second

    width = weights[1].shape[1]
    for k in range(3):
        step(0, (k,), f32(own[2, :, pl.ds(k * width, width)]), DECAY_RATE, LEARN_RATE)
    everything = (slice(None), slice(None))
    step(1, everything, f32(own[2, :, pl.ds(3 * width, width)]), DECAY_RATE, OUTPUT_RATE)
    for k in range(4):
        cols = (slice(None), pl.ds(k * width, width))
        step(2, cols, f32(own[1, :, pl.ds(k * width, width)]), DECAY_RATE, LEARN_RATE)
        step(3, cols, f32(own[0, :, pl.ds(k * width, width)]), DECAY_RATE, LEARN_RATE)

    @pl.when(step_id == pl.num_programs(0) - 1)
    def _():
        for copy in copies_out:
            copy.wait()

    @pl.when(step_id == 0)
    def _():
        lanes = weights[4].shape[1]
        step(4, everything, small[0:8, 0:lanes], 0.0, VECTOR_RATE)
        step(5, everything, small[8:11, :], 0.0, BIAS_RATE)


def adam(layer, dtokens, norm, own, small, weights, moments):
    def turn(values):
        a, b, c, d, e, g = values
        return a, b.T, c, d.T, e, g.reshape(3, 128)

    arrays = turn(weights) + turn([m[0] for m in moments]) + turn([m[1] for m in moments])
    rows, cols = arrays[2].shape
    width = cols // 4
    slab = 16
    anywhere = pl.BlockSpec(memory_space=pl.ANY)
    specs = [
        pl.BlockSpec((3, slab, width), lambda i: (0, i, 0)),
        pl.BlockSpec((slab, width), lambda i: (i, 0)),
        pl.BlockSpec((slab, cols), lambda i: (i, 0)),
        pl.BlockSpec((slab, cols), lambda i: (i, 0)),
        pl.BlockSpec(arrays[4].shape, lambda i: (0, 0)),
        pl.BlockSpec(arrays[5].shape, lambda i: (0, 0)),
    ]
    outs = pl.pallas_call(
        adam_kernel,
        grid=(rows // slab,),
        out_shape=tuple(jax.ShapeDtypeStruct(a.shape, a.dtype) for a in arrays[:6] for _ in range(3))
        + (jax.ShapeDtypeStruct(layer.shape, layer.dtype), jax.ShapeDtypeStruct(dtokens.shape, dtokens.dtype), jax.ShapeDtypeStruct((1, 1), jnp.float32)),
        in_specs=[
            anywhere,
            anywhere,
            pl.BlockSpec(norm.shape, lambda i: (0, 0)),
            pl.BlockSpec((3, slab, cols), lambda i: (0, i, 0)),
            pl.BlockSpec(small.shape, lambda i: (0, 0)),
        ] + specs * 3,
        out_specs=tuple(s for s in specs for _ in range(3)) + (anywhere, anywhere, pl.BlockSpec(memory_space=pltpu.SMEM)),
        scratch_shapes=[pltpu.VMEM(layer.shape, layer.dtype), pltpu.VMEM(dtokens.shape, dtokens.dtype), pltpu.SemaphoreType.DMA((4,))],
        compiler_params=pltpu.CompilerParams(vmem_limit_bytes=64 * 2**20 - 2**16),
    )(layer, dtokens, norm, own, small, *arrays)

    def back(k, v):
        return v.T if k in (1, 3) else v.reshape(-1) if k == 5 else v

    return (outs[18], outs[19], outs[20].reshape(())) + tuple(back(i // 3, v) for i, v in enumerate(outs[:18]))


def masks(mask_place, mask_count, gradient, length):
    seqs, slots = mask_place.shape
    padded = -(-slots // 16) * 16
    live = jnp.arange(padded)[None, :] < mask_count[:, None]
    spots = jnp.pad(mask_place, ((0, 0), (0, padded - slots)), constant_values=-1)
    pick = (spots[:, :, None] == jnp.arange(length)[None, None, :]) & live[:, :, None]
    gradient = jnp.pad(gradient, ((0, 0), (0, padded - slots), (0, 0)))
    gradient = jnp.where(live[:, :, None], gradient, jnp.zeros_like(gradient))
    return pick, gradient.reshape(seqs * padded, -1)


def update(weights, moments, grads, grad_norm):
    factor = CLIP_LIMIT / jnp.maximum(grad_norm, CLIP_LIMIT)
    rates = (LEARN_RATE, OUTPUT_RATE, LEARN_RATE, LEARN_RATE, VECTOR_RATE, BIAS_RATE)
    out = ()
    for k in range(6):
        out += adam_step(weights[k], *moments[k], grads[k], factor, DECAY_RATE if k < 4 else 0.0, rates[k])
    return out


def natural(own_attn, own_up, own_down, own_vectors, own_bias):
    width = own_up.shape[1] // 4
    own_qkv = jnp.swapaxes(own_attn[:, : 3 * width].reshape(-1, 3, width), 0, 1)
    return own_qkv, own_attn[:, 3 * width :].T, own_up, own_down.T, own_vectors, own_bias


def pack(qkv, out, up, down):
    attn = jnp.concatenate([qkv[0], qkv[1], qkv[2], out.T], axis=1)
    return attn.astype(jnp.bfloat16), up.astype(jnp.bfloat16), down.T.astype(jnp.bfloat16)


def plain(tokens, mask_place, mask_count, gradient, weights, moments):
    low = jnp.bfloat16
    seqs, length, width = tokens.shape
    pick, gradient = masks(mask_place, mask_count, gradient, length)
    padded = pick.shape[1]
    flat = tokens.reshape(seqs * length, width)
    attn_w, up_w, down_w = (lax.all_gather(v, "wide", axis=0, tiled=True) for v in pack(*weights[:4]))
    vec = lax.all_gather(weights[4].astype(low), "wide", axis=1, tiled=True).astype(jnp.float32)
    bias = lax.all_gather(weights[5].astype(low), "wide", axis=0, tiled=True).astype(jnp.float32)
    wq, wk, wv, wo = (attn_w[:, k * width : (k + 1) * width] for k in range(4))
    query = (mm(flat, wq, NN) + vec[0]).astype(low)
    key = mm(flat, wk, NN, low)
    value = (mm(flat, wv, NN) + vec[1]).astype(low)
    query, key, value = (split_heads(v, seqs, length) for v in (query, key, value))
    mixed = lax.map(attend, (query, key, value)).reshape(seqs * length, width)

    def middle(rows, mixed):
        pre_one = rows.astype(jnp.float32) + (mm(mixed, wo, NT) + vec[2])
        hidden, normed, inverse = layer_norm(pre_one, vec[3], vec[4])
        hidden_low = hidden.astype(low)
        upper = mm(hidden_low, up_w, NN) + bias
        cumul = 0.5 * (1.0 + lax.erf(upper * SQRT_HALF))
        active = (upper * cumul).astype(low)
        pre_two = hidden + (mm(active, down_w, NT) + vec[5])
        return layer_norm(pre_two, vec[6], vec[7]), normed, inverse, hidden_low, upper, cumul, active

    layer_out = middle(flat, mixed)[0][0].astype(low)
    pick_low = pick.astype(low)

    def take(values):
        values = values.reshape(seqs, length, width)
        return jnp.einsum("sil,sld->sid", pick_low, values, preferred_element_type=jnp.float32).astype(low)

    rows_m = take(flat).reshape(seqs * padded, width)
    mixed_m = take(mixed).reshape(seqs * padded, width)
    query_m = split_heads(take(query), seqs, padded)
    (_, normed_two, inverse_two), normed_one, inverse_one, hidden_m, upper, cumul, active = middle(rows_m, mixed_m)
    dpre_two, dgain_two, dshift_two = norm_back(gradient.astype(jnp.float32), normed_two, inverse_two, vec[6])
    dbias_two = jnp.sum(dpre_two, axis=0)
    dtwo_low = dpre_two.astype(low)
    ddown = mm(dtwo_low, active, TN)
    dactive = mm(dtwo_low, down_w, NN)
    density = jnp.exp(-0.5 * upper * upper) * INV_ROOT_TWO_PI
    dupper = dactive * (cumul + upper * density)
    dup_bias = jnp.sum(dupper, axis=0)
    dupper_low = dupper.astype(low)
    dup = mm(hidden_m, dupper_low, TN)
    dhidden = dpre_two + mm(dupper_low, up_w, NT)
    dpre_one, dgain_one, dshift_one = norm_back(dhidden, normed_one, inverse_one, vec[3])
    dbias_out = jnp.sum(dpre_one, axis=0)
    done_low = dpre_one.astype(low)
    dout = mm(done_low, mixed_m, TN)
    dmixed = split_heads(mm(done_low, wo, NN, low), seqs, padded)
    dquery, dkey, dvalue = lax.map(attend_back, (query_m, key, value, dmixed))
    dquery = dquery.reshape(seqs * padded, width)
    dkey = dkey.reshape(seqs * length, width)
    dvalue = dvalue.reshape(seqs * length, width)
    dbias_query = jnp.sum(dquery, axis=0)
    dbias_value = jnp.sum(dvalue, axis=0)
    dquery, dkey, dvalue = dquery.astype(low), dkey.astype(low), dvalue.astype(low)
    dattn = jnp.concatenate([mm(rows_m, dquery, TN), mm(flat, dkey, TN), mm(flat, dvalue, TN), dout], axis=1)
    masked_part = dpre_one + mm(dquery, wq, NT)
    dtokens = spread(pick, masked_part) + mm(dkey, wk, NT) + mm(dvalue, wv, NT)
    dvectors = jnp.stack(
        [dbias_query, dbias_value, dbias_out, dgain_one, dshift_one, dbias_two, dgain_two, dshift_two]
    )

    def owned(value, dim):
        return lax.psum(lax.psum_scatter(value, "wide", scatter_dimension=dim, tiled=True), "narrow")

    grads = (owned(dattn, 0), owned(dup, 0), owned(ddown, 0), owned(dvectors, 1), owned(dup_bias, 0))
    grad_norm = jnp.sqrt(lax.psum(sum(jnp.sum(v * v) for v in grads), "wide"))
    return (layer_out, dtokens, grad_norm) + update(weights, moments, natural(*grads), grad_norm)


def spread(pick, rows):
    seqs, padded, length = pick.shape
    return jnp.einsum(
        "sil,sid->sld",
        pick.astype(jnp.float32),
        rows.reshape(seqs, padded, -1),
        precision=lax.Precision.HIGHEST,
        preferred_element_type=jnp.float32,
    ).reshape(seqs * length, -1)


def tailored(tokens, mask_place, mask_count, gradient, weights, moments):
    seqs, length, width = tokens.shape
    flat = tokens.reshape(seqs * length, width)
    layer_out, dtokens, own, small, grad_norm = whole_step(*weights, flat, mask_place, mask_count, gradient)
    return adam(layer_out, dtokens, grad_norm, own, small, weights, moments)


def shards(body, tokens, mask_place, mask_count, masked_output_gradient, *parameters):
    seqs, length, width = tokens.shape
    weights = parameters[0::3]
    moments = tuple(zip(parameters[1::3], parameters[2::3]))
    layer_out, dtokens, *rest = body(tokens, mask_place, mask_count, masked_output_gradient, weights, moments)
    return (layer_out.reshape(seqs, length, width), dtokens.reshape(seqs, length, width), *rest)


def solution(mesh):
    body = tailored if mesh.shape["wide"] == 8 and mesh.shape["narrow"] == 4 else plain
    data = P(("wide", "narrow"))
    rows = P("wide")
    columns = P(None, "wide")
    weights = (columns,) * 6 + (rows,) * 3 + (columns,) * 6 + (rows,) * 3
    return jax.shard_map(
        functools.partial(shards, body),
        mesh=mesh,
        in_specs=(data,) * 4 + weights,
        out_specs=(data, data, P()) + weights,
        check_vma=False,
    )
```

```python
import functools

import jax
import jax.numpy as jnp
from jax import lax
from jax.experimental import pallas as pl
from jax.experimental.pallas import tpu as pltpu
from jax.sharding import PartitionSpec as P

HEADS = 12
HEAD_DIM = 64
STEP = 10

LN_EPS = 1e-06
SQRT_HALF = 0.7071067811865476
INV_ROOT_TWO_PI = 0.3989422804014327
CLIP_LIMIT = 1.0
BETA_ONE = 0.9
BETA_TWO = 0.999
LEARN_RATE = 0.05
OUTPUT_RATE = 0.2
VECTOR_RATE = 0.5
BIAS_RATE = 0.3
DECAY_RATE = 0.01
ADAM_EPS = 1e-08

MESH = pl.DeviceIdType.MESH


def when(cond, body):
    if callable(cond):
        cond = cond()
    if cond is None:
        body()
    else:
        pl.when(cond)(body)


class Sends:
    def __init__(self):
        self.started = []

    def start(self, cond, make):
        when(cond, lambda: make().start())
        self.started.append((cond, make))

    def finish(self):
        for cond, make in self.started:
            when(cond, lambda make=make: make().wait_send())


def both(a, b):
    return b if a is None else (a if b is None else jnp.logical_and(a, b))


def place():
    w, n = lax.axis_index("wide"), lax.axis_index("narrow")
    return w // 2, lax.rem(w, 2), n // 2, lax.rem(n, 2)


def flip(v):
    return 1 - v


def dev(z, y, x, c):
    return (z * 2 + y, x * 2 + c)


def meet(z, y, x, c, diagonal):
    bar = pltpu.get_barrier_semaphore()
    peers = [(None, dev(z, flip(y), x, c)), (None, dev(z, y, flip(x), c)), (None, dev(z, y, x, flip(c)))]
    if diagonal:
        peers.append((None, dev(z, y, flip(x), flip(c))))
    peers += [(z > 0, dev(z - 1, y, x, c)), (z < 3, dev(z + 1, y, x, c))]
    for cond, peer in peers:
        when(cond, lambda peer=peer: pl.semaphore_signal(bar, inc=1, device_id=peer, device_id_type=MESH))
    inner = jnp.logical_and(z > 0, z < 3)
    count = 4 if diagonal else 3
    pl.semaphore_wait(bar, count + 1 + jnp.where(inner, 1, 0))


def gather_kernel(rows, cols, attn, up, down, small, attn_full, up_full, down_full, small_full, send_sem, recv_sem, small_send, small_recv, own_sem):
    z, y, x, c = place()
    edge = x == c
    third = cols // 3
    mine, across = x + c, 2 * flip(x)
    fulls = (attn_full, up_full, down_full)
    shards = (attn, up, down)
    sends = Sends()
    zl, zh = z > 0, z < 3

    def spot(p, zz, yy, t):
        return fulls[p].at[pl.ds(pl.multiple_of((zz * 2 + yy) * rows, rows), rows), pl.ds(pl.multiple_of(t * third, third), third)]

    def push(cond, p, zz, yy, t, kind, to, src=None):
        def make():
            w = zz * 2 + yy
            where = spot(p, zz, yy, t)
            return pltpu.make_async_remote_copy(
                src_ref=where if src is None else src,
                dst_ref=where,
                send_sem=send_sem.at[kind, p, w],
                recv_sem=recv_sem.at[p, w, t],
                device_id=to,
                device_id_type=MESH,
            )

        sends.start(cond, make)

    def small_push(cond, zz, yy, kind, to, src=None):
        def make():
            w = zz * 2 + yy
            where = small_full.at[w]
            return pltpu.make_async_remote_copy(
                src_ref=where if src is None else src,
                dst_ref=where,
                send_sem=small_send.at[kind, w],
                recv_sem=small_recv.at[w],
                device_id=to,
                device_id_type=MESH,
            )

        sends.start(cond, make)

    def arrive(cond, p, zz, yy, t):
        def body():
            where = spot(p, zz, yy, t)
            w = zz * 2 + yy
            pltpu.make_async_remote_copy(where, where, send_sem.at[0, p, w], recv_sem.at[p, w, t], dev(z, y, x, c), device_id_type=MESH).wait_recv()

        when(cond, body)

    def small_arrive(cond, zz, yy):
        def body():
            w = zz * 2 + yy
            pltpu.make_async_remote_copy(small_full.at[w], small_full.at[w], small_send.at[0, w], small_recv.at[w], dev(z, y, x, c), device_id_type=MESH).wait_recv()

        when(cond, body)

    UP, DOWN, SIDE, OVER, NEAR, PASS = range(6)
    above, below, beside = dev(z + 1, y, x, c), dev(z - 1, y, x, c), dev(z, flip(y), x, c)
    over, near = dev(z, y, flip(x), c), dev(z, y, x, flip(c))

    def own(p):
        src = shards[p].at[:, pl.ds(pl.multiple_of(mine * third, third), third)]
        push(zh, p, z, y, mine, UP, above, src)
        push(zl, p, z, y, mine, DOWN, below, src)
        push(None, p, z, y, mine, SIDE, beside, src)

    def z_step(p, d):
        for cond, zz, onward, kind, to in ((z - d >= 0, z - d, zh, UP, above), (z + d <= 3, z + d, zl, DOWN, below)):
            arrive(cond, p, zz, y, mine)
            push(both(cond, onward), p, zz, y, mine, kind, to)
            push(cond, p, zz, y, mine, SIDE, beside)
            push(both(cond, edge), p, zz, y, mine, OVER, over)
            push(cond, p, zz, y, mine, NEAR, near)

    def y_step(p, d):
        steps = ((None, z),) if d == 0 else ((z - d >= 0, z - d), (z + d <= 3, z + d))
        for cond, zz in steps:
            arrive(cond, p, zz, flip(y), mine)
            push(both(cond, edge), p, zz, flip(y), mine, OVER, over)
            push(cond, p, zz, flip(y), mine, NEAR, near)

    def x_step(p, d):
        mid = jnp.logical_not(edge)
        for yy in (y, flip(y)):
            if d == 0:
                steps = () if yy is y else ((None, z),)
            else:
                steps = ((z - d >= 0, z - d), (z + d <= 3, z + d))
            for cond, zz in steps:
                cond = both(cond, mid)
                arrive(cond, p, zz, yy, across)
                push(cond, p, zz, yy, across, PASS, near)

    def last(p, d):
        for yy in (y, flip(y)):
            if d == 0:
                steps = () if yy is y else ((None, z),)
            else:
                steps = ((z - d >= 0, z - d), (z + d <= 3, z + d))
            for cond, zz in steps:
                arrive(cond, p, zz, yy, x + flip(c))
                arrive(both(cond, edge), p, zz, yy, across)

    def small_z(d):
        for cond, zz, onward, kind, to in ((z - d >= 0, z - d, zh, UP, above), (z + d <= 3, z + d, zl, DOWN, below)):
            small_arrive(cond, zz, y)
            small_push(both(cond, onward), zz, y, kind, to)
            small_push(cond, zz, y, SIDE, beside)

    meet(z, y, x, c, False)
    small_push(zh, z, y, UP, above, small)
    small_push(zl, z, y, DOWN, below, small)
    small_push(None, z, y, SIDE, beside, small)
    own(0)
    w = z * 2 + y
    copies = []
    for p in range(3):
        copies.append(pltpu.make_async_copy(shards[p], fulls[p].at[pl.ds(pl.multiple_of(w * rows, rows), rows)], own_sem.at[p]))
    copies.append(pltpu.make_async_copy(small, small_full.at[w], own_sem.at[3]))
    for copy in copies:
        copy.start()
    for d in range(1, 4):
        small_z(d)
    order = [
        lambda: z_step(0, 1), lambda: own(1), lambda: y_step(0, 0), lambda: z_step(0, 2), lambda: y_step(0, 1), lambda: x_step(0, 0), lambda: z_step(0, 3),
        lambda: y_step(0, 2), lambda: x_step(0, 1), lambda: z_step(1, 1), lambda: own(2), lambda: y_step(0, 3), lambda: x_step(0, 2), lambda: z_step(1, 2), lambda: y_step(1, 0), lambda: x_step(0, 3), lambda: z_step(1, 3),
        lambda: y_step(1, 1), lambda: x_step(1, 0), lambda: z_step(2, 1), lambda: y_step(1, 2), lambda: x_step(1, 1), lambda: z_step(2, 2), lambda: y_step(1, 3), lambda: x_step(1, 2), lambda: z_step(2, 3),
        lambda: y_step(2, 0), lambda: x_step(1, 3), lambda: y_step(2, 1), lambda: x_step(2, 0), lambda: y_step(2, 2), lambda: x_step(2, 1), lambda: y_step(2, 3), lambda: x_step(2, 2), lambda: x_step(2, 3),
    ]
    for step in order:
        step()
    for d in range(4):
        for cond, zz in (((None, z),) if d == 0 else ((z - d >= 0, z - d), (z + d <= 3, z + d))):
            small_arrive(cond, zz, flip(y))
    for p in range(3):
        for d in range(4):
            last(p, d)
    sends.finish()
    for copy in copies:
        copy.wait()


def gather(attn, up, down, small):
    rows, cols = attn.shape
    full = jax.ShapeDtypeStruct((8 * rows, cols), attn.dtype)
    anywhere = pl.BlockSpec(memory_space=pl.ANY)
    return pl.pallas_call(
        functools.partial(gather_kernel, rows, cols),
        out_shape=(full, full, full, jax.ShapeDtypeStruct((8,) + small.shape, small.dtype)),
        in_specs=[anywhere] * 4,
        out_specs=(anywhere,) * 4,
        scratch_shapes=[
            pltpu.SemaphoreType.DMA((6, 3, 8)),
            pltpu.SemaphoreType.DMA((3, 8, 3)),
            pltpu.SemaphoreType.DMA((3, 8)),
            pltpu.SemaphoreType.DMA((8,)),
            pltpu.SemaphoreType.DMA((4,)),
        ],
        compiler_params=pltpu.CompilerParams(collective_id=0, has_side_effects=True),
    )(attn, up, down, small)


def layer_norm(values, gain, shift):
    center = values - jnp.mean(values, axis=-1, keepdims=True)
    inverse = lax.rsqrt(jnp.mean(center * center, axis=-1, keepdims=True) + LN_EPS)
    normed = center * inverse
    return (normed * gain + shift, normed, inverse)


def norm_back(incoming, normed, inverse, gain):
    dgain = jnp.sum(incoming * normed, axis=0)
    dshift = jnp.sum(incoming, axis=0)
    scaled = incoming * gain
    dvalues = inverse * (
        scaled
        - jnp.mean(scaled, axis=-1, keepdims=True)
        - normed * jnp.mean(scaled * normed, axis=-1, keepdims=True)
    )
    return (dvalues, dgain, dshift)


def mm(a, b, dims, out=jnp.float32):
    return lax.dot_general(a, b, (dims, ((), ())), preferred_element_type=jnp.float32).astype(out)


NN = ((1,), (0,))
NT = ((1,), (1,))
TN = ((0,), (0,))


def split_heads(values, seqs, length):
    return values.reshape(seqs, length, HEADS, HEAD_DIM)


def attend(pieces):
    query, key, value = pieces
    raw = jnp.einsum("qhe,khe->hqk", query, key, preferred_element_type=jnp.float32) * HEAD_DIM ** (
        -0.5
    )
    peak = jnp.max(raw, axis=-1, keepdims=True)
    expo = jnp.exp(raw - peak)
    total = jnp.sum(expo, axis=-1, keepdims=True)
    probs = (expo / total).astype(jnp.bfloat16)
    mixed = jnp.einsum("hqk,khe->qhe", probs, value, preferred_element_type=jnp.float32)
    return mixed.astype(jnp.bfloat16)


def attend_back(pieces):
    query, key, value, dmixed = pieces
    scale = HEAD_DIM ** (-0.5)
    raw = jnp.einsum("qhe,khe->hqk", query, key, preferred_element_type=jnp.float32) * scale
    probs = jax.nn.softmax(raw, axis=-1)
    dprobs = jnp.einsum("qhe,khe->hqk", dmixed, value, preferred_element_type=jnp.float32)
    dscore = probs * (dprobs - jnp.sum(dprobs * probs, axis=-1, keepdims=True))
    dscore = (dscore * scale).astype(jnp.bfloat16)
    dquery = jnp.einsum("hqk,khe->qhe", dscore, key, preferred_element_type=jnp.float32)
    dkey = jnp.einsum("hqk,qhe->khe", dscore, query, preferred_element_type=jnp.float32)
    dvalue = jnp.einsum(
        "hqk,qhe->khe", probs.astype(jnp.bfloat16), dmixed, preferred_element_type=jnp.float32
    )
    return (dquery, dkey, dvalue)


def adam_step(weight, first, second, grad, factor, decay, rate):
    grad = grad * factor
    first_new = BETA_ONE * first + (1.0 - BETA_ONE) * grad
    second_new = BETA_TWO * second + (1.0 - BETA_TWO) * grad * grad
    mean_hat = first_new / (1.0 - BETA_ONE**STEP)
    square_hat = second_new / (1.0 - BETA_TWO**STEP)
    weight_new = weight - rate * (mean_hat / (jnp.sqrt(square_hat) + ADAM_EPS) + decay * weight)
    return (weight_new, first_new, second_new)


GATHER_ORDER = (
    ("z_step", 0, 1),
    ("y_step", 0, 0),
    ("z_step", 0, 2),
    ("own", 1),
    ("y_step", 0, 1),
    ("x_step", 0, 0),
    ("y_step", 0, 2),
    ("z_step", 0, 3),
    ("y_step", 0, 3),
    ("z_step", 1, 1),
    ("x_step", 0, 2),
    ("x_step", 0, 1),
    ("y_step", 1, 0),
    ("vectors_in",),
    ("z_step", 1, 2),
    ("x_step", 0, 3),
    ("last", 0),
    ("loop", "project", 4, {0: (("own", 2),), 1: (("y_step", 1, 1),)}),
    ("z_step", 1, 3),
    ("loop", "attend", 12, {0: (("y_step", 1, 2),), 2: (("z_step", 2, 1),), 4: (("y_step", 2, 0),), 5: (("y_step", 1, 3),), 7: (("x_step", 1, 1), ("z_step", 2, 2),), 9: (("y_step", 2, 1),)}),
    ("z_step", 2, 3),
    ("loop", "middle", 4, {0: (("y_step", 2, 2), ("x_step", 1, 2), ("x_step", 1, 0),), 1: (("x_step", 1, 3),)}),
    ("masked",),
    ("y_step", 2, 3),
    ("x_step", 2, 0),
    ("last", 1),
    ("save_hidden",),
    ("loop", "upper", 4, {1: (("x_step", 2, 1),), 2: (("x_step", 2, 2), ("x_step", 2, 3),)}),
    ("last", 2),
)


def dot(a, b, dims):
    return lax.dot_general(a, b, (dims, ((), ())), preferred_element_type=jnp.float32)


NN = ((1,), (0,))
NT = ((1,), (1,))
TN = ((0,), (0,))
LOW = jnp.bfloat16


def norm(values, gain, shift):
    center = values - jnp.mean(values, axis=-1, keepdims=True)
    inverse = lax.rsqrt(jnp.mean(center * center, axis=-1, keepdims=True) + LN_EPS)
    normed = center * inverse
    return normed * gain + shift, normed, inverse


def norm_pull(incoming, normed, inverse, gain):
    dgain = jnp.sum(incoming * normed, axis=0, keepdims=True)
    dshift = jnp.sum(incoming, axis=0, keepdims=True)
    scaled = incoming * gain
    return (
        inverse * (scaled - jnp.mean(scaled, axis=-1, keepdims=True) - normed * jnp.mean(scaled * normed, axis=-1, keepdims=True)),
        dgain,
        dshift,
    )


def forward_part(
    rows, seqs, length, padded, sends,
    qkv_h, out_h, up_h, down_h, vectors, up_bias, tokens_h, place_m, count_m, grad_m, hidden_o,
    attn_full, up_full, down_full, small_full, small_f, tokens, pick_t, kv, vec, qbias, bias,
    query_m, rows_m, mixed_m, hid_m, act_m, slope, dtwo, dlow, dvec, normed_one, inverse_one,
    send_sem, recv_sem, small_send, small_recv, load_sem, save_sem, pair_send, pair_recv,
):
    qkv_f = out_f = up_f = down_f = queries = mixed = hidden = pick = ytwo = hid_f = grad = None
    z, y, x, c = place()
    width = tokens.shape[1]
    total = tokens.shape[0]
    cols = up_h.shape[1]
    edge = x == c
    third = cols // 3
    mine, across = x + c, 2 * flip(x)
    fulls = (attn_full, up_full, down_full)
    w = z * 2 + y
    mine_rows = pl.ds(pl.multiple_of(w * rows, 32), rows)
    zl, zh = z > 0, z < 3
    count = seqs * padded

    def spot(p, zz, yy, t):
        return fulls[p].at[pl.ds(pl.multiple_of((zz * 2 + yy) * rows, rows), rows), pl.ds(pl.multiple_of(t * third, third), third)]

    def push(cond, p, zz, yy, t, kind, to):
        def make():
            whose = zz * 2 + yy
            where = spot(p, zz, yy, t)
            return pltpu.make_async_remote_copy(
                src_ref=where,
                dst_ref=where,
                send_sem=send_sem.at[kind, p, whose],
                recv_sem=recv_sem.at[p, whose, t],
                device_id=to,
                device_id_type=MESH,
            )

        sends.start(cond, make)

    def arrive(cond, p, zz, yy, t):
        def body():
            where = spot(p, zz, yy, t)
            whose = zz * 2 + yy
            pltpu.make_async_remote_copy(where, where, send_sem.at[0, p, whose], recv_sem.at[p, whose, t], dev(z, y, x, c), device_id_type=MESH).wait_recv()

        when(cond, body)

    UP, DOWN, SIDE, OVER, NEAR, PASS = range(6)
    above, below, beside = dev(z + 1, y, x, c), dev(z - 1, y, x, c), dev(z, flip(y), x, c)
    over, near = dev(z, y, flip(x), c), dev(z, y, x, flip(c))

    other_y = flip(y)
    span = {d: ((z - d >= 0, z - d), (z + d <= 3, z + d)) for d in range(1, 4)}
    span[0] = ((None, z),)
    mid = jnp.logical_not(edge)

    def around(d):
        return span[d]

    def also(a, b):
        return lambda: both(a, b)

    def own(p):
        push(zh, p, z, y, mine, UP, above)
        push(zl, p, z, y, mine, DOWN, below)
        push(None, p, z, y, mine, SIDE, beside)

    def z_step(p, d):
        for (cond, zz), onward, kind, to in zip(span[d], (zh, zl), (UP, DOWN), (above, below)):
            arrive(cond, p, zz, y, mine)
            push(also(cond, onward), p, zz, y, mine, kind, to)
            push(also(cond, edge) if d == 1 else cond, p, zz, y, mine, SIDE, beside)
            push(also(cond, edge), p, zz, y, mine, OVER, over)
            push(cond, p, zz, y, mine, NEAR, near)

    def y_step(p, d):
        for cond, zz in around(d):
            arrive(cond, p, zz, other_y, mine)
            if d == 0:
                push(also(zh, mid), p, zz, other_y, mine, UP, above)
                push(also(zl, mid), p, zz, other_y, mine, DOWN, below)
            push(also(cond, edge), p, zz, other_y, mine, OVER, over)
            push(cond, p, zz, other_y, mine, NEAR, near)

    def x_step(p, d):
        for yy in (y, other_y):
            for cond, zz in () if d == 0 and yy is y else around(d):
                arrive(also(cond, mid), p, zz, yy, across)
                push(also(cond, mid), p, zz, yy, across, PASS, near)

    def last(p):
        for d in range(4):
            for yy in (y, other_y):
                for cond, zz in () if d == 0 and yy is y else around(d):
                    arrive(cond, p, zz, yy, x + flip(c))
                    arrive(both(cond, edge), p, zz, yy, across)

    saves = []

    def keep(src, dst, k):
        copy = pltpu.make_async_copy(src, dst, save_sem.at[k])
        copy.start()
        saves.append(copy)

    swaps = []

    def swap(ref, k):
        def make():
            return pltpu.make_async_remote_copy(ref.at[0], ref.at[1], pair_send.at[k], pair_recv.at[k], near, device_id_type=MESH)

        sends.start(None, make)
        swaps.append(make)

    def peer(k):
        return lax.rem(w + k, 8)

    def small_copy(k, whose):
        return pltpu.make_async_remote_copy(
            small_full.at[whose], small_full.at[whose], small_send.at[k], small_recv.at[whose], (peer(k), x * 2 + c), device_id_type=MESH
        )

    def small_out():
        small_f[...] = jnp.zeros_like(small_f)
        small_f[0:8, 0:rows] = vectors[...]
        for r in range(3):
            small_f[8 + r : 9 + r, :] = up_bias[pl.ds(r * 128, 128)].reshape(1, 128)
        small_full[w] = small_f[...].astype(LOW)
        for k in range(1, 8):
            sends.start(None, lambda k=k: small_copy(k, w))

    def attn_shard():
        loads[1].wait()
        loads[2].wait()
        for k in range(3):
            attn_full[mine_rows, pl.ds(k * width, width)] = qkv_f[k].astype(LOW)
        attn_full[mine_rows, pl.ds(3 * width, width)] = out_f[...].astype(LOW)

    def up_shard():
        loads[3].wait()
        up_full[mine_rows, :] = up_f[...].astype(LOW)

    def down_shard():
        loads[4].wait()
        down_full[mine_rows, :] = down_f[...].astype(LOW)

    def masks():
        slots = place_m.shape[1]
        for s in range(seqs):
            hit = lax.broadcasted_iota(jnp.int32, (length, slots), 0) == place_m[s : s + 1, :]
            live = lax.broadcasted_iota(jnp.int32, (length, slots), 1) < count_m[s]
            hit = jnp.logical_and(hit, live).astype(jnp.float32).astype(LOW)
            row = lax.broadcasted_iota(jnp.int32, (padded, slots), 0)
            slot = lax.broadcasted_iota(jnp.int32, (padded, slots), 1)
            same = (row == slot).astype(jnp.float32).astype(LOW)
            kept = jnp.logical_and(row == slot, slot < count_m[s]).astype(jnp.float32).astype(LOW)
            pick[s] = dot(same, hit, NT).astype(LOW)
            pick_t[s] = dot(hit, same, NT).astype(LOW)
            grad[pl.ds(s * padded, padded), :] = dot(kept, f32(grad_m[...])[:, s, :].astype(LOW), NN)

    def vectors_in():
        loads[0].wait()
        for k in range(1, 8):
            small_copy(k, peer(k)).wait_recv()
        at = lax.broadcasted_iota(jnp.int32, (128, width), 0)
        to = lax.broadcasted_iota(jnp.int32, (128, width), 1)
        total = jnp.zeros((16, width), jnp.float32)
        for k in range(8):
            place_k = jnp.logical_and(at + k * rows == to, at < rows).astype(jnp.float32).astype(LOW)
            total += dot(small_full[k], place_k, NN)
            for r in range(3):
                bias[:, pl.ds(k * 384 + r * 128, 128)] = small_full[k, 8 + r : 9 + r, :].astype(jnp.float32)
        vec[...] = total[:8]
        qbias[0] = total[0:1]
        qbias[1] = jnp.zeros((1, width), jnp.float32)
        qbias[2] = total[1:2]

    def tile(i):
        return pl.ds(pl.multiple_of(i * 256, 256), 256)

    def project(i):
        r = tile(i)
        for k in range(3):
            value = dot(tokens[r, :], attn_full[:, pl.ds(k * width, width)], NN) + qbias[k]
            if k == 0:
                queries[r, :] = (value * 0.125).astype(LOW)
            else:
                kv[k - 1, r, :] = value.astype(LOW)

    def attend(step):
        s, j = step // (width // 128), lax.rem(step, width // 128)
        lane = lax.broadcasted_iota(jnp.int32, (length, 128), 1) < 64
        cs = pl.ds(pl.multiple_of(j * 128, 128), 128)
        rs = pl.ds(pl.multiple_of(s * length, length), length)
        key, value = kv[0, rs, cs], kv[1, rs, cs]
        zero, one = jnp.zeros_like(key), jnp.ones_like(key)
        keys = (jnp.where(lane, key, zero), jnp.where(lane, zero, key))
        values = (jnp.where(lane, value, one), jnp.where(lane, one, value))
        for q in range(length // 256):
            r = pl.ds(pl.multiple_of(s * length + q * 256, 256), 256)
            query = queries[r, cs]
            parts = []
            for h in range(2):
                score = dot(query, keys[h], NT)
                expo = jnp.exp(score - jnp.max(score, axis=-1, keepdims=True))
                parts.append(dot(expo.astype(LOW), values[h], NN))
            left = lane[:256]
            top = jnp.where(left, parts[0], parts[1])
            under = pltpu.roll(jnp.where(left, parts[1], parts[0]), 64, 1)
            mixed[r, cs] = (top / under).astype(LOW)

    def middle(i):
        r = tile(i)
        pre = tokens[r, :].astype(jnp.float32) + (dot(mixed[r, :], attn_full[:, pl.ds(3 * width, width)], NT) + vec[2:3, :])
        hidden[r, :] = norm(pre, vec[3:4, :], vec[4:5, :])[0]

    def masked_rows():
        for s in range(seqs):
            r = pl.ds(s * padded, padded)
            rs = pl.ds(s * length, length)
            rows_m[0, r, :] = dot(pick[s], tokens[rs, :], NN).astype(LOW)
            mixed_m[0, r, :] = dot(pick[s], mixed[rs, :], NN).astype(LOW)
            query_m[r, :] = dot(pick[s], queries[rs, :], NN).astype(LOW)
        pre = rows_m[0].astype(jnp.float32) + (dot(mixed_m[0], attn_full[:, pl.ds(3 * width, width)], NT) + vec[2:3, :])
        value, normed, inverse = norm(pre, vec[3:4, :], vec[4:5, :])
        hid_f[...] = value
        hid_m[0] = value.astype(LOW)
        normed_one[...] = normed
        inverse_one[...] = jnp.broadcast_to(inverse, inverse_one.shape)
        swap(rows_m, 0)
        swap(mixed_m, 1)
        swap(hid_m, 2)

    def upper(k):
        f = pl.ds(pl.multiple_of(k * 768, 768), 768)
        u = dot(hid_m[0], up_full[:, f], NN) + bias[:, f]
        cumul = 0.5 * (1.0 + lax.erf(u * SQRT_HALF))
        act_m[0, :, f] = (u * cumul).astype(LOW)
        slope[:, f] = cumul + u * (jnp.exp(-0.5 * u * u) * INV_ROOT_TWO_PI)

    def after_upper():
        swap(act_m, 3)

    def lower():
        for k in range(3):
            n = pl.ds(k * 256, 256)
            ytwo[:, n] = dot(act_m[0], down_full[n, :], NT)

        pre = hid_f[...] + (ytwo[...] + vec[5:6, :])
        _, normed, inverse = norm(pre, vec[6:7, :], vec[7:8, :])
        value, dgain, dshift = norm_pull(grad[...], normed, inverse, vec[6:7, :])
        dtwo[...] = value
        dlow[0] = value.astype(LOW)
        dvec[...] = jnp.zeros_like(dvec)
        dvec[5:6, :] = jnp.sum(value, axis=0, keepdims=True)
        dvec[6:7, :] = dgain
        dvec[7:8, :] = dshift
        swap(dlow, 4)

    loads = [pltpu.make_async_copy(tokens_h, tokens, load_sem.at[4])]
    loads[0].start()

    def prepare(*refs):
        nonlocal qkv_f, out_f, up_f, down_f
        qkv_f, out_f, up_f, down_f = refs
        for k, src in enumerate((qkv_h, out_h, up_h, down_h)):
            loads.append(pltpu.make_async_copy(src, refs[k], load_sem.at[k]))
            loads[-1].start()
        bar = pltpu.get_barrier_semaphore()
        for to in [near, over, dev(z, y, flip(x), flip(c))] + [(peer(k), x * 2 + c) for k in range(1, 8)]:
            pl.semaphore_signal(bar, inc=1, device_id=to, device_id_type=MESH)
        attn_shard()
        pl.semaphore_wait(bar, 10)
        own(0)
        small_out()
        up_shard()
        down_shard()

    f = jnp.float32
    v = pltpu.VMEM
    pl.run_scoped(prepare, v(qkv_h.shape, f), v(out_h.shape, f), v(up_h.shape, f), v(down_h.shape, f))

    def save_hidden():
        keep(hidden, hidden_o, 0)

    steps = {
        "z_step": z_step, "y_step": y_step, "x_step": x_step, "own": own, "last": last, "vectors_in": vectors_in,
        "masked": masked_rows, "save_hidden": save_hidden,
    }
    pieces = {"project": project, "attend": attend, "middle": middle, "upper": upper}

    def perform(plan):
        for name, *rest in plan:
            if name == "loop":
                piece, n, table = rest

                @pl.loop(0, n)
                def _(i):
                    pieces[piece](i)
                    for k in sorted(table):
                        pl.when(i == k)(lambda k=k: perform(table[k]))
            else:
                steps[name](*rest)

    def run(*refs):
        nonlocal queries, mixed, hidden, pick, ytwo, hid_f, grad
        queries, mixed, hidden, pick, ytwo, hid_f, grad = refs
        masks()
        perform(GATHER_ORDER)
        after_upper()
        lower()
        for make in swaps:
            make().wait_recv()
        for copy in saves:
            copy.wait()

    pl.run_scoped(
        run, v((total, width), LOW), v((total, width), LOW), v((total, width), f), v((seqs, padded, length), LOW), v((count, width), f), v((count, width), f), v((count, width), f)
    )


E = 768
M = 1536
SLAB = 32
ORDER = (0, 1, 2, 3)
BESIDE_ATTENTION = {0: (("add_x", 0, 0),), 4: (("add_x", 0, 1),), 7: (("grads", 1, 0), ("add_x", 0, 2), ("grads", 1, 3),), 9: (("grads", 1, 1), ("add_y", 0, 0), ("line", 0, 0),), 10: (("grads", 1, 2),)}
BESIDE_KEYS = (("add_y", 0, 1), ("line", 0, 1), ("add_x", 1, 0), ("add_x", 1, 1), ("add_y", 0, 2), ("line", 0, 2),)
BESIDE_TOKENS = {1: (("add_x", 0, 3), ("attention_grads", 0), ("add_x", 2, 0), ("add_x", 1, 2),), 2: (("add_y", 1, 0), ("line", 1, 0),), 3: (("add_y", 1, 1), ("attention_grads", 1),)}
BESIDE_FEED_FORWARD = {0: (("line", 1, 1),), 3: (("add_x", 2, 1),), 5: (("add_y", 0, 3), ("add_x", 1, 3), ("add_y", 2, 0), ("line", 2, 0), ("add_y", 1, 2),), 6: (("line", 1, 2), ("attention_grads", 2),), 7: (("add_y", 2, 1),), 8: (("attention_grads", 3), ("add_x", 2, 2), ("line", 2, 1), ("owner", 0), ("add_y", 1, 3), ("add_x", 2, 3),), 10: (("owner", 1),), 11: (("add_y", 2, 2), ("line", 2, 2),), 12: (("add_y", 2, 3), ("middle_x", 0), ("owner", 2), ("relay", 1), ("middle_x", 1), ("arrived", 1),), 13: (("relay", 0), ("arrived", 0),), 14: (("middle_x", 2),)}
LAST = (("relay", 2), ("arrived", 2),)


def slabs(rows, body):
    @pl.loop(0, rows // SLAB)
    def _(i):
        body(pl.multiple_of(i * SLAB, SLAB))


def f32(v):
    return v.astype(jnp.float32)


def backward_part(
    rows, seqs, length, padded, sends,
    attn, up, down, vec, bias, kv, hidden_h, query_m, rows_m, mixed_m, hid_m, act_m, slope, dtwo, dlow, normed, inverse, dvec, pick_t, tokens,
    layer_h, dtokens_h, out, small_out, norm_out,
    dupper, dbias, done, dquery, part,
    acc, xb, yr, zr, mr,
    sall, sall2, ssib, sx, sy, norms, squares,
    tile_sem, out_sem, pair_s, pair_r, dup_s, dup_r, sib_s, sib_r, x_s, x_r, y_s, y_r, z_s, z_r, m_s, m_r, f_s, f_r, sm_s, sm_r, sy_r, n_s, n_r,
):
    left = right = dhid = dpre = dmix = dkv = tokens_t = htile = ytile = ltile = None
    z, y, x, c = place()
    edge = x == c
    mid = jnp.logical_not(edge)
    width = E
    count = seqs * padded
    total = seqs * length
    pair = rows * 2
    me = dev(z, y, x, c)
    above, below, beside = dev(z + 1, y, x, c), dev(z - 1, y, x, c), dev(z, flip(y), x, c)
    over, near, diag = dev(z, y, flip(x), c), dev(z, y, x, flip(c)), dev(z, y, flip(x), flip(c))
    ecol = pl.multiple_of(x * 2304, 768)
    ocol = pl.multiple_of(flip(x) * 2304, 768)

    def copy(src, dst, ss, rs, to):
        return pltpu.make_async_remote_copy(src_ref=src, dst_ref=dst, send_sem=ss, recv_sem=rs, device_id=to, device_id_type=MESH)

    def wait(cond, dst, rs):
        when(cond, lambda: copy(dst, dst, rs, rs, me).wait_recv())

    def turn(k):
        picks = ((3, 3, 0, 0), (2, 0, 3, 1), (1, 2, 1, 2), (0, 1, 2, 3))[k]
        value = jnp.int32(picks[0])
        for zv in range(1, 4):
            value = jnp.where(z == zv, picks[zv], value)
        return value

    def zrows(k):
        return pl.ds(pl.multiple_of(turn(k) * pair, pair), pair)

    def wrows(zz, yy):
        return pl.ds(pl.multiple_of((zz * 2 + yy) * rows, rows), rows)

    def add_x(p, zz):
        @pl.when(edge)
        def _():
            wait(None, xb.at[p, zrows(zz)], x_r.at[p, zz])

            base = turn(zz) * pair

            def one(i):
                r = pl.ds(pl.multiple_of(base + i, SLAB), SLAB)
                acc[p, r, pl.ds(0, E)] = (f32(acc[p, r, pl.ds(0, E)]) + f32(xb[p, r, :])).astype(LOW)

            slabs(pair, one)

        push_y(edge, p, zz, E)

    def push_x(p, zz):
        sends.start(mid, lambda: copy(xb.at[p, zrows(zz)], xb.at[p, zrows(zz)], x_s.at[p, zz], x_r.at[p, zz], over))

    def push_y(cond, p, zz, wide):
        sends.start(cond, lambda: copy(
            acc.at[p, wrows(turn(zz), flip(y)), pl.ds(0, wide)], yr.at[p, zz, :, pl.ds(0, wide)], y_s.at[p, zz], y_r.at[p, zz], beside))

    def add_into(cond, p, zz, buffer, slot, sem):
        for role, wide in ((edge, E), (mid, M)):
            @pl.when(both(cond, role))
            def _():
                wait(None, buffer.at[p, slot, :, pl.ds(0, wide)], sem)
                base = (zz * 2 + y) * rows

                def one(i):
                    here = pl.ds(pl.multiple_of(base + i, SLAB), SLAB)
                    acc[p, here, pl.ds(0, wide)] = (f32(acc[p, here, pl.ds(0, wide)]) + f32(buffer[p, slot, pl.ds(i, SLAB), pl.ds(0, wide)])).astype(LOW)

                slabs(rows, one)

    def add_y(p, zz):
        add_into(None, p, turn(zz), yr, zz, y_r.at[p, zz])

    def z_push(cond, p, spot, k, to):
        for role, wide in ((edge, E), (mid, M)):
            def make(wide=wide):
                zz, slot = spot()
                return copy(acc.at[p, wrows(zz, y), pl.ds(0, wide)], zr.at[p, slot, :, pl.ds(0, wide)], z_s.at[k, p, zz], z_r.at[k, p, zz], to)

            sends.start(lambda role=role: both(cond(), role), make)

    def line(p, t):
        def upward():
            return both(z <= t, z < 3)

        def up_spot():
            zz = jnp.where(upward(), 3 + z - t, 0)
            return zz, zz

        def downward():
            return both(3 - z <= t, z > 0)

        def down_spot():
            zz = jnp.where(downward(), z + t - 3, 0)
            return zz, jnp.where(zz == z - 1, 4, zz)

        zz = up_spot()[0]
        add_into(both(upward(), z > 0), p, zz, zr, zz, z_r.at[0, p, zz])
        z_push(upward, p, up_spot, 0, above)
        zz = down_spot()[0]
        add_into(both(downward(), z < 3), p, zz, zr, zz, z_r.at[1, p, zz])
        z_push(downward, p, down_spot, 1, below)

    def owner(p):
        add_into(z > 0, p, z, zr, z, z_r.at[0, p, z])
        add_into(z < 3, p, z, zr, 4, z_r.at[1, p, z])
        sends.start(mid, lambda: copy(acc.at[p, wrows(z, y)], mr.at[p], m_s.at[p], m_r.at[p], diag))
        base = (z * 2 + y) * rows

        @pl.when(edge)
        def _():
            def one(i):
                out[p, pl.ds(i, SLAB), pl.ds(ecol, E)] = acc[p, pl.ds(pl.multiple_of(base + i, SLAB), SLAB), pl.ds(0, E)]

            slabs(rows, one)

        for k, to in enumerate((near, over)):
            sends.start(edge, lambda k=k, to=to: copy(
                out.at[p, :, pl.ds(ecol, E)], out.at[p, :, pl.ds(ecol, E)], f_s.at[p, k], f_r.at[p, x], to))

    def middle_x(p):
        base = (z * 2 + y) * rows

        @pl.when(mid)
        def _():
            wait(None, mr.at[p], m_r.at[p])

            def one(i):
                out[p, pl.ds(i, SLAB), pl.ds(E, M)] = (f32(acc[p, pl.ds(pl.multiple_of(base + i, SLAB), SLAB), :]) + f32(mr[p, pl.ds(i, SLAB), :])).astype(LOW)

            slabs(rows, one)

        sends.start(mid, lambda: copy(out.at[p, :, pl.ds(E, M)], out.at[p, :, pl.ds(E, M)], f_s.at[p, 0], f_r.at[p, 2], near))

    def relay(p):
        wait(mid, out.at[p, :, pl.ds(ocol, E)], f_r.at[p, flip(x)])
        sends.start(mid, lambda: copy(out.at[p, :, pl.ds(ocol, E)], out.at[p, :, pl.ds(ocol, E)], f_s.at[p, 1], f_r.at[p, flip(x)], near))

    def arrived(p):
        wait(edge, out.at[p, :, pl.ds(ocol, E)], f_r.at[p, flip(x)])
        wait(mid, out.at[p, :, pl.ds(ecol, E)], f_r.at[p, x])
        wait(edge, out.at[p, :, pl.ds(E, M)], f_r.at[p, 2])

        def body(i, sums):
            v = f32(out[p, pl.ds(pl.multiple_of(i * 16, 16), 16), :])
            v = v * v
            for k in range(v.shape[1] // 128):
                sums = sums + v[:, k * 128 : (k + 1) * 128]
            return sums

        squares[...] = lax.fori_loop(0, rows // 16, body, squares[...])

    swaps = []

    def swap(ref, k):
        def make():
            return copy(ref.at[0], ref.at[1], pair_s.at[k], pair_r.at[k], near)

        make().start()
        swaps.append(make)

    def transpose_into(ref):
        for k in range(2):
            left[k] = ref[k].T

    def product(zz, ref, cols):
        return (dot(left[0, zrows(zz), :], ref[0, :, cols], NN) + dot(left[1, zrows(zz), :], ref[1, :, cols], NN)).astype(LOW)

    def grads(p, zz, ref):
        @pl.when(mid)
        def _():
            xb[p, zrows(zz), :] = product(zz, ref, pl.ds(ocol, E))

        push_x(p, zz)

        @pl.when(mid)
        def _():
            for k in range(2):
                acc[p, zrows(zz), pl.ds(k * E, E)] = product(zz, ref, pl.ds(E + k * E, E))

        push_y(mid, p, zz, M)

        @pl.when(edge)
        def _():
            acc[p, zrows(zz), pl.ds(0, E)] = product(zz, ref, pl.ds(ecol, E))

    def dup_copy(k):
        f = pl.ds(k * 768, 768)
        return copy(dupper.at[0, :, f], dupper.at[1, :, f], dup_s.at[k], dup_r.at[k], near)

    def upper_back(k):
        f = pl.ds(k * 768, 768)
        value = dot(dlow[0], down[:, f], NN) * slope[:, f]
        dbias[:, f] = jnp.sum(value, axis=0, keepdims=True)
        dupper[0, :, f] = value.astype(LOW)
        dup_copy(k).start()

    def hidden_back():
        @pl.loop(0, 3)
        def _(k):
            n = pl.ds(pl.multiple_of(k * 256, 256), 256)
            dhid[:, n] = dot(dupper[0], up[n, :], NT)

        value, dgain, dshift = norm_pull(dtwo[...] + dhid[...], normed[...], inverse[:, :1], vec[3:4, :])
        dpre[...] = value
        done[0] = value.astype(LOW)
        swap(done, 0)
        dvec[2:3, :] = jnp.sum(value, axis=0, keepdims=True)
        dvec[3:4, :] = dgain
        dvec[4:5, :] = dshift
        dmix[...] = dot(done[0], attn[:, pl.ds(3 * width, width)], NN).astype(LOW)

    def attend_back(step):
        s, j = step // 6, lax.rem(step, 6)
        cs = pl.ds(pl.multiple_of(j * 128, 128), 128)
        rs = pl.ds(pl.multiple_of(s * length, length), length)
        ms = pl.ds(pl.multiple_of(s * padded, padded), padded)
        lane = lax.broadcasted_iota(jnp.int32, (padded, 128), 1) < 64

        def halves(v):
            zero = jnp.zeros_like(v)
            return jnp.concatenate([jnp.where(lane, v, zero), jnp.where(lane, zero, v)], axis=0)

        key, value = kv[0, rs, cs], kv[1, rs, cs]
        queries, mixes = halves(query_m[ms, cs]), halves(dmix[ms, cs])
        score = dot(key, queries, NT)
        expo = jnp.exp(score - jnp.max(score, axis=0, keepdims=True))
        probs = expo / jnp.sum(expo, axis=0, keepdims=True)
        dprobs = dot(value, mixes, NT)
        dscore = (probs * (dprobs - jnp.sum(dprobs * probs, axis=0, keepdims=True))).astype(LOW)
        dkv[0, rs, cs] = dot(dscore, queries, NN).astype(LOW)
        dvalue = dot(probs.astype(LOW), mixes, NN)
        dkv[1, rs, cs] = dvalue.astype(LOW)
        dq = dot(dscore, key, TN) * 0.125
        dq = jnp.where(lane, dq[:padded], dq[padded:])
        dquery[0, ms, cs] = dq.astype(LOW)
        first = s == 0
        sums = jnp.concatenate([jnp.sum(dq, axis=0, keepdims=True), jnp.sum(dvalue, axis=0, keepdims=True)], axis=0)
        dvec[0:2, cs] = sums + jnp.where(first, 0.0, dvec[0:2, cs])

    def key_value_grads():
        for i in range(total // 256):
            r = pl.ds(i * 256, 256)
            tokens_t[:, r] = tokens[r, :].T

        def fill(store):
            @pl.loop(0, 8)
            def _(i):
                k = lax.rem(i, 2)
                n = pl.ds(pl.multiple_of(i // 2 * pair, pair), pair)
                store(n, pl.ds(pl.multiple_of(k * E, E), E), dot(tokens_t[n, :], dkv[k], NN).astype(LOW))

        @pl.when(mid)
        def _():
            def store(n, cols, value):
                acc[2, n, cols] = value

            fill(store)

        @pl.when(edge)
        def _():
            def store(n, cols, value):
                part[n, cols] = value

            fill(store)

        for zz in ORDER:
            sends.start(edge, lambda zz=zz: copy(part.at[zrows(zz)], part.at[zrows(zz)], sib_s.at[zz], sib_r.at[zz], near))

    def attention_sides():
        for k in range(2):
            left[k] = jnp.where(c == 0, rows_m[k], done[k]).T
            right[k] = jnp.where(c == 0, dquery[k], mixed_m[k])

    def attention_grads(zz):
        @pl.when(mid)
        def _():
            xb[2, zrows(zz), :] = product(zz, right, pl.ds(0, E))

        push_x(2, zz)

        @pl.when(mid)
        def _():
            wait(None, part.at[zrows(zz)], sib_r.at[zz])

            base = turn(zz) * pair

            def one(i):
                r = pl.ds(pl.multiple_of(base + i, SLAB), SLAB)
                acc[2, r, :] = (f32(acc[2, r, :]) + f32(part[r, :])).astype(LOW)

            slabs(pair, one)

        push_y(mid, 2, zz, M)

        @pl.when(edge)
        def _():
            acc[2, zrows(zz), pl.ds(0, E)] = product(zz, right, pl.ds(0, E))

    def tile_load(i):
        slot = lax.rem(i, 2)
        return pltpu.make_async_copy(hidden_h.at[pl.ds(pl.multiple_of(i * 256, 256), 256)], htile.at[slot], tile_sem.at[slot])

    def layer_store(i):
        slot = lax.rem(i, 2)
        return pltpu.make_async_copy(ltile.at[slot], layer_h.at[pl.ds(pl.multiple_of(i * 256, 256), 256)], out_sem.at[slot])

    def feed_forward(step):
        i, k = step // 4, lax.rem(step, 4)
        slot = lax.rem(i, 2)

        @pl.when(k == 0)
        def _():
            tile_load(i).wait()

            @pl.when(i + 1 < total // 256)
            def _():
                tile_load(i + 1).start()

        f = pl.ds(pl.multiple_of(k * 768, 768), 768)
        u = dot(htile[slot].astype(LOW), up[:, f], NN) + bias[:, f]
        a = (u * (0.5 * (1.0 + lax.erf(u * SQRT_HALF)))).astype(LOW)
        ytile[...] = dot(a, down[:, f], NT) + jnp.where(k == 0, htile[slot] + vec[5:6, :], ytile[...])

        @pl.when(k == 3)
        def _():
            @pl.when(i >= 2)
            def _():
                layer_store(i - 2).wait()

            ltile[slot] = norm(ytile[...], vec[6:7, :], vec[7:8, :])[0].astype(LOW)
            layer_store(i).start()

    def token_store(i):
        slot = lax.rem(i, 2)
        return pltpu.make_async_copy(htile.at[slot], dtokens_h.at[pl.ds(pl.multiple_of(i * 256, 256), 256)], out_sem.at[2 + slot])

    def masked_tokens():
        dpre[...] = dpre[...] + dot(dquery[0], attn[:, pl.ds(0, width)], NT)

    def tokens_back(i):
        slot = lax.rem(i, 2)

        @pl.when(i >= 2)
        def _():
            token_store(i - 2).wait()

        r = pl.ds(pl.multiple_of(i * 256, 256), 256)
        s = i // (length // 256)
        pick = pick_t[s, pl.ds(pl.multiple_of(lax.rem(i, length // 256) * 256, 256), 256), :]
        value = dpre[pl.ds(pl.multiple_of(s * padded, padded), padded), :]
        high = value.astype(LOW)
        rest = (value - f32(high)).astype(LOW)
        htile[slot] = (
            dot(dkv[0, r, :], attn[:, pl.ds(width, width)], NT) + dot(dkv[1, r, :], attn[:, pl.ds(2 * width, width)], NT) + (dot(pick, high, NN) + dot(pick, rest, NN))
        )
        token_store(i).start()

    def small_start():
        squares[...] = jnp.zeros_like(squares)
        for w in range(8):
            sall[w] = jnp.zeros((16, 128), jnp.float32)
            turned = dvec[...] if w == 0 else pltpu.roll(dvec[...], width - rows * w, 1)
            lane = lax.broadcasted_iota(jnp.int32, (8, 128), 1)
            sall[w, 0:8, :] = jnp.where(lane < rows, turned[:, :128], 0.0)
            for r in range(3):
                sall[w, 8 + r : 9 + r, :] = dbias[:, pl.ds(w * 384 + r * 128, 128)]
        sends.start(None, lambda: copy(sall, ssib, sm_s.at[0], sm_r.at[0], near))

    def small_x():
        wait(None, ssib, sm_r.at[0])
        ssib[...] = sall[...] + ssib[...]
        sends.start(None, lambda: copy(ssib, sx, sm_s.at[1], sm_r.at[1], over))

    w = z * 2 + y

    def peer(k):
        return lax.rem(w + k, 8)

    def small_y():
        wait(None, sx, sm_r.at[1])
        sall2[...] = ssib[...] + sx[...]
        for k in range(1, 8):
            sends.start(None, lambda k=k: copy(sall2.at[peer(k)], sy.at[w], sm_s.at[1 + k], sy_r.at[w], (peer(k), x * 2 + c)))
        sy[w] = sall2[w]

    def small_add():
        for k in range(1, 8):
            wait(None, sy.at[peer(k)], sy_r.at[peer(k)])
        value = sy[0]
        for k in range(1, 8):
            value = value + sy[k]
        small_out[...] = value

    def square_sum():
        value = small_out[...]
        total_squares = jnp.sum(squares[...] + value * value)
        norms[w] = jnp.full((8, 128), total_squares, jnp.float32)
        for k in range(1, 8):
            sends.start(None, lambda k=k: copy(norms.at[w], norms.at[w], n_s.at[k], n_r.at[w], (peer(k), x * 2 + c)))
        for k in range(1, 8):
            wait(None, norms.at[peer(k)], n_r.at[peer(k)])
        whole = norms[0]
        for k in range(1, 8):
            whole = whole + norms[k]
        norm_out[...] = jnp.sqrt(whole)

    moves = {
        "add_x": add_x, "add_y": add_y, "line": line, "owner": owner, "middle_x": middle_x, "relay": relay, "arrived": arrived,
        "grads": lambda p, zz: grads(p, zz, dupper), "attention_grads": lambda zz: attention_grads(zz),
    }
    small_moves = {("add_y", 1, 0): small_y, ("owner", 1): small_add}

    def run(steps):
        for name, *rest in steps:
            moves[name](*rest)
            small_moves.get((name, *rest), lambda: None)()

    def looped(n, body, table):
        @pl.loop(0, n)
        def _(i):
            body(i)
            for k in sorted(table):
                pl.when(i == k)(lambda k=k: run(table[k]))

    tile = total // 256
    f = jnp.float32
    v = pltpu.VMEM

    def compute(*refs):
        nonlocal left, right, dhid, dpre, dmix, dkv, tokens_t, htile, ytile, ltile
        left, right, dhid, dpre, dmix, dkv, tokens_t, htile, ytile, ltile = refs
        transpose_into(dlow)
        for zz in ORDER:
            grads(0, zz, act_m)
        for k in range(4):
            upper_back(k)
        transpose_into(hid_m)
        hidden_back()
        for k in range(4):
            dup_copy(k).wait_recv()
        looped(seqs * 6, attend_back, BESIDE_ATTENTION)
        swap(dquery, 1)
        small_start()
        key_value_grads()
        small_x()
        run(BESIDE_KEYS)
        for make in swaps:
            make().wait_recv()
        attention_sides()
        masked_tokens()
        looped(tile, tokens_back, BESIDE_TOKENS)
        for i in range(tile - 2, tile):
            token_store(i).wait()
        tile_load(0).start()
        looped(tile * 4, feed_forward, BESIDE_FEED_FORWARD)
        for i in range(tile - 2, tile):
            layer_store(i).wait()

    pl.run_scoped(
        compute,
        v((2, width, count), LOW), v((2, count, width), LOW), v((count, width), f), v((count, width), f), v((count, width), LOW), v((2, total, width), LOW),
        v((width, total), LOW), v((2, 256, width), f), v((256, width), f), v((2, 256, width), LOW),
    )
    run(LAST)
    square_sum()
    for make in swaps:
        make().wait_send()
    for k in range(4):
        dup_copy(k).wait_send()


def step_kernel(rows, seqs, length, padded, *refs):
    refs = list(refs)

    def take(n):
        got, refs[:] = refs[:n], refs[n:]
        return got

    raw = take(10)
    layer_h, dtokens_h, out, small_out, norm_out, hidden_h = take(6)
    weights, (small_full, small_f, tokens, pick_t, kv, vec, qbias, bias) = take(3), take(8)
    masked = take(11)
    query_m, rows_m, mixed_m, hid_m, act_m, slope, dtwo, dlow, dvec, normed, inverse = masked
    sems = take(8)
    sends = Sends()
    forward_part(rows, seqs, length, padded, sends, *raw, hidden_h, *weights, small_full, small_f, tokens, pick_t, kv, vec, qbias, bias, *masked, *sems)
    backward_part(
        rows, seqs, length, padded, sends, *weights, vec, bias, kv, hidden_h, query_m, rows_m, mixed_m, hid_m, act_m, slope, dtwo, dlow, normed, inverse, dvec, pick_t, tokens,
        layer_h, dtokens_h, out, small_out, norm_out, *refs,
    )
    sends.finish()


def whole_step(qkv, out, up, down, vectors, up_bias, tokens, place_m, count_m, grad_m):
    rows, cols = up.shape
    out, down, grad_m = out.T, down.T, jnp.swapaxes(grad_m, 0, 1)
    total, width = tokens.shape
    seqs, slots = place_m.shape
    length = total // seqs
    padded = -(-slots // 16) * 16
    count = seqs * padded
    shape = jax.ShapeDtypeStruct
    f = jnp.float32
    anywhere = pl.BlockSpec(memory_space=pl.ANY)
    vm = pl.BlockSpec(memory_space=pltpu.VMEM)
    dma = pltpu.SemaphoreType.DMA
    v = pltpu.VMEM
    one = (16, 128)
    scratch = [
        v((width, cols), LOW), v((width, cols), LOW), v((width, cols), LOW),
        v((8,) + one, LOW), v(one, f), v((total, width), LOW), v((seqs, length, padded), LOW), v((2, total, width), LOW), v((8, width), f), v((3, 1, width), f), v((1, cols), f),
        v((count, width), LOW), v((2, count, width), LOW), v((2, count, width), LOW), v((2, count, width), LOW), v((2, count, cols), LOW),
        v((count, cols), f), v((count, width), f), v((2, count, width), LOW), v((8, width), f), v((count, width), f), v((count, 128), f),
        dma((6, 3, 8)), dma((3, 8, 3)), dma((8,)), dma((8,)), dma((5,)), dma((1,)), dma((5,)), dma((5,)),
        v((2, count, cols), LOW), v((1, cols), f), v((2, count, width), LOW), v((2, count, width), LOW), v((width, M), LOW),
        v((3, width, M), LOW), v((3, width, E), LOW), v((3, 4, rows, M), LOW), v((3, 5, rows, M), LOW), v((3, rows, M), LOW),
        v((8,) + one, f), v((8,) + one, f), v((8,) + one, f), v((8,) + one, f), v((8,) + one, f), v((8, 8, 128), f), v(one, f),
        dma((2,)), dma((4,)), dma((2,)), dma((2,)), dma((4,)), dma((4,)), dma((4,)), dma((4,)), dma((3, 4)), dma((3, 4)), dma((3, 4)), dma((3, 4)),
        dma((2, 3, 4)), dma((2, 3, 4)), dma((3,)), dma((3,)), dma((3, 3)), dma((3, 3)), dma((9,)), dma((2,)), dma((8,)), dma((8,)), dma((8,)),
    ]
    return pl.pallas_call(
        functools.partial(step_kernel, rows, seqs, length, padded),
        out_shape=(shape((total, width), LOW), shape((total, width), f), shape((3, rows, cols), LOW), shape(one, f), shape((8, 128), f), shape((total, width), f)),
        in_specs=[anywhere] * 4 + [vm] * 2 + [anywhere, vm, pl.BlockSpec(memory_space=pltpu.SMEM), vm],
        out_specs=(anywhere, anywhere, vm, vm, vm, anywhere),
        scratch_shapes=scratch,
        compiler_params=pltpu.CompilerParams(collective_id=0, has_side_effects=True, vmem_limit_bytes=64 * 2**20 - 2**16),
    )(qkv, out, up, down, vectors, up_bias, tokens, place_m, count_m, grad_m)[:5]


def adam_kernel(layer, dtokens, norm, own, small, *refs):
    weights, firsts, seconds = refs[0:6], refs[6:12], refs[12:18]
    outs = refs[18:36]
    layer_o, dtokens_o, norm_o, layer_v, dtokens_v, sem = refs[36:]
    step_id = pl.program_id(0)
    copies_in = [pltpu.make_async_copy(layer, layer_v, sem.at[0]), pltpu.make_async_copy(dtokens, dtokens_v, sem.at[1])]
    copies_out = [pltpu.make_async_copy(layer_v, layer_o, sem.at[2]), pltpu.make_async_copy(dtokens_v, dtokens_o, sem.at[3])]

    @pl.when(step_id == 0)
    def _():
        for copy in copies_in:
            copy.start()
        norm_o[0, 0] = jnp.max(norm[...])

    @pl.when(step_id == 2)
    def _():
        for first, then in zip(copies_in, copies_out):
            first.wait()
            then.start()

    factor = CLIP_LIMIT / jnp.maximum(norm[0:1, 0:1], CLIP_LIMIT)

    def step(k, where, grad, decay, rate):
        grad = grad * factor.reshape((1,) * grad.ndim)
        weight = weights[k][where]
        first = BETA_ONE * firsts[k][where] + (1.0 - BETA_ONE) * grad
        second = BETA_TWO * seconds[k][where] + (1.0 - BETA_TWO) * grad * grad
        mean_hat = first * (1.0 / (1.0 - BETA_ONE**STEP))
        square_hat = second * (1.0 / (1.0 - BETA_TWO**STEP))
        outs[3 * k][where] = weight - rate * (mean_hat / (jnp.sqrt(square_hat) + ADAM_EPS) + decay * weight)
        outs[3 * k + 1][where] = first
        outs[3 * k + 2][where] = second

    width = weights[1].shape[1]
    for k in range(3):
        step(0, (k,), f32(own[2, :, pl.ds(k * width, width)]), DECAY_RATE, LEARN_RATE)
    everything = (slice(None), slice(None))
    step(1, everything, f32(own[2, :, pl.ds(3 * width, width)]), DECAY_RATE, OUTPUT_RATE)
    for k in range(4):
        cols = (slice(None), pl.ds(k * width, width))
        step(2, cols, f32(own[1, :, pl.ds(k * width, width)]), DECAY_RATE, LEARN_RATE)
        step(3, cols, f32(own[0, :, pl.ds(k * width, width)]), DECAY_RATE, LEARN_RATE)

    @pl.when(step_id == pl.num_programs(0) - 1)
    def _():
        for copy in copies_out:
            copy.wait()

    @pl.when(step_id == 0)
    def _():
        lanes = weights[4].shape[1]
        step(4, everything, small[0:8, 0:lanes], 0.0, VECTOR_RATE)
        step(5, everything, small[8:11, :], 0.0, BIAS_RATE)


def adam(layer, dtokens, norm, own, small, weights, moments):
    def turn(values):
        a, b, c, d, e, g = values
        return a, b.T, c, d.T, e, g.reshape(3, 128)

    arrays = turn(weights) + turn([m[0] for m in moments]) + turn([m[1] for m in moments])
    rows, cols = arrays[2].shape
    width = cols // 4
    slab = 16
    anywhere = pl.BlockSpec(memory_space=pl.ANY)
    specs = [
        pl.BlockSpec((3, slab, width), lambda i: (0, i, 0)),
        pl.BlockSpec((slab, width), lambda i: (i, 0)),
        pl.BlockSpec((slab, cols), lambda i: (i, 0)),
        pl.BlockSpec((slab, cols), lambda i: (i, 0)),
        pl.BlockSpec(arrays[4].shape, lambda i: (0, 0)),
        pl.BlockSpec(arrays[5].shape, lambda i: (0, 0)),
    ]
    outs = pl.pallas_call(
        adam_kernel,
        grid=(rows // slab,),
        out_shape=tuple(jax.ShapeDtypeStruct(a.shape, a.dtype) for a in arrays[:6] for _ in range(3))
        + (jax.ShapeDtypeStruct(layer.shape, layer.dtype), jax.ShapeDtypeStruct(dtokens.shape, dtokens.dtype), jax.ShapeDtypeStruct((1, 1), jnp.float32)),
        in_specs=[
            anywhere,
            anywhere,
            pl.BlockSpec(norm.shape, lambda i: (0, 0)),
            pl.BlockSpec((3, slab, cols), lambda i: (0, i, 0)),
            pl.BlockSpec(small.shape, lambda i: (0, 0)),
        ] + specs * 3,
        out_specs=tuple(s for s in specs for _ in range(3)) + (anywhere, anywhere, pl.BlockSpec(memory_space=pltpu.SMEM)),
        scratch_shapes=[pltpu.VMEM(layer.shape, layer.dtype), pltpu.VMEM(dtokens.shape, dtokens.dtype), pltpu.SemaphoreType.DMA((4,))],
        compiler_params=pltpu.CompilerParams(vmem_limit_bytes=64 * 2**20 - 2**16),
    )(layer, dtokens, norm, own, small, *arrays)

    def back(k, v):
        return v.T if k in (1, 3) else v.reshape(-1) if k == 5 else v

    return (outs[18], outs[19], outs[20].reshape(())) + tuple(back(i // 3, v) for i, v in enumerate(outs[:18]))


def masks(mask_place, mask_count, gradient, length):
    seqs, slots = mask_place.shape
    padded = -(-slots // 16) * 16
    live = jnp.arange(padded)[None, :] < mask_count[:, None]
    spots = jnp.pad(mask_place, ((0, 0), (0, padded - slots)), constant_values=-1)
    pick = (spots[:, :, None] == jnp.arange(length)[None, None, :]) & live[:, :, None]
    gradient = jnp.pad(gradient, ((0, 0), (0, padded - slots), (0, 0)))
    gradient = jnp.where(live[:, :, None], gradient, jnp.zeros_like(gradient))
    return pick, gradient.reshape(seqs * padded, -1)


def update(weights, moments, grads, grad_norm):
    factor = CLIP_LIMIT / jnp.maximum(grad_norm, CLIP_LIMIT)
    rates = (LEARN_RATE, OUTPUT_RATE, LEARN_RATE, LEARN_RATE, VECTOR_RATE, BIAS_RATE)
    out = ()
    for k in range(6):
        out += adam_step(weights[k], *moments[k], grads[k], factor, DECAY_RATE if k < 4 else 0.0, rates[k])
    return out


def natural(own_attn, own_up, own_down, own_vectors, own_bias):
    width = own_up.shape[1] // 4
    own_qkv = jnp.swapaxes(own_attn[:, : 3 * width].reshape(-1, 3, width), 0, 1)
    return own_qkv, own_attn[:, 3 * width :].T, own_up, own_down.T, own_vectors, own_bias


def pack(qkv, out, up, down):
    attn = jnp.concatenate([qkv[0], qkv[1], qkv[2], out.T], axis=1)
    return attn.astype(jnp.bfloat16), up.astype(jnp.bfloat16), down.T.astype(jnp.bfloat16)


def plain(tokens, mask_place, mask_count, gradient, weights, moments):
    low = jnp.bfloat16
    seqs, length, width = tokens.shape
    pick, gradient = masks(mask_place, mask_count, gradient, length)
    padded = pick.shape[1]
    flat = tokens.reshape(seqs * length, width)
    attn_w, up_w, down_w = (lax.all_gather(v, "wide", axis=0, tiled=True) for v in pack(*weights[:4]))
    vec = lax.all_gather(weights[4].astype(low), "wide", axis=1, tiled=True).astype(jnp.float32)
    bias = lax.all_gather(weights[5].astype(low), "wide", axis=0, tiled=True).astype(jnp.float32)
    wq, wk, wv, wo = (attn_w[:, k * width : (k + 1) * width] for k in range(4))
    query = (mm(flat, wq, NN) + vec[0]).astype(low)
    key = mm(flat, wk, NN, low)
    value = (mm(flat, wv, NN) + vec[1]).astype(low)
    query, key, value = (split_heads(v, seqs, length) for v in (query, key, value))
    mixed = lax.map(attend, (query, key, value)).reshape(seqs * length, width)

    def middle(rows, mixed):
        pre_one = rows.astype(jnp.float32) + (mm(mixed, wo, NT) + vec[2])
        hidden, normed, inverse = layer_norm(pre_one, vec[3], vec[4])
        hidden_low = hidden.astype(low)
        upper = mm(hidden_low, up_w, NN) + bias
        cumul = 0.5 * (1.0 + lax.erf(upper * SQRT_HALF))
        active = (upper * cumul).astype(low)
        pre_two = hidden + (mm(active, down_w, NT) + vec[5])
        return layer_norm(pre_two, vec[6], vec[7]), normed, inverse, hidden_low, upper, cumul, active

    layer_out = middle(flat, mixed)[0][0].astype(low)
    pick_low = pick.astype(low)

    def take(values):
        values = values.reshape(seqs, length, width)
        return jnp.einsum("sil,sld->sid", pick_low, values, preferred_element_type=jnp.float32).astype(low)

    rows_m = take(flat).reshape(seqs * padded, width)
    mixed_m = take(mixed).reshape(seqs * padded, width)
    query_m = split_heads(take(query), seqs, padded)
    (_, normed_two, inverse_two), normed_one, inverse_one, hidden_m, upper, cumul, active = middle(rows_m, mixed_m)
    dpre_two, dgain_two, dshift_two = norm_back(gradient.astype(jnp.float32), normed_two, inverse_two, vec[6])
    dbias_two = jnp.sum(dpre_two, axis=0)
    dtwo_low = dpre_two.astype(low)
    ddown = mm(dtwo_low, active, TN)
    dactive = mm(dtwo_low, down_w, NN)
    density = jnp.exp(-0.5 * upper * upper) * INV_ROOT_TWO_PI
    dupper = dactive * (cumul + upper * density)
    dup_bias = jnp.sum(dupper, axis=0)
    dupper_low = dupper.astype(low)
    dup = mm(hidden_m, dupper_low, TN)
    dhidden = dpre_two + mm(dupper_low, up_w, NT)
    dpre_one, dgain_one, dshift_one = norm_back(dhidden, normed_one, inverse_one, vec[3])
    dbias_out = jnp.sum(dpre_one, axis=0)
    done_low = dpre_one.astype(low)
    dout = mm(done_low, mixed_m, TN)
    dmixed = split_heads(mm(done_low, wo, NN, low), seqs, padded)
    dquery, dkey, dvalue = lax.map(attend_back, (query_m, key, value, dmixed))
    dquery = dquery.reshape(seqs * padded, width)
    dkey = dkey.reshape(seqs * length, width)
    dvalue = dvalue.reshape(seqs * length, width)
    dbias_query = jnp.sum(dquery, axis=0)
    dbias_value = jnp.sum(dvalue, axis=0)
    dquery, dkey, dvalue = dquery.astype(low), dkey.astype(low), dvalue.astype(low)
    dattn = jnp.concatenate([mm(rows_m, dquery, TN), mm(flat, dkey, TN), mm(flat, dvalue, TN), dout], axis=1)
    masked_part = dpre_one + mm(dquery, wq, NT)
    dtokens = spread(pick, masked_part) + mm(dkey, wk, NT) + mm(dvalue, wv, NT)
    dvectors = jnp.stack(
        [dbias_query, dbias_value, dbias_out, dgain_one, dshift_one, dbias_two, dgain_two, dshift_two]
    )

    def owned(value, dim):
        return lax.psum(lax.psum_scatter(value, "wide", scatter_dimension=dim, tiled=True), "narrow")

    grads = (owned(dattn, 0), owned(dup, 0), owned(ddown, 0), owned(dvectors, 1), owned(dup_bias, 0))
    grad_norm = jnp.sqrt(lax.psum(sum(jnp.sum(v * v) for v in grads), "wide"))
    return (layer_out, dtokens, grad_norm) + update(weights, moments, natural(*grads), grad_norm)


def spread(pick, rows):
    seqs, padded, length = pick.shape
    return jnp.einsum(
        "sil,sid->sld",
        pick.astype(jnp.float32),
        rows.reshape(seqs, padded, -1),
        precision=lax.Precision.HIGHEST,
        preferred_element_type=jnp.float32,
    ).reshape(seqs * length, -1)


def tailored(tokens, mask_place, mask_count, gradient, weights, moments):
    seqs, length, width = tokens.shape
    flat = tokens.reshape(seqs * length, width)
    layer_out, dtokens, own, small, grad_norm = whole_step(*weights, flat, mask_place, mask_count, gradient)
    return adam(layer_out, dtokens, grad_norm, own, small, weights, moments)


def shards(body, tokens, mask_place, mask_count, masked_output_gradient, *parameters):
    seqs, length, width = tokens.shape
    weights = parameters[0::3]
    moments = tuple(zip(parameters[1::3], parameters[2::3]))
    layer_out, dtokens, *rest = body(tokens, mask_place, mask_count, masked_output_gradient, weights, moments)
    return (layer_out.reshape(seqs, length, width), dtokens.reshape(seqs, length, width), *rest)


def solution(mesh):
    body = tailored if mesh.shape["wide"] == 8 and mesh.shape["narrow"] == 4 else plain
    data = P(("wide", "narrow"))
    rows = P("wide")
    columns = P(None, "wide")
    weights = (columns,) * 6 + (rows,) * 3 + (columns,) * 6 + (rows,) * 3
    return jax.shard_map(
        functools.partial(shards, body),
        mesh=mesh,
        in_specs=(data,) * 4 + weights,
        out_specs=(data, data, P()) + weights,
        check_vma=False,
    )
```

```python
import functools

import jax
import jax.numpy as jnp
from jax import lax
from jax.experimental import pallas as pl
from jax.experimental.pallas import tpu as pltpu
from jax.sharding import PartitionSpec as P

HEADS = 12
HEAD_DIM = 64
STEP = 10

LN_EPS = 1e-06
SQRT_HALF = 0.7071067811865476
INV_ROOT_TWO_PI = 0.3989422804014327
CLIP_LIMIT = 1.0
BETA_ONE = 0.9
BETA_TWO = 0.999
LEARN_RATE = 0.05
OUTPUT_RATE = 0.2
VECTOR_RATE = 0.5
BIAS_RATE = 0.3
DECAY_RATE = 0.01
ADAM_EPS = 1e-08

MESH = pl.DeviceIdType.MESH


def when(cond, body):
    if callable(cond):
        cond = cond()
    if cond is None:
        body()
    else:
        pl.when(cond)(body)


class Sends:
    def __init__(self):
        self.started = []

    def start(self, cond, make):
        when(cond, lambda: make().start())
        self.started.append((cond, make))

    def finish(self):
        for cond, make in self.started:
            when(cond, lambda make=make: make().wait_send())


def both(a, b):
    return b if a is None else (a if b is None else jnp.logical_and(a, b))


def place():
    w, n = lax.axis_index("wide"), lax.axis_index("narrow")
    return w // 2, lax.rem(w, 2), n // 2, lax.rem(n, 2)


def flip(v):
    return 1 - v


def dev(z, y, x, c):
    return (z * 2 + y, x * 2 + c)


def meet(z, y, x, c, diagonal):
    bar = pltpu.get_barrier_semaphore()
    peers = [(None, dev(z, flip(y), x, c)), (None, dev(z, y, flip(x), c)), (None, dev(z, y, x, flip(c)))]
    if diagonal:
        peers.append((None, dev(z, y, flip(x), flip(c))))
    peers += [(z > 0, dev(z - 1, y, x, c)), (z < 3, dev(z + 1, y, x, c))]
    for cond, peer in peers:
        when(cond, lambda peer=peer: pl.semaphore_signal(bar, inc=1, device_id=peer, device_id_type=MESH))
    inner = jnp.logical_and(z > 0, z < 3)
    count = 4 if diagonal else 3
    pl.semaphore_wait(bar, count + 1 + jnp.where(inner, 1, 0))


def gather_kernel(rows, cols, attn, up, down, small, attn_full, up_full, down_full, small_full, send_sem, recv_sem, small_send, small_recv, own_sem):
    z, y, x, c = place()
    edge = x == c
    third = cols // 3
    mine, across = x + c, 2 * flip(x)
    fulls = (attn_full, up_full, down_full)
    shards = (attn, up, down)
    sends = Sends()
    zl, zh = z > 0, z < 3

    def spot(p, zz, yy, t):
        return fulls[p].at[pl.ds(pl.multiple_of((zz * 2 + yy) * rows, rows), rows), pl.ds(pl.multiple_of(t * third, third), third)]

    def push(cond, p, zz, yy, t, kind, to, src=None):
        def make():
            w = zz * 2 + yy
            where = spot(p, zz, yy, t)
            return pltpu.make_async_remote_copy(
                src_ref=where if src is None else src,
                dst_ref=where,
                send_sem=send_sem.at[kind, p, w],
                recv_sem=recv_sem.at[p, w, t],
                device_id=to,
                device_id_type=MESH,
            )

        sends.start(cond, make)

    def small_push(cond, zz, yy, kind, to, src=None):
        def make():
            w = zz * 2 + yy
            where = small_full.at[w]
            return pltpu.make_async_remote_copy(
                src_ref=where if src is None else src,
                dst_ref=where,
                send_sem=small_send.at[kind, w],
                recv_sem=small_recv.at[w],
                device_id=to,
                device_id_type=MESH,
            )

        sends.start(cond, make)

    def arrive(cond, p, zz, yy, t):
        def body():
            where = spot(p, zz, yy, t)
            w = zz * 2 + yy
            pltpu.make_async_remote_copy(where, where, send_sem.at[0, p, w], recv_sem.at[p, w, t], dev(z, y, x, c), device_id_type=MESH).wait_recv()

        when(cond, body)

    def small_arrive(cond, zz, yy):
        def body():
            w = zz * 2 + yy
            pltpu.make_async_remote_copy(small_full.at[w], small_full.at[w], small_send.at[0, w], small_recv.at[w], dev(z, y, x, c), device_id_type=MESH).wait_recv()

        when(cond, body)

    UP, DOWN, SIDE, OVER, NEAR, PASS = range(6)
    above, below, beside = dev(z + 1, y, x, c), dev(z - 1, y, x, c), dev(z, flip(y), x, c)
    over, near = dev(z, y, flip(x), c), dev(z, y, x, flip(c))

    def own(p):
        src = shards[p].at[:, pl.ds(pl.multiple_of(mine * third, third), third)]
        push(zh, p, z, y, mine, UP, above, src)
        push(zl, p, z, y, mine, DOWN, below, src)
        push(None, p, z, y, mine, SIDE, beside, src)

    def z_step(p, d):
        for cond, zz, onward, kind, to in ((z - d >= 0, z - d, zh, UP, above), (z + d <= 3, z + d, zl, DOWN, below)):
            arrive(cond, p, zz, y, mine)
            push(both(cond, onward), p, zz, y, mine, kind, to)
            push(cond, p, zz, y, mine, SIDE, beside)
            push(both(cond, edge), p, zz, y, mine, OVER, over)
            push(cond, p, zz, y, mine, NEAR, near)

    def y_step(p, d):
        steps = ((None, z),) if d == 0 else ((z - d >= 0, z - d), (z + d <= 3, z + d))
        for cond, zz in steps:
            arrive(cond, p, zz, flip(y), mine)
            push(both(cond, edge), p, zz, flip(y), mine, OVER, over)
            push(cond, p, zz, flip(y), mine, NEAR, near)

    def x_step(p, d):
        mid = jnp.logical_not(edge)
        for yy in (y, flip(y)):
            if d == 0:
                steps = () if yy is y else ((None, z),)
            else:
                steps = ((z - d >= 0, z - d), (z + d <= 3, z + d))
            for cond, zz in steps:
                cond = both(cond, mid)
                arrive(cond, p, zz, yy, across)
                push(cond, p, zz, yy, across, PASS, near)

    def last(p, d):
        for yy in (y, flip(y)):
            if d == 0:
                steps = () if yy is y else ((None, z),)
            else:
                steps = ((z - d >= 0, z - d), (z + d <= 3, z + d))
            for cond, zz in steps:
                arrive(cond, p, zz, yy, x + flip(c))
                arrive(both(cond, edge), p, zz, yy, across)

    def small_z(d):
        for cond, zz, onward, kind, to in ((z - d >= 0, z - d, zh, UP, above), (z + d <= 3, z + d, zl, DOWN, below)):
            small_arrive(cond, zz, y)
            small_push(both(cond, onward), zz, y, kind, to)
            small_push(cond, zz, y, SIDE, beside)

    meet(z, y, x, c, False)
    small_push(zh, z, y, UP, above, small)
    small_push(zl, z, y, DOWN, below, small)
    small_push(None, z, y, SIDE, beside, small)
    own(0)
    w = z * 2 + y
    copies = []
    for p in range(3):
        copies.append(pltpu.make_async_copy(shards[p], fulls[p].at[pl.ds(pl.multiple_of(w * rows, rows), rows)], own_sem.at[p]))
    copies.append(pltpu.make_async_copy(small, small_full.at[w], own_sem.at[3]))
    for copy in copies:
        copy.start()
    for d in range(1, 4):
        small_z(d)
    order = [
        lambda: z_step(0, 1), lambda: own(1), lambda: y_step(0, 0), lambda: z_step(0, 2), lambda: y_step(0, 1), lambda: x_step(0, 0), lambda: z_step(0, 3),
        lambda: y_step(0, 2), lambda: x_step(0, 1), lambda: z_step(1, 1), lambda: own(2), lambda: y_step(0, 3), lambda: x_step(0, 2), lambda: z_step(1, 2), lambda: y_step(1, 0), lambda: x_step(0, 3), lambda: z_step(1, 3),
        lambda: y_step(1, 1), lambda: x_step(1, 0), lambda: z_step(2, 1), lambda: y_step(1, 2), lambda: x_step(1, 1), lambda: z_step(2, 2), lambda: y_step(1, 3), lambda: x_step(1, 2), lambda: z_step(2, 3),
        lambda: y_step(2, 0), lambda: x_step(1, 3), lambda: y_step(2, 1), lambda: x_step(2, 0), lambda: y_step(2, 2), lambda: x_step(2, 1), lambda: y_step(2, 3), lambda: x_step(2, 2), lambda: x_step(2, 3),
    ]
    for step in order:
        step()
    for d in range(4):
        for cond, zz in (((None, z),) if d == 0 else ((z - d >= 0, z - d), (z + d <= 3, z + d))):
            small_arrive(cond, zz, flip(y))
    for p in range(3):
        for d in range(4):
            last(p, d)
    sends.finish()
    for copy in copies:
        copy.wait()


def gather(attn, up, down, small):
    rows, cols = attn.shape
    full = jax.ShapeDtypeStruct((8 * rows, cols), attn.dtype)
    anywhere = pl.BlockSpec(memory_space=pl.ANY)
    return pl.pallas_call(
        functools.partial(gather_kernel, rows, cols),
        out_shape=(full, full, full, jax.ShapeDtypeStruct((8,) + small.shape, small.dtype)),
        in_specs=[anywhere] * 4,
        out_specs=(anywhere,) * 4,
        scratch_shapes=[
            pltpu.SemaphoreType.DMA((6, 3, 8)),
            pltpu.SemaphoreType.DMA((3, 8, 3)),
            pltpu.SemaphoreType.DMA((3, 8)),
            pltpu.SemaphoreType.DMA((8,)),
            pltpu.SemaphoreType.DMA((4,)),
        ],
        compiler_params=pltpu.CompilerParams(collective_id=0, has_side_effects=True),
    )(attn, up, down, small)


def layer_norm(values, gain, shift):
    center = values - jnp.mean(values, axis=-1, keepdims=True)
    inverse = lax.rsqrt(jnp.mean(center * center, axis=-1, keepdims=True) + LN_EPS)
    normed = center * inverse
    return (normed * gain + shift, normed, inverse)


def norm_back(incoming, normed, inverse, gain):
    dgain = jnp.sum(incoming * normed, axis=0)
    dshift = jnp.sum(incoming, axis=0)
    scaled = incoming * gain
    dvalues = inverse * (
        scaled
        - jnp.mean(scaled, axis=-1, keepdims=True)
        - normed * jnp.mean(scaled * normed, axis=-1, keepdims=True)
    )
    return (dvalues, dgain, dshift)


def mm(a, b, dims, out=jnp.float32):
    return lax.dot_general(a, b, (dims, ((), ())), preferred_element_type=jnp.float32).astype(out)


NN = ((1,), (0,))
NT = ((1,), (1,))
TN = ((0,), (0,))


def split_heads(values, seqs, length):
    return values.reshape(seqs, length, HEADS, HEAD_DIM)


def attend(pieces):
    query, key, value = pieces
    raw = jnp.einsum("qhe,khe->hqk", query, key, preferred_element_type=jnp.float32) * HEAD_DIM ** (
        -0.5
    )
    peak = jnp.max(raw, axis=-1, keepdims=True)
    expo = jnp.exp(raw - peak)
    total = jnp.sum(expo, axis=-1, keepdims=True)
    probs = (expo / total).astype(jnp.bfloat16)
    mixed = jnp.einsum("hqk,khe->qhe", probs, value, preferred_element_type=jnp.float32)
    return mixed.astype(jnp.bfloat16)


def attend_back(pieces):
    query, key, value, dmixed = pieces
    scale = HEAD_DIM ** (-0.5)
    raw = jnp.einsum("qhe,khe->hqk", query, key, preferred_element_type=jnp.float32) * scale
    probs = jax.nn.softmax(raw, axis=-1)
    dprobs = jnp.einsum("qhe,khe->hqk", dmixed, value, preferred_element_type=jnp.float32)
    dscore = probs * (dprobs - jnp.sum(dprobs * probs, axis=-1, keepdims=True))
    dscore = (dscore * scale).astype(jnp.bfloat16)
    dquery = jnp.einsum("hqk,khe->qhe", dscore, key, preferred_element_type=jnp.float32)
    dkey = jnp.einsum("hqk,qhe->khe", dscore, query, preferred_element_type=jnp.float32)
    dvalue = jnp.einsum(
        "hqk,qhe->khe", probs.astype(jnp.bfloat16), dmixed, preferred_element_type=jnp.float32
    )
    return (dquery, dkey, dvalue)


def adam_step(weight, first, second, grad, factor, decay, rate):
    grad = grad * factor
    first_new = BETA_ONE * first + (1.0 - BETA_ONE) * grad
    second_new = BETA_TWO * second + (1.0 - BETA_TWO) * grad * grad
    mean_hat = first_new / (1.0 - BETA_ONE**STEP)
    square_hat = second_new / (1.0 - BETA_TWO**STEP)
    weight_new = weight - rate * (mean_hat / (jnp.sqrt(square_hat) + ADAM_EPS) + decay * weight)
    return (weight_new, first_new, second_new)


GATHER_ORDER = (
    ("z_step", 0, 1),
    ("y_step", 0, 0),
    ("z_step", 0, 2),
    ("own", 1),
    ("y_step", 0, 1),
    ("x_step", 0, 0),
    ("y_step", 0, 2),
    ("z_step", 0, 3),
    ("y_step", 0, 3),
    ("z_step", 1, 1),
    ("x_step", 0, 2),
    ("x_step", 0, 1),
    ("y_step", 1, 0),
    ("vectors_in",),
    ("z_step", 1, 2),
    ("x_step", 0, 3),
    ("last", 0),
    ("loop", "project", 4, {0: (("own", 2),), 1: (("y_step", 1, 1),)}),
    ("z_step", 1, 3),
    ("loop", "attend", 12, {0: (("y_step", 1, 2),), 2: (("z_step", 2, 1),), 4: (("y_step", 2, 0),), 5: (("y_step", 1, 3),), 7: (("x_step", 1, 1), ("z_step", 2, 2),), 9: (("y_step", 2, 1),)}),
    ("z_step", 2, 3),
    ("loop", "middle", 4, {0: (("y_step", 2, 2), ("x_step", 1, 2), ("x_step", 1, 0),), 1: (("x_step", 1, 3),)}),
    ("masked",),
    ("y_step", 2, 3),
    ("x_step", 2, 0),
    ("last", 1),
    ("save_hidden",),
    ("loop", "upper", 4, {1: (("x_step", 2, 1),), 2: (("x_step", 2, 2), ("x_step", 2, 3),)}),
    ("last", 2),
)


def dot(a, b, dims):
    return lax.dot_general(a, b, (dims, ((), ())), preferred_element_type=jnp.float32)


NN = ((1,), (0,))
NT = ((1,), (1,))
TN = ((0,), (0,))
LOW = jnp.bfloat16


def norm(values, gain, shift):
    center = values - jnp.mean(values, axis=-1, keepdims=True)
    inverse = lax.rsqrt(jnp.mean(center * center, axis=-1, keepdims=True) + LN_EPS)
    normed = center * inverse
    return normed * gain + shift, normed, inverse


def norm_pull(incoming, normed, inverse, gain):
    dgain = jnp.sum(incoming * normed, axis=0, keepdims=True)
    dshift = jnp.sum(incoming, axis=0, keepdims=True)
    scaled = incoming * gain
    return (
        inverse * (scaled - jnp.mean(scaled, axis=-1, keepdims=True) - normed * jnp.mean(scaled * normed, axis=-1, keepdims=True)),
        dgain,
        dshift,
    )


def forward_part(
    rows, seqs, length, padded, sends,
    qkv_h, out_h, up_h, down_h, vectors, up_bias, tokens_h, place_m, count_m, grad_m, hidden_o,
    attn_full, up_full, down_full, small_full, small_f, tokens, pick_t, kv, vec, qbias, bias,
    query_m, rows_m, mixed_m, hid_m, act_m, slope, dtwo, dlow, dvec, normed_one, inverse_one,
    send_sem, recv_sem, small_send, small_recv, load_sem, save_sem, pair_send, pair_recv,
):
    qkv_f = out_f = up_f = down_f = queries = mixed = hidden = pick = ytwo = hid_f = grad = None
    z, y, x, c = place()
    width = tokens.shape[1]
    total = tokens.shape[0]
    cols = up_h.shape[1]
    edge = x == c
    third = cols // 3
    mine, across = x + c, 2 * flip(x)
    fulls = (attn_full, up_full, down_full)
    w = z * 2 + y
    mine_rows = pl.ds(pl.multiple_of(w * rows, 32), rows)
    zl, zh = z > 0, z < 3
    count = seqs * padded

    def spot(p, zz, yy, t):
        return fulls[p].at[pl.ds(pl.multiple_of((zz * 2 + yy) * rows, rows), rows), pl.ds(pl.multiple_of(t * third, third), third)]

    def push(cond, p, zz, yy, t, kind, to):
        def make():
            whose = zz * 2 + yy
            where = spot(p, zz, yy, t)
            return pltpu.make_async_remote_copy(
                src_ref=where,
                dst_ref=where,
                send_sem=send_sem.at[kind, p, whose],
                recv_sem=recv_sem.at[p, whose, t],
                device_id=to,
                device_id_type=MESH,
            )

        sends.start(cond, make)

    def arrive(cond, p, zz, yy, t):
        def body():
            where = spot(p, zz, yy, t)
            whose = zz * 2 + yy
            pltpu.make_async_remote_copy(where, where, send_sem.at[0, p, whose], recv_sem.at[p, whose, t], dev(z, y, x, c), device_id_type=MESH).wait_recv()

        when(cond, body)

    UP, DOWN, SIDE, OVER, NEAR, PASS = range(6)
    above, below, beside = dev(z + 1, y, x, c), dev(z - 1, y, x, c), dev(z, flip(y), x, c)
    over, near = dev(z, y, flip(x), c), dev(z, y, x, flip(c))

    other_y = flip(y)
    span = {d: ((z - d >= 0, z - d), (z + d <= 3, z + d)) for d in range(1, 4)}
    span[0] = ((None, z),)
    mid = jnp.logical_not(edge)

    def around(d):
        return span[d]

    def also(a, b):
        return lambda: both(a, b)

    def own(p):
        push(zh, p, z, y, mine, UP, above)
        push(zl, p, z, y, mine, DOWN, below)
        push(None, p, z, y, mine, SIDE, beside)

    def z_step(p, d):
        for (cond, zz), onward, kind, to in zip(span[d], (zh, zl), (UP, DOWN), (above, below)):
            arrive(cond, p, zz, y, mine)
            push(also(cond, onward), p, zz, y, mine, kind, to)
            push(also(cond, edge) if d == 1 else cond, p, zz, y, mine, SIDE, beside)
            push(also(cond, edge), p, zz, y, mine, OVER, over)
            push(cond, p, zz, y, mine, NEAR, near)

    def y_step(p, d):
        for cond, zz in around(d):
            arrive(cond, p, zz, other_y, mine)
            if d == 0:
                push(also(zh, mid), p, zz, other_y, mine, UP, above)
                push(also(zl, mid), p, zz, other_y, mine, DOWN, below)
            push(also(cond, edge), p, zz, other_y, mine, OVER, over)
            push(cond, p, zz, other_y, mine, NEAR, near)

    def x_step(p, d):
        for yy in (y, other_y):
            for cond, zz in () if d == 0 and yy is y else around(d):
                arrive(also(cond, mid), p, zz, yy, across)
                push(also(cond, mid), p, zz, yy, across, PASS, near)

    def last(p):
        for d in range(4):
            for yy in (y, other_y):
                for cond, zz in () if d == 0 and yy is y else around(d):
                    arrive(cond, p, zz, yy, x + flip(c))
                    arrive(both(cond, edge), p, zz, yy, across)

    saves = []

    def keep(src, dst, k):
        copy = pltpu.make_async_copy(src, dst, save_sem.at[k])
        copy.start()
        saves.append(copy)

    swaps = []

    def swap(ref, k):
        def make():
            return pltpu.make_async_remote_copy(ref.at[0], ref.at[1], pair_send.at[k], pair_recv.at[k], near, device_id_type=MESH)

        sends.start(None, make)
        swaps.append(make)

    def peer(k):
        return lax.rem(w + k, 8)

    def small_copy(k, whose):
        return pltpu.make_async_remote_copy(
            small_full.at[whose], small_full.at[whose], small_send.at[k], small_recv.at[whose], (peer(k), x * 2 + c), device_id_type=MESH
        )

    def small_out():
        small_f[...] = jnp.zeros_like(small_f)
        small_f[0:8, 0:rows] = vectors[...]
        for r in range(3):
            small_f[8 + r : 9 + r, :] = up_bias[pl.ds(r * 128, 128)].reshape(1, 128)
        small_full[w] = small_f[...].astype(LOW)
        for k in range(1, 8):
            sends.start(None, lambda k=k: small_copy(k, w))

    def attn_shard():
        loads[1].wait()
        loads[2].wait()
        for k in range(3):
            attn_full[mine_rows, pl.ds(k * width, width)] = qkv_f[k].astype(LOW)
        attn_full[mine_rows, pl.ds(3 * width, width)] = out_f[...].astype(LOW)

    def up_shard():
        loads[3].wait()
        up_full[mine_rows, :] = up_f[...].astype(LOW)

    def down_shard():
        loads[4].wait()
        down_full[mine_rows, :] = down_f[...].astype(LOW)

    def masks():
        slots = place_m.shape[1]
        for s in range(seqs):
            hit = lax.broadcasted_iota(jnp.int32, (length, slots), 0) == place_m[s : s + 1, :]
            live = lax.broadcasted_iota(jnp.int32, (length, slots), 1) < count_m[s]
            hit = jnp.logical_and(hit, live).astype(jnp.float32).astype(LOW)
            row = lax.broadcasted_iota(jnp.int32, (padded, slots), 0)
            slot = lax.broadcasted_iota(jnp.int32, (padded, slots), 1)
            same = (row == slot).astype(jnp.float32).astype(LOW)
            kept = jnp.logical_and(row == slot, slot < count_m[s]).astype(jnp.float32).astype(LOW)
            pick[s] = dot(same, hit, NT).astype(LOW)
            pick_t[s] = dot(hit, same, NT).astype(LOW)
            grad[pl.ds(s * padded, padded), :] = dot(kept, f32(grad_m[...])[:, s, :].astype(LOW), NN)

    def vectors_in():
        loads[0].wait()
        for k in range(1, 8):
            small_copy(k, peer(k)).wait_recv()
        at = lax.broadcasted_iota(jnp.int32, (128, width), 0)
        to = lax.broadcasted_iota(jnp.int32, (128, width), 1)
        total = jnp.zeros((16, width), jnp.float32)
        for k in range(8):
            place_k = jnp.logical_and(at + k * rows == to, at < rows).astype(jnp.float32).astype(LOW)
            total += dot(small_full[k], place_k, NN)
            for r in range(3):
                bias[:, pl.ds(k * 384 + r * 128, 128)] = small_full[k, 8 + r : 9 + r, :].astype(jnp.float32)
        vec[...] = total[:8]
        qbias[0] = total[0:1]
        qbias[1] = jnp.zeros((1, width), jnp.float32)
        qbias[2] = total[1:2]

    def tile(i):
        return pl.ds(pl.multiple_of(i * 256, 256), 256)

    def project(i):
        r = tile(i)
        for k in range(3):
            value = dot(tokens[r, :], attn_full[:, pl.ds(k * width, width)], NN) + qbias[k]
            if k == 0:
                queries[r, :] = (value * 0.125).astype(LOW)
            else:
                kv[k - 1, r, :] = value.astype(LOW)

    def attend(step):
        s, j = step // (width // 128), lax.rem(step, width // 128)
        lane = lax.broadcasted_iota(jnp.int32, (length, 128), 1) < 64
        cs = pl.ds(pl.multiple_of(j * 128, 128), 128)
        rs = pl.ds(pl.multiple_of(s * length, length), length)
        key, value = kv[0, rs, cs], kv[1, rs, cs]
        zero, one = jnp.zeros_like(key), jnp.ones_like(key)
        keys = (jnp.where(lane, key, zero), jnp.where(lane, zero, key))
        values = (jnp.where(lane, value, one), jnp.where(lane, one, value))
        for q in range(length // 256):
            r = pl.ds(pl.multiple_of(s * length + q * 256, 256), 256)
            query = queries[r, cs]
            parts = []
            for h in range(2):
                score = dot(query, keys[h], NT)
                expo = jnp.exp(score - jnp.max(score, axis=-1, keepdims=True))
                parts.append(dot(expo.astype(LOW), values[h], NN))
            left = lane[:256]
            top = jnp.where(left, parts[0], parts[1])
            under = pltpu.roll(jnp.where(left, parts[1], parts[0]), 64, 1)
            mixed[r, cs] = (top / under).astype(LOW)

    def middle(i):
        r = tile(i)
        pre = tokens[r, :].astype(jnp.float32) + (dot(mixed[r, :], attn_full[:, pl.ds(3 * width, width)], NT) + vec[2:3, :])
        hidden[r, :] = norm(pre, vec[3:4, :], vec[4:5, :])[0]

    def masked_rows():
        for s in range(seqs):
            r = pl.ds(s * padded, padded)
            rs = pl.ds(s * length, length)
            rows_m[0, r, :] = dot(pick[s], tokens[rs, :], NN).astype(LOW)
            mixed_m[0, r, :] = dot(pick[s], mixed[rs, :], NN).astype(LOW)
            query_m[r, :] = dot(pick[s], queries[rs, :], NN).astype(LOW)
        pre = rows_m[0].astype(jnp.float32) + (dot(mixed_m[0], attn_full[:, pl.ds(3 * width, width)], NT) + vec[2:3, :])
        value, normed, inverse = norm(pre, vec[3:4, :], vec[4:5, :])
        hid_f[...] = value
        hid_m[0] = value.astype(LOW)
        normed_one[...] = normed
        inverse_one[...] = jnp.broadcast_to(inverse, inverse_one.shape)
        swap(rows_m, 0)
        swap(mixed_m, 1)
        swap(hid_m, 2)

    def upper(k):
        f = pl.ds(pl.multiple_of(k * 768, 768), 768)
        u = dot(hid_m[0], up_full[:, f], NN) + bias[:, f]
        cumul = 0.5 * (1.0 + lax.erf(u * SQRT_HALF))
        act_m[0, :, f] = (u * cumul).astype(LOW)
        slope[:, f] = cumul + u * (jnp.exp(-0.5 * u * u) * INV_ROOT_TWO_PI)

    def after_upper():
        swap(act_m, 3)

    def lower():
        for k in range(3):
            n = pl.ds(k * 256, 256)
            ytwo[:, n] = dot(act_m[0], down_full[n, :], NT)

        pre = hid_f[...] + (ytwo[...] + vec[5:6, :])
        _, normed, inverse = norm(pre, vec[6:7, :], vec[7:8, :])
        value, dgain, dshift = norm_pull(grad[...], normed, inverse, vec[6:7, :])
        dtwo[...] = value
        dlow[0] = value.astype(LOW)
        dvec[...] = jnp.zeros_like(dvec)
        dvec[5:6, :] = jnp.sum(value, axis=0, keepdims=True)
        dvec[6:7, :] = dgain
        dvec[7:8, :] = dshift
        swap(dlow, 4)

    loads = [pltpu.make_async_copy(tokens_h, tokens, load_sem.at[4])]
    loads[0].start()

    def prepare(*refs):
        nonlocal qkv_f, out_f, up_f, down_f
        qkv_f, out_f, up_f, down_f = refs
        for k, src in enumerate((qkv_h, out_h, up_h, down_h)):
            loads.append(pltpu.make_async_copy(src, refs[k], load_sem.at[k]))
            loads[-1].start()
        bar = pltpu.get_barrier_semaphore()
        for to in [near, over, dev(z, y, flip(x), flip(c))] + [(peer(k), x * 2 + c) for k in range(1, 8)]:
            pl.semaphore_signal(bar, inc=1, device_id=to, device_id_type=MESH)
        attn_shard()
        pl.semaphore_wait(bar, 10)
        own(0)
        small_out()
        up_shard()
        down_shard()

    f = jnp.float32
    v = pltpu.VMEM
    pl.run_scoped(prepare, v(qkv_h.shape, f), v(out_h.shape, f), v(up_h.shape, f), v(down_h.shape, f))

    def save_hidden():
        keep(hidden, hidden_o, 0)

    steps = {
        "z_step": z_step, "y_step": y_step, "x_step": x_step, "own": own, "last": last, "vectors_in": vectors_in,
        "masked": masked_rows, "save_hidden": save_hidden,
    }
    pieces = {"project": project, "attend": attend, "middle": middle, "upper": upper}

    def perform(plan):
        for name, *rest in plan:
            if name == "loop":
                piece, n, table = rest

                @pl.loop(0, n)
                def _(i):
                    pieces[piece](i)
                    for k in sorted(table):
                        pl.when(i == k)(lambda k=k: perform(table[k]))
            else:
                steps[name](*rest)

    def run(*refs):
        nonlocal queries, mixed, hidden, pick, ytwo, hid_f, grad
        queries, mixed, hidden, pick, ytwo, hid_f, grad = refs
        masks()
        perform(GATHER_ORDER)
        after_upper()
        lower()
        for make in swaps:
            make().wait_recv()
        for copy in saves:
            copy.wait()

    pl.run_scoped(
        run, v((total, width), LOW), v((total, width), LOW), v((total, width), f), v((seqs, padded, length), LOW), v((count, width), f), v((count, width), f), v((count, width), f)
    )


E = 768
M = 1536
SLAB = 32
ORDER = (0, 1, 2, 3)
BESIDE_ATTENTION = {4: (("add_x", 0, 0),), 7: (("add_x", 0, 1),), 8: (("add_x", 0, 2), ("grads", 1, 0),), 9: (("add_y", 0, 0), ("grads", 1, 1), ("line", 0, 0),), 10: (("add_x", 1, 0),)}
BESIDE_KEYS = (("grads", 1, 3), ("grads", 1, 2), ("add_y", 0, 1), ("line", 0, 1), ("add_y", 0, 2), ("line", 0, 2), ("add_x", 1, 1),)
BESIDE_TOKENS = {2: (("attention_grads", 0), ("add_x", 2, 0), ("add_x", 0, 3), ("add_y", 1, 0), ("line", 1, 0),)}
BESIDE_FEED_FORWARD = {0: (("add_y", 1, 1), ("attention_grads", 1), ("add_x", 1, 2), ("line", 1, 1), ("add_x", 2, 1),), 2: (("add_x", 1, 3),), 5: (("add_y", 2, 0), ("line", 2, 0), ("attention_grads", 2), ("add_y", 1, 2),), 6: (("add_x", 2, 2), ("line", 1, 2), ("attention_grads", 3), ("add_y", 2, 1), ("add_y", 0, 3),), 8: (("line", 2, 1), ("owner", 0),), 11: (("add_x", 2, 3), ("add_y", 1, 3), ("owner", 1), ("add_y", 2, 2), ("line", 2, 2),), 13: (("add_y", 2, 3),), 14: (("owner", 2), ("relay", 1), ("middle_x", 1), ("middle_x", 0), ("relay", 0), ("arrived", 0),)}
LAST = (("middle_x", 2), ("arrived", 1), ("relay", 2), ("arrived", 2),)


def slabs(rows, body):
    @pl.loop(0, rows // SLAB)
    def _(i):
        body(pl.multiple_of(i * SLAB, SLAB))


def f32(v):
    return v.astype(jnp.float32)


def backward_part(
    rows, seqs, length, padded, sends,
    attn, up, down, vec, bias, kv, hidden_h, query_m, rows_m, mixed_m, hid_m, act_m, slope, dtwo, dlow, normed, inverse, dvec, pick_t, tokens,
    layer_h, dtokens_h, out, small_out, norm_out,
    dupper, dbias, done, dquery, part,
    acc, xb, yr, zr, mr,
    sall, sall2, ssib, sx, sy, norms, squares,
    tile_sem, out_sem, pair_s, pair_r, dup_s, dup_r, sib_s, sib_r, x_s, x_r, y_s, y_r, z_s, z_r, m_s, m_r, f_s, f_r, sm_s, sm_r, sy_r, n_s, n_r,
):
    left = right = dhid = dpre = dmix = dkv = tokens_t = htile = ytile = ltile = None
    z, y, x, c = place()
    edge = x == c
    mid = jnp.logical_not(edge)
    width = E
    count = seqs * padded
    total = seqs * length
    pair = rows * 2
    me = dev(z, y, x, c)
    above, below, beside = dev(z + 1, y, x, c), dev(z - 1, y, x, c), dev(z, flip(y), x, c)
    over, near, diag = dev(z, y, flip(x), c), dev(z, y, x, flip(c)), dev(z, y, flip(x), flip(c))
    ecol = pl.multiple_of(x * 2304, 768)
    ocol = pl.multiple_of(flip(x) * 2304, 768)

    def copy(src, dst, ss, rs, to):
        return pltpu.make_async_remote_copy(src_ref=src, dst_ref=dst, send_sem=ss, recv_sem=rs, device_id=to, device_id_type=MESH)

    def wait(cond, dst, rs):
        when(cond, lambda: copy(dst, dst, rs, rs, me).wait_recv())

    def turn(k):
        picks = ((3, 3, 0, 0), (2, 0, 3, 1), (1, 2, 1, 2), (0, 1, 2, 3))[k]
        value = jnp.int32(picks[0])
        for zv in range(1, 4):
            value = jnp.where(z == zv, picks[zv], value)
        return value

    def zrows(k):
        return pl.ds(pl.multiple_of(turn(k) * pair, pair), pair)

    def wrows(zz, yy):
        return pl.ds(pl.multiple_of((zz * 2 + yy) * rows, rows), rows)

    def add_x(p, zz):
        @pl.when(edge)
        def _():
            wait(None, xb.at[p, zrows(zz)], x_r.at[p, zz])

            base = turn(zz) * pair

            def one(i):
                r = pl.ds(pl.multiple_of(base + i, SLAB), SLAB)
                acc[p, r, pl.ds(0, E)] = (f32(acc[p, r, pl.ds(0, E)]) + f32(xb[p, r, :])).astype(LOW)

            slabs(pair, one)

        push_y(edge, p, zz, E)

    def push_x(p, zz):
        sends.start(mid, lambda: copy(xb.at[p, zrows(zz)], xb.at[p, zrows(zz)], x_s.at[p, zz], x_r.at[p, zz], over))

    def push_y(cond, p, zz, wide):
        sends.start(cond, lambda: copy(
            acc.at[p, wrows(turn(zz), flip(y)), pl.ds(0, wide)], yr.at[p, zz, :, pl.ds(0, wide)], y_s.at[p, zz], y_r.at[p, zz], beside))

    def add_into(cond, p, zz, buffer, slot, sem):
        for role, wide in ((edge, E), (mid, M)):
            @pl.when(both(cond, role))
            def _():
                wait(None, buffer.at[p, slot, :, pl.ds(0, wide)], sem)
                base = (zz * 2 + y) * rows

                def one(i):
                    here = pl.ds(pl.multiple_of(base + i, SLAB), SLAB)
                    acc[p, here, pl.ds(0, wide)] = (f32(acc[p, here, pl.ds(0, wide)]) + f32(buffer[p, slot, pl.ds(i, SLAB), pl.ds(0, wide)])).astype(LOW)

                slabs(rows, one)

    def add_y(p, zz):
        add_into(None, p, turn(zz), yr, zz, y_r.at[p, zz])

    def z_push(cond, p, spot, k, to):
        for role, wide in ((edge, E), (mid, M)):
            def make(wide=wide):
                zz, slot = spot()
                return copy(acc.at[p, wrows(zz, y), pl.ds(0, wide)], zr.at[p, slot, :, pl.ds(0, wide)], z_s.at[k, p, zz], z_r.at[k, p, zz], to)

            sends.start(lambda role=role: both(cond(), role), make)

    def line(p, t):
        def upward():
            return both(z <= t, z < 3)

        def up_spot():
            zz = jnp.where(upward(), 3 + z - t, 0)
            return zz, zz

        def downward():
            return both(3 - z <= t, z > 0)

        def down_spot():
            zz = jnp.where(downward(), z + t - 3, 0)
            return zz, jnp.where(zz == z - 1, 4, zz)

        zz = up_spot()[0]
        add_into(both(upward(), z > 0), p, zz, zr, zz, z_r.at[0, p, zz])
        z_push(upward, p, up_spot, 0, above)
        zz = down_spot()[0]
        add_into(both(downward(), z < 3), p, zz, zr, zz, z_r.at[1, p, zz])
        z_push(downward, p, down_spot, 1, below)

    def owner(p):
        add_into(z > 0, p, z, zr, z, z_r.at[0, p, z])
        add_into(z < 3, p, z, zr, 4, z_r.at[1, p, z])
        sends.start(mid, lambda: copy(acc.at[p, wrows(z, y)], mr.at[p], m_s.at[p], m_r.at[p], diag))
        base = (z * 2 + y) * rows

        @pl.when(edge)
        def _():
            def one(i):
                out[p, pl.ds(i, SLAB), pl.ds(ecol, E)] = acc[p, pl.ds(pl.multiple_of(base + i, SLAB), SLAB), pl.ds(0, E)]

            slabs(rows, one)

        for k, to in enumerate((near, over)):
            sends.start(edge, lambda k=k, to=to: copy(
                out.at[p, :, pl.ds(ecol, E)], out.at[p, :, pl.ds(ecol, E)], f_s.at[p, k], f_r.at[p, x], to))

    def middle_x(p):
        base = (z * 2 + y) * rows

        @pl.when(mid)
        def _():
            wait(None, mr.at[p], m_r.at[p])

            def one(i):
                out[p, pl.ds(i, SLAB), pl.ds(E, M)] = (f32(acc[p, pl.ds(pl.multiple_of(base + i, SLAB), SLAB), :]) + f32(mr[p, pl.ds(i, SLAB), :])).astype(LOW)

            slabs(rows, one)

        sends.start(mid, lambda: copy(out.at[p, :, pl.ds(E, M)], out.at[p, :, pl.ds(E, M)], f_s.at[p, 0], f_r.at[p, 2], near))

    def relay(p):
        wait(mid, out.at[p, :, pl.ds(ocol, E)], f_r.at[p, flip(x)])
        sends.start(mid, lambda: copy(out.at[p, :, pl.ds(ocol, E)], out.at[p, :, pl.ds(ocol, E)], f_s.at[p, 1], f_r.at[p, flip(x)], near))

    def arrived(p):
        wait(edge, out.at[p, :, pl.ds(ocol, E)], f_r.at[p, flip(x)])
        wait(mid, out.at[p, :, pl.ds(ecol, E)], f_r.at[p, x])
        wait(edge, out.at[p, :, pl.ds(E, M)], f_r.at[p, 2])

        def body(i, sums):
            v = f32(out[p, pl.ds(pl.multiple_of(i * 16, 16), 16), :])
            v = v * v
            for k in range(v.shape[1] // 128):
                sums = sums + v[:, k * 128 : (k + 1) * 128]
            return sums

        squares[...] = lax.fori_loop(0, rows // 16, body, squares[...])

    swaps = []

    def swap(ref, k):
        def make():
            return copy(ref.at[0], ref.at[1], pair_s.at[k], pair_r.at[k], near)

        make().start()
        swaps.append(make)

    def transpose_into(ref):
        for k in range(2):
            left[k] = ref[k].T

    def product(zz, ref, cols):
        return (dot(left[0, zrows(zz), :], ref[0, :, cols], NN) + dot(left[1, zrows(zz), :], ref[1, :, cols], NN)).astype(LOW)

    def grads(p, zz, ref):
        @pl.when(mid)
        def _():
            xb[p, zrows(zz), :] = product(zz, ref, pl.ds(ocol, E))

        push_x(p, zz)

        @pl.when(mid)
        def _():
            for k in range(2):
                acc[p, zrows(zz), pl.ds(k * E, E)] = product(zz, ref, pl.ds(E + k * E, E))

        push_y(mid, p, zz, M)

        @pl.when(edge)
        def _():
            acc[p, zrows(zz), pl.ds(0, E)] = product(zz, ref, pl.ds(ecol, E))

    def dup_copy(k):
        f = pl.ds(k * 768, 768)
        return copy(dupper.at[0, :, f], dupper.at[1, :, f], dup_s.at[k], dup_r.at[k], near)

    def upper_back(k):
        f = pl.ds(k * 768, 768)
        value = dot(dlow[0], down[:, f], NN) * slope[:, f]
        dbias[:, f] = jnp.sum(value, axis=0, keepdims=True)
        dupper[0, :, f] = value.astype(LOW)
        dup_copy(k).start()

    def hidden_back():
        for k in range(3):
            n = pl.ds(k * 256, 256)
            dhid[:, n] = dot(dupper[0], up[n, :], NT)

        value, dgain, dshift = norm_pull(dtwo[...] + dhid[...], normed[...], inverse[:, :1], vec[3:4, :])
        dpre[...] = value
        done[0] = value.astype(LOW)
        swap(done, 0)
        dvec[2:3, :] = jnp.sum(value, axis=0, keepdims=True)
        dvec[3:4, :] = dgain
        dvec[4:5, :] = dshift
        dmix[...] = dot(done[0], attn[:, pl.ds(3 * width, width)], NN).astype(LOW)

    def attend_back(step):
        s, j = step // 6, lax.rem(step, 6)
        cs = pl.ds(pl.multiple_of(j * 128, 128), 128)
        rs = pl.ds(pl.multiple_of(s * length, length), length)
        ms = pl.ds(pl.multiple_of(s * padded, padded), padded)
        lane = lax.broadcasted_iota(jnp.int32, (padded, 128), 1) < 64

        def halves(v):
            zero = jnp.zeros_like(v)
            return jnp.concatenate([jnp.where(lane, v, zero), jnp.where(lane, zero, v)], axis=0)

        key, value = kv[0, rs, cs], kv[1, rs, cs]
        queries, mixes = halves(query_m[ms, cs]), halves(dmix[ms, cs])
        score = dot(key, queries, NT)
        expo = jnp.exp(score - jnp.max(score, axis=0, keepdims=True))
        probs = expo / jnp.sum(expo, axis=0, keepdims=True)
        dprobs = dot(value, mixes, NT)
        dscore = (probs * (dprobs - jnp.sum(dprobs * probs, axis=0, keepdims=True))).astype(LOW)
        dkv[0, rs, cs] = dot(dscore, queries, NN).astype(LOW)
        dvalue = dot(probs.astype(LOW), mixes, NN)
        dkv[1, rs, cs] = dvalue.astype(LOW)
        dq = dot(dscore, key, TN) * 0.125
        dq = jnp.where(lane, dq[:padded], dq[padded:])
        dquery[0, ms, cs] = dq.astype(LOW)
        first = s == 0
        sums = jnp.concatenate([jnp.sum(dq, axis=0, keepdims=True), jnp.sum(dvalue, axis=0, keepdims=True)], axis=0)
        dvec[0:2, cs] = sums + jnp.where(first, 0.0, dvec[0:2, cs])

    def key_value_grads():
        for i in range(total // 256):
            r = pl.ds(i * 256, 256)
            tokens_t[:, r] = tokens[r, :].T

        def fill(store):
            @pl.loop(0, 8)
            def _(i):
                k = lax.rem(i, 2)
                n = pl.ds(pl.multiple_of(i // 2 * pair, pair), pair)
                store(n, pl.ds(pl.multiple_of(k * E, E), E), dot(tokens_t[n, :], dkv[k], NN).astype(LOW))

        @pl.when(mid)
        def _():
            def store(n, cols, value):
                acc[2, n, cols] = value

            fill(store)

        @pl.when(edge)
        def _():
            def store(n, cols, value):
                part[n, cols] = value

            fill(store)

        for zz in ORDER:
            sends.start(edge, lambda zz=zz: copy(part.at[zrows(zz)], part.at[zrows(zz)], sib_s.at[zz], sib_r.at[zz], near))

    def attention_sides():
        for k in range(2):
            left[k] = jnp.where(c == 0, rows_m[k], done[k]).T
            right[k] = jnp.where(c == 0, dquery[k], mixed_m[k])

    def attention_grads(zz):
        @pl.when(mid)
        def _():
            xb[2, zrows(zz), :] = product(zz, right, pl.ds(0, E))

        push_x(2, zz)

        @pl.when(mid)
        def _():
            wait(None, part.at[zrows(zz)], sib_r.at[zz])

            base = turn(zz) * pair

            def one(i):
                r = pl.ds(pl.multiple_of(base + i, SLAB), SLAB)
                acc[2, r, :] = (f32(acc[2, r, :]) + f32(part[r, :])).astype(LOW)

            slabs(pair, one)

        push_y(mid, 2, zz, M)

        @pl.when(edge)
        def _():
            acc[2, zrows(zz), pl.ds(0, E)] = product(zz, right, pl.ds(0, E))

    def tile_load(i):
        slot = lax.rem(i, 2)
        return pltpu.make_async_copy(hidden_h.at[pl.ds(pl.multiple_of(i * 256, 256), 256)], htile.at[slot], tile_sem.at[slot])

    def layer_store(i):
        slot = lax.rem(i, 2)
        return pltpu.make_async_copy(ltile.at[slot], layer_h.at[pl.ds(pl.multiple_of(i * 256, 256), 256)], out_sem.at[slot])

    def feed_forward(step):
        i, k = step // 4, lax.rem(step, 4)
        slot = lax.rem(i, 2)

        @pl.when(k == 0)
        def _():
            tile_load(i).wait()

            @pl.when(i + 1 < total // 256)
            def _():
                tile_load(i + 1).start()

        f = pl.ds(pl.multiple_of(k * 768, 768), 768)
        u = dot(htile[slot].astype(LOW), up[:, f], NN) + bias[:, f]
        a = (u * (0.5 * (1.0 + lax.erf(u * SQRT_HALF)))).astype(LOW)
        ytile[...] = dot(a, down[:, f], NT) + jnp.where(k == 0, htile[slot] + vec[5:6, :], ytile[...])

        @pl.when(k == 3)
        def _():
            @pl.when(i >= 2)
            def _():
                layer_store(i - 2).wait()

            ltile[slot] = norm(ytile[...], vec[6:7, :], vec[7:8, :])[0].astype(LOW)
            layer_store(i).start()

    def token_store(i):
        slot = lax.rem(i, 2)
        return pltpu.make_async_copy(htile.at[slot], dtokens_h.at[pl.ds(pl.multiple_of(i * 256, 256), 256)], out_sem.at[2 + slot])

    def masked_tokens():
        dpre[...] = dpre[...] + dot(dquery[0], attn[:, pl.ds(0, width)], NT)

    def tokens_back(i):
        slot = lax.rem(i, 2)

        @pl.when(i >= 2)
        def _():
            token_store(i - 2).wait()

        r = pl.ds(pl.multiple_of(i * 256, 256), 256)
        s = i // (length // 256)
        pick = pick_t[s, pl.ds(pl.multiple_of(lax.rem(i, length // 256) * 256, 256), 256), :]
        value = dpre[pl.ds(pl.multiple_of(s * padded, padded), padded), :]
        high = value.astype(LOW)
        rest = (value - f32(high)).astype(LOW)
        htile[slot] = (
            dot(dkv[0, r, :], attn[:, pl.ds(width, width)], NT) + dot(dkv[1, r, :], attn[:, pl.ds(2 * width, width)], NT) + (dot(pick, high, NN) + dot(pick, rest, NN))
        )
        token_store(i).start()

    def small_start():
        squares[...] = jnp.zeros_like(squares)
        for w in range(8):
            sall[w] = jnp.zeros((16, 128), jnp.float32)
            turned = dvec[...] if w == 0 else pltpu.roll(dvec[...], width - rows * w, 1)
            lane = lax.broadcasted_iota(jnp.int32, (8, 128), 1)
            sall[w, 0:8, :] = jnp.where(lane < rows, turned[:, :128], 0.0)
            for r in range(3):
                sall[w, 8 + r : 9 + r, :] = dbias[:, pl.ds(w * 384 + r * 128, 128)]
        sends.start(None, lambda: copy(sall, ssib, sm_s.at[0], sm_r.at[0], near))

    def small_x():
        wait(None, ssib, sm_r.at[0])
        ssib[...] = sall[...] + ssib[...]
        sends.start(None, lambda: copy(ssib, sx, sm_s.at[1], sm_r.at[1], over))

    w = z * 2 + y

    def peer(k):
        return lax.rem(w + k, 8)

    def small_y():
        wait(None, sx, sm_r.at[1])
        sall2[...] = ssib[...] + sx[...]
        for k in range(1, 8):
            sends.start(None, lambda k=k: copy(sall2.at[peer(k)], sy.at[w], sm_s.at[1 + k], sy_r.at[w], (peer(k), x * 2 + c)))
        sy[w] = sall2[w]

    def small_add():
        for k in range(1, 8):
            wait(None, sy.at[peer(k)], sy_r.at[peer(k)])
        value = sy[0]
        for k in range(1, 8):
            value = value + sy[k]
        small_out[...] = value

    def square_sum():
        value = small_out[...]
        total_squares = jnp.sum(squares[...] + value * value)
        norms[w] = jnp.full((8, 128), total_squares, jnp.float32)
        for k in range(1, 8):
            sends.start(None, lambda k=k: copy(norms.at[w], norms.at[w], n_s.at[k], n_r.at[w], (peer(k), x * 2 + c)))
        for k in range(1, 8):
            wait(None, norms.at[peer(k)], n_r.at[peer(k)])
        whole = norms[0]
        for k in range(1, 8):
            whole = whole + norms[k]
        norm_out[...] = jnp.sqrt(whole)

    moves = {
        "add_x": add_x, "add_y": add_y, "line": line, "owner": owner, "middle_x": middle_x, "relay": relay, "arrived": arrived,
        "grads": lambda p, zz: grads(p, zz, dupper), "attention_grads": lambda zz: attention_grads(zz),
    }
    small_moves = {("add_y", 1, 0): small_y, ("owner", 1): small_add}

    def run(steps):
        for name, *rest in steps:
            moves[name](*rest)
            small_moves.get((name, *rest), lambda: None)()

    def looped(n, body, table):
        @pl.loop(0, n)
        def _(i):
            body(i)
            for k in sorted(table):
                pl.when(i == k)(lambda k=k: run(table[k]))

    tile = total // 256
    f = jnp.float32
    v = pltpu.VMEM

    def compute(*refs):
        nonlocal left, right, dhid, dpre, dmix, dkv, tokens_t, htile, ytile, ltile
        left, right, dhid, dpre, dmix, dkv, tokens_t, htile, ytile, ltile = refs
        transpose_into(dlow)
        for zz in ORDER:
            grads(0, zz, act_m)
        for k in range(4):
            upper_back(k)
        transpose_into(hid_m)
        hidden_back()
        for k in range(4):
            dup_copy(k).wait_recv()
        looped(seqs * 6, attend_back, BESIDE_ATTENTION)
        swap(dquery, 1)
        small_start()
        key_value_grads()
        small_x()
        run(BESIDE_KEYS)
        for make in swaps:
            make().wait_recv()
        attention_sides()
        masked_tokens()
        looped(tile, tokens_back, BESIDE_TOKENS)
        for i in range(tile - 2, tile):
            token_store(i).wait()
        tile_load(0).start()
        looped(tile * 4, feed_forward, BESIDE_FEED_FORWARD)
        for i in range(tile - 2, tile):
            layer_store(i).wait()

    pl.run_scoped(
        compute,
        v((2, width, count), LOW), v((2, count, width), LOW), v((count, width), f), v((count, width), f), v((count, width), LOW), v((2, total, width), LOW),
        v((width, total), LOW), v((2, 256, width), f), v((256, width), f), v((2, 256, width), LOW),
    )
    run(LAST)
    square_sum()
    for make in swaps:
        make().wait_send()
    for k in range(4):
        dup_copy(k).wait_send()


def step_kernel(rows, seqs, length, padded, *refs):
    refs = list(refs)

    def take(n):
        got, refs[:] = refs[:n], refs[n:]
        return got

    raw = take(10)
    layer_h, dtokens_h, out, small_out, norm_out, hidden_h = take(6)
    weights, (small_full, small_f, tokens, pick_t, kv, vec, qbias, bias) = take(3), take(8)
    masked = take(11)
    query_m, rows_m, mixed_m, hid_m, act_m, slope, dtwo, dlow, dvec, normed, inverse = masked
    sems = take(8)
    sends = Sends()
    forward_part(rows, seqs, length, padded, sends, *raw, hidden_h, *weights, small_full, small_f, tokens, pick_t, kv, vec, qbias, bias, *masked, *sems)
    backward_part(
        rows, seqs, length, padded, sends, *weights, vec, bias, kv, hidden_h, query_m, rows_m, mixed_m, hid_m, act_m, slope, dtwo, dlow, normed, inverse, dvec, pick_t, tokens,
        layer_h, dtokens_h, out, small_out, norm_out, *refs,
    )
    sends.finish()


def whole_step(qkv, out, up, down, vectors, up_bias, tokens, place_m, count_m, grad_m):
    rows, cols = up.shape
    out, down, grad_m = out.T, down.T, jnp.swapaxes(grad_m, 0, 1)
    total, width = tokens.shape
    seqs, slots = place_m.shape
    length = total // seqs
    padded = -(-slots // 16) * 16
    count = seqs * padded
    shape = jax.ShapeDtypeStruct
    f = jnp.float32
    anywhere = pl.BlockSpec(memory_space=pl.ANY)
    vm = pl.BlockSpec(memory_space=pltpu.VMEM)
    dma = pltpu.SemaphoreType.DMA
    v = pltpu.VMEM
    one = (16, 128)
    scratch = [
        v((width, cols), LOW), v((width, cols), LOW), v((width, cols), LOW),
        v((8,) + one, LOW), v(one, f), v((total, width), LOW), v((seqs, length, padded), LOW), v((2, total, width), LOW), v((8, width), f), v((3, 1, width), f), v((1, cols), f),
        v((count, width), LOW), v((2, count, width), LOW), v((2, count, width), LOW), v((2, count, width), LOW), v((2, count, cols), LOW),
        v((count, cols), f), v((count, width), f), v((2, count, width), LOW), v((8, width), f), v((count, width), f), v((count, 128), f),
        dma((6, 3, 8)), dma((3, 8, 3)), dma((8,)), dma((8,)), dma((5,)), dma((1,)), dma((5,)), dma((5,)),
        v((2, count, cols), LOW), v((1, cols), f), v((2, count, width), LOW), v((2, count, width), LOW), v((width, M), LOW),
        v((3, width, M), LOW), v((3, width, E), LOW), v((3, 4, rows, M), LOW), v((3, 5, rows, M), LOW), v((3, rows, M), LOW),
        v((8,) + one, f), v((8,) + one, f), v((8,) + one, f), v((8,) + one, f), v((8,) + one, f), v((8, 8, 128), f), v(one, f),
        dma((2,)), dma((4,)), dma((2,)), dma((2,)), dma((4,)), dma((4,)), dma((4,)), dma((4,)), dma((3, 4)), dma((3, 4)), dma((3, 4)), dma((3, 4)),
        dma((2, 3, 4)), dma((2, 3, 4)), dma((3,)), dma((3,)), dma((3, 3)), dma((3, 3)), dma((9,)), dma((2,)), dma((8,)), dma((8,)), dma((8,)),
    ]
    return pl.pallas_call(
        functools.partial(step_kernel, rows, seqs, length, padded),
        out_shape=(shape((total, width), LOW), shape((total, width), f), shape((3, rows, cols), LOW), shape(one, f), shape((8, 128), f), shape((total, width), f)),
        in_specs=[anywhere] * 4 + [vm] * 2 + [anywhere, vm, pl.BlockSpec(memory_space=pltpu.SMEM), vm],
        out_specs=(anywhere, anywhere, vm, vm, vm, anywhere),
        scratch_shapes=scratch,
        compiler_params=pltpu.CompilerParams(collective_id=0, has_side_effects=True, vmem_limit_bytes=64 * 2**20 - 2**16),
    )(qkv, out, up, down, vectors, up_bias, tokens, place_m, count_m, grad_m)[:5]


def adam_kernel(layer, dtokens, norm, own, small, *refs):
    weights, firsts, seconds = refs[0:6], refs[6:12], refs[12:18]
    outs = refs[18:36]
    layer_o, dtokens_o, norm_o, layer_v, dtokens_v, sem = refs[36:]
    step_id = pl.program_id(0)
    copies_in = [pltpu.make_async_copy(layer, layer_v, sem.at[0]), pltpu.make_async_copy(dtokens, dtokens_v, sem.at[1])]
    copies_out = [pltpu.make_async_copy(layer_v, layer_o, sem.at[2]), pltpu.make_async_copy(dtokens_v, dtokens_o, sem.at[3])]

    @pl.when(step_id == 0)
    def _():
        for copy in copies_in:
            copy.start()
        norm_o[0, 0] = jnp.max(norm[...])

    @pl.when(step_id == 2)
    def _():
        for first, then in zip(copies_in, copies_out):
            first.wait()
            then.start()

    factor = CLIP_LIMIT / jnp.maximum(norm[0:1, 0:1], CLIP_LIMIT)

    def step(k, where, grad, decay, rate):
        grad = grad * factor.reshape((1,) * grad.ndim)
        weight = weights[k][where]
        first = BETA_ONE * firsts[k][where] + (1.0 - BETA_ONE) * grad
        second = BETA_TWO * seconds[k][where] + (1.0 - BETA_TWO) * grad * grad
        mean_hat = first * (1.0 / (1.0 - BETA_ONE**STEP))
        square_hat = second * (1.0 / (1.0 - BETA_TWO**STEP))
        outs[3 * k][where] = weight - rate * (mean_hat / (jnp.sqrt(square_hat) + ADAM_EPS) + decay * weight)
        outs[3 * k + 1][where] = first
        outs[3 * k + 2][where] = second

    width = weights[1].shape[1]
    for k in range(3):
        step(0, (k,), f32(own[2, :, pl.ds(k * width, width)]), DECAY_RATE, LEARN_RATE)
    everything = (slice(None), slice(None))
    step(1, everything, f32(own[2, :, pl.ds(3 * width, width)]), DECAY_RATE, OUTPUT_RATE)
    for k in range(4):
        cols = (slice(None), pl.ds(k * width, width))
        step(2, cols, f32(own[1, :, pl.ds(k * width, width)]), DECAY_RATE, LEARN_RATE)
        step(3, cols, f32(own[0, :, pl.ds(k * width, width)]), DECAY_RATE, LEARN_RATE)

    @pl.when(step_id == pl.num_programs(0) - 1)
    def _():
        for copy in copies_out:
            copy.wait()

    @pl.when(step_id == 0)
    def _():
        lanes = weights[4].shape[1]
        step(4, everything, small[0:8, 0:lanes], 0.0, VECTOR_RATE)
        step(5, everything, small[8:11, :], 0.0, BIAS_RATE)


def adam(layer, dtokens, norm, own, small, weights, moments):
    def turn(values):
        a, b, c, d, e, g = values
        return a, b.T, c, d.T, e, g.reshape(3, 128)

    arrays = turn(weights) + turn([m[0] for m in moments]) + turn([m[1] for m in moments])
    rows, cols = arrays[2].shape
    width = cols // 4
    slab = 16
    anywhere = pl.BlockSpec(memory_space=pl.ANY)
    specs = [
        pl.BlockSpec((3, slab, width), lambda i: (0, i, 0)),
        pl.BlockSpec((slab, width), lambda i: (i, 0)),
        pl.BlockSpec((slab, cols), lambda i: (i, 0)),
        pl.BlockSpec((slab, cols), lambda i: (i, 0)),
        pl.BlockSpec(arrays[4].shape, lambda i: (0, 0)),
        pl.BlockSpec(arrays[5].shape, lambda i: (0, 0)),
    ]
    outs = pl.pallas_call(
        adam_kernel,
        grid=(rows // slab,),
        out_shape=tuple(jax.ShapeDtypeStruct(a.shape, a.dtype) for a in arrays[:6] for _ in range(3))
        + (jax.ShapeDtypeStruct(layer.shape, layer.dtype), jax.ShapeDtypeStruct(dtokens.shape, dtokens.dtype), jax.ShapeDtypeStruct((1, 1), jnp.float32)),
        in_specs=[
            anywhere,
            anywhere,
            pl.BlockSpec(norm.shape, lambda i: (0, 0)),
            pl.BlockSpec((3, slab, cols), lambda i: (0, i, 0)),
            pl.BlockSpec(small.shape, lambda i: (0, 0)),
        ] + specs * 3,
        out_specs=tuple(s for s in specs for _ in range(3)) + (anywhere, anywhere, pl.BlockSpec(memory_space=pltpu.SMEM)),
        scratch_shapes=[pltpu.VMEM(layer.shape, layer.dtype), pltpu.VMEM(dtokens.shape, dtokens.dtype), pltpu.SemaphoreType.DMA((4,))],
        compiler_params=pltpu.CompilerParams(vmem_limit_bytes=64 * 2**20 - 2**16),
    )(layer, dtokens, norm, own, small, *arrays)

    def back(k, v):
        return v.T if k in (1, 3) else v.reshape(-1) if k == 5 else v

    return (outs[18], outs[19], outs[20].reshape(())) + tuple(back(i // 3, v) for i, v in enumerate(outs[:18]))


def masks(mask_place, mask_count, gradient, length):
    seqs, slots = mask_place.shape
    padded = -(-slots // 16) * 16
    live = jnp.arange(padded)[None, :] < mask_count[:, None]
    spots = jnp.pad(mask_place, ((0, 0), (0, padded - slots)), constant_values=-1)
    pick = (spots[:, :, None] == jnp.arange(length)[None, None, :]) & live[:, :, None]
    gradient = jnp.pad(gradient, ((0, 0), (0, padded - slots), (0, 0)))
    gradient = jnp.where(live[:, :, None], gradient, jnp.zeros_like(gradient))
    return pick, gradient.reshape(seqs * padded, -1)


def update(weights, moments, grads, grad_norm):
    factor = CLIP_LIMIT / jnp.maximum(grad_norm, CLIP_LIMIT)
    rates = (LEARN_RATE, OUTPUT_RATE, LEARN_RATE, LEARN_RATE, VECTOR_RATE, BIAS_RATE)
    out = ()
    for k in range(6):
        out += adam_step(weights[k], *moments[k], grads[k], factor, DECAY_RATE if k < 4 else 0.0, rates[k])
    return out


def natural(own_attn, own_up, own_down, own_vectors, own_bias):
    width = own_up.shape[1] // 4
    own_qkv = jnp.swapaxes(own_attn[:, : 3 * width].reshape(-1, 3, width), 0, 1)
    return own_qkv, own_attn[:, 3 * width :].T, own_up, own_down.T, own_vectors, own_bias


def pack(qkv, out, up, down):
    attn = jnp.concatenate([qkv[0], qkv[1], qkv[2], out.T], axis=1)
    return attn.astype(jnp.bfloat16), up.astype(jnp.bfloat16), down.T.astype(jnp.bfloat16)


def plain(tokens, mask_place, mask_count, gradient, weights, moments):
    low = jnp.bfloat16
    seqs, length, width = tokens.shape
    pick, gradient = masks(mask_place, mask_count, gradient, length)
    padded = pick.shape[1]
    flat = tokens.reshape(seqs * length, width)
    attn_w, up_w, down_w = (lax.all_gather(v, "wide", axis=0, tiled=True) for v in pack(*weights[:4]))
    vec = lax.all_gather(weights[4].astype(low), "wide", axis=1, tiled=True).astype(jnp.float32)
    bias = lax.all_gather(weights[5].astype(low), "wide", axis=0, tiled=True).astype(jnp.float32)
    wq, wk, wv, wo = (attn_w[:, k * width : (k + 1) * width] for k in range(4))
    query = (mm(flat, wq, NN) + vec[0]).astype(low)
    key = mm(flat, wk, NN, low)
    value = (mm(flat, wv, NN) + vec[1]).astype(low)
    query, key, value = (split_heads(v, seqs, length) for v in (query, key, value))
    mixed = lax.map(attend, (query, key, value)).reshape(seqs * length, width)

    def middle(rows, mixed):
        pre_one = rows.astype(jnp.float32) + (mm(mixed, wo, NT) + vec[2])
        hidden, normed, inverse = layer_norm(pre_one, vec[3], vec[4])
        hidden_low = hidden.astype(low)
        upper = mm(hidden_low, up_w, NN) + bias
        cumul = 0.5 * (1.0 + lax.erf(upper * SQRT_HALF))
        active = (upper * cumul).astype(low)
        pre_two = hidden + (mm(active, down_w, NT) + vec[5])
        return layer_norm(pre_two, vec[6], vec[7]), normed, inverse, hidden_low, upper, cumul, active

    layer_out = middle(flat, mixed)[0][0].astype(low)
    pick_low = pick.astype(low)

    def take(values):
        values = values.reshape(seqs, length, width)
        return jnp.einsum("sil,sld->sid", pick_low, values, preferred_element_type=jnp.float32).astype(low)

    rows_m = take(flat).reshape(seqs * padded, width)
    mixed_m = take(mixed).reshape(seqs * padded, width)
    query_m = split_heads(take(query), seqs, padded)
    (_, normed_two, inverse_two), normed_one, inverse_one, hidden_m, upper, cumul, active = middle(rows_m, mixed_m)
    dpre_two, dgain_two, dshift_two = norm_back(gradient.astype(jnp.float32), normed_two, inverse_two, vec[6])
    dbias_two = jnp.sum(dpre_two, axis=0)
    dtwo_low = dpre_two.astype(low)
    ddown = mm(dtwo_low, active, TN)
    dactive = mm(dtwo_low, down_w, NN)
    density = jnp.exp(-0.5 * upper * upper) * INV_ROOT_TWO_PI
    dupper = dactive * (cumul + upper * density)
    dup_bias = jnp.sum(dupper, axis=0)
    dupper_low = dupper.astype(low)
    dup = mm(hidden_m, dupper_low, TN)
    dhidden = dpre_two + mm(dupper_low, up_w, NT)
    dpre_one, dgain_one, dshift_one = norm_back(dhidden, normed_one, inverse_one, vec[3])
    dbias_out = jnp.sum(dpre_one, axis=0)
    done_low = dpre_one.astype(low)
    dout = mm(done_low, mixed_m, TN)
    dmixed = split_heads(mm(done_low, wo, NN, low), seqs, padded)
    dquery, dkey, dvalue = lax.map(attend_back, (query_m, key, value, dmixed))
    dquery = dquery.reshape(seqs * padded, width)
    dkey = dkey.reshape(seqs * length, width)
    dvalue = dvalue.reshape(seqs * length, width)
    dbias_query = jnp.sum(dquery, axis=0)
    dbias_value = jnp.sum(dvalue, axis=0)
    dquery, dkey, dvalue = dquery.astype(low), dkey.astype(low), dvalue.astype(low)
    dattn = jnp.concatenate([mm(rows_m, dquery, TN), mm(flat, dkey, TN), mm(flat, dvalue, TN), dout], axis=1)
    masked_part = dpre_one + mm(dquery, wq, NT)
    dtokens = spread(pick, masked_part) + mm(dkey, wk, NT) + mm(dvalue, wv, NT)
    dvectors = jnp.stack(
        [dbias_query, dbias_value, dbias_out, dgain_one, dshift_one, dbias_two, dgain_two, dshift_two]
    )

    def owned(value, dim):
        return lax.psum(lax.psum_scatter(value, "wide", scatter_dimension=dim, tiled=True), "narrow")

    grads = (owned(dattn, 0), owned(dup, 0), owned(ddown, 0), owned(dvectors, 1), owned(dup_bias, 0))
    grad_norm = jnp.sqrt(lax.psum(sum(jnp.sum(v * v) for v in grads), "wide"))
    return (layer_out, dtokens, grad_norm) + update(weights, moments, natural(*grads), grad_norm)


def spread(pick, rows):
    seqs, padded, length = pick.shape
    return jnp.einsum(
        "sil,sid->sld",
        pick.astype(jnp.float32),
        rows.reshape(seqs, padded, -1),
        precision=lax.Precision.HIGHEST,
        preferred_element_type=jnp.float32,
    ).reshape(seqs * length, -1)


def tailored(tokens, mask_place, mask_count, gradient, weights, moments):
    seqs, length, width = tokens.shape
    flat = tokens.reshape(seqs * length, width)
    layer_out, dtokens, own, small, grad_norm = whole_step(*weights, flat, mask_place, mask_count, gradient)
    return adam(layer_out, dtokens, grad_norm, own, small, weights, moments)


def shards(body, tokens, mask_place, mask_count, masked_output_gradient, *parameters):
    seqs, length, width = tokens.shape
    weights = parameters[0::3]
    moments = tuple(zip(parameters[1::3], parameters[2::3]))
    layer_out, dtokens, *rest = body(tokens, mask_place, mask_count, masked_output_gradient, weights, moments)
    return (layer_out.reshape(seqs, length, width), dtokens.reshape(seqs, length, width), *rest)


def solution(mesh):
    body = tailored if mesh.shape["wide"] == 8 and mesh.shape["narrow"] == 4 else plain
    data = P(("wide", "narrow"))
    rows = P("wide")
    columns = P(None, "wide")
    weights = (columns,) * 6 + (rows,) * 3 + (columns,) * 6 + (rows,) * 3
    return jax.shard_map(
        functools.partial(shards, body),
        mesh=mesh,
        in_specs=(data,) * 4 + weights,
        out_specs=(data, data, P()) + weights,
        check_vma=False,
    )
```
